32 devices in a mesh: groups: 2 (over y), det: 4 (over z), wafer: 2 (over x), rep: 2 (over core).
Axes of the slice: x: 2, y: 2, z: 4, core: 2. Of those that a mesh axis runs over, the one named last changes fastest.
Arguments:
- tod: float32 [4, 32, 4096], P(('groups', 'wafer'), 'det', 'rep'), parts along dimension 0, may hold values from -6 to 6
- psi: float32 [4, 32, 4096], P(('groups', 'wafer'), 'det', 'rep'), parts along dimension 0, may hold values from -3.140625 to 3.140625
- point_row: int32 [4, 32, 32], P(('groups', 'wafer'), 'det', 'rep'), parts along dimension 0, may hold values from 0 to 24575
- hit_list: int32 [4, 4, 2, 8, 32], P(('groups', 'wafer'), 'det', 'rep'), parts along dimension 0, may hold values from 0 to 128, as said below
- group_id: int32 [4, 32], P(('groups', 'wafer'), 'det'), parts along dimension 0, may hold values from 0 to 3, as said below
- a_zero: float32 [4, 32], P(('groups', 'wafer'), 'det'), parts along dimension 0, may hold values from 2 to 8
- band_coef: float32 [4, 32, 4], P(('groups', 'wafer'), 'det'), parts along dimension 0, may hold values from -0.2 to 0.2
- band_lag: int32 [4, 32, 4], P(('groups', 'wafer'), 'det'), parts along dimension 0, may hold values from 1 to 16
Outputs:
- solution: float32 [393216, 192], P(('groups', 'det', 'wafer')), parts along dimension 0
- residual: float32 [393216, 192], P(('groups', 'det', 'wafer')), parts along dimension 0
The draws below stay inside these ranges and needn't reach their ends.
There are 2 independent parts, one for each index of `groups`. The reference program is written for one: setup_inputs(seed, part) draws one part's arguments, and reference() takes and returns one part's arrays. A program takes and returns all parts, laid end to end along the dimension named above; each array names one. Nothing has to cross between parts.
Inputs may be any that keep to these rules, and one draw needn't show every extreme that they name: `hit_list`: every sample block of a device (numbers 0 to 127) stands exactly once in that device's table; unused entries hold 128. In every draw some owner receives 32 blocks from every device. `group_id`: in every draw one readout group of some wafer has no detector.
All inputs are finite; a program needn't handle non-finite values.
Results may differ from the reference program's by a relative error of at most 0.0003.
Values sent between devices are 32-bit elements; how exact they have to be, the bound alone decides.
No kernel may reach another device: no remote copies, remote signals or barrier semaphores. Data moves between devices by JAX's collectives and lax.ppermute only.
A program may use at most 448 MiB of HBM per device.

```python
import math
import jax
import jax.numpy as jnp
from jax import lax

BLOCKS = 196608
PBLOCK = 64
SBLOCK = 128
DET_DEV = 8
NSUB = 4
LAG = 16
NLAG = 4
ITERS = 3
WAFERS = 2
DETW = 32
NTIME = 4096
TBLK_DEV = 16
NTBLK = 32
SBLK_DEV = 128
OWNERS = 8
OWN_BLK = 24576
CAP = 32
N_DET = 4
N_REP = 2


def draw_hit_list(key, part):
    key = jax.random.fold_in(key, 11)
    hot_key, device_key = jax.random.split(key)
    hot_owner = jax.random.randint(hot_key, (), 0, OWNERS)
    device_keys = jax.random.split(device_key, WAFERS * N_DET * N_REP)

    def one_device(device_seed):
        slot_key, order_key = jax.random.split(device_seed)
        others = CAP + jax.random.permutation(slot_key, OWNERS * CAP - CAP)
        chosen = jnp.concatenate([jnp.arange(CAP, dtype=jnp.int32), others[:SBLK_DEV - CAP].astype(jnp.int32)])
        slot_owner = (chosen // CAP + hot_owner) % OWNERS
        slot_place = chosen % CAP
        block_order = jax.random.permutation(order_key, SBLK_DEV).astype(jnp.int32)
        empty_table = jnp.full((OWNERS, CAP), SBLK_DEV, jnp.int32)
        return empty_table.at[slot_owner, slot_place].set(block_order)
    return jax.vmap(one_device)(device_keys).reshape(WAFERS, N_DET, N_REP, OWNERS, CAP)


def draw_group_id(key, part):
    key = jax.random.fold_in(key, 5)
    group_key, wafer_key, empty_key = jax.random.split(key, 3)
    readout = jax.random.randint(group_key, (WAFERS, DETW), 0, NSUB).astype(jnp.int32)
    empty_wafer = jax.random.randint(wafer_key, (), 0, WAFERS)
    empty_group = jax.random.randint(empty_key, (), 0, NSUB)
    moved = jnp.where(readout == empty_group, (readout + 1) % NSUB, readout)
    chosen_row = jnp.arange(WAFERS, dtype=jnp.int32)[:, None] == empty_wafer
    return jnp.where(chosen_row, moved, readout).astype(jnp.int32)


def set_ends(values, key, least, top_value):
    dims = values.shape
    index_at = [jax.random.randint(jax.random.fold_in(key, axis), (), 0, dims[axis]) for axis in range(len(dims))]
    values = values.at[tuple(index_at)].set(least)
    longest = dims.index(max(dims))
    index_at[longest] = (index_at[longest] + 1) % dims[longest]
    return values.at[tuple(index_at)].set(top_value)


def steps_of(stream_key, shape, cuts, low, high):
    gain = 1.0
    for position, blocks in cuts:
        heights = jax.random.uniform(jax.random.fold_in(jax.random.fold_in(stream_key, 6), position), (blocks,), jnp.float32, low / len(cuts), high / len(cuts))
        gain = gain * jnp.repeat(jnp.exp(heights), shape[position] // blocks).reshape((-1,) + (1,) * (len(shape) - 1 - position))
    return gain


def centred(stream_key, dims, width, reach, shards=(), held_as=jnp.bfloat16):
    level = steps_of(stream_key, dims, shards, -0.22, 0.18) if shards else 1.0
    array = jax.random.normal(stream_key, dims, jnp.float32) * width * level
    return jnp.minimum(jnp.maximum(array, -reach), reach).astype(held_as)


def setup_inputs(seed: int = 0, part: int = 0) -> dict:
    keys = jax.random.split(jax.random.key(seed), 9)
    part_keys = jax.random.split(jax.random.fold_in(keys[8], part), 9)
    return {
        "tod": centred(part_keys[0], (WAFERS, DETW, NTIME), 1.0, 6.0, ((0, 2), (1, 4), (2, 2)), jnp.float32),
        "psi": jnp.clip(jax.random.uniform(part_keys[1], (WAFERS, DETW, NTIME), jnp.float32, -3.140625, 3.140625), -3.140625, 3.140625),
        "point_row": set_ends(jax.random.randint(part_keys[2], (WAFERS, DETW, NTBLK), 0, OWN_BLK), jax.random.fold_in(part_keys[2], 1), 0, OWN_BLK - 1).astype(jnp.int32),
        "hit_list": draw_hit_list(jax.random.fold_in(jax.random.fold_in(keys[8], part), 71), part),
        "group_id": draw_group_id(jax.random.fold_in(jax.random.fold_in(keys[8], part), 71), part),
        "a_zero": jnp.clip(jnp.exp(math.log(8.0) - 1.3862944 * jax.random.uniform(part_keys[5], (WAFERS, DETW), jnp.float32) ** steps_of(part_keys[5], (WAFERS, DETW), ((0, 2), (1, 4)), -0.2, 0.2)), 2.0, 8.0),
        "band_coef": jnp.clip(jax.random.uniform(part_keys[6], (WAFERS, DETW, NLAG), jnp.float32, -0.2, 0.2) * steps_of(part_keys[6], (WAFERS, DETW, NLAG), ((0, 2), (1, 4)), -0.4, 0.0), -0.2, 0.2),
        "band_lag": set_ends(jax.random.randint(part_keys[7], (WAFERS, DETW, NLAG), 1, LAG + 1), jax.random.fold_in(part_keys[7], 1), 1, LAG).astype(jnp.int32),
    }


prior_weight = 1.0


def reference(tod, psi, point_row, hit_list, group_id, a_zero, band_coef, band_lag):
    highest = lax.Precision.HIGHEST
    owner_grid = jnp.broadcast_to(jnp.arange(OWNERS, dtype=jnp.int32)[:, None], (OWNERS, CAP)).reshape(-1)
    tables = hit_list.reshape(WAFERS * N_DET * N_REP, OWNERS * CAP)

    def invert(slot_table):
        return jnp.zeros((SBLK_DEV + 1,), jnp.int32).at[slot_table].set(owner_grid)[:SBLK_DEV]

    owner_of = jax.vmap(invert)(tables)
    owner_of = owner_of.reshape(WAFERS, N_DET, N_REP, DET_DEV, TBLK_DEV).transpose(0, 1, 3, 2, 4)
    owner_of = owner_of.reshape(WAFERS, DETW, NTBLK)
    pixel_block = owner_of * OWN_BLK + point_row
    detector = jnp.arange(DETW, dtype=jnp.int32)
    within = (jnp.arange(SBLOCK, dtype=jnp.int32)[None, :] + 3 * detector[:, None]) % PBLOCK
    base_index = pixel_block[:, :, :, None] * (3 * PBLOCK) + within[None, :, None, :]
    base_index = base_index.reshape(WAFERS, DETW, NTIME)
    cosine_two = jnp.cos(2.0 * psi)
    sine_two = jnp.sin(2.0 * psi)

    def project(sky_map):
        flat_map = sky_map.reshape(-1)
        return flat_map[base_index] + cosine_two * flat_map[base_index + PBLOCK] + sine_two * flat_map[base_index + 2 * PBLOCK]

    def accumulate(term_one, term_two, term_three):
        accumulated = jnp.zeros((BLOCKS * 3 * PBLOCK,), jnp.float32)
        accumulated = accumulated.at[base_index].add(term_one)
        accumulated = accumulated.at[base_index + PBLOCK].add(term_two)
        accumulated = accumulated.at[base_index + 2 * PBLOCK].add(term_three)
        return accumulated.reshape(BLOCKS, 3 * PBLOCK)

    def back_project(stream):
        return accumulate(stream, cosine_two * stream, sine_two * stream)

    member = (group_id[:, :, None] == jnp.arange(NSUB, dtype=jnp.int32)[None, None, :]).astype(jnp.float32)
    counts = jnp.maximum(jnp.sum(member, axis=1), 1.0)

    def remove_common(stream):
        group_sums = jnp.einsum("wdg,wdt->wgt", member, stream, precision=highest)
        group_means = group_sums / counts[:, :, None]
        return stream - jnp.einsum("wdg,wgt->wdt", member, group_means, precision=highest)

    lag_table = (band_lag[:, :, :, None] == jnp.arange(1, LAG + 1, dtype=jnp.int32)[None, None, None, :]).astype(jnp.float32)
    lag_weight = jnp.einsum("wdj,wdjl->wdl", band_coef, lag_table, precision=highest)

    def band_filter(stream):
        padded = jnp.pad(stream, ((0, 0), (0, 0), (LAG, LAG)))
        result = a_zero[:, :, None] * stream
        for offset in range(1, LAG + 1):
            later = padded[:, :, LAG + offset:LAG + offset + NTIME]
            earlier = padded[:, :, LAG - offset:LAG - offset + NTIME]
            result = result + lag_weight[:, :, offset - 1:offset] * (later + earlier)
        return result

    def weigh_stream(stream):
        return remove_common(band_filter(remove_common(stream)))

    def operator(sky_map):
        return back_project(weigh_stream(project(sky_map))) + prior_weight * sky_map

    base_weight = jnp.broadcast_to(a_zero[:, :, None], tod.shape)
    diagonal = accumulate(base_weight, base_weight * (cosine_two * cosine_two), base_weight * (sine_two * sine_two)) + prior_weight
    inverse_diag = 1.0 / diagonal
    right_side = back_project(weigh_stream(tod))
    solution = jnp.zeros_like(right_side)
    residual = right_side
    precond = inverse_diag * residual
    direction = precond
    energy = jnp.sum(residual * precond)
    for iteration in range(ITERS):
        image_map = operator(direction)
        step_size = energy / jnp.sum(direction * image_map)
        solution = solution + step_size * direction
        residual = residual - step_size * image_map
        precond = inverse_diag * residual
        energy_next = jnp.sum(residual * precond)
        direction = precond + (energy_next / energy) * direction
        energy = energy_next
    return solution, residual
```

```python
import functools

import jax
import jax.numpy as jnp
from jax import lax
from jax.experimental import pallas as pl
from jax.experimental.pallas import tpu as pltpu
from jax.sharding import PartitionSpec as P

BLOCKS = 196608
PBLOCK = 64
SBLOCK = 128
NSUB = 4
LAG = 16
ITERS = 3


prior_weight = 1.0


def with_halo(block, sides, width):
    for axis, dim in sides:
        count = lax.axis_size(axis)
        forward = [(i, i + 1) for i in range(count - 1)]
        backward = [(target, source) for source, target in forward]
        low = lax.ppermute(
            lax.slice_in_dim(block, block.shape[dim] - width, None, axis=dim), axis, forward
        )
        high = lax.ppermute(lax.slice_in_dim(block, 0, width, axis=dim), axis, backward)
        block = jnp.concatenate([low, block, high], axis=dim)
    return block


def distributed(tod, psi, point_row, hit_list, group_id, a_zero, band_coef, band_lag):
    highest = lax.Precision.HIGHEST
    samples = tod[0]
    angles = psi[0]
    det_count, time_count = samples.shape
    time_blocks = time_count // SBLOCK
    block_count = det_count * time_blocks
    send_table = hit_list[0, 0, 0]
    owner_count, capacity = send_table.shape
    owner_rows = BLOCKS // owner_count
    block_width = 3 * PBLOCK
    detector = lax.axis_index("det") * det_count + jnp.arange(det_count, dtype=jnp.int32)
    within = (jnp.arange(SBLOCK, dtype=jnp.int32)[None, :] + 3 * detector[:, None]) % PBLOCK
    pixel_table = (within[:, :, None] == jnp.arange(PBLOCK, dtype=jnp.int32)[None, None, :]).astype(
        jnp.float32
    )
    cosine_two = jnp.cos(2.0 * angles).reshape(det_count, time_blocks, SBLOCK)
    sine_two = jnp.sin(2.0 * angles).reshape(det_count, time_blocks, SBLOCK)
    slot_ids = send_table.reshape(-1)
    row_source = jnp.concatenate([point_row[0].reshape(-1), jnp.zeros((1,), jnp.int32)])
    slot_rows = row_source[slot_ids].astype(jnp.float32).reshape(owner_count, capacity)
    member = (group_id[0][:, None] == jnp.arange(NSUB, dtype=jnp.int32)[None, :]).astype(
        jnp.float32
    )
    member_count = jnp.sum(member, axis=0)
    lag_table = (
        band_lag[0][:, :, None] == jnp.arange(1, LAG + 1, dtype=jnp.int32)[None, None, :]
    ).astype(jnp.float32)
    lag_weight = jnp.einsum("dj,djl->dl", band_coef[0], lag_table, precision=highest)
    base_weight = a_zero[0]

    def slot_payload(by_block):
        width = by_block.shape[1]
        extended = jnp.concatenate([by_block, jnp.zeros((1, width), by_block.dtype)])
        return extended[slot_ids].reshape(owner_count, capacity, width)

    def deliver(payload):
        width = payload.shape[-1]
        got_values, got_rows = (
            lax.all_to_all(payload, ("det", "wafer"), split_axis=0, concat_axis=0, tiled=True),
            lax.all_to_all(slot_rows, ("det", "wafer"), split_axis=0, concat_axis=0, tiled=True),
        )
        return (got_values, got_rows)

    def back_project(stream, squared):
        shaped = stream.reshape(det_count, time_blocks, SBLOCK)
        first = cosine_two * cosine_two if squared else cosine_two
        second = sine_two * sine_two if squared else sine_two
        stacked = jnp.stack([shaped, first * shaped, second * shaped], axis=2)
        stokes = jnp.einsum("dkcs,dsp->dkcp", stacked, pixel_table, precision=highest)
        return stokes.reshape(block_count, block_width)

    def to_owners(stream, squared):
        got_values, got_rows = deliver(slot_payload(back_project(stream, squared)))
        pair_values, pair_rows = (
            lax.all_gather(got_values, "rep", axis=0, tiled=True),
            lax.all_gather(got_rows, "rep", axis=0, tiled=True),
        )
        target_rows = pair_rows.reshape(-1).astype(jnp.int32)
        summed = (
            jnp.zeros((owner_rows, block_width), jnp.float32)
            .at[target_rows]
            .add(pair_values.reshape(-1, block_width))
        )
        return (summed, got_rows.astype(jnp.int32))

    def remove_common(stream):
        local_sums = jnp.einsum("dg,dt->gt", member, stream, precision=highest)
        group_sums, group_counts = lax.psum((local_sums, member_count), "det")
        group_means = group_sums / jnp.maximum(group_counts, 1.0)[:, None]
        return stream - jnp.einsum("dg,gt->dt", member, group_means, precision=highest)

    def band_filter(stream):
        padded = with_halo(stream, (("rep", 1),), LAG)
        result = base_weight[:, None] * stream
        for offset in range(1, LAG + 1):
            later = padded[:, LAG + offset : LAG + offset + time_count]
            earlier = padded[:, LAG - offset : LAG - offset + time_count]
            result = result + lag_weight[:, offset - 1 : offset] * (later + earlier)
        return result

    def weigh_stream(stream):
        return remove_common(band_filter(remove_common(stream)))

    weight_stream = jnp.broadcast_to(base_weight[:, None], (det_count, time_count))
    diag_sum, serve_rows = to_owners(weight_stream, True)
    inverse_diag = 1.0 / (diag_sum + prior_weight)
    right_side = to_owners(weigh_stream(samples), False)[0]
    solution = jnp.zeros_like(right_side)
    residual = right_side

    def inner(left_map, right_map):
        return lax.psum(jnp.sum(left_map * right_map), ("det", "wafer"))

    precond = inverse_diag * residual
    direction = precond
    energy = inner(residual, precond)
    for iteration in range(ITERS):
        from_blocks = direction[serve_rows.reshape(-1)].reshape(owner_count, capacity, block_width)
        return_width = from_blocks.shape[-1]
        returned = lax.all_to_all(
            from_blocks, ("det", "wafer"), split_axis=0, concat_axis=0, tiled=True
        )
        return_placed = jnp.zeros((block_count + 1, return_width), jnp.float32)
        return_placed = return_placed.at[slot_ids].set(returned.reshape(-1, return_width))
        blocks = return_placed[:block_count].reshape(det_count, time_blocks, 3, PBLOCK)
        project_stokes = jnp.einsum("dkcp,dsp->dkcs", blocks, pixel_table, precision=highest)
        project_stream = (
            project_stokes[:, :, 0]
            + cosine_two * project_stokes[:, :, 1]
            + sine_two * project_stokes[:, :, 2]
        )
        seen_stream = project_stream.reshape(det_count, time_count)
        image_map = to_owners(weigh_stream(seen_stream), False)[0] + prior_weight * direction
        step_size = energy / inner(direction, image_map)
        solution = solution + step_size * direction
        residual = residual - step_size * image_map
        precond = inverse_diag * residual
        energy_next = inner(residual, precond)
        direction = precond + energy_next / energy * direction
        energy = energy_next
    return (solution, residual)


LANES = 128
ROWS = 8
OUT_TILES = 4
BIG = float(1 << 24)
VMEM_BYTES = 60 << 20


def lane_take(block, index):
    return jnp.take_along_axis(block, index, axis=1, mode="promise_in_bounds")


def cosine_sine_double(angle):
    turns = jnp.floor(angle * 1.2732395447351628 + 0.5)
    reduced = 2.0 * angle - turns * 1.5703125
    reduced = reduced - turns * 4.837512969970703125e-4
    reduced = reduced - turns * 7.54978995489188216e-8
    square = reduced * reduced
    sine = (-1.9515295891e-4 * square + 8.3321608736e-3) * square - 1.6666654611e-1
    sine = sine * square * reduced + reduced
    cosine = (2.443315711809948e-5 * square - 1.388731625493765e-3) * square
    cosine = (cosine + 4.166664568298827e-2) * square * square - 0.5 * square + 1.0
    quarter = turns.astype(jnp.int32)
    odd = (quarter & 1) == 1
    first = jnp.where(odd, sine, cosine)
    second = jnp.where(odd, cosine, sine)
    first = jnp.where(((quarter + 1) & 2) == 2, -first, first)
    second = jnp.where((quarter & 2) == 2, -second, second)
    return first, second


def whole_part_kernel(
    shape, own_ref, part_ref, x_ref, r_ref,
    cos_ref, sin_ref, clean_ref, inverse_ref, x_map, r_map, d_map, image_map, weight_ref,
    member_ref, share_ref, base_ref, coef_ref, lag_ref, high_ref, low_ref, place_ref, full_ref,
    code_ref, table_ref, start_ref, rows_ref, sorted_ref, column_ref, x_buffer, r_buffer,
    table_smem, start_smem, twin_smem, table_sem, x_sem, r_sem,
):
    wafers, dets, reps, tiles, owners, capacity, owner_rows, lag_count = shape
    teams = wafers * dets
    devices = teams * reps
    blocks = reps * tiles
    total = devices * tiles * ROWS
    span = tiles * LANES
    params = 2 * span
    extra = params + LANES
    groups = owner_rows // LANES
    lane = lax.broadcasted_iota(jnp.int32, (ROWS, LANES), 1)
    sub = lax.broadcasted_iota(jnp.int32, (ROWS, LANES), 0)
    lane_f = lane.astype(jnp.float32)
    own = own_ref[0]
    first_row = (own * owner_rows).astype(jnp.float32)

    def wide(column):
        return jnp.broadcast_to(column, (ROWS, LANES))

    def fold(block):
        return block + pltpu.roll(block, LANES // 2, 1)

    for team in range(teams):
        values = part_ref[team * reps, :, params : params + LANES]
        base_ref[team] = wide(values[:, tiles + 1 : tiles + 2])
        for group in range(NSUB):
            member_ref[team, group] = wide(
                (values[:, tiles : tiles + 1] == float(group)).astype(jnp.float32)
            )
        for j in range(lag_count):
            at = tiles + 2 + j
            coef_ref[team, j] = wide(values[:, at : at + 1])
            lag_ref[team, j] = wide(values[:, at + lag_count : at + lag_count + 1].astype(jnp.int32))
        clean_ref[team, 0] = jnp.zeros((ROWS, LANES), jnp.float32)
        clean_ref[team, blocks + 1] = jnp.zeros((ROWS, LANES), jnp.float32)
    for wafer in range(wafers):
        for group in range(NSUB):
            count = member_ref[wafer * dets, group]
            for i in range(1, dets):
                count = count + member_ref[wafer * dets + i, group]
            count = jnp.sum(count, axis=0, keepdims=True)
            share_ref[wafer, group] = wide(1.0 / jnp.maximum(count, 1.0))

    def survey(device, carry):
        team = device // reps
        values = part_ref[device, :, params : params + LANES]
        base = base_ref[team]
        codes = jnp.full((ROWS, LANES), BIG, jnp.float32)
        for b in range(tiles):
            at = device * tiles + b
            first, second = cosine_sine_double(part_ref[device, :, b * LANES : (b + 1) * LANES])
            cos_ref[at] = first
            sin_ref[at] = second
            image_map[at, 0] = base + base
            image_map[at, 1] = fold(base * (first * first))
            image_map[at, 2] = fold(base * (second * second))
            ids = wide(values[:, b : b + 1])
            least = jnp.full((ROWS, LANES), BIG, jnp.float32)
            for other in range(devices):
                row = part_ref[other, 0:1, extra : extra + LANES]
                least = jnp.minimum(least, jnp.where(ids == row, lane_f + float(other * LANES), BIG))
            least = jnp.min(least, axis=1, keepdims=True)
            mine = (device * LANES + sub[:, 0:1] * tiles + b).astype(jnp.float32)
            weight_ref[at] = wide(jnp.where(least == mine, 0.5, 0.0))
            code = jnp.where(least < mine, mine * float(total) + least, BIG)
            codes = jnp.where(lane == b, code, codes)
            local_row = ids - first_row
            high = jnp.floor(local_row * (1.0 / LANES))
            low = local_row - high * LANES
            at_row = pl.ds(pl.multiple_of(at * ROWS, ROWS), ROWS)
            high_ref[at_row, 0:LANES] = (high == lane_f).astype(jnp.float32)
            high_ref[at_row, LANES : 2 * LANES] = (high == lane_f + LANES).astype(jnp.float32)
            low_ref[at_row, :] = (low == lane_f).astype(jnp.float32)
        code_ref[device] = codes
        return carry

    lax.fori_loop(0, devices, survey, 0)

    def exact_dot(left, right, dims):
        return lax.dot_general(
            left.astype(jnp.bfloat16), right.astype(jnp.bfloat16), (dims, ((), ())),
            preferred_element_type=jnp.float32,
        )

    depth = 2 * LANES
    hits = exact_dot(high_ref[...], low_ref[...], ((0,), (0,)))
    full = jnp.minimum(hits, 1.0)
    full_ref[...] = full
    before = (
        lax.broadcasted_iota(jnp.int32, (LANES, LANES), 0)
        < lax.broadcasted_iota(jnp.int32, (LANES, LANES), 1)
    ).astype(jnp.float32)
    above = (
        lax.broadcasted_iota(jnp.int32, (depth, depth), 1)
        < lax.broadcasted_iota(jnp.int32, (depth, depth), 0)
    ).astype(jnp.float32)
    in_tile = exact_dot(full, before, ((1,), (0,)))
    tile_sum = exact_dot(full, jnp.ones((LANES, LANES), jnp.float32), ((1,), (0,)))
    start = exact_dot(above, tile_sum, ((1,), (0,)))
    place = in_tile + start
    place_ref[...] = place.astype(jnp.int32)
    start_ref[...] = start.astype(jnp.int32)
    place_high = jnp.floor(place * (1.0 / LANES))
    place_low = place - place_high * LANES

    def rank_of(device, carry):
        at_rows = pl.ds(pl.multiple_of(device * LANES, LANES), LANES)
        high = high_ref[at_rows, :]
        rank = LANES * exact_dot(high, place_high, ((1,), (0,))) + exact_dot(
            high, place_low, ((1,), (0,))
        )
        rank = jnp.sum(rank * low_ref[at_rows, :], axis=1, keepdims=True)
        table = jnp.zeros((ROWS, LANES), jnp.float32)
        for b in range(tiles):
            table = jnp.where(lane == b, rank[b * ROWS : (b + 1) * ROWS], table)
        table_ref[device, 0:ROWS] = table.astype(jnp.int32)
        table_ref[device, ROWS : 2 * ROWS] = part_ref[device, :, extra : extra + LANES].astype(
            jnp.int32
        )
        return carry

    lax.fori_loop(0, devices, rank_of, 0)
    copies = (
        pltpu.make_async_copy(table_ref, table_smem, table_sem.at[0]),
        pltpu.make_async_copy(start_ref, start_smem, table_sem.at[1]),
    )
    for copy in copies:
        copy.start()
    for copy in copies:
        copy.wait()

    def next_code(last):
        found = jnp.full((ROWS, LANES), BIG, jnp.float32)
        for device in range(devices):
            codes = code_ref[device]
            found = jnp.minimum(found, jnp.where(codes > last, codes, BIG))
        return jnp.min(found)

    def take_twin(state):
        count, code = state
        twin_smem[count] = code.astype(jnp.int32)
        return count + 1, next_code(code)

    twin_count, _ = lax.while_loop(
        lambda state: state[1] < BIG, take_twin, (jnp.int32(0), next_code(jnp.float32(-1.0)))
    )

    def locate(number):
        device = lax.div(number, LANES)
        inside = lax.rem(number, LANES)
        row = lax.div(inside, tiles)
        detector = lax.rem(lax.div(device, reps), dets) * ROWS + row
        return device * tiles + lax.rem(inside, tiles), row, detector

    def merge_twins(target):
        def gather_one(n, carry):
            code = twin_smem[n]
            at, row, detector = locate(lax.div(code, total))
            lead_at, lead_row, lead_detector = locate(lax.rem(code, total))
            shift = (3 * (detector - lead_detector)) & (PBLOCK - 1)
            for c in range(3):
                moved = pltpu.roll(wide(target[at, c, pl.ds(row, 1), :]), shift, 1)
                target[lead_at, c, pl.ds(lead_row, 1), :] += moved[0:1]
            return carry

        def spread_one(n, carry):
            code = twin_smem[n]
            at, row, detector = locate(lax.div(code, total))
            lead_at, lead_row, lead_detector = locate(lax.rem(code, total))
            shift = (3 * (lead_detector - detector)) & (PBLOCK - 1)
            for c in range(3):
                moved = pltpu.roll(wide(target[lead_at, c, pl.ds(lead_row, 1), :]), shift, 1)
                target[at, c, pl.ds(row, 1), :] = moved[0:1]
            return carry

        lax.fori_loop(0, twin_count, gather_one, 0)
        lax.fori_loop(0, twin_count, spread_one, 0)

    def remove_common(wafer, streams):
        means = []
        for group in range(NSUB):
            part = member_ref[wafer * dets, group] * streams[0]
            for i in range(1, dets):
                part = part + member_ref[wafer * dets + i, group] * streams[i]
            means.append(jnp.sum(part, axis=0, keepdims=True) * share_ref[wafer, group])
        result = []
        for i in range(dets):
            stream = streams[i]
            for group in range(NSUB):
                stream = stream - member_ref[wafer * dets + i, group] * means[group]
            result.append(stream)
        return result

    def loop(count, body, carry, unroll):
        def several(n, carry):
            for k in range(unroll):
                carry = body(n * unroll + k, carry)
            return carry

        return lax.fori_loop(0, count // unroll, several, carry)

    def first_removal(stream_of, carry):
        for wafer in range(wafers):

            def one_time(block, carry):
                streams = []
                for i in range(dets):
                    stream, carry = stream_of(wafer * dets + i, block, carry)
                    streams.append(stream)
                for i, stream in enumerate(remove_common(wafer, streams)):
                    clean_ref[wafer * dets + i, block + 1] = stream
                return carry

            carry = loop(blocks, one_time, carry, 2)
        return carry

    def filter_and_return(target):
        carry = jnp.zeros((ROWS, LANES), jnp.float32)
        for wafer in range(wafers):

            def one_time(block, carry):
                streams = []
                for i in range(dets):
                    team = wafer * dets + i
                    here = clean_ref[team, block + 1]
                    after = clean_ref[team, block + 2]
                    ahead = clean_ref[team, block]
                    result = base_ref[team] * here
                    for j in range(lag_count):
                        lag = lag_ref[team, j]
                        later = lane_take(
                            jnp.where(lane < lag, after, here), (lane + lag) & (LANES - 1)
                        )
                        earlier = lane_take(
                            jnp.where(lane >= LANES - lag, ahead, here), (lane - lag) & (LANES - 1)
                        )
                        result = result + coef_ref[team, j] * (later + earlier)
                    carry = carry + here * result
                    streams.append(result)
                for i, stream in enumerate(remove_common(wafer, streams)):
                    at = (wafer * dets + i) * blocks + block
                    target[at, 0] = fold(stream)
                    target[at, 1] = fold(cos_ref[at] * stream)
                    target[at, 2] = fold(sin_ref[at] * stream)
                return carry

            carry = loop(blocks, one_time, carry, 2)
        return carry

    def whole_sum(values):
        values = jnp.sum(values, axis=0, keepdims=True)
        return wide(jnp.sum(values, axis=1, keepdims=True))

    zero = jnp.zeros((ROWS, LANES), jnp.float32)
    count = teams * blocks

    merge_twins(image_map)

    def data_stream(team, block, carry):
        device = team * reps + lax.div(block, tiles)
        at = pl.multiple_of(span + lax.rem(block, tiles) * LANES, LANES)
        return part_ref[device, :, pl.ds(at, LANES)], carry

    first_removal(data_stream, 0)
    filter_and_return(r_map)
    merge_twins(r_map)

    def begin(at, carry):
        parts = zero
        for c in range(3):
            inverse = 1.0 / (image_map[at, c] + prior_weight)
            inverse_ref[at, c] = inverse
            residual = r_map[at, c]
            parts = parts + residual * (inverse * residual)
        return carry + weight_ref[at] * parts

    energy = whole_sum(loop(count, begin, zero, 2))
    factor = zero
    for iteration in range(ITERS):
        last = iteration == ITERS - 1

        def seen_stream(team, block, carry):
            at = team * blocks + block
            parts = []
            for c in range(3):
                part = inverse_ref[at, c] * r_map[at, c]
                if iteration:
                    part = part + factor * d_map[at, c]
                d_map[at, c] = part
                parts.append(part)
            squares = parts[0] * parts[0] + parts[1] * parts[1] + parts[2] * parts[2]
            stream = parts[0] + cos_ref[at] * parts[1] + sin_ref[at] * parts[2]
            return stream, carry + weight_ref[at] * squares

        prior = first_removal(seen_stream, zero)
        product = filter_and_return(image_map)
        merge_twins(image_map)
        step = energy / whole_sum(product + prior_weight * prior)

        def advance(at):
            new_x, new_r = [], []
            for c in range(3):
                direction = d_map[at, c]
                image = image_map[at, c] + prior_weight * direction
                move = step * direction
                new_x.append(x_map[at, c] + move if iteration else move)
                new_r.append(r_map[at, c] - step * image)
            return new_x, new_r

        if not last:

            def update(at, carry):
                new_x, new_r = advance(at)
                parts = zero
                for c in range(3):
                    x_map[at, c] = new_x[c]
                    r_map[at, c] = new_r[c]
                    parts = parts + new_r[c] * (inverse_ref[at, c] * new_r[c])
                return carry + weight_ref[at] * parts

            next_energy = whole_sum(loop(count, update, zero, 2))
            factor = next_energy / energy
            energy = next_energy
        else:

            def place_pixels(at, carry):
                new_x, new_r = advance(at)
                team = lax.rem(lax.div(at, blocks), dets)
                turn = (lane - 3 * (team * ROWS + sub)) & (LANES - 1)
                values = [lane_take(value, turn) for value in new_x + new_r]
                rows = pl.ds(pl.multiple_of(at * ROWS, ROWS), ROWS)
                for c in range(3):
                    rows_ref[rows, c * LANES : (c + 1) * LANES] = jnp.where(
                        lane < PBLOCK, values[2 * c], values[2 * c + 1]
                    )
                return carry

            loop(count, place_pixels, 0, 2)

    slots = devices * capacity
    flat = own * capacity
    hit_row = ROWS + 1 + lax.div(flat, LANES)
    hit_lane = lax.rem(flat, LANES)

    def pick(device, carry):
        for c in range(capacity):
            number = table_smem[device, hit_row, hit_lane + c]
            valid = number < LANES
            number = jnp.where(valid, number, 0)
            row = lax.div(number, tiles)
            column = lax.rem(number, tiles)
            source = (device * tiles + column) * ROWS + row
            target = jnp.where(valid, table_smem[device, row, column], slots)
            sorted_ref[pl.ds(target, 1), :] = rows_ref[pl.ds(source, 1), :]
        return carry

    lax.fori_loop(0, devices, pick, 0)
    for tile in range(slots // LANES):
        column_ref[tile] = sorted_ref[tile * LANES : (tile + 1) * LANES, :].T

    height = 3 * PBLOCK
    step_width = OUT_TILES * LANES

    def store_copies(n, slot):
        to = pl.ds(pl.multiple_of(n * step_width, step_width), step_width)
        return (
            pltpu.make_async_copy(x_buffer.at[slot], x_ref.at[:, to], x_sem.at[slot]),
            pltpu.make_async_copy(r_buffer.at[slot], r_ref.at[:, to], r_sem.at[slot]),
        )

    def write(n, carry):
        slot = lax.rem(n, 2)

        @pl.when(n >= 2)
        def _():
            for copy in store_copies(n - 2, slot):
                copy.wait()

        for k in range(OUT_TILES):
            group = n * OUT_TILES + k
            tile = lax.div(start_smem[group, 0], LANES)
            index = wide(place_ref[pl.ds(group, 1), :]) & (LANES - 1)
            split = wide(start_ref[pl.ds(group, 1), :]) & (LANES - 1)
            present = wide(full_ref[pl.ds(group, 1), :]) > 0.0
            follow = lane < split
            for s in range(height // ROWS):
                for buffer, offset in ((x_buffer, 0), (r_buffer, height)):
                    rows = slice(offset + s * ROWS, offset + (s + 1) * ROWS)
                    window = jnp.where(follow, column_ref[tile + 1, rows, :], column_ref[tile, rows, :])
                    buffer[slot, s * ROWS : (s + 1) * ROWS, k * LANES : (k + 1) * LANES] = jnp.where(
                        present, lane_take(window, index), 0.0
                    )
        for copy in store_copies(n, slot):
            copy.start()
        return carry

    steps = groups // OUT_TILES
    lax.fori_loop(0, steps, write, 0)
    for n in (steps - 2, steps - 1):
        for copy in store_copies(n, n % 2):
            copy.wait()


def part_shape(sizes, tod, hit_list, band_lag):
    det_count, time_count = tod.shape[1:]
    owners, capacity = hit_list.shape[3:]
    return (
        sizes["wafer"], sizes["det"], sizes["rep"], time_count // SBLOCK,
        owners, capacity, BLOCKS // owners, band_lag.shape[2],
    ), det_count


def fits_one_device(shape, det_count):
    wafers, dets, reps, tiles, owners, capacity, owner_rows, lag_count = shape
    devices = wafers * dets * reps
    total = devices * tiles * det_count
    table_rows = owners * capacity // LANES
    groups = owner_rows // LANES
    return (
        det_count == ROWS
        and tiles * ROWS == LANES
        and tiles + 2 + 2 * lag_count <= LANES
        and reps * tiles % 2 == 0
        and owners * capacity % LANES == 0
        and LANES % capacity == 0
        and table_rows < ROWS
        and devices * capacity % LANES == 0
        and owner_rows % (LANES * OUT_TILES) == 0
        and 2 * OUT_TILES <= groups <= 2 * LANES
        and total * total < BIG
    )


def whole_part(shape, tod, psi, point_row, hit_list, group_id, a_zero, band_coef, band_lag):
    wafers, dets, reps, tiles, owners, capacity, owner_rows, lag_count = shape
    teams = wafers * dets
    devices = teams * reps
    blocks = reps * tiles
    count = devices * tiles
    total = count * ROWS
    slots = devices * capacity
    table = hit_list[0, 0, 0]
    found = table[:, :, None] == jnp.arange(LANES, dtype=jnp.int32)[None, None, :]
    owner = jnp.arange(owners, dtype=jnp.int32)[:, None, None]
    owner_of = jnp.sum(jnp.where(found, owner, 0), axis=(0, 1)).reshape(ROWS, tiles)
    ids = (owner_of * owner_rows + point_row[0]).astype(jnp.float32)
    per_detector = jnp.concatenate(
        [
            ids, group_id[0][:, None].astype(jnp.float32), a_zero[0][:, None], band_coef[0],
            band_lag[0].astype(jnp.float32),
        ],
        axis=1,
    )
    per_detector = jnp.pad(per_detector, ((0, 0), (0, LANES - per_detector.shape[1])))
    tables = jnp.concatenate([ids.reshape(-1), table.reshape(-1).astype(jnp.float32)])
    tables = jnp.pad(tables, (0, ROWS * LANES - tables.shape[0])).reshape(ROWS, LANES)
    payload = jnp.concatenate([psi[0], tod[0], per_detector, tables], axis=1)
    gathered = lax.all_gather(payload, ("wafer", "det", "rep"), axis=0, tiled=False)
    own = (lax.axis_index("det") * wafers + lax.axis_index("wafer")).astype(jnp.int32).reshape(1)

    height = 3 * PBLOCK
    f32 = jnp.float32
    stream = pltpu.VMEM((count, ROWS, LANES), f32)
    sky = pltpu.VMEM((count, 3, ROWS, LANES), f32)
    x_turned, r_turned = pl.pallas_call(
        functools.partial(whole_part_kernel, shape),
        out_shape=[jax.ShapeDtypeStruct((height, owner_rows), f32)] * 2,
        in_specs=[pl.BlockSpec(memory_space=pltpu.SMEM), pl.BlockSpec(memory_space=pltpu.VMEM)],
        out_specs=[pl.BlockSpec(memory_space=pl.ANY)] * 2,
        scratch_shapes=[
            stream, stream, pltpu.VMEM((teams, blocks + 2, ROWS, LANES), f32),
            sky, sky, sky, sky, sky, stream,
            pltpu.VMEM((teams, NSUB, ROWS, LANES), f32),
            pltpu.VMEM((wafers, NSUB, ROWS, LANES), f32),
            pltpu.VMEM((teams, ROWS, LANES), f32),
            pltpu.VMEM((teams, lag_count, ROWS, LANES), f32),
            pltpu.VMEM((teams, lag_count, ROWS, LANES), jnp.int32),
            pltpu.VMEM((total, 2 * LANES), f32),
            pltpu.VMEM((total, LANES), f32),
            pltpu.VMEM((2 * LANES, LANES), jnp.int32),
            pltpu.VMEM((2 * LANES, LANES), f32),
            pltpu.VMEM((devices, ROWS, LANES), f32),
            pltpu.VMEM((devices, 2 * ROWS, LANES), jnp.int32),
            pltpu.VMEM((2 * LANES, LANES), jnp.int32),
            pltpu.VMEM((total, 2 * height), f32),
            pltpu.VMEM((slots + ROWS, 2 * height), f32),
            pltpu.VMEM((slots // LANES + 2, 2 * height, LANES), f32),
            pltpu.VMEM((2, height, OUT_TILES * LANES), f32),
            pltpu.VMEM((2, height, OUT_TILES * LANES), f32),
            pltpu.SMEM((devices, 2 * ROWS, LANES), jnp.int32),
            pltpu.SMEM((2 * LANES, LANES), jnp.int32),
            pltpu.SMEM((total,), jnp.int32),
            pltpu.SemaphoreType.DMA((2,)),
            pltpu.SemaphoreType.DMA((2,)),
            pltpu.SemaphoreType.DMA((2,)),
        ],
        compiler_params=pltpu.CompilerParams(vmem_limit_bytes=VMEM_BYTES),
        name="map_maker",
    )(own, gathered)
    return x_turned.T, r_turned.T


def local(sizes, *arguments):
    tod, hit_list, band_lag = arguments[0], arguments[3], arguments[7]
    shape, det_count = part_shape(sizes, tod, hit_list, band_lag)
    if fits_one_device(shape, det_count):
        return whole_part(shape, *arguments)
    return distributed(*arguments)


def solution(mesh):
    placed = (
        P(("groups", "wafer"), "det", "rep"),
        P(("groups", "wafer"), "det", "rep"),
        P(("groups", "wafer"), "det", "rep"),
        P(("groups", "wafer"), "det", "rep", None, None),
        P(("groups", "wafer"), "det"),
        P(("groups", "wafer"), "det"),
        P(("groups", "wafer"), "det", None),
        P(("groups", "wafer"), "det", None),
    )
    return jax.shard_map(
        functools.partial(local, mesh.shape),
        mesh=mesh,
        in_specs=placed,
        out_specs=(P(("groups", "det", "wafer"), None), P(("groups", "det", "wafer"), None)),
        check_vma=False,
    )
```

```python
import functools

import jax
import jax.numpy as jnp
from jax import lax
from jax.experimental import pallas as pl
from jax.experimental.pallas import tpu as pltpu
from jax.sharding import PartitionSpec as P

BLOCKS = 196608
PBLOCK = 64
SBLOCK = 128
NSUB = 4
LAG = 16
ITERS = 3


prior_weight = 1.0


def with_halo(block, sides, width):
    for axis, dim in sides:
        count = lax.axis_size(axis)
        forward = [(i, i + 1) for i in range(count - 1)]
        backward = [(target, source) for source, target in forward]
        low = lax.ppermute(
            lax.slice_in_dim(block, block.shape[dim] - width, None, axis=dim), axis, forward
        )
        high = lax.ppermute(lax.slice_in_dim(block, 0, width, axis=dim), axis, backward)
        block = jnp.concatenate([low, block, high], axis=dim)
    return block


def distributed(tod, psi, point_row, hit_list, group_id, a_zero, band_coef, band_lag):
    highest = lax.Precision.HIGHEST
    samples = tod[0]
    angles = psi[0]
    det_count, time_count = samples.shape
    time_blocks = time_count // SBLOCK
    block_count = det_count * time_blocks
    send_table = hit_list[0, 0, 0]
    owner_count, capacity = send_table.shape
    owner_rows = BLOCKS // owner_count
    block_width = 3 * PBLOCK
    detector = lax.axis_index("det") * det_count + jnp.arange(det_count, dtype=jnp.int32)
    within = (jnp.arange(SBLOCK, dtype=jnp.int32)[None, :] + 3 * detector[:, None]) % PBLOCK
    pixel_table = (within[:, :, None] == jnp.arange(PBLOCK, dtype=jnp.int32)[None, None, :]).astype(
        jnp.float32
    )
    cosine_two = jnp.cos(2.0 * angles).reshape(det_count, time_blocks, SBLOCK)
    sine_two = jnp.sin(2.0 * angles).reshape(det_count, time_blocks, SBLOCK)
    slot_ids = send_table.reshape(-1)
    row_source = jnp.concatenate([point_row[0].reshape(-1), jnp.zeros((1,), jnp.int32)])
    slot_rows = row_source[slot_ids].astype(jnp.float32).reshape(owner_count, capacity)
    member = (group_id[0][:, None] == jnp.arange(NSUB, dtype=jnp.int32)[None, :]).astype(
        jnp.float32
    )
    member_count = jnp.sum(member, axis=0)
    lag_table = (
        band_lag[0][:, :, None] == jnp.arange(1, LAG + 1, dtype=jnp.int32)[None, None, :]
    ).astype(jnp.float32)
    lag_weight = jnp.einsum("dj,djl->dl", band_coef[0], lag_table, precision=highest)
    base_weight = a_zero[0]

    def slot_payload(by_block):
        width = by_block.shape[1]
        extended = jnp.concatenate([by_block, jnp.zeros((1, width), by_block.dtype)])
        return extended[slot_ids].reshape(owner_count, capacity, width)

    def deliver(payload):
        width = payload.shape[-1]
        got_values, got_rows = (
            lax.all_to_all(payload, ("det", "wafer"), split_axis=0, concat_axis=0, tiled=True),
            lax.all_to_all(slot_rows, ("det", "wafer"), split_axis=0, concat_axis=0, tiled=True),
        )
        return (got_values, got_rows)

    def back_project(stream, squared):
        shaped = stream.reshape(det_count, time_blocks, SBLOCK)
        first = cosine_two * cosine_two if squared else cosine_two
        second = sine_two * sine_two if squared else sine_two
        stacked = jnp.stack([shaped, first * shaped, second * shaped], axis=2)
        stokes = jnp.einsum("dkcs,dsp->dkcp", stacked, pixel_table, precision=highest)
        return stokes.reshape(block_count, block_width)

    def to_owners(stream, squared):
        got_values, got_rows = deliver(slot_payload(back_project(stream, squared)))
        pair_values, pair_rows = (
            lax.all_gather(got_values, "rep", axis=0, tiled=True),
            lax.all_gather(got_rows, "rep", axis=0, tiled=True),
        )
        target_rows = pair_rows.reshape(-1).astype(jnp.int32)
        summed = (
            jnp.zeros((owner_rows, block_width), jnp.float32)
            .at[target_rows]
            .add(pair_values.reshape(-1, block_width))
        )
        return (summed, got_rows.astype(jnp.int32))

    def remove_common(stream):
        local_sums = jnp.einsum("dg,dt->gt", member, stream, precision=highest)
        group_sums, group_counts = lax.psum((local_sums, member_count), "det")
        group_means = group_sums / jnp.maximum(group_counts, 1.0)[:, None]
        return stream - jnp.einsum("dg,gt->dt", member, group_means, precision=highest)

    def band_filter(stream):
        padded = with_halo(stream, (("rep", 1),), LAG)
        result = base_weight[:, None] * stream
        for offset in range(1, LAG + 1):
            later = padded[:, LAG + offset : LAG + offset + time_count]
            earlier = padded[:, LAG - offset : LAG - offset + time_count]
            result = result + lag_weight[:, offset - 1 : offset] * (later + earlier)
        return result

    def weigh_stream(stream):
        return remove_common(band_filter(remove_common(stream)))

    weight_stream = jnp.broadcast_to(base_weight[:, None], (det_count, time_count))
    diag_sum, serve_rows = to_owners(weight_stream, True)
    inverse_diag = 1.0 / (diag_sum + prior_weight)
    right_side = to_owners(weigh_stream(samples), False)[0]
    solution = jnp.zeros_like(right_side)
    residual = right_side

    def inner(left_map, right_map):
        return lax.psum(jnp.sum(left_map * right_map), ("det", "wafer"))

    precond = inverse_diag * residual
    direction = precond
    energy = inner(residual, precond)
    for iteration in range(ITERS):
        from_blocks = direction[serve_rows.reshape(-1)].reshape(owner_count, capacity, block_width)
        return_width = from_blocks.shape[-1]
        returned = lax.all_to_all(
            from_blocks, ("det", "wafer"), split_axis=0, concat_axis=0, tiled=True
        )
        return_placed = jnp.zeros((block_count + 1, return_width), jnp.float32)
        return_placed = return_placed.at[slot_ids].set(returned.reshape(-1, return_width))
        blocks = return_placed[:block_count].reshape(det_count, time_blocks, 3, PBLOCK)
        project_stokes = jnp.einsum("dkcp,dsp->dkcs", blocks, pixel_table, precision=highest)
        project_stream = (
            project_stokes[:, :, 0]
            + cosine_two * project_stokes[:, :, 1]
            + sine_two * project_stokes[:, :, 2]
        )
        seen_stream = project_stream.reshape(det_count, time_count)
        image_map = to_owners(weigh_stream(seen_stream), False)[0] + prior_weight * direction
        step_size = energy / inner(direction, image_map)
        solution = solution + step_size * direction
        residual = residual - step_size * image_map
        precond = inverse_diag * residual
        energy_next = inner(residual, precond)
        direction = precond + energy_next / energy * direction
        energy = energy_next
    return (solution, residual)


LANES = 128
ROWS = 8
OUT_TILES = 4
PAIR_BATCH = 4
BIG = float(1 << 24)
VMEM_BYTES = 60 << 20


def lane_take(block, index):
    return jnp.take_along_axis(block, index, axis=1, mode="promise_in_bounds")


def wide(values):
    return jnp.broadcast_to(values, (ROWS, LANES))


def tile_iotas():
    lane = lax.broadcasted_iota(jnp.int32, (ROWS, LANES), 1)
    sub = lax.broadcasted_iota(jnp.int32, (ROWS, LANES), 0)
    return lane, sub


def cosine_sine_double(angle):
    turns = jnp.floor(angle * 1.2732395447351628 + 0.5)
    reduced = 2.0 * angle - turns * 1.5703125
    reduced = reduced - turns * 4.837512969970703125e-4
    reduced = reduced - turns * 7.54978995489188216e-8
    square = reduced * reduced
    sine = (-1.9515295891e-4 * square + 8.3321608736e-3) * square - 1.6666654611e-1
    sine = sine * square * reduced + reduced
    cosine = (2.443315711809948e-5 * square - 1.388731625493765e-3) * square
    cosine = (cosine + 4.166664568298827e-2) * square * square - 0.5 * square + 1.0
    quarter = turns.astype(jnp.int32)
    odd = (quarter & 1) == 1
    first = jnp.where(odd, sine, cosine)
    second = jnp.where(odd, cosine, sine)
    first = jnp.where(((quarter + 1) & 2) == 2, -first, first)
    second = jnp.where((quarter & 2) == 2, -second, second)
    return first, second


def pack_kernel(shape, row_ref, hit_ref, group_ref, base_ref, coef_ref, lag_ref, out_ref):
    wafers, dets, reps, tiles, owners, capacity, owner_rows, lag_count = shape
    lane, sub = tile_iotas()
    lists = hit_ref[...]
    owner_hits = jnp.zeros((ROWS, LANES), jnp.float32)
    for c in range(capacity):
        owner_hits = owner_hits + jnp.where(wide(lists[:, c : c + 1]) == lane, 1.0, 0.0)
    owner_of = jnp.sum(owner_hits * sub.astype(jnp.float32), axis=0, keepdims=True)
    owner_of = lane_take(wide(owner_of), (lane + sub * tiles) & (LANES - 1))
    spread = jnp.zeros((ROWS, LANES), jnp.float32)
    rows = row_ref[...].astype(jnp.float32)
    for b in range(tiles):
        spread = jnp.where(lane == b, wide(rows[:, b : b + 1]), spread)
    ids = jnp.where(lane < tiles, owner_of * float(owner_rows) + spread, 0.0)

    def column(row):
        values = jnp.zeros((ROWS, LANES), jnp.float32)
        for k in range(ROWS):
            values = jnp.where(sub == k, wide(row[:, k : k + 1]), values)
        return values

    table = jnp.where(lane == tiles, column(group_ref[...].astype(jnp.float32)), ids)
    table = jnp.where(lane == tiles + 1, column(base_ref[...]), table)
    for j in range(lag_count):
        at = tiles + 2 + j
        table = jnp.where(lane == at, column(coef_ref[j : j + 1, :]), table)
        lag = lag_ref[j : j + 1, :].astype(jnp.float32)
        table = jnp.where(lane == at + lag_count, column(lag), table)
    out_ref[:, 0:LANES] = table
    along = jnp.where((lane & (ROWS - 1)) == sub, lane_take(ids, lane >> 3), 0.0)
    out_ref[:, LANES : 2 * LANES] = wide(jnp.sum(along, axis=0, keepdims=True))
    hits = jnp.full((ROWS, LANES), LANES, jnp.int32)
    for c in range(capacity):
        number = wide(lists[:, c : c + 1])
        place = (number & (tiles - 1)) * ROWS + (number >> (tiles.bit_length() - 1))
        hits = jnp.where(lane == c, jnp.where(number < LANES, place, LANES), hits)
    out_ref[:, 2 * LANES : 3 * LANES] = hits.astype(jnp.float32)


def list_kernel(
    shape, own_ref, part_ref,
    weight_ref, place_ref, full_ref, start_ref, size_ref, pair_ref, group_ref, source_ref, target_ref,
    code_ref, high_ref, low_ref, table_ref, table_smem, table_sem,
):
    wafers, dets, reps, tiles, owners, capacity, owner_rows, lag_count = shape
    devices = wafers * dets * reps
    blocks = reps * tiles
    total = devices * tiles * ROWS
    slots = devices * capacity
    lane, sub = tile_iotas()
    lane_f = lane.astype(jnp.float32)
    own = own_ref[0]
    first_row = (own * owner_rows).astype(jnp.float32)
    many = float(total * total)

    def exact_dot(left, right):
        return jnp.dot(
            left.astype(jnp.bfloat16), right.astype(jnp.bfloat16),
            preferred_element_type=jnp.float32,
        )

    depth = 2 * LANES
    tall = lax.broadcasted_iota(jnp.int32, (depth, LANES), 0).astype(jnp.float32)

    def survey(device, hits):
        values = part_ref[device, :, 0:LANES]
        codes = jnp.full((ROWS, LANES), BIG, jnp.float32)
        for b in range(tiles):
            at = device * tiles + b
            ids = wide(values[:, b : b + 1])
            least = jnp.full((ROWS, LANES), BIG, jnp.float32)
            matches = jnp.zeros((ROWS, LANES), jnp.float32)
            for other in range(devices):
                same = ids == part_ref[other, :, LANES : 2 * LANES]
                least = jnp.minimum(least, jnp.where(same, lane_f + float(other * LANES), BIG))
                matches = matches + jnp.where(same, 1.0, 0.0)
            least = jnp.min(least, axis=1, keepdims=True)
            matches = jnp.sum(matches, axis=1, keepdims=True)
            mine = (at * ROWS + sub[:, 0:1]).astype(jnp.float32)
            weight_ref[at] = wide(jnp.where(least == mine, 0.5, 0.0))
            code = mine * float(total) + least + jnp.where(matches > 2.0, many, 0.0)
            code = jnp.where(least < mine, code, BIG)
            codes = jnp.where(lane == b, code, codes)
            local_row = ids - first_row
            high = jnp.floor(local_row * (1.0 / LANES))
            low = local_row - high * LANES
            at_row = pl.ds(pl.multiple_of(at * ROWS, ROWS), ROWS)
            high_ref[at_row, 0:LANES] = (high == lane_f).astype(jnp.float32)
            high_ref[at_row, LANES:depth] = (high == lane_f + LANES).astype(jnp.float32)
            low_ref[at_row, :] = (low == lane_f).astype(jnp.float32)
        code_ref[device] = codes
        along = jnp.floor((part_ref[device, 0:1, LANES : 2 * LANES] - first_row) * (1.0 / LANES))
        along = (jnp.broadcast_to(along, (depth, LANES)) == tall).astype(jnp.float32)
        at_rows = pl.ds(pl.multiple_of(device * LANES, LANES), LANES)
        return hits + exact_dot(along, low_ref[at_rows, :])

    hits = lax.fori_loop(0, devices, survey, jnp.zeros((depth, LANES), jnp.float32))
    full = jnp.minimum(hits, 1.0)
    full_ref[...] = full
    before = (
        lax.broadcasted_iota(jnp.int32, (LANES, LANES), 0)
        < lax.broadcasted_iota(jnp.int32, (LANES, LANES), 1)
    ).astype(jnp.float32)
    above = (
        lax.broadcasted_iota(jnp.int32, (depth, depth), 1)
        < lax.broadcasted_iota(jnp.int32, (depth, depth), 0)
    ).astype(jnp.float32)
    tile_sum = exact_dot(full, jnp.ones((LANES, LANES), jnp.float32))
    start = exact_dot(above, tile_sum)
    place = exact_dot(full, before) + start
    place_ref[...] = place.astype(jnp.int32)
    start_ref[...] = start.astype(jnp.int32)
    place_high = jnp.floor(place * (1.0 / LANES))
    place_low = place - place_high * LANES

    def rank_of(device, carry):
        at_rows = pl.ds(pl.multiple_of(device * LANES, LANES), LANES)
        high = high_ref[at_rows, :]
        rank = LANES * exact_dot(high, place_high) + exact_dot(high, place_low)
        rank = jnp.sum(rank * low_ref[at_rows, :], axis=1, keepdims=True)
        table = jnp.zeros((ROWS, LANES), jnp.float32)
        for b in range(tiles):
            table = jnp.where(lane == b, rank[b * ROWS : (b + 1) * ROWS], table)
        table_ref[device, 0:ROWS] = table.astype(jnp.int32)
        table_ref[device, ROWS : 2 * ROWS] = part_ref[device, :, 2 * LANES : 3 * LANES].astype(
            jnp.int32
        )
        return carry

    lax.fori_loop(0, devices, rank_of, 0)
    copy = pltpu.make_async_copy(table_ref, table_smem, table_sem.at[0])
    copy.start()

    def next_code(last):
        found = jnp.full((ROWS, LANES), BIG, jnp.float32)
        for device in range(devices):
            codes = code_ref[device]
            found = jnp.minimum(found, jnp.where(codes > last, codes, BIG))
        return jnp.min(found)

    def detector(key):
        return lax.rem(lax.div(key, blocks * ROWS), dets) * ROWS + lax.rem(key, ROWS)

    def take(list_ref, offset):
        def one(state):
            count, code = state
            number = (code - offset).astype(jnp.int32)
            key = lax.div(number, total)
            lead = lax.rem(number, total)
            list_ref[0, count] = key
            list_ref[1, count] = lead
            list_ref[2, count] = (3 * (detector(key) - detector(lead))) & (PBLOCK - 1)
            return count + 1, next_code(code)

        return one

    pairs, code = lax.while_loop(
        lambda state: state[1] < many, take(pair_ref, 0.0),
        (jnp.int32(0), next_code(jnp.float32(-1.0))),
    )
    grouped, _ = lax.while_loop(
        lambda state: state[1] < BIG, take(group_ref, many), (jnp.int32(0), code)
    )
    batches = lax.div(pairs + PAIR_BATCH - 1, PAIR_BATCH)

    def fill(n, carry):
        pair_ref[0, n] = total
        pair_ref[1, n] = total + 1
        pair_ref[2, n] = 0
        return carry

    lax.fori_loop(pairs, batches * PAIR_BATCH, fill, 0)
    size_ref[0] = batches
    size_ref[1] = grouped
    copy.wait()

    def pick(device, carry):
        for c in range(capacity):
            number = table_smem[device, ROWS + own, c]
            valid = number < LANES
            number = jnp.where(valid, number, 0)
            rank = table_smem[device, number & (ROWS - 1), number >> 3]
            source_ref[device, c] = device * LANES + number
            target_ref[device, c] = jnp.where(valid, rank, slots)
        return carry

    lax.fori_loop(0, devices, pick, 0)


def map_kernel(
    shape, size_ref, pair_ref, group_ref, source_ref, target_ref, start_smem,
    part_ref, psi_ref, tod_ref, weight_ref, place_ref, full_ref, start_ref, x_ref, r_ref,
    cos_ref, sin_ref, clean_ref, noise_ref, inverse_ref, x_map, r_map, d_map, image_map,
    member_ref, share_ref, base_ref, coef_ref, lag_ref,
    rows_ref, sorted_ref, column_ref, x_buffer, r_buffer, x_sem, r_sem,
):
    wafers, dets, reps, tiles, owners, capacity, owner_rows, lag_count = shape
    teams = wafers * dets
    devices = teams * reps
    blocks = reps * tiles
    count = devices * tiles
    groups = owner_rows // LANES
    slots = devices * capacity
    lane, sub = tile_iotas()
    zero = jnp.zeros((ROWS, LANES), jnp.float32)

    def fold(block):
        return block + pltpu.roll(block, LANES // 2, 1)

    def whole_sum(values):
        values = jnp.sum(values, axis=0, keepdims=True)
        return wide(jnp.sum(values, axis=1, keepdims=True))

    def loop(times, body, carry, unroll):
        def several(n, carry):
            for k in range(unroll):
                carry = body(n * unroll + k, carry)
            return carry

        return lax.fori_loop(0, times // unroll, several, carry)

    for team in range(teams):
        values = part_ref[team * reps, :, 0:LANES]
        base_ref[team] = wide(values[:, tiles + 1 : tiles + 2])
        for group in range(NSUB):
            member_ref[team, group] = wide(
                (values[:, tiles : tiles + 1] == float(group)).astype(jnp.float32)
            )
        for j in range(lag_count):
            at = tiles + 2 + j
            coef_ref[team, j] = wide(values[:, at : at + 1])
            lag_ref[team, j] = wide(values[:, at + lag_count : at + lag_count + 1].astype(jnp.int32))
        clean_ref[team, 0] = zero
        clean_ref[team, blocks + 1] = zero
    for wafer in range(wafers):
        for group in range(NSUB):
            members = member_ref[wafer * dets, group]
            for i in range(1, dets):
                members = members + member_ref[wafer * dets + i, group]
            members = jnp.sum(members, axis=0, keepdims=True)
            share_ref[wafer, group] = wide(1.0 / jnp.maximum(members, 1.0))
    for c in range(3):
        image_map[count, c] = zero
        r_map[count, c] = zero

    def survey(at, carry):
        device = lax.div(at, tiles)
        place = pl.ds(pl.multiple_of(lax.rem(at, tiles) * LANES, LANES), LANES)
        first, second = cosine_sine_double(psi_ref[device, :, place])
        base = base_ref[lax.div(device, reps)]
        cos_ref[at] = first
        sin_ref[at] = second
        image_map[at, 0] = base + base
        image_map[at, 1] = fold(base * (first * first))
        image_map[at, 2] = fold(base * (second * second))
        return carry

    loop(count, survey, 0, 4)

    def merge_twins(target):
        def pair_batch(n, carry):
            found = []
            for k in range(PAIR_BATCH):
                key, lead, shift = (pair_ref[j, n * PAIR_BATCH + k] for j in range(3))
                spots = [
                    (lax.shift_right_logical(spot, 3), pl.ds(spot & (ROWS - 1), 1))
                    for spot in (key, lead)
                ]
                values = [[target[at, c, row, :] for c in range(3)] for at, row in spots]
                found.append((spots, shift, values))
            for spots, shift, values in found:
                turns = (shift, (LANES - shift) & (LANES - 1))
                for (at, row), own, other, turn in zip(
                    spots, values, values[::-1], turns[::-1]
                ):
                    for c in range(3):
                        target[at, c, row, :] = own[c] + pltpu.roll(wide(other[c]), turn, 1)[0:1]
            return carry

        def gather_one(n, carry):
            key, lead, shift = (group_ref[j, n] for j in range(3))
            at, row = lax.shift_right_logical(key, 3), key & (ROWS - 1)
            lead_at, lead_row = lax.shift_right_logical(lead, 3), lead & (ROWS - 1)
            for c in range(3):
                moved = pltpu.roll(wide(target[at, c, pl.ds(row, 1), :]), shift, 1)
                target[lead_at, c, pl.ds(lead_row, 1), :] += moved[0:1]
            return carry

        def spread_one(n, carry):
            key, lead, shift = (group_ref[j, n] for j in range(3))
            at, row = lax.shift_right_logical(key, 3), key & (ROWS - 1)
            lead_at, lead_row = lax.shift_right_logical(lead, 3), lead & (ROWS - 1)
            turn = (LANES - shift) & (LANES - 1)
            for c in range(3):
                moved = pltpu.roll(wide(target[lead_at, c, pl.ds(lead_row, 1), :]), turn, 1)
                target[at, c, pl.ds(row, 1), :] = moved[0:1]
            return carry

        lax.fori_loop(0, size_ref[0], pair_batch, 0)
        lax.fori_loop(0, size_ref[1], gather_one, 0)
        lax.fori_loop(0, size_ref[1], spread_one, 0)

    def remove_common(members, shares, streams):
        means = []
        for group in range(NSUB):
            part = members[0][group] * streams[0]
            for i in range(1, dets):
                part = part + members[i][group] * streams[i]
            means.append(jnp.sum(part, axis=0, keepdims=True) * shares[group])
        result = []
        for i in range(dets):
            common = members[i][0] * means[0]
            for group in range(1, NSUB):
                common = common + members[i][group] * means[group]
            result.append(streams[i] - common)
        return result

    def removal_pass(stream_of, place, carry):
        for wafer in range(wafers):
            first = wafer * dets
            members = [[member_ref[first + i, g] for g in range(NSUB)] for i in range(dets)]
            shares = [share_ref[wafer, g] for g in range(NSUB)]

            def one_time(block, carry):
                streams = []
                for i in range(dets):
                    stream, carry = stream_of(first + i, block, carry)
                    streams.append(stream)
                for i, stream in enumerate(remove_common(members, shares, streams)):
                    place(first + i, block, stream)
                return carry

            carry = loop(blocks, one_time, carry, 2)
        return carry

    def keep_clean(team, block, stream):
        clean_ref[team, block + 1] = stream

    def filter_pass():
        def one_team(team, carry):
            base = base_ref[team]
            coefs = [coef_ref[team, j] for j in range(lag_count)]
            lags = [lag_ref[team, j] for j in range(lag_count)]
            later_turns = [(lane + lag) & (LANES - 1) for lag in lags]
            earlier_turns = [(lane - lag) & (LANES - 1) for lag in lags]

            def one_time(block, state):
                ahead, here, carry = state
                after = clean_ref[team, block + 2]
                result = base * here
                for j in range(lag_count):
                    later = lane_take(jnp.where(lane < lags[j], after, here), later_turns[j])
                    earlier = lane_take(
                        jnp.where(lane >= LANES - lags[j], ahead, here), earlier_turns[j]
                    )
                    result = result + coefs[j] * (later + earlier)
                noise_ref[team * blocks + block] = result
                return here, after, carry + here * result

            return loop(blocks, one_time, (clean_ref[team, 0], clean_ref[team, 1], carry), 4)[2]

        return lax.fori_loop(0, teams, one_team, zero)

    def return_pass(target):
        def noise_stream(team, block, carry):
            return noise_ref[team * blocks + block], carry

        def add_back(team, block, stream):
            at = team * blocks + block
            target[at, 0] = fold(stream)
            target[at, 1] = fold(cos_ref[at] * stream)
            target[at, 2] = fold(sin_ref[at] * stream)

        removal_pass(noise_stream, add_back, 0)
        merge_twins(target)

    merge_twins(image_map)

    def data_stream(team, block, carry):
        device = team * reps + lax.div(block, tiles)
        at = pl.multiple_of(lax.rem(block, tiles) * LANES, LANES)
        return tod_ref[device, :, pl.ds(at, LANES)], carry

    removal_pass(data_stream, keep_clean, 0)
    filter_pass()
    return_pass(r_map)

    def begin(at, carry):
        parts = zero
        for c in range(3):
            inverse = 1.0 / (image_map[at, c] + prior_weight)
            inverse_ref[at, c] = inverse
            residual = r_map[at, c]
            parts = parts + residual * (inverse * residual)
        return carry + weight_ref[at] * parts

    energy = whole_sum(loop(count, begin, zero, 4))
    factor = zero
    for iteration in range(ITERS):
        last = iteration == ITERS - 1

        def seen_stream(team, block, carry):
            at = team * blocks + block
            parts = []
            for c in range(3):
                part = inverse_ref[at, c] * r_map[at, c]
                if iteration:
                    part = part + factor * d_map[at, c]
                d_map[at, c] = part
                parts.append(part)
            squares = parts[0] * parts[0] + parts[1] * parts[1] + parts[2] * parts[2]
            stream = parts[0] + cos_ref[at] * parts[1] + sin_ref[at] * parts[2]
            return stream, carry + weight_ref[at] * squares

        prior = removal_pass(seen_stream, keep_clean, zero)
        product = filter_pass()
        return_pass(image_map)
        step = energy / whole_sum(product + prior_weight * prior)

        def advance(at):
            new_x, new_r = [], []
            for c in range(3):
                direction = d_map[at, c]
                image = image_map[at, c] + prior_weight * direction
                move = step * direction
                new_x.append(x_map[at, c] + move if iteration else move)
                new_r.append(r_map[at, c] - step * image)
            return new_x, new_r

        if not last:

            def update(at, carry):
                new_x, new_r = advance(at)
                parts = zero
                for c in range(3):
                    x_map[at, c] = new_x[c]
                    r_map[at, c] = new_r[c]
                    parts = parts + new_r[c] * (inverse_ref[at, c] * new_r[c])
                return carry + weight_ref[at] * parts

            next_energy = whole_sum(loop(count, update, zero, 4))
            factor = next_energy / energy
            energy = next_energy
        else:

            def place_pixels(at, carry):
                new_x, new_r = advance(at)
                team = lax.rem(lax.div(at, blocks), dets)
                turn = (lane - 3 * (team * ROWS + sub)) & (LANES - 1)
                values = [lane_take(value, turn) for value in new_x + new_r]
                rows = pl.ds(pl.multiple_of(at * ROWS, ROWS), ROWS)
                for c in range(3):
                    rows_ref[rows, c * LANES : (c + 1) * LANES] = jnp.where(
                        lane < PBLOCK, values[2 * c], values[2 * c + 1]
                    )
                return carry

            loop(count, place_pixels, 0, 4)

    def pick(device, carry):
        for c in range(capacity):
            source, target = source_ref[device, c], target_ref[device, c]
            sorted_ref[pl.ds(target, 1), :] = rows_ref[pl.ds(source, 1), :]
        return carry

    lax.fori_loop(0, devices, pick, 0)
    for tile in range(slots // LANES):
        column_ref[tile] = sorted_ref[tile * LANES : (tile + 1) * LANES, :].T

    height = 3 * PBLOCK
    step_width = OUT_TILES * LANES

    def store_copies(n, slot):
        to = pl.ds(pl.multiple_of(n * step_width, step_width), step_width)
        return (
            pltpu.make_async_copy(x_buffer.at[slot], x_ref.at[:, to], x_sem.at[slot]),
            pltpu.make_async_copy(r_buffer.at[slot], r_ref.at[:, to], r_sem.at[slot]),
        )

    def write(n, carry):
        slot = lax.rem(n, 2)

        @pl.when(n >= 2)
        def _():
            for copy in store_copies(n - 2, slot):
                copy.wait()

        for k in range(OUT_TILES):
            group = n * OUT_TILES + k
            tile = lax.div(start_smem[group, 0], LANES)
            index = wide(place_ref[pl.ds(group, 1), :]) & (LANES - 1)
            split = wide(start_ref[pl.ds(group, 1), :]) & (LANES - 1)
            present = wide(full_ref[pl.ds(group, 1), :]) > 0.0
            follow = lane < split
            for s in range(height // ROWS):
                for buffer, offset in ((x_buffer, 0), (r_buffer, height)):
                    rows = slice(offset + s * ROWS, offset + (s + 1) * ROWS)
                    window = jnp.where(follow, column_ref[tile + 1, rows, :], column_ref[tile, rows, :])
                    buffer[slot, s * ROWS : (s + 1) * ROWS, k * LANES : (k + 1) * LANES] = jnp.where(
                        present, lane_take(window, index), 0.0
                    )
        for copy in store_copies(n, slot):
            copy.start()
        return carry

    steps = groups // OUT_TILES
    lax.fori_loop(0, steps, write, 0)
    for n in (steps - 2, steps - 1):
        for copy in store_copies(n, n % 2):
            copy.wait()


def part_shape(sizes, tod, hit_list, band_lag):
    det_count, time_count = tod.shape[1:]
    owners, capacity = hit_list.shape[3:]
    return (
        sizes["wafer"], sizes["det"], sizes["rep"], time_count // SBLOCK,
        owners, capacity, BLOCKS // owners, band_lag.shape[2],
    ), det_count


def fits_one_device(shape, det_count):
    wafers, dets, reps, tiles, owners, capacity, owner_rows, lag_count = shape
    devices = wafers * dets * reps
    total = devices * tiles * det_count
    groups = owner_rows // LANES
    return (
        det_count == ROWS
        and owners == ROWS
        and tiles * ROWS == LANES
        and tiles + 2 + 2 * lag_count <= LANES
        and reps * tiles % 4 == 0
        and capacity <= LANES
        and devices * capacity % LANES == 0
        and owner_rows % (LANES * OUT_TILES) == 0
        and 2 * OUT_TILES <= groups <= 2 * LANES
        and 2 * total * total <= BIG
    )


def whole_part(shape, tod, psi, point_row, hit_list, group_id, a_zero, band_coef, band_lag):
    wafers, dets, reps, tiles, owners, capacity, owner_rows, lag_count = shape
    teams = wafers * dets
    devices = teams * reps
    blocks = reps * tiles
    count = devices * tiles
    total = count * ROWS
    slots = devices * capacity
    height = 3 * PBLOCK
    f32, i32 = jnp.float32, jnp.int32
    part_axes = ("wafer", "det", "rep")
    vmem, smem = pl.BlockSpec(memory_space=pltpu.VMEM), pl.BlockSpec(memory_space=pltpu.SMEM)
    params = pltpu.CompilerParams(vmem_limit_bytes=VMEM_BYTES)
    tables = pl.pallas_call(
        functools.partial(pack_kernel, shape),
        out_shape=jax.ShapeDtypeStruct((ROWS, 3 * LANES), f32),
        in_specs=[vmem] * 6,
        out_specs=vmem,
        compiler_params=params,
        name="pack",
    )(point_row[0], hit_list[0, 0, 0], group_id, a_zero, band_coef[0].T, band_lag[0].T)
    tables = lax.all_gather(tables, part_axes, axis=0, tiled=False)
    angles = lax.all_gather(psi, part_axes, axis=0, tiled=True)
    samples = lax.all_gather(tod, part_axes, axis=0, tiled=True)
    own = (lax.axis_index("det") * wafers + lax.axis_index("wafer")).astype(i32).reshape(1)
    weight, place, full, start, size, pair, group, source, target = pl.pallas_call(
        functools.partial(list_kernel, shape),
        out_shape=[
            jax.ShapeDtypeStruct((count, ROWS, LANES), f32),
            jax.ShapeDtypeStruct((2 * LANES, LANES), i32),
            jax.ShapeDtypeStruct((2 * LANES, LANES), f32),
            jax.ShapeDtypeStruct((2 * LANES, LANES), i32),
            jax.ShapeDtypeStruct((2,), i32),
            jax.ShapeDtypeStruct((3, total), i32),
            jax.ShapeDtypeStruct((3, total), i32),
            jax.ShapeDtypeStruct((devices, capacity), i32),
            jax.ShapeDtypeStruct((devices, capacity), i32),
        ],
        in_specs=[smem, vmem],
        out_specs=[vmem] * 4 + [smem] * 5,
        scratch_shapes=[
            pltpu.VMEM((devices, ROWS, LANES), f32),
            pltpu.VMEM((total, 2 * LANES), f32),
            pltpu.VMEM((total, LANES), f32),
            pltpu.VMEM((devices, 2 * ROWS, LANES), i32),
            pltpu.SMEM((devices, 2 * ROWS, LANES), i32),
            pltpu.SemaphoreType.DMA((1,)),
        ],
        compiler_params=params,
        cost_estimate=pl.CostEstimate(flops=10**9, bytes_accessed=4 * 10**6, transcendentals=0),
        name="lists",
    )(own, tables)
    stream = pltpu.VMEM((count, ROWS, LANES), f32)
    sky = pltpu.VMEM((count, 3, ROWS, LANES), f32)
    sky_and_spare = pltpu.VMEM((count + 1, 3, ROWS, LANES), f32)
    x_turned, r_turned = pl.pallas_call(
        functools.partial(map_kernel, shape),
        out_shape=[jax.ShapeDtypeStruct((height, owner_rows), f32)] * 2,
        in_specs=[smem] * 6 + [vmem] * 7,
        out_specs=[pl.BlockSpec(memory_space=pl.ANY)] * 2,
        scratch_shapes=[
            stream, stream, pltpu.VMEM((teams, blocks + 2, ROWS, LANES), f32), stream,
            sky, sky, sky_and_spare, sky, sky_and_spare,
            pltpu.VMEM((teams, NSUB, ROWS, LANES), f32),
            pltpu.VMEM((wafers, NSUB, ROWS, LANES), f32),
            pltpu.VMEM((teams, ROWS, LANES), f32),
            pltpu.VMEM((teams, lag_count, ROWS, LANES), f32),
            pltpu.VMEM((teams, lag_count, ROWS, LANES), i32),
            pltpu.VMEM((total, 2 * height), f32),
            pltpu.VMEM((slots + ROWS, 2 * height), f32),
            pltpu.VMEM((slots // LANES + 2, 2 * height, LANES), f32),
            pltpu.VMEM((2, height, OUT_TILES * LANES), f32),
            pltpu.VMEM((2, height, OUT_TILES * LANES), f32),
            pltpu.SemaphoreType.DMA((2,)),
            pltpu.SemaphoreType.DMA((2,)),
        ],
        compiler_params=params,
        name="map_maker",
    )(
        size, pair, group, source, target, start[:, 0:1], tables, angles, samples, weight, place,
        full, start,
    )
    return x_turned.T, r_turned.T


def local(sizes, *arguments):
    tod, hit_list, band_lag = arguments[0], arguments[3], arguments[7]
    shape, det_count = part_shape(sizes, tod, hit_list, band_lag)
    if fits_one_device(shape, det_count):
        return whole_part(shape, *arguments)
    return distributed(*arguments)


def solution(mesh):
    placed = (
        P(("groups", "wafer"), "det", "rep"),
        P(("groups", "wafer"), "det", "rep"),
        P(("groups", "wafer"), "det", "rep"),
        P(("groups", "wafer"), "det", "rep", None, None),
        P(("groups", "wafer"), "det"),
        P(("groups", "wafer"), "det"),
        P(("groups", "wafer"), "det", None),
        P(("groups", "wafer"), "det", None),
    )
    return jax.shard_map(
        functools.partial(local, mesh.shape),
        mesh=mesh,
        in_specs=placed,
        out_specs=(P(("groups", "det", "wafer"), None), P(("groups", "det", "wafer"), None)),
        check_vma=False,
    )
```

```python
import functools

import jax
import jax.numpy as jnp
from jax import lax
from jax.experimental import pallas as pl
from jax.experimental.pallas import tpu as pltpu
from jax.sharding import PartitionSpec as P

BLOCKS = 196608
PBLOCK = 64
SBLOCK = 128
NSUB = 4
LAG = 16
ITERS = 3


prior_weight = 1.0


def with_halo(block, sides, width):
    for axis, dim in sides:
        count = lax.axis_size(axis)
        forward = [(i, i + 1) for i in range(count - 1)]
        backward = [(target, source) for source, target in forward]
        low = lax.ppermute(
            lax.slice_in_dim(block, block.shape[dim] - width, None, axis=dim), axis, forward
        )
        high = lax.ppermute(lax.slice_in_dim(block, 0, width, axis=dim), axis, backward)
        block = jnp.concatenate([low, block, high], axis=dim)
    return block


def distributed(tod, psi, point_row, hit_list, group_id, a_zero, band_coef, band_lag):
    highest = lax.Precision.HIGHEST
    samples = tod[0]
    angles = psi[0]
    det_count, time_count = samples.shape
    time_blocks = time_count // SBLOCK
    block_count = det_count * time_blocks
    send_table = hit_list[0, 0, 0]
    owner_count, capacity = send_table.shape
    owner_rows = BLOCKS // owner_count
    block_width = 3 * PBLOCK
    detector = lax.axis_index("det") * det_count + jnp.arange(det_count, dtype=jnp.int32)
    within = (jnp.arange(SBLOCK, dtype=jnp.int32)[None, :] + 3 * detector[:, None]) % PBLOCK
    pixel_table = (within[:, :, None] == jnp.arange(PBLOCK, dtype=jnp.int32)[None, None, :]).astype(
        jnp.float32
    )
    cosine_two = jnp.cos(2.0 * angles).reshape(det_count, time_blocks, SBLOCK)
    sine_two = jnp.sin(2.0 * angles).reshape(det_count, time_blocks, SBLOCK)
    slot_ids = send_table.reshape(-1)
    row_source = jnp.concatenate([point_row[0].reshape(-1), jnp.zeros((1,), jnp.int32)])
    slot_rows = row_source[slot_ids].astype(jnp.float32).reshape(owner_count, capacity)
    member = (group_id[0][:, None] == jnp.arange(NSUB, dtype=jnp.int32)[None, :]).astype(
        jnp.float32
    )
    member_count = jnp.sum(member, axis=0)
    lag_table = (
        band_lag[0][:, :, None] == jnp.arange(1, LAG + 1, dtype=jnp.int32)[None, None, :]
    ).astype(jnp.float32)
    lag_weight = jnp.einsum("dj,djl->dl", band_coef[0], lag_table, precision=highest)
    base_weight = a_zero[0]

    def slot_payload(by_block):
        width = by_block.shape[1]
        extended = jnp.concatenate([by_block, jnp.zeros((1, width), by_block.dtype)])
        return extended[slot_ids].reshape(owner_count, capacity, width)

    def deliver(payload):
        width = payload.shape[-1]
        got_values, got_rows = (
            lax.all_to_all(payload, ("det", "wafer"), split_axis=0, concat_axis=0, tiled=True),
            lax.all_to_all(slot_rows, ("det", "wafer"), split_axis=0, concat_axis=0, tiled=True),
        )
        return (got_values, got_rows)

    def back_project(stream, squared):
        shaped = stream.reshape(det_count, time_blocks, SBLOCK)
        first = cosine_two * cosine_two if squared else cosine_two
        second = sine_two * sine_two if squared else sine_two
        stacked = jnp.stack([shaped, first * shaped, second * shaped], axis=2)
        stokes = jnp.einsum("dkcs,dsp->dkcp", stacked, pixel_table, precision=highest)
        return stokes.reshape(block_count, block_width)

    def to_owners(stream, squared):
        got_values, got_rows = deliver(slot_payload(back_project(stream, squared)))
        pair_values, pair_rows = (
            lax.all_gather(got_values, "rep", axis=0, tiled=True),
            lax.all_gather(got_rows, "rep", axis=0, tiled=True),
        )
        target_rows = pair_rows.reshape(-1).astype(jnp.int32)
        summed = (
            jnp.zeros((owner_rows, block_width), jnp.float32)
            .at[target_rows]
            .add(pair_values.reshape(-1, block_width))
        )
        return (summed, got_rows.astype(jnp.int32))

    def remove_common(stream):
        local_sums = jnp.einsum("dg,dt->gt", member, stream, precision=highest)
        group_sums, group_counts = lax.psum((local_sums, member_count), "det")
        group_means = group_sums / jnp.maximum(group_counts, 1.0)[:, None]
        return stream - jnp.einsum("dg,gt->dt", member, group_means, precision=highest)

    def band_filter(stream):
        padded = with_halo(stream, (("rep", 1),), LAG)
        result = base_weight[:, None] * stream
        for offset in range(1, LAG + 1):
            later = padded[:, LAG + offset : LAG + offset + time_count]
            earlier = padded[:, LAG - offset : LAG - offset + time_count]
            result = result + lag_weight[:, offset - 1 : offset] * (later + earlier)
        return result

    def weigh_stream(stream):
        return remove_common(band_filter(remove_common(stream)))

    weight_stream = jnp.broadcast_to(base_weight[:, None], (det_count, time_count))
    diag_sum, serve_rows = to_owners(weight_stream, True)
    inverse_diag = 1.0 / (diag_sum + prior_weight)
    right_side = to_owners(weigh_stream(samples), False)[0]
    solution = jnp.zeros_like(right_side)
    residual = right_side

    def inner(left_map, right_map):
        return lax.psum(jnp.sum(left_map * right_map), ("det", "wafer"))

    precond = inverse_diag * residual
    direction = precond
    energy = inner(residual, precond)
    for iteration in range(ITERS):
        from_blocks = direction[serve_rows.reshape(-1)].reshape(owner_count, capacity, block_width)
        return_width = from_blocks.shape[-1]
        returned = lax.all_to_all(
            from_blocks, ("det", "wafer"), split_axis=0, concat_axis=0, tiled=True
        )
        return_placed = jnp.zeros((block_count + 1, return_width), jnp.float32)
        return_placed = return_placed.at[slot_ids].set(returned.reshape(-1, return_width))
        blocks = return_placed[:block_count].reshape(det_count, time_blocks, 3, PBLOCK)
        project_stokes = jnp.einsum("dkcp,dsp->dkcs", blocks, pixel_table, precision=highest)
        project_stream = (
            project_stokes[:, :, 0]
            + cosine_two * project_stokes[:, :, 1]
            + sine_two * project_stokes[:, :, 2]
        )
        seen_stream = project_stream.reshape(det_count, time_count)
        image_map = to_owners(weigh_stream(seen_stream), False)[0] + prior_weight * direction
        step_size = energy / inner(direction, image_map)
        solution = solution + step_size * direction
        residual = residual - step_size * image_map
        precond = inverse_diag * residual
        energy_next = inner(residual, precond)
        direction = precond + energy_next / energy * direction
        energy = energy_next
    return (solution, residual)


LANES = 128
ROWS = 8
OUT_TILES = 4
PAIR_BATCH = 4
TIME_BATCH = 4
BIG = float(1 << 24)
VMEM_BYTES = 60 << 20


def lane_take(block, index):
    return jnp.take_along_axis(block, index, axis=1, mode="promise_in_bounds")


def wide(values):
    return jnp.broadcast_to(values, (ROWS, LANES))


def tile_iotas():
    lane = lax.broadcasted_iota(jnp.int32, (ROWS, LANES), 1)
    sub = lax.broadcasted_iota(jnp.int32, (ROWS, LANES), 0)
    return lane, sub


def cosine_sine_double(angle):
    turns = jnp.floor(angle * 1.2732395447351628 + 0.5)
    reduced = 2.0 * angle - turns * 1.5703125
    reduced = reduced - turns * 4.837512969970703125e-4
    reduced = reduced - turns * 7.54978995489188216e-8
    square = reduced * reduced
    sine = (-1.9515295891e-4 * square + 8.3321608736e-3) * square - 1.6666654611e-1
    sine = sine * square * reduced + reduced
    cosine = (2.443315711809948e-5 * square - 1.388731625493765e-3) * square
    cosine = (cosine + 4.166664568298827e-2) * square * square - 0.5 * square + 1.0
    quarter = turns.astype(jnp.int32)
    odd = (quarter & 1) == 1
    first = jnp.where(odd, sine, cosine)
    second = jnp.where(odd, cosine, sine)
    first = jnp.where(((quarter + 1) & 2) == 2, -first, first)
    second = jnp.where((quarter & 2) == 2, -second, second)
    return first, second


def pack_kernel(
    shape, angle_ref, row_ref, hit_ref, group_ref, base_ref, coef_ref, lag_ref, out_ref
):
    wafers, dets, reps, tiles, owners, capacity, owner_rows, lag_count = shape
    lane, sub = tile_iotas()
    span = tiles * LANES
    out_ref[:, 0:span] = angle_ref[...]
    lists = hit_ref[...]
    owner_hits = jnp.zeros((ROWS, LANES), jnp.float32)
    for c in range(capacity):
        owner_hits = owner_hits + jnp.where(wide(lists[:, c : c + 1]) == lane, 1.0, 0.0)
    owner_of = jnp.sum(owner_hits * sub.astype(jnp.float32), axis=0, keepdims=True)
    owner_of = lane_take(wide(owner_of), (lane + sub * tiles) & (LANES - 1))
    spread = jnp.zeros((ROWS, LANES), jnp.float32)
    rows = row_ref[...].astype(jnp.float32)
    for b in range(tiles):
        spread = jnp.where(lane == b, wide(rows[:, b : b + 1]), spread)
    ids = jnp.where(lane < tiles, owner_of * float(owner_rows) + spread, 0.0)

    def column(row):
        values = jnp.zeros((ROWS, LANES), jnp.float32)
        for k in range(ROWS):
            values = jnp.where(sub == k, wide(row[:, k : k + 1]), values)
        return values

    table = jnp.where(lane == tiles, column(group_ref[...].astype(jnp.float32)), ids)
    table = jnp.where(lane == tiles + 1, column(base_ref[...]), table)
    for j in range(lag_count):
        at = tiles + 2 + j
        table = jnp.where(lane == at, column(coef_ref[j : j + 1, :]), table)
        lag = lag_ref[j : j + 1, :].astype(jnp.float32)
        table = jnp.where(lane == at + lag_count, column(lag), table)
    out_ref[:, span : span + LANES] = table
    along = jnp.where((lane & (ROWS - 1)) == sub, lane_take(ids, lane >> 3), 0.0)
    out_ref[:, span + LANES : span + 2 * LANES] = wide(jnp.sum(along, axis=0, keepdims=True))
    hits = jnp.full((ROWS, LANES), LANES, jnp.int32)
    for c in range(capacity):
        number = wide(lists[:, c : c + 1])
        place = (number & (tiles - 1)) * ROWS + (number >> (tiles.bit_length() - 1))
        hits = jnp.where(lane == c, jnp.where(number < LANES, place, LANES), hits)
    out_ref[:, span + 2 * LANES : span + 3 * LANES] = hits.astype(jnp.float32)


def tile_limit(shape):
    wafers, dets, reps, tiles, owners, capacity = shape[:6]
    return 2 * (wafers * dets * reps * capacity // LANES) + 1


def part_copies(shape, place_ref, own_refs, columns, to_ref, sem):
    wafers, dets, reps = shape[:3]
    here_ref, across_ref, other_ref = own_refs
    copies = []
    for swap_rep in range(reps):
        for swap_wafer in range(wafers):
            for shift in range(dets):
                if swap_rep:
                    source = other_ref.at[swap_wafer, shift]
                else:
                    source = (across_ref if swap_wafer else here_ref).at[shift]
                wafer = place_ref[0] ^ swap_wafer
                det = place_ref[1] - shift
                det = jnp.where(det < 0, det + dets, det)
                rep = place_ref[2] ^ swap_rep
                device = (wafer * dets + det) * reps + rep
                copies.append(
                    pltpu.make_async_copy(
                        source.at[:, columns], to_ref.at[device], sem.at[len(copies)]
                    )
                )
    return copies


def list_kernel(
    shape, self_ref, here_ref, across_ref, other_ref,
    weight_ref, place_ref, full_ref, size_ref, pair_ref, group_ref, source_ref, target_ref, start_ref,
    part_ref, code_ref, high_ref, low_ref, table_ref, count_ref, table_smem, count_smem, part_sem,
    table_sem,
):
    wafers, dets, reps, tiles, owners, capacity, owner_rows, lag_count = shape
    devices = wafers * dets * reps
    blocks = reps * tiles
    total = devices * tiles * ROWS
    lane, sub = tile_iotas()
    lane_f = lane.astype(jnp.float32)
    own = self_ref[1] * wafers + self_ref[0]
    first_row = (own * owner_rows).astype(jnp.float32)
    many = float(total * total)
    span = tiles * LANES
    copies = part_copies(
        shape, self_ref, (here_ref, across_ref, other_ref), pl.ds(span, 3 * LANES), part_ref,
        part_sem,
    )
    for copy in copies:
        copy.start()
    for copy in copies:
        copy.wait()

    def exact_dot(left, right):
        return jnp.dot(
            left.astype(jnp.bfloat16), right.astype(jnp.bfloat16),
            preferred_element_type=jnp.float32,
        )

    depth = 2 * LANES
    tall = lax.broadcasted_iota(jnp.int32, (depth, LANES), 0).astype(jnp.float32)

    def survey(device, hits):
        values = part_ref[device, :, 0:LANES]
        codes = jnp.full((ROWS, LANES), BIG, jnp.float32)
        for b in range(tiles):
            at = device * tiles + b
            ids = wide(values[:, b : b + 1])
            least = jnp.full((ROWS, LANES), BIG, jnp.float32)
            matches = jnp.zeros((ROWS, LANES), jnp.float32)
            for other in range(devices):
                same = ids == part_ref[other, :, LANES : 2 * LANES]
                least = jnp.minimum(least, jnp.where(same, lane_f + float(other * LANES), BIG))
                matches = matches + jnp.where(same, 1.0, 0.0)
            least = jnp.min(least, axis=1, keepdims=True)
            matches = jnp.sum(matches, axis=1, keepdims=True)
            mine = (at * ROWS + sub[:, 0:1]).astype(jnp.float32)
            weight_ref[at] = wide(jnp.where(least == mine, 0.5, 0.0))
            code = mine * float(total) + least + jnp.where(matches > 2.0, many, 0.0)
            code = jnp.where(least < mine, code, BIG)
            codes = jnp.where(lane == b, code, codes)
            local_row = ids - first_row
            high = jnp.floor(local_row * (1.0 / LANES))
            low = local_row - high * LANES
            at_row = pl.ds(pl.multiple_of(at * ROWS, ROWS), ROWS)
            high_ref[at_row, 0:LANES] = (high == lane_f).astype(jnp.float32)
            high_ref[at_row, LANES:depth] = (high == lane_f + LANES).astype(jnp.float32)
            low_ref[at_row, :] = (low == lane_f).astype(jnp.float32)
        code_ref[device] = codes
        along = jnp.floor((part_ref[device, 0:1, LANES : 2 * LANES] - first_row) * (1.0 / LANES))
        along = (jnp.broadcast_to(along, (depth, LANES)) == tall).astype(jnp.float32)
        at_rows = pl.ds(pl.multiple_of(device * LANES, LANES), LANES)
        return hits + exact_dot(along, low_ref[at_rows, :])

    hits = lax.fori_loop(0, devices, survey, jnp.zeros((depth, LANES), jnp.float32))
    full = jnp.minimum(hits, 1.0)
    full_ref[...] = full
    counts = lax.dot_general(
        jnp.ones((ROWS, LANES), jnp.bfloat16), full.astype(jnp.bfloat16), (((1,), (1,)), ((), ())),
        preferred_element_type=jnp.float32,
    )
    count_ref[...] = counts.astype(jnp.int32)
    count_copy = pltpu.make_async_copy(count_ref, count_smem, table_sem.at[1])
    count_copy.start()
    before = (
        lax.broadcasted_iota(jnp.int32, (LANES, LANES), 0)
        < lax.broadcasted_iota(jnp.int32, (LANES, LANES), 1)
    ).astype(jnp.float32)
    place = exact_dot(full, before)
    place_ref[...] = place.astype(jnp.int32)

    def rank_of(device, carry):
        at_rows = pl.ds(pl.multiple_of(device * LANES, LANES), LANES)
        inside = exact_dot(high_ref[at_rows, :], place)
        inside = jnp.sum(inside * low_ref[at_rows, :], axis=1, keepdims=True)
        table = jnp.zeros((ROWS, LANES), jnp.float32)
        for b in range(tiles):
            table = jnp.where(lane == b, inside[b * ROWS : (b + 1) * ROWS], table)
        high = jnp.floor((part_ref[device, :, 0:LANES] - first_row) * (1.0 / LANES))
        table_ref[device, 0:ROWS] = (table + high * LANES).astype(jnp.int32)
        table_ref[device, ROWS : 2 * ROWS] = part_ref[device, :, 2 * LANES : 3 * LANES].astype(
            jnp.int32
        )
        return carry

    lax.fori_loop(0, devices, rank_of, 0)
    copy = pltpu.make_async_copy(table_ref, table_smem, table_sem.at[0])
    copy.start()

    def next_code(last):
        found = jnp.full((ROWS, LANES), BIG, jnp.float32)
        for device in range(devices):
            codes = code_ref[device]
            found = jnp.minimum(found, jnp.where(codes > last, codes, BIG))
        return jnp.min(found)

    def detector(key):
        return lax.rem(lax.div(key, blocks * ROWS), dets) * ROWS + lax.rem(key, ROWS)

    def take(list_ref, offset):
        def one(state):
            count, code = state
            number = (code - offset).astype(jnp.int32)
            key = lax.div(number, total)
            lead = lax.rem(number, total)
            list_ref[0, count] = key
            list_ref[1, count] = lead
            list_ref[2, count] = (3 * (detector(key) - detector(lead))) & (PBLOCK - 1)
            return count + 1, next_code(code)

        return one

    pairs, code = lax.while_loop(
        lambda state: state[1] < many, take(pair_ref, 0.0),
        (jnp.int32(0), next_code(jnp.float32(-1.0))),
    )
    grouped, _ = lax.while_loop(
        lambda state: state[1] < BIG, take(group_ref, many), (jnp.int32(0), code)
    )
    batches = lax.div(pairs + PAIR_BATCH - 1, PAIR_BATCH)

    def fill(n, carry):
        pair_ref[0, n] = total
        pair_ref[1, n] = total + 1
        pair_ref[2, n] = 0
        return carry

    lax.fori_loop(pairs, batches * PAIR_BATCH, fill, 0)
    size_ref[0] = batches
    size_ref[1] = grouped
    count_copy.wait()

    def set_start(group, used):
        number = count_smem[0, group]
        start = jnp.where((used & (LANES - 1)) + number > LANES, (used + LANES - 1) & -LANES, used)
        start_ref[group] = start
        return start + number

    size_ref[2] = lax.fori_loop(0, owner_rows // LANES, set_start, jnp.int32(0))
    copy.wait()

    def pick(device, carry):
        for c in range(capacity):
            number = table_smem[device, ROWS + own, c]
            valid = number < LANES
            number = jnp.where(valid, number, 0)
            rank = table_smem[device, number & (ROWS - 1), number >> 3]
            group = jnp.where(valid, rank >> 7, 0)
            target = start_ref[group] + (rank & (LANES - 1))
            source_ref[device, c] = device * LANES + number
            target_ref[device, c] = jnp.where(valid, target, tile_limit(shape) * LANES)
        return carry

    lax.fori_loop(0, devices, pick, 0)


def map_kernel(
    shape, self_ref, size_ref, pair_ref, group_ref, source_ref, target_ref,
    here_ref, across_ref, other_ref, tod_here_ref, tod_across_ref, tod_other_ref, weight_ref,
    column_ref, part_ref, tod_ref, cos_ref, sin_ref, clean_ref, noise_ref, inverse_ref, x_map, r_map, d_map, image_map,
    member_ref, share_ref, base_ref, coef_ref, lag_ref,
    rows_ref, sorted_ref, part_sem, tod_sem,
):
    wafers, dets, reps, tiles, owners, capacity, owner_rows, lag_count = shape
    teams = wafers * dets
    devices = teams * reps
    blocks = reps * tiles
    count = devices * tiles
    lane, sub = tile_iotas()
    zero = jnp.zeros((ROWS, LANES), jnp.float32)

    def fold(block):
        return block + pltpu.roll(block, LANES // 2, 1)

    def whole_sum(values):
        values = jnp.sum(values, axis=0, keepdims=True)
        return wide(jnp.sum(values, axis=1, keepdims=True))

    def loop(times, body, carry, unroll):
        def several(n, carry):
            for k in range(unroll):
                carry = body(n * unroll + k, carry)
            return carry

        return lax.fori_loop(0, times // unroll, several, carry)

    span = tiles * LANES
    part_moves = part_copies(
        shape, self_ref, (here_ref, across_ref, other_ref), pl.ds(0, span + LANES), part_ref, part_sem
    )
    tod_moves = part_copies(
        shape, self_ref, (tod_here_ref, tod_across_ref, tod_other_ref), pl.ds(0, span), tod_ref,
        tod_sem,
    )
    for copy in part_moves + tod_moves:
        copy.start()
    for copy in part_moves:
        copy.wait()

    for team in range(teams):
        values = part_ref[team * reps, :, span : span + LANES]
        base_ref[team] = wide(values[:, tiles + 1 : tiles + 2])
        for group in range(NSUB):
            member_ref[team, group] = wide(
                (values[:, tiles : tiles + 1] == float(group)).astype(jnp.float32)
            )
        for j in range(lag_count):
            at = tiles + 2 + j
            coef_ref[team, j] = wide(values[:, at : at + 1])
            lag_ref[team, j] = wide(values[:, at + lag_count : at + lag_count + 1].astype(jnp.int32))
        clean_ref[team, 0] = zero
        clean_ref[team, blocks + 1] = zero
    for wafer in range(wafers):
        for group in range(NSUB):
            members = member_ref[wafer * dets, group]
            for i in range(1, dets):
                members = members + member_ref[wafer * dets + i, group]
            members = jnp.sum(members, axis=0, keepdims=True)
            share_ref[wafer, group] = wide(1.0 / jnp.maximum(members, 1.0))
    for c in range(3):
        image_map[count, c] = zero
        r_map[count, c] = zero

    def survey(at, carry):
        device = lax.div(at, tiles)
        place = pl.ds(pl.multiple_of(lax.rem(at, tiles) * LANES, LANES), LANES)
        first, second = cosine_sine_double(part_ref[device, :, place])
        base = base_ref[lax.div(device, reps)]
        cos_ref[at] = first
        sin_ref[at] = second
        image_map[at, 0] = base + base
        image_map[at, 1] = fold(base * (first * first))
        image_map[at, 2] = fold(base * (second * second))
        return carry

    loop(count, survey, 0, 8)

    def merge_twins(target):
        def pair_batch(n, carry):
            found = []
            for k in range(PAIR_BATCH):
                key, lead, shift = (pair_ref[j, n * PAIR_BATCH + k] for j in range(3))
                spots = [
                    (lax.shift_right_logical(spot, 3), pl.ds(spot & (ROWS - 1), 1))
                    for spot in (key, lead)
                ]
                values = [[target[at, c, row, :] for c in range(3)] for at, row in spots]
                found.append((spots, shift, values))
            for spots, shift, values in found:
                turns = (shift, (LANES - shift) & (LANES - 1))
                for (at, row), own, other, turn in zip(
                    spots, values, values[::-1], turns[::-1]
                ):
                    for c in range(3):
                        target[at, c, row, :] = own[c] + pltpu.roll(wide(other[c]), turn, 1)[0:1]
            return carry

        def gather_one(n, carry):
            key, lead, shift = (group_ref[j, n] for j in range(3))
            at, row = lax.shift_right_logical(key, 3), key & (ROWS - 1)
            lead_at, lead_row = lax.shift_right_logical(lead, 3), lead & (ROWS - 1)
            for c in range(3):
                moved = pltpu.roll(wide(target[at, c, pl.ds(row, 1), :]), shift, 1)
                target[lead_at, c, pl.ds(lead_row, 1), :] += moved[0:1]
            return carry

        def spread_one(n, carry):
            key, lead, shift = (group_ref[j, n] for j in range(3))
            at, row = lax.shift_right_logical(key, 3), key & (ROWS - 1)
            lead_at, lead_row = lax.shift_right_logical(lead, 3), lead & (ROWS - 1)
            turn = (LANES - shift) & (LANES - 1)
            for c in range(3):
                moved = pltpu.roll(wide(target[lead_at, c, pl.ds(lead_row, 1), :]), turn, 1)
                target[at, c, pl.ds(row, 1), :] = moved[0:1]
            return carry

        lax.fori_loop(0, size_ref[0], pair_batch, 0)
        lax.fori_loop(0, size_ref[1], gather_one, 0)
        lax.fori_loop(0, size_ref[1], spread_one, 0)

    def over_detectors(values):
        for turn in (4, 2, 1):
            values = values + pltpu.roll(values, turn, 0)
        return values

    def removal_pass(stream_of, place, carry):
        for wafer in range(wafers):
            first = wafer * dets

            def some_times(batch, carry):
                times = [batch * TIME_BATCH + k for k in range(TIME_BATCH)]
                streams, parts = [], [[None] * NSUB for _ in times]
                for i in range(dets):
                    members = [member_ref[first + i, g] for g in range(NSUB)]
                    streams.append([])
                    for k, block in enumerate(times):
                        stream, carry = stream_of(first + i, block, carry)
                        streams[i].append(stream)
                        for g in range(NSUB):
                            term = members[g] * stream
                            parts[k][g] = term if i == 0 else parts[k][g] + term
                means = [
                    [over_detectors(parts[k][g]) * share_ref[wafer, g] for g in range(NSUB)]
                    for k in range(TIME_BATCH)
                ]
                for i in range(dets):
                    members = [member_ref[first + i, g] for g in range(NSUB)]
                    for k, block in enumerate(times):
                        common = members[0] * means[k][0]
                        for g in range(1, NSUB):
                            common = common + members[g] * means[k][g]
                        place(first + i, block, streams[i][k] - common)
                return carry

            carry = lax.fori_loop(0, blocks // TIME_BATCH, some_times, carry)
        return carry

    def keep_clean(team, block, stream):
        clean_ref[team, block + 1] = stream

    def filter_pass():
        def one_team(team, carry):
            base = base_ref[team]
            coefs = [coef_ref[team, j] for j in range(lag_count)]
            lags = [lag_ref[team, j] for j in range(lag_count)]
            later_turns = [(lane + lag) & (LANES - 1) for lag in lags]
            earlier_turns = [(lane - lag) & (LANES - 1) for lag in lags]

            def one_time(block, state):
                ahead, here, carry = state
                after = clean_ref[team, block + 2]
                result = base * here
                for j in range(lag_count):
                    later = lane_take(jnp.where(lane < lags[j], after, here), later_turns[j])
                    earlier = lane_take(
                        jnp.where(lane >= LANES - lags[j], ahead, here), earlier_turns[j]
                    )
                    result = result + coefs[j] * (later + earlier)
                noise_ref[team * blocks + block] = result
                return here, after, carry + here * result

            return loop(blocks, one_time, (clean_ref[team, 0], clean_ref[team, 1], carry), 8)[2]

        return lax.fori_loop(0, teams, one_team, zero)

    def return_pass(target):
        def noise_stream(team, block, carry):
            return noise_ref[team * blocks + block], carry

        def add_back(team, block, stream):
            at = team * blocks + block
            target[at, 0] = fold(stream)
            target[at, 1] = fold(cos_ref[at] * stream)
            target[at, 2] = fold(sin_ref[at] * stream)

        removal_pass(noise_stream, add_back, 0)
        merge_twins(target)

    merge_twins(image_map)

    for copy in tod_moves:
        copy.wait()

    def data_stream(team, block, carry):
        device = team * reps + lax.div(block, tiles)
        at = pl.multiple_of(lax.rem(block, tiles) * LANES, LANES)
        return tod_ref[device, :, pl.ds(at, LANES)], carry

    removal_pass(data_stream, keep_clean, 0)
    filter_pass()
    return_pass(r_map)

    def begin(at, carry):
        parts = zero
        for c in range(3):
            inverse = 1.0 / (image_map[at, c] + prior_weight)
            inverse_ref[at, c] = inverse
            residual = r_map[at, c]
            parts = parts + residual * (inverse * residual)
        return carry + weight_ref[at] * parts

    energy = whole_sum(loop(count, begin, zero, 8))
    factor = zero
    for iteration in range(ITERS):
        last = iteration == ITERS - 1

        def seen_stream(team, block, carry):
            at = team * blocks + block
            parts = []
            for c in range(3):
                part = inverse_ref[at, c] * r_map[at, c]
                if iteration:
                    part = part + factor * d_map[at, c]
                d_map[at, c] = part
                parts.append(part)
            squares = parts[0] * parts[0] + parts[1] * parts[1] + parts[2] * parts[2]
            stream = parts[0] + cos_ref[at] * parts[1] + sin_ref[at] * parts[2]
            return stream, carry + weight_ref[at] * squares

        prior = removal_pass(seen_stream, keep_clean, zero)
        product = filter_pass()
        return_pass(image_map)
        step = energy / whole_sum(product + prior_weight * prior)

        def advance(at):
            new_x, new_r = [], []
            for c in range(3):
                direction = d_map[at, c]
                image = image_map[at, c] + prior_weight * direction
                move = step * direction
                new_x.append(x_map[at, c] + move if iteration else move)
                new_r.append(r_map[at, c] - step * image)
            return new_x, new_r

        if not last:

            def update(at, carry):
                new_x, new_r = advance(at)
                parts = zero
                for c in range(3):
                    x_map[at, c] = new_x[c]
                    r_map[at, c] = new_r[c]
                    parts = parts + new_r[c] * (inverse_ref[at, c] * new_r[c])
                return carry + weight_ref[at] * parts

            next_energy = whole_sum(loop(count, update, zero, 8))
            factor = next_energy / energy
            energy = next_energy
        else:

            def place_pixels(at, carry):
                new_x, new_r = advance(at)
                team = lax.rem(lax.div(at, blocks), dets)
                turn = (lane - 3 * (team * ROWS + sub)) & (LANES - 1)
                values = [lane_take(value, turn) for value in new_x + new_r]
                rows = pl.ds(pl.multiple_of(at * ROWS, ROWS), ROWS)
                for c in range(3):
                    rows_ref[rows, c * LANES : (c + 1) * LANES] = jnp.where(
                        lane < PBLOCK, values[2 * c], values[2 * c + 1]
                    )
                return carry

            loop(count, place_pixels, 0, 8)

    def pick(device, carry):
        for c in range(capacity):
            source, target = source_ref[device, c], target_ref[device, c]
            sorted_ref[pl.ds(target, 1), :] = rows_ref[pl.ds(source, 1), :]
        return carry

    lax.fori_loop(0, devices, pick, 0)

    def turn(tile, carry):
        rows = pl.ds(pl.multiple_of(tile * LANES, LANES), LANES)
        column_ref[tile] = sorted_ref[rows, :].T
        return carry

    lax.fori_loop(0, lax.div(size_ref[2] + LANES - 1, LANES), turn, 0)


def write_kernel(start_ref, column_ref, place_ref, full_ref, x_ref, r_ref):
    height = 3 * PBLOCK
    for k in range(OUT_TILES):
        group = pl.program_id(0) * OUT_TILES + k
        start = start_ref[group]
        tile = lax.shift_right_logical(start, 7)
        index = (wide(place_ref[pl.ds(group, 1), :]) + start) & (LANES - 1)
        present = wide(full_ref[pl.ds(group, 1), :]) > 0.0
        for s in range(height // ROWS):
            for out_ref, offset in ((x_ref, 0), (r_ref, height)):
                values = column_ref[tile, offset + s * ROWS : offset + (s + 1) * ROWS, :]
                out_ref[s * ROWS : (s + 1) * ROWS, k * LANES : (k + 1) * LANES] = jnp.where(
                    present, lane_take(values, index), 0.0
                )


def part_shape(sizes, tod, hit_list, band_lag):
    det_count, time_count = tod.shape[1:]
    owners, capacity = hit_list.shape[3:]
    return (
        sizes["wafer"], sizes["det"], sizes["rep"], time_count // SBLOCK,
        owners, capacity, BLOCKS // owners, band_lag.shape[2],
    ), det_count


def fits_one_device(shape, det_count):
    wafers, dets, reps, tiles, owners, capacity, owner_rows, lag_count = shape
    devices = wafers * dets * reps
    total = devices * tiles * det_count
    groups = owner_rows // LANES
    return (
        det_count == ROWS
        and owners == ROWS
        and tiles * ROWS == LANES
        and tiles + 2 + 2 * lag_count <= LANES
        and (wafers, reps) == (2, 2)
        and reps * tiles % 8 == 0
        and capacity <= LANES
        and devices * capacity % LANES == 0
        and owner_rows % (LANES * OUT_TILES) == 0
        and groups <= 2 * LANES
        and 2 * total * total <= BIG
    )


def whole_part(shape, tod, psi, point_row, hit_list, group_id, a_zero, band_coef, band_lag):
    wafers, dets, reps, tiles, owners, capacity, owner_rows, lag_count = shape
    teams = wafers * dets
    devices = teams * reps
    blocks = reps * tiles
    count = devices * tiles
    total = count * ROWS
    slots = devices * capacity
    height = 3 * PBLOCK
    span = tiles * LANES
    hit_tiles = tile_limit(shape)
    f32, i32 = jnp.float32, jnp.int32
    vmem, smem = pl.BlockSpec(memory_space=pltpu.VMEM), pl.BlockSpec(memory_space=pltpu.SMEM)
    anywhere = pl.BlockSpec(memory_space=pl.ANY)
    params = pltpu.CompilerParams(vmem_limit_bytes=VMEM_BYTES)
    wafer_swap = [(0, 1), (1, 0)]

    def along_det(block):
        moved = [
            lax.ppermute(block, "det", [(i, (i + shift) % dets) for i in range(dets)])
            for shift in range(1, dets)
        ]
        return [block] + moved

    def across(blocks_here):
        here = jnp.stack(blocks_here)
        other_wafer = lax.ppermute(here, "wafer", wafer_swap)
        other_rep = lax.ppermute(jnp.stack([here, other_wafer]), "rep", wafer_swap)
        return here, other_wafer, other_rep

    packed = pl.pallas_call(
        functools.partial(pack_kernel, shape),
        out_shape=jax.ShapeDtypeStruct((ROWS, span + 3 * LANES), f32),
        in_specs=[vmem] * 7,
        out_specs=vmem,
        compiler_params=params,
        name="pack",
    )(psi[0], point_row[0], hit_list[0, 0, 0], group_id, a_zero, band_coef[0].T, band_lag[0].T)
    columns = along_det(packed)
    samples, *columns = lax.optimization_barrier((tod[0], *columns))
    angle_blocks = across(columns)
    sample_blocks = across(along_det(samples))
    place_here = jnp.stack([lax.axis_index(axis) for axis in ("wafer", "det", "rep")]).astype(i32)
    weight, place, full, size, pair, group, source, target, start = pl.pallas_call(
        functools.partial(list_kernel, shape),
        out_shape=[
            jax.ShapeDtypeStruct((count, ROWS, LANES), f32),
            jax.ShapeDtypeStruct((2 * LANES, LANES), i32),
            jax.ShapeDtypeStruct((2 * LANES, LANES), f32),
            jax.ShapeDtypeStruct((3,), i32),
            jax.ShapeDtypeStruct((3, total), i32),
            jax.ShapeDtypeStruct((3, total), i32),
            jax.ShapeDtypeStruct((devices, capacity), i32),
            jax.ShapeDtypeStruct((devices, capacity), i32),
            jax.ShapeDtypeStruct((2 * LANES,), i32),
        ],
        in_specs=[smem] + [anywhere] * 3,
        out_specs=[vmem] * 3 + [smem] * 6,
        scratch_shapes=[
            pltpu.VMEM((devices, ROWS, 3 * LANES), f32),
            pltpu.VMEM((devices, ROWS, LANES), f32),
            pltpu.VMEM((total, 2 * LANES), f32),
            pltpu.VMEM((total, LANES), f32),
            pltpu.VMEM((devices, 2 * ROWS, LANES), i32),
            pltpu.VMEM((ROWS, 2 * LANES), i32),
            pltpu.SMEM((devices, 2 * ROWS, LANES), i32),
            pltpu.SMEM((ROWS, 2 * LANES), i32),
            pltpu.SemaphoreType.DMA((devices,)),
            pltpu.SemaphoreType.DMA((2,)),
        ],
        compiler_params=params,
        cost_estimate=pl.CostEstimate(flops=10**9, bytes_accessed=4 * 10**6, transcendentals=0),
        name="lists",
    )(place_here, *angle_blocks)
    stream = pltpu.VMEM((count, ROWS, LANES), f32)
    sky = pltpu.VMEM((count, 3, ROWS, LANES), f32)
    sky_and_spare = pltpu.VMEM((count + 1, 3, ROWS, LANES), f32)
    columns = pl.pallas_call(
        functools.partial(map_kernel, shape),
        out_shape=jax.ShapeDtypeStruct((hit_tiles, 2 * height, LANES), f32),
        in_specs=[smem] * 6 + [anywhere] * 6 + [vmem],
        out_specs=vmem,
        scratch_shapes=[
            pltpu.VMEM((devices, ROWS, span + LANES), f32),
            pltpu.VMEM((devices, ROWS, span), f32),
            stream, stream, pltpu.VMEM((teams, blocks + 2, ROWS, LANES), f32), stream,
            sky, sky, sky_and_spare, sky, sky_and_spare,
            pltpu.VMEM((teams, NSUB, ROWS, LANES), f32),
            pltpu.VMEM((wafers, NSUB, ROWS, LANES), f32),
            pltpu.VMEM((teams, ROWS, LANES), f32),
            pltpu.VMEM((teams, lag_count, ROWS, LANES), f32),
            pltpu.VMEM((teams, lag_count, ROWS, LANES), i32),
            pltpu.VMEM((total, 2 * height), f32),
            pltpu.VMEM((hit_tiles * LANES + ROWS, 2 * height), f32),
            pltpu.SemaphoreType.DMA((devices,)),
            pltpu.SemaphoreType.DMA((devices,)),
        ],
        compiler_params=params,
        name="map_maker",
    )(place_here, size, pair, group, source, target, *angle_blocks, *sample_blocks, weight)
    out_block = pl.BlockSpec((height, OUT_TILES * LANES), lambda n: (0, n))
    x_turned, r_turned = pl.pallas_call(
        write_kernel,
        grid=(owner_rows // (OUT_TILES * LANES),),
        out_shape=[jax.ShapeDtypeStruct((height, owner_rows), f32)] * 2,
        in_specs=[smem, vmem, vmem, vmem],
        out_specs=[out_block, out_block],
        compiler_params=params,
        name="write",
    )(start, columns, place, full)
    return x_turned.T, r_turned.T


def local(sizes, *arguments):
    tod, hit_list, band_lag = arguments[0], arguments[3], arguments[7]
    shape, det_count = part_shape(sizes, tod, hit_list, band_lag)
    if fits_one_device(shape, det_count):
        return whole_part(shape, *arguments)
    return distributed(*arguments)


def solution(mesh):
    placed = (
        P(("groups", "wafer"), "det", "rep"),
        P(("groups", "wafer"), "det", "rep"),
        P(("groups", "wafer"), "det", "rep"),
        P(("groups", "wafer"), "det", "rep", None, None),
        P(("groups", "wafer"), "det"),
        P(("groups", "wafer"), "det"),
        P(("groups", "wafer"), "det", None),
        P(("groups", "wafer"), "det", None),
    )
    return jax.shard_map(
        functools.partial(local, mesh.shape),
        mesh=mesh,
        in_specs=placed,
        out_specs=(P(("groups", "det", "wafer"), None), P(("groups", "det", "wafer"), None)),
        check_vma=False,
    )
```

```python
import functools

import jax
import jax.numpy as jnp
from jax import lax
from jax.experimental import pallas as pl
from jax.experimental.pallas import tpu as pltpu
from jax.sharding import PartitionSpec as P

BLOCKS = 196608
PBLOCK = 64
SBLOCK = 128
NSUB = 4
LAG = 16
ITERS = 3


prior_weight = 1.0


def with_halo(block, sides, width):
    for axis, dim in sides:
        count = lax.axis_size(axis)
        forward = [(i, i + 1) for i in range(count - 1)]
        backward = [(target, source) for source, target in forward]
        low = lax.ppermute(
            lax.slice_in_dim(block, block.shape[dim] - width, None, axis=dim), axis, forward
        )
        high = lax.ppermute(lax.slice_in_dim(block, 0, width, axis=dim), axis, backward)
        block = jnp.concatenate([low, block, high], axis=dim)
    return block


def distributed(tod, psi, point_row, hit_list, group_id, a_zero, band_coef, band_lag):
    highest = lax.Precision.HIGHEST
    samples = tod[0]
    angles = psi[0]
    det_count, time_count = samples.shape
    time_blocks = time_count // SBLOCK
    block_count = det_count * time_blocks
    send_table = hit_list[0, 0, 0]
    owner_count, capacity = send_table.shape
    owner_rows = BLOCKS // owner_count
    block_width = 3 * PBLOCK
    detector = lax.axis_index("det") * det_count + jnp.arange(det_count, dtype=jnp.int32)
    within = (jnp.arange(SBLOCK, dtype=jnp.int32)[None, :] + 3 * detector[:, None]) % PBLOCK
    pixel_table = (within[:, :, None] == jnp.arange(PBLOCK, dtype=jnp.int32)[None, None, :]).astype(
        jnp.float32
    )
    cosine_two = jnp.cos(2.0 * angles).reshape(det_count, time_blocks, SBLOCK)
    sine_two = jnp.sin(2.0 * angles).reshape(det_count, time_blocks, SBLOCK)
    slot_ids = send_table.reshape(-1)
    row_source = jnp.concatenate([point_row[0].reshape(-1), jnp.zeros((1,), jnp.int32)])
    slot_rows = row_source[slot_ids].astype(jnp.float32).reshape(owner_count, capacity)
    member = (group_id[0][:, None] == jnp.arange(NSUB, dtype=jnp.int32)[None, :]).astype(
        jnp.float32
    )
    member_count = jnp.sum(member, axis=0)
    lag_table = (
        band_lag[0][:, :, None] == jnp.arange(1, LAG + 1, dtype=jnp.int32)[None, None, :]
    ).astype(jnp.float32)
    lag_weight = jnp.einsum("dj,djl->dl", band_coef[0], lag_table, precision=highest)
    base_weight = a_zero[0]

    def slot_payload(by_block):
        width = by_block.shape[1]
        extended = jnp.concatenate([by_block, jnp.zeros((1, width), by_block.dtype)])
        return extended[slot_ids].reshape(owner_count, capacity, width)

    def deliver(payload):
        width = payload.shape[-1]
        got_values, got_rows = (
            lax.all_to_all(payload, ("det", "wafer"), split_axis=0, concat_axis=0, tiled=True),
            lax.all_to_all(slot_rows, ("det", "wafer"), split_axis=0, concat_axis=0, tiled=True),
        )
        return (got_values, got_rows)

    def back_project(stream, squared):
        shaped = stream.reshape(det_count, time_blocks, SBLOCK)
        first = cosine_two * cosine_two if squared else cosine_two
        second = sine_two * sine_two if squared else sine_two
        stacked = jnp.stack([shaped, first * shaped, second * shaped], axis=2)
        stokes = jnp.einsum("dkcs,dsp->dkcp", stacked, pixel_table, precision=highest)
        return stokes.reshape(block_count, block_width)

    def to_owners(stream, squared):
        got_values, got_rows = deliver(slot_payload(back_project(stream, squared)))
        pair_values, pair_rows = (
            lax.all_gather(got_values, "rep", axis=0, tiled=True),
            lax.all_gather(got_rows, "rep", axis=0, tiled=True),
        )
        target_rows = pair_rows.reshape(-1).astype(jnp.int32)
        summed = (
            jnp.zeros((owner_rows, block_width), jnp.float32)
            .at[target_rows]
            .add(pair_values.reshape(-1, block_width))
        )
        return (summed, got_rows.astype(jnp.int32))

    def remove_common(stream):
        local_sums = jnp.einsum("dg,dt->gt", member, stream, precision=highest)
        group_sums, group_counts = lax.psum((local_sums, member_count), "det")
        group_means = group_sums / jnp.maximum(group_counts, 1.0)[:, None]
        return stream - jnp.einsum("dg,gt->dt", member, group_means, precision=highest)

    def band_filter(stream):
        padded = with_halo(stream, (("rep", 1),), LAG)
        result = base_weight[:, None] * stream
        for offset in range(1, LAG + 1):
            later = padded[:, LAG + offset : LAG + offset + time_count]
            earlier = padded[:, LAG - offset : LAG - offset + time_count]
            result = result + lag_weight[:, offset - 1 : offset] * (later + earlier)
        return result

    def weigh_stream(stream):
        return remove_common(band_filter(remove_common(stream)))

    weight_stream = jnp.broadcast_to(base_weight[:, None], (det_count, time_count))
    diag_sum, serve_rows = to_owners(weight_stream, True)
    inverse_diag = 1.0 / (diag_sum + prior_weight)
    right_side = to_owners(weigh_stream(samples), False)[0]
    solution = jnp.zeros_like(right_side)
    residual = right_side

    def inner(left_map, right_map):
        return lax.psum(jnp.sum(left_map * right_map), ("det", "wafer"))

    precond = inverse_diag * residual
    direction = precond
    energy = inner(residual, precond)
    for iteration in range(ITERS):
        from_blocks = direction[serve_rows.reshape(-1)].reshape(owner_count, capacity, block_width)
        return_width = from_blocks.shape[-1]
        returned = lax.all_to_all(
            from_blocks, ("det", "wafer"), split_axis=0, concat_axis=0, tiled=True
        )
        return_placed = jnp.zeros((block_count + 1, return_width), jnp.float32)
        return_placed = return_placed.at[slot_ids].set(returned.reshape(-1, return_width))
        blocks = return_placed[:block_count].reshape(det_count, time_blocks, 3, PBLOCK)
        project_stokes = jnp.einsum("dkcp,dsp->dkcs", blocks, pixel_table, precision=highest)
        project_stream = (
            project_stokes[:, :, 0]
            + cosine_two * project_stokes[:, :, 1]
            + sine_two * project_stokes[:, :, 2]
        )
        seen_stream = project_stream.reshape(det_count, time_count)
        image_map = to_owners(weigh_stream(seen_stream), False)[0] + prior_weight * direction
        step_size = energy / inner(direction, image_map)
        solution = solution + step_size * direction
        residual = residual - step_size * image_map
        precond = inverse_diag * residual
        energy_next = inner(residual, precond)
        direction = precond + energy_next / energy * direction
        energy = energy_next
    return (solution, residual)


LANES = 128
ROWS = 8
OUT_TILES = 8
PAIR_BATCH = 4
BIG = float(1 << 24)
VMEM_BYTES = 60 << 20


def wide(values):
    return jnp.broadcast_to(values, (ROWS, LANES))


def tile_iotas():
    lane = lax.broadcasted_iota(jnp.int32, (ROWS, LANES), 1)
    sub = lax.broadcasted_iota(jnp.int32, (ROWS, LANES), 0)
    return lane, sub


def cosine_sine_double(angle):
    turns = jnp.floor(angle * 1.2732395447351628 + 0.5)
    reduced = 2.0 * angle - turns * 1.5703125
    reduced = reduced - turns * 4.837512969970703125e-4
    reduced = reduced - turns * 7.54978995489188216e-8
    square = reduced * reduced
    sine = (-1.9515295891e-4 * square + 8.3321608736e-3) * square - 1.6666654611e-1
    sine = sine * square * reduced + reduced
    cosine = (2.443315711809948e-5 * square - 1.388731625493765e-3) * square
    cosine = (cosine + 4.166664568298827e-2) * square * square - 0.5 * square + 1.0
    quarter = turns.astype(jnp.int32)
    odd = (quarter & 1) == 1
    first = jnp.where(odd, sine, cosine)
    second = jnp.where(odd, cosine, sine)
    first = jnp.where(((quarter + 1) & 2) == 2, -first, first)
    second = jnp.where((quarter & 2) == 2, -second, second)
    return first, second


def pack_kernel(
    shape, angle_ref, tod_ref, row_ref, hit_ref, group_ref, base_ref, coef_ref, lag_ref,
    table_ref, angle_rows_ref, tod_rows_ref,
):
    wafers, dets, reps, tiles, owners, capacity, owner_rows, lag_count = shape
    lane, sub = tile_iotas()
    lists = hit_ref[...]
    owner_hits = jnp.zeros((ROWS, LANES), jnp.float32)
    for c in range(capacity):
        owner_hits = owner_hits + jnp.where(wide(lists[:, c : c + 1]) == lane, 1.0, 0.0)
    owner_of = jnp.sum(owner_hits * sub.astype(jnp.float32), axis=0, keepdims=True)

    def spread(values, width):
        return jnp.concatenate(
            [values, jnp.zeros((values.shape[0], LANES - width), values.dtype)], axis=1
        )

    rows = spread(row_ref[...].astype(jnp.float32), tiles)
    ids = owner_of * float(owner_rows) + rows[0:1]
    for k in range(1, ROWS):
        ids = ids + pltpu.roll(rows[k : k + 1], k * tiles, 1)
    floats = spread(base_ref[...], ROWS)
    whole = spread(group_ref[...].astype(jnp.float32), ROWS)
    for j in range(lag_count):
        at = (j + 1) * ROWS
        floats = floats + pltpu.roll(spread(coef_ref[j : j + 1, :], ROWS), at, 1)
        lag = lag_ref[j : j + 1, :].astype(jnp.float32)
        whole = whole + pltpu.roll(spread(lag, ROWS), at, 1)
    table = jnp.where(sub == 0, wide(ids), jnp.where(sub == 1, wide(floats), wide(whole)))
    table_ref[:, 0:LANES] = table
    table_ref[:, LANES : 2 * LANES] = spread(lists.astype(jnp.float32), capacity)
    for b in range(tiles):
        angle_rows_ref[:, b, :] = angle_ref[:, b * LANES : (b + 1) * LANES]
        tod_rows_ref[:, b, :] = tod_ref[:, b * LANES : (b + 1) * LANES]


def part_copies(shape, self_ref, refs, target, sem):
    wafers, dets, reps = shape[:3]
    here_ref, across_ref, other_ref = refs
    copies = []
    for swap_rep in range(reps):
        for swap_wafer in range(wafers):
            for shift in range(dets):
                if swap_rep:
                    source = other_ref.at[swap_wafer, shift]
                else:
                    source = (across_ref if swap_wafer else here_ref).at[shift]
                wafer = self_ref[0] ^ swap_wafer
                det = self_ref[1] - shift
                det = jnp.where(det < 0, det + dets, det)
                device = (wafer * dets + det) * reps + (self_ref[2] ^ swap_rep)
                copies.append(
                    pltpu.make_async_copy(source, target(device), sem.at[len(copies)])
                )
    return copies


def list_kernel(
    shape, self_ref, here_ref, across_ref, other_ref,
    weight_ref, place_ref, start_ref, float_ref, whole_ref,
    size_ref, pair_ref, group_ref, source_ref, target_ref,
    part_ref, code_ref, lead_ref, rank_ref, hits_ref, rank_smem, hits_smem, part_sem, table_sem,
):
    wafers, dets, reps, tiles, owners, capacity, owner_rows, lag_count = shape
    devices = wafers * dets * reps
    total = devices * LANES
    slots = devices * capacity
    lane, sub = tile_iotas()
    lane_f = lane.astype(jnp.float32)
    own = self_ref[1] * wafers + self_ref[0]
    first_row = (own * owner_rows).astype(jnp.float32)
    copies = part_copies(
        shape, self_ref, (here_ref, across_ref, other_ref), lambda d: part_ref.at[d], part_sem
    )
    for copy in copies:
        copy.start()
    for copy in copies:
        copy.wait()

    depth = 2 * LANES
    tall = lax.broadcasted_iota(jnp.int32, (depth, LANES), 0).astype(jnp.float32)

    def exact_dot(left, right, dims=((1,), (0,))):
        return lax.dot_general(
            left.astype(jnp.bfloat16), right.astype(jnp.bfloat16), (dims, ((), ())),
            preferred_element_type=jnp.float32,
        )

    def one_hots(device):
        local_row = part_ref[device, 0:1, 0:LANES] - first_row
        high = jnp.floor(local_row * (1.0 / LANES))
        low = local_row - high * LANES
        high = (jnp.broadcast_to(high, (depth, LANES)) == tall).astype(jnp.float32)
        low = (jnp.broadcast_to(low, (LANES, LANES)) == tall[0:LANES]).astype(jnp.float32)
        return high, low

    def survey(device, hits):
        float_ref[device] = part_ref[device, :, 0:LANES]
        whole_ref[device] = part_ref[device, :, 0:LANES].astype(jnp.int32)
        own_hits = jnp.where(sub == own, part_ref[device, :, LANES : 2 * LANES], 0.0)
        own_hits = jnp.sum(own_hits, axis=0, keepdims=True)
        hits_ref[pl.ds(device, 1), :] = own_hits.astype(jnp.int32)
        ids = jnp.broadcast_to(part_ref[device, 0:1, 0:LANES], (LANES, LANES)).T
        ids = [ids[j * ROWS : (j + 1) * ROWS] for j in range(tiles)]

        def compare(other, state):
            key, least = state
            row = wide(part_ref[other, 0:1, 0:LANES])
            least = [
                jnp.minimum(least[j], jnp.where(ids[j] == row, key, BIG)) for j in range(tiles)
            ]
            return key + LANES, least

        none = jnp.full((ROWS, LANES), BIG, jnp.float32)
        _, least = lax.fori_loop(0, device + 1, compare, (lane_f, [none] * tiles))
        codes, leads = none, none
        for j in range(tiles):
            lead = jnp.min(least[j], axis=1, keepdims=True)
            mine = (device * LANES + j * ROWS + sub[:, 0:1]).astype(jnp.float32)
            weight_ref[device * tiles + j] = wide(jnp.where(lead == mine, 0.5, 0.0))
            later = lead < mine
            leads = jnp.where(lane == j, jnp.where(later, lead, BIG), leads)
            codes = jnp.where(lane == j, jnp.where(later, mine * float(total) + lead, BIG), codes)
        code_ref[device] = codes
        lead_ref[device] = leads
        high, low = one_hots(device)
        return hits + exact_dot(high, low, ((1,), (1,)))

    hits = lax.fori_loop(0, devices, survey, jnp.zeros((depth, LANES), jnp.float32))
    full = jnp.minimum(hits, 1.0)

    def ordered(size, axis):
        first = lax.broadcasted_iota(jnp.int32, (size, size), axis)
        second = lax.broadcasted_iota(jnp.int32, (size, size), 1 - axis)
        return (first < second).astype(jnp.float32)

    counts = exact_dot(jnp.ones((ROWS, LANES), jnp.float32), full, ((1,), (1,)))
    start_ref[...] = exact_dot(counts, ordered(depth, 0)).astype(jnp.int32)
    sums = exact_dot(full, jnp.ones((LANES, LANES), jnp.float32))
    place = exact_dot(full, ordered(LANES, 0)) + exact_dot(ordered(depth, 1), sums)
    place_ref[...] = jnp.where(full > 0.0, place, -1.0).astype(jnp.int32)
    place_high = jnp.floor(place * (1.0 / LANES))
    place_parts = jnp.concatenate([place_high, place - place_high * LANES], axis=0)

    def rank_of(device, carry):
        high, low = one_hots(device)
        parts = exact_dot(place_parts, low)
        rank = high * (parts[0:depth] * LANES + parts[depth : 2 * depth])
        rank_ref[pl.ds(device, 1), :] = jnp.sum(rank, axis=0, keepdims=True).astype(jnp.int32)
        return carry

    lax.fori_loop(0, devices, rank_of, 0)
    copies = (
        pltpu.make_async_copy(rank_ref, rank_smem, table_sem.at[0]),
        pltpu.make_async_copy(hits_ref, hits_smem, table_sem.at[1]),
    )
    for copy in copies:
        copy.start()

    def next_code(last):
        found = jnp.full((ROWS, LANES), BIG, jnp.float32)
        for device in range(devices):
            codes = code_ref[device]
            found = jnp.minimum(found, jnp.where(codes > last, codes, BIG))
        return jnp.min(found)

    def detector(key):
        team = lax.rem(lax.div(key, reps * LANES), dets)
        return team * ROWS + lax.rem(lax.div(key, tiles), ROWS)

    def take(state):
        pairs, grouped, code = state
        number = code.astype(jnp.int32)
        key = lax.div(number, total)
        lead = lax.rem(number, total)
        shift = (3 * (detector(key) - detector(lead))) & (PBLOCK - 1)
        wanted = lead.astype(jnp.float32)
        same = jnp.zeros((ROWS, LANES), jnp.float32)
        for device in range(devices):
            same = same + jnp.where(lead_ref[device] == wanted, 1.0, 0.0)
        alone = jnp.sum(same) < 1.5
        for list_ref, at in ((pair_ref, pairs), (group_ref, grouped)):
            list_ref[0, at] = key
            list_ref[1, at] = lead
            list_ref[2, at] = shift
        return (
            pairs + jnp.where(alone, 1, 0), grouped + jnp.where(alone, 0, 1), next_code(code)
        )

    pairs, grouped, _ = lax.while_loop(
        lambda state: state[2] < BIG, take,
        (jnp.int32(0), jnp.int32(0), next_code(jnp.float32(-1.0))),
    )
    batches = lax.div(pairs + PAIR_BATCH - 1, PAIR_BATCH)

    def fill(n, carry):
        pair_ref[0, n] = total
        pair_ref[1, n] = total + 1
        pair_ref[2, n] = 0
        return carry

    lax.fori_loop(pairs, batches * PAIR_BATCH, fill, 0)
    size_ref[0] = batches
    size_ref[1] = grouped
    for copy in copies:
        copy.wait()

    def pick(device, carry):
        for c in range(capacity):
            number = hits_smem[device, c]
            valid = number < LANES
            number = jnp.where(valid, number, 0)
            source_ref[device, c] = device * LANES + number
            target_ref[device, c] = jnp.where(valid, rank_smem[device, number], slots + LANES)
        return carry

    lax.fori_loop(0, devices, pick, 0)


def map_kernel(
    shape, self_ref, size_ref, pair_ref, group_ref, source_ref, target_ref, float_smem, whole_smem,
    angle_here_ref, angle_across_ref, angle_other_ref, tod_here_ref, tod_across_ref, tod_other_ref,
    weight_ref, column_ref,
    angle_ref, tod_ref, cos_ref, sin_ref, clean_ref, noise_ref,
    inverse_ref, x_map, r_map, d_map, image_map, share_ref, rows_ref, sorted_ref,
    angle_sem, tod_sem, *sum_refs,
):
    wafers, dets, reps, tiles, owners, capacity, owner_rows, lag_count = shape
    devices = wafers * dets * reps
    halves = tiles // ROWS
    octets = reps * halves
    wafer_dets = dets * ROWS
    count = devices * tiles
    lane, sub = tile_iotas()
    zero = jnp.zeros((ROWS, LANES), jnp.float32)
    first_sums, second_sums = sum_refs[:wafers], sum_refs[wafers:]

    def copies_of(refs, to_ref, sem):
        return part_copies(
            shape, self_ref, refs, lambda d: to_ref.at[pl.ds(d * tiles, tiles)], sem
        )

    angle_moves = copies_of((angle_here_ref, angle_across_ref, angle_other_ref), angle_ref, angle_sem)
    tod_moves = copies_of((tod_here_ref, tod_across_ref, tod_other_ref), tod_ref, tod_sem)
    for copy in angle_moves + tod_moves:
        copy.start()

    def fold(block):
        return block + pltpu.roll(block, LANES // 2, 1)

    def whole_sum(values):
        values = jnp.sum(values, axis=0, keepdims=True)
        return wide(jnp.sum(values, axis=1, keepdims=True))

    def loop(times, body, carry, unroll):
        def several(n, carry):
            for k in range(unroll):
                carry = body(n * unroll + k, carry)
            return carry

        return lax.fori_loop(0, times // unroll, several, carry)

    def device_of(wafer, n):
        return (wafer * dets + lax.shift_right_logical(n, 3)) * reps

    def register_of(wafer, n, octet):
        device = device_of(wafer, n) + octet // halves
        return device * tiles + (n & (ROWS - 1)) * halves + octet % halves

    def group_of(wafer, n):
        return whole_smem[device_of(wafer, n), 2, n & (ROWS - 1)]

    def rows_of(octet, ahead=0):
        return pl.ds(octet * ROWS + ahead, ROWS)

    def count_members(n, counts):
        result = []
        for wafer in range(wafers):
            group = group_of(wafer, n)
            result += [
                counts[wafer * NSUB + g] + jnp.where(group == g, 1, 0) for g in range(NSUB)
            ]
        return tuple(result)

    members = lax.fori_loop(0, wafer_dets, count_members, (jnp.int32(0),) * (wafers * NSUB))
    for k, member in enumerate(members):
        share_ref[k] = 1.0 / jnp.maximum(zero + member.astype(jnp.float32), 1.0)
    for c in range(3):
        image_map[count, c] = zero
        r_map[count, c] = zero

    def clear_ends(detector, carry):
        clean_ref[detector, 0:ROWS, :] = zero
        clean_ref[detector, (octets + 1) * ROWS : (octets + 2) * ROWS, :] = zero
        return carry

    lax.fori_loop(0, wafers * wafer_dets, clear_ends, 0)

    def clear_sorted(n, carry):
        at = pl.ds(pl.multiple_of(n * ROWS, ROWS), ROWS)
        sorted_ref[at, :] = jnp.zeros((ROWS, 6 * PBLOCK), jnp.float32)
        return carry

    lax.fori_loop(0, sorted_ref.shape[0] // ROWS, clear_sorted, 0)
    for copy in angle_moves:
        copy.wait()

    def survey(at, carry):
        first, second = cosine_sine_double(angle_ref[at])
        inside = lax.shift_right_logical(at, halves.bit_length() - 1) & (ROWS - 1)
        base = float_smem[lax.div(at, tiles), 1, inside]
        cos_ref[at] = first
        sin_ref[at] = second
        image_map[at, 0] = zero + (base + base)
        image_map[at, 1] = fold(base * (first * first))
        image_map[at, 2] = fold(base * (second * second))
        return carry

    loop(count, survey, 0, 8)

    def merge_twins(target):
        def pair_batch(n, carry):
            found = []
            for k in range(PAIR_BATCH):
                key, lead, shift = (pair_ref[j, n * PAIR_BATCH + k] for j in range(3))
                spots = [
                    (lax.shift_right_logical(spot, 3), pl.ds(spot & (ROWS - 1), 1))
                    for spot in (key, lead)
                ]
                values = [[target[at, c, row, :] for c in range(3)] for at, row in spots]
                found.append((spots, shift, values))
            for spots, shift, values in found:
                turns = (shift, (LANES - shift) & (LANES - 1))
                for (at, row), own, other, turn in zip(
                    spots, values, values[::-1], turns[::-1]
                ):
                    for c in range(3):
                        target[at, c, row, :] = own[c] + pltpu.roll(wide(other[c]), turn, 1)[0:1]
            return carry

        def gather_one(n, carry):
            key, lead, shift = (group_ref[j, n] for j in range(3))
            at, row = lax.shift_right_logical(key, 3), key & (ROWS - 1)
            lead_at, lead_row = lax.shift_right_logical(lead, 3), lead & (ROWS - 1)
            for c in range(3):
                moved = pltpu.roll(wide(target[at, c, pl.ds(row, 1), :]), shift, 1)
                target[lead_at, c, pl.ds(lead_row, 1), :] += moved[0:1]
            return carry

        def spread_one(n, carry):
            key, lead, shift = (group_ref[j, n] for j in range(3))
            at, row = lax.shift_right_logical(key, 3), key & (ROWS - 1)
            lead_at, lead_row = lax.shift_right_logical(lead, 3), lead & (ROWS - 1)
            turn = (LANES - shift) & (LANES - 1)
            for c in range(3):
                moved = pltpu.roll(wide(target[lead_at, c, pl.ds(lead_row, 1), :]), turn, 1)
                target[at, c, pl.ds(row, 1), :] = moved[0:1]
            return carry

        lax.fori_loop(0, size_ref[0], pair_batch, 0)
        lax.fori_loop(0, size_ref[1], gather_one, 0)
        lax.fori_loop(0, size_ref[1], spread_one, 0)

    def clear_sums(refs):
        for ref in refs:
            for group in range(NSUB):
                for octet in range(octets):
                    ref[group, rows_of(octet), :] = zero

    def average(refs):
        for wafer, ref in enumerate(refs):
            for group in range(NSUB):
                for octet in range(octets):
                    ref[group, rows_of(octet), :] *= share_ref[wafer * NSUB + group]

    def sum_streams(stream_of, carry):
        clear_sums(first_sums)

        def one_detector(n, carry):
            for wafer in range(wafers):
                group = group_of(wafer, n)
                for octet in range(octets):
                    stream, carry = stream_of(register_of(wafer, n, octet), carry)
                    clean_ref[wafer * wafer_dets + n, rows_of(octet, ROWS), :] = stream
                    first_sums[wafer][group, rows_of(octet), :] += stream
            return carry

        carry = loop(wafer_dets, one_detector, carry, 2)
        average(first_sums)
        return carry

    def filter_streams():
        def one_removal(n, carry):
            for wafer in range(wafers):
                group = group_of(wafer, n)
                for octet in range(octets):
                    clean_ref[wafer * wafer_dets + n, rows_of(octet, ROWS), :] -= first_sums[wafer][
                        group, rows_of(octet), :
                    ]
            return carry

        loop(wafer_dets, one_removal, 0, 4)
        clear_sums(second_sums)

        def one_filter(n, carry):
            for wafer in range(wafers):
                device, inside = device_of(wafer, n), n & (ROWS - 1)
                detector = wafer * wafer_dets + n
                group = group_of(wafer, n)
                base = float_smem[device, 1, inside]
                coefs = [float_smem[device, 1, (j + 1) * ROWS + inside] for j in range(lag_count)]
                lags = [whole_smem[device, 2, (j + 1) * ROWS + inside] for j in range(lag_count)]
                for octet in range(octets):
                    here = clean_ref[detector, rows_of(octet, ROWS), :]
                    after = clean_ref[detector, rows_of(octet, ROWS + 1), :]
                    ahead = clean_ref[detector, rows_of(octet, ROWS - 1), :]
                    result = base * here
                    for coef, lag in zip(coefs, lags):
                        later = pltpu.roll(jnp.where(lane < lag, after, here), LANES - lag, 1)
                        earlier = pltpu.roll(jnp.where(lane >= LANES - lag, ahead, here), lag, 1)
                        result = result + coef * (later + earlier)
                    noise_ref[detector, rows_of(octet), :] = result
                    second_sums[wafer][group, rows_of(octet), :] += result
                    carry = carry + here * result
            return carry

        product = loop(wafer_dets, one_filter, zero, 1)
        average(second_sums)
        return product

    def return_streams(target):
        def one_return(n, carry):
            for wafer in range(wafers):
                group = group_of(wafer, n)
                for octet in range(octets):
                    at = register_of(wafer, n, octet)
                    stream = noise_ref[wafer * wafer_dets + n, rows_of(octet), :]
                    stream = stream - second_sums[wafer][group, rows_of(octet), :]
                    target[at, 0] = fold(stream)
                    target[at, 1] = fold(cos_ref[at] * stream)
                    target[at, 2] = fold(sin_ref[at] * stream)
            return carry

        loop(wafer_dets, one_return, 0, 2)
        merge_twins(target)

    merge_twins(image_map)
    for copy in tod_moves:
        copy.wait()
    sum_streams(lambda at, carry: (tod_ref[at], carry), 0)
    filter_streams()
    return_streams(r_map)

    def begin(at, carry):
        parts = zero
        for c in range(3):
            inverse = 1.0 / (image_map[at, c] + prior_weight)
            inverse_ref[at, c] = inverse
            residual = r_map[at, c]
            parts = parts + residual * (inverse * residual)
        return carry + weight_ref[at] * parts

    energy = whole_sum(loop(count, begin, zero, 8))
    factor = zero
    for iteration in range(ITERS):
        last = iteration == ITERS - 1

        def seen_stream(at, carry):
            parts = []
            for c in range(3):
                part = inverse_ref[at, c] * r_map[at, c]
                if iteration:
                    part = part + factor * d_map[at, c]
                d_map[at, c] = part
                parts.append(part)
            squares = parts[0] * parts[0] + parts[1] * parts[1] + parts[2] * parts[2]
            stream = parts[0] + cos_ref[at] * parts[1] + sin_ref[at] * parts[2]
            return stream, carry + weight_ref[at] * squares

        prior = sum_streams(seen_stream, zero)
        product = filter_streams()
        return_streams(image_map)
        step = energy / whole_sum(product + prior_weight * prior)

        def advance(at):
            new_x, new_r = [], []
            for c in range(3):
                direction = d_map[at, c]
                image = image_map[at, c] + prior_weight * direction
                move = step * direction
                new_x.append(x_map[at, c] + move if iteration else move)
                new_r.append(r_map[at, c] - step * image)
            return new_x, new_r

        if not last:

            def update(at, carry):
                new_x, new_r = advance(at)
                parts = zero
                for c in range(3):
                    x_map[at, c] = new_x[c]
                    r_map[at, c] = new_r[c]
                    parts = parts + new_r[c] * (inverse_ref[at, c] * new_r[c])
                return carry + weight_ref[at] * parts

            next_energy = whole_sum(loop(count, update, zero, 8))
            factor = next_energy / energy
            energy = next_energy
        else:

            def place_pixels(at, carry):
                new_x, new_r = advance(at)
                team = lax.rem(lax.div(at, reps * tiles), dets)
                inside = lax.shift_right_logical(at, halves.bit_length() - 1) & (ROWS - 1)
                turn = (3 * (team * ROWS + inside)) & (PBLOCK - 1)
                values = [pltpu.roll(value, turn, 1) for value in new_x + new_r]
                rows = pl.ds(pl.multiple_of(at * ROWS, ROWS), ROWS)
                for c in range(3):
                    rows_ref[rows, c * LANES : (c + 1) * LANES] = jnp.where(
                        lane < PBLOCK, values[2 * c], values[2 * c + 1]
                    )
                return carry

            loop(count, place_pixels, 0, 8)

    def pick(device, carry):
        for c in range(capacity):
            source, target = source_ref[device, c], target_ref[device, c]
            sorted_ref[pl.ds(target, 1), :] = rows_ref[pl.ds(source, 1), :]
        return carry

    lax.fori_loop(0, devices, pick, 0)

    def turn_tile(tile, carry):
        columns = sorted_ref[pl.ds(pl.multiple_of(tile * LANES, LANES), LANES), :].T
        high = columns.astype(jnp.bfloat16)
        column_ref[tile, :, 0:LANES] = high
        column_ref[tile, :, LANES : 2 * LANES] = (columns - high.astype(jnp.float32)).astype(
            jnp.bfloat16
        )
        return carry

    lax.fori_loop(0, column_ref.shape[0], turn_tile, 0)


def write_kernel(start_ref, column_ref, place_ref, x_ref, r_ref):
    height = 3 * PBLOCK
    depth = lax.broadcasted_iota(jnp.int32, (LANES, LANES), 0)
    for pair in range(OUT_TILES // 2):
        group = pl.program_id(0) * OUT_TILES + 2 * pair
        start, end = start_ref[0, group], start_ref[0, group + 2]
        first = lax.shift_right_logical(start, 7)
        last = lax.shift_right_logical(jnp.maximum(end - 1, start), 7)
        places = [jnp.broadcast_to(place_ref[pl.ds(group + k, 1), :], (LANES, LANES)) for k in (0, 1)]
        columns = slice(pair * 2 * LANES, (pair + 1) * 2 * LANES)

        def spread(tile):
            chosen = jnp.concatenate(
                [
                    jnp.where(place == depth + tile * LANES, 1.0, 0.0).astype(jnp.bfloat16)
                    for place in places
                ],
                axis=1,
            )
            chosen = jnp.concatenate([chosen, chosen], axis=0)
            return jnp.dot(column_ref[tile], chosen, preferred_element_type=jnp.float32)

        values = spread(first)
        x_ref[:, columns] = values[:height]
        r_ref[:, columns] = values[height:]

        def further(tile, carry):
            values = spread(tile)
            x_ref[:, columns] += values[:height]
            r_ref[:, columns] += values[height:]
            return carry

        lax.fori_loop(first + 1, last + 1, further, 0)


def part_shape(sizes, tod, hit_list, band_lag):
    det_count, time_count = tod.shape[1:]
    owners, capacity = hit_list.shape[3:]
    return (
        sizes["wafer"], sizes["det"], sizes["rep"], time_count // SBLOCK,
        owners, capacity, BLOCKS // owners, band_lag.shape[2],
    ), det_count


def fits_one_device(shape, det_count):
    wafers, dets, reps, tiles, owners, capacity, owner_rows, lag_count = shape
    devices = wafers * dets * reps
    total = devices * tiles * det_count
    groups = owner_rows // LANES
    return (
        det_count == ROWS
        and owners == ROWS
        and tiles * ROWS == LANES
        and tiles % ROWS == 0
        and (wafers, reps) == (2, 2)
        and (1 + lag_count) * ROWS <= LANES
        and capacity <= LANES
        and devices * capacity % LANES == 0
        and owner_rows % (LANES * OUT_TILES) == 0
        and groups + 2 <= 2 * LANES
        and total * total < BIG
    )


def whole_part(shape, tod, psi, point_row, hit_list, group_id, a_zero, band_coef, band_lag):
    wafers, dets, reps, tiles, owners, capacity, owner_rows, lag_count = shape
    devices = wafers * dets * reps
    octets = reps * tiles // ROWS
    detectors = wafers * dets * ROWS
    count = devices * tiles
    total = count * ROWS
    slots = devices * capacity
    height = 3 * PBLOCK
    f32, i32 = jnp.float32, jnp.int32
    vmem, smem = pl.BlockSpec(memory_space=pltpu.VMEM), pl.BlockSpec(memory_space=pltpu.SMEM)
    anywhere = pl.BlockSpec(memory_space=pl.ANY)
    params = pltpu.CompilerParams(vmem_limit_bytes=VMEM_BYTES)
    swap = [(0, 1), (1, 0)]

    def along_det(block):
        moved = [
            lax.ppermute(block, "det", [(i, (i + shift) % dets) for i in range(dets)])
            for shift in range(1, dets)
        ]
        return [block] + moved

    def other_wafer(here):
        return lax.ppermute(here, "wafer", swap)

    def other_rep(here, across):
        return here, across, lax.ppermute(jnp.stack([here, across]), "rep", swap)

    tables, angles, samples = pl.pallas_call(
        functools.partial(pack_kernel, shape),
        out_shape=[
            jax.ShapeDtypeStruct((ROWS, 2 * LANES), f32),
            jax.ShapeDtypeStruct((ROWS, tiles, LANES), f32),
            jax.ShapeDtypeStruct((ROWS, tiles, LANES), f32),
        ],
        in_specs=[vmem] * 8,
        out_specs=[vmem] * 3,
        compiler_params=params,
        name="pack",
    )(
        psi[0], tod[0], point_row[0], hit_list[0, 0, 0], group_id, a_zero, band_coef[0].T,
        band_lag[0].T,
    )
    angles, samples = (stream.reshape(tiles, ROWS, LANES) for stream in (angles, samples))
    place_here = jnp.stack([lax.axis_index(axis) for axis in ("wafer", "det", "rep")]).astype(i32)
    angles, *tables = lax.optimization_barrier((angles, *along_det(tables)))
    tables = jnp.stack(tables)
    table_blocks = other_rep(tables, other_wafer(tables))
    samples, angles, *table_blocks = lax.optimization_barrier(
        (samples, jnp.stack(along_det(angles)), *table_blocks)
    )
    angles_across = other_wafer(angles)
    samples = jnp.stack(along_det(samples))
    lists = pl.pallas_call(
        functools.partial(list_kernel, shape),
        out_shape=[
            jax.ShapeDtypeStruct((count, ROWS, LANES), f32),
            jax.ShapeDtypeStruct((2 * LANES, LANES), i32),
            jax.ShapeDtypeStruct((ROWS, 2 * LANES), i32),
            jax.ShapeDtypeStruct((devices, ROWS, LANES), f32),
            jax.ShapeDtypeStruct((devices, ROWS, LANES), i32),
            jax.ShapeDtypeStruct((2,), i32),
            jax.ShapeDtypeStruct((3, total), i32),
            jax.ShapeDtypeStruct((3, total), i32),
            jax.ShapeDtypeStruct((devices, capacity), i32),
            jax.ShapeDtypeStruct((devices, capacity), i32),
        ],
        in_specs=[smem] + [anywhere] * 3,
        out_specs=[vmem] * 5 + [smem] * 5,
        scratch_shapes=[
            pltpu.VMEM((devices, ROWS, 2 * LANES), f32),
            pltpu.VMEM((devices, ROWS, LANES), f32),
            pltpu.VMEM((devices, ROWS, LANES), f32),
            pltpu.VMEM((devices, LANES), i32),
            pltpu.VMEM((devices, LANES), i32),
            pltpu.SMEM((devices, LANES), i32),
            pltpu.SMEM((devices, LANES), i32),
            pltpu.SemaphoreType.DMA((devices,)),
            pltpu.SemaphoreType.DMA((2,)),
        ],
        compiler_params=params,
        cost_estimate=pl.CostEstimate(flops=10**9, bytes_accessed=4 * 10**7, transcendentals=0),
        name="lists",
    )(place_here, *table_blocks)
    angles, angles_across, samples, *lists = lax.optimization_barrier(
        (angles, angles_across, samples, *lists)
    )
    weight, place, start, floats, whole, size, pair, group, source, target = lists
    angle_blocks = other_rep(angles, angles_across)
    sample_blocks = other_rep(samples, other_wafer(samples))
    stream = pltpu.VMEM((count, ROWS, LANES), f32)
    sky = pltpu.VMEM((count, 3, ROWS, LANES), f32)
    sky_and_spare = pltpu.VMEM((count + 1, 3, ROWS, LANES), f32)
    group_sums = pltpu.VMEM((NSUB, octets * ROWS, LANES), f32)
    columns = pl.pallas_call(
        functools.partial(map_kernel, shape),
        out_shape=jax.ShapeDtypeStruct((slots // LANES + 1, 2 * height, 2 * LANES), jnp.bfloat16),
        in_specs=[smem] * 8 + [anywhere] * 6 + [vmem],
        out_specs=vmem,
        scratch_shapes=[
            stream, stream, stream, stream,
            pltpu.VMEM((detectors, (octets + 2) * ROWS, LANES), f32),
            pltpu.VMEM((detectors, octets * ROWS, LANES), f32),
            sky, sky, sky_and_spare, sky, sky_and_spare,
            pltpu.VMEM((wafers * NSUB, ROWS, LANES), f32),
            pltpu.VMEM((total, 2 * height), f32),
            pltpu.VMEM((slots + LANES + ROWS, 2 * height), f32),
            pltpu.SemaphoreType.DMA((devices,)),
            pltpu.SemaphoreType.DMA((devices,)),
        ] + [group_sums] * (2 * wafers),
        compiler_params=params,
        name="map_maker",
    )(
        place_here, size, pair, group, source, target, floats, whole, *angle_blocks,
        *sample_blocks, weight,
    )
    out_block = pl.BlockSpec((height, OUT_TILES * LANES), lambda n: (0, n))
    x_turned, r_turned = pl.pallas_call(
        write_kernel,
        grid=(owner_rows // (OUT_TILES * LANES),),
        out_shape=[jax.ShapeDtypeStruct((height, owner_rows), f32)] * 2,
        in_specs=[smem, vmem, vmem],
        out_specs=[out_block, out_block],
        compiler_params=params,
        name="write",
    )(start, columns, place)
    return x_turned.T, r_turned.T


def local(sizes, *arguments):
    tod, hit_list, band_lag = arguments[0], arguments[3], arguments[7]
    shape, det_count = part_shape(sizes, tod, hit_list, band_lag)
    if fits_one_device(shape, det_count):
        return whole_part(shape, *arguments)
    return distributed(*arguments)


def solution(mesh):
    placed = (
        P(("groups", "wafer"), "det", "rep"),
        P(("groups", "wafer"), "det", "rep"),
        P(("groups", "wafer"), "det", "rep"),
        P(("groups", "wafer"), "det", "rep", None, None),
        P(("groups", "wafer"), "det"),
        P(("groups", "wafer"), "det"),
        P(("groups", "wafer"), "det", None),
        P(("groups", "wafer"), "det", None),
    )
    return jax.shard_map(
        functools.partial(local, mesh.shape),
        mesh=mesh,
        in_specs=placed,
        out_specs=(P(("groups", "det", "wafer"), None), P(("groups", "det", "wafer"), None)),
        check_vma=False,
    )
```

```python
import functools

import jax
import jax.numpy as jnp
from jax import lax
from jax.experimental import pallas as pl
from jax.experimental.pallas import tpu as pltpu
from jax.sharding import PartitionSpec as P

BLOCKS = 196608
PBLOCK = 64
SBLOCK = 128
NSUB = 4
LAG = 16
ITERS = 3


prior_weight = 1.0


def with_halo(block, sides, width):
    for axis, dim in sides:
        count = lax.axis_size(axis)
        forward = [(i, i + 1) for i in range(count - 1)]
        backward = [(target, source) for source, target in forward]
        low = lax.ppermute(
            lax.slice_in_dim(block, block.shape[dim] - width, None, axis=dim), axis, forward
        )
        high = lax.ppermute(lax.slice_in_dim(block, 0, width, axis=dim), axis, backward)
        block = jnp.concatenate([low, block, high], axis=dim)
    return block


def distributed(tod, psi, point_row, hit_list, group_id, a_zero, band_coef, band_lag):
    highest = lax.Precision.HIGHEST
    samples = tod[0]
    angles = psi[0]
    det_count, time_count = samples.shape
    time_blocks = time_count // SBLOCK
    block_count = det_count * time_blocks
    send_table = hit_list[0, 0, 0]
    owner_count, capacity = send_table.shape
    owner_rows = BLOCKS // owner_count
    block_width = 3 * PBLOCK
    detector = lax.axis_index("det") * det_count + jnp.arange(det_count, dtype=jnp.int32)
    within = (jnp.arange(SBLOCK, dtype=jnp.int32)[None, :] + 3 * detector[:, None]) % PBLOCK
    pixel_table = (within[:, :, None] == jnp.arange(PBLOCK, dtype=jnp.int32)[None, None, :]).astype(
        jnp.float32
    )
    cosine_two = jnp.cos(2.0 * angles).reshape(det_count, time_blocks, SBLOCK)
    sine_two = jnp.sin(2.0 * angles).reshape(det_count, time_blocks, SBLOCK)
    slot_ids = send_table.reshape(-1)
    row_source = jnp.concatenate([point_row[0].reshape(-1), jnp.zeros((1,), jnp.int32)])
    slot_rows = row_source[slot_ids].astype(jnp.float32).reshape(owner_count, capacity)
    member = (group_id[0][:, None] == jnp.arange(NSUB, dtype=jnp.int32)[None, :]).astype(
        jnp.float32
    )
    member_count = jnp.sum(member, axis=0)
    lag_table = (
        band_lag[0][:, :, None] == jnp.arange(1, LAG + 1, dtype=jnp.int32)[None, None, :]
    ).astype(jnp.float32)
    lag_weight = jnp.einsum("dj,djl->dl", band_coef[0], lag_table, precision=highest)
    base_weight = a_zero[0]

    def slot_payload(by_block):
        width = by_block.shape[1]
        extended = jnp.concatenate([by_block, jnp.zeros((1, width), by_block.dtype)])
        return extended[slot_ids].reshape(owner_count, capacity, width)

    def deliver(payload):
        width = payload.shape[-1]
        got_values, got_rows = (
            lax.all_to_all(payload, ("det", "wafer"), split_axis=0, concat_axis=0, tiled=True),
            lax.all_to_all(slot_rows, ("det", "wafer"), split_axis=0, concat_axis=0, tiled=True),
        )
        return (got_values, got_rows)

    def back_project(stream, squared):
        shaped = stream.reshape(det_count, time_blocks, SBLOCK)
        first = cosine_two * cosine_two if squared else cosine_two
        second = sine_two * sine_two if squared else sine_two
        stacked = jnp.stack([shaped, first * shaped, second * shaped], axis=2)
        stokes = jnp.einsum("dkcs,dsp->dkcp", stacked, pixel_table, precision=highest)
        return stokes.reshape(block_count, block_width)

    def to_owners(stream, squared):
        got_values, got_rows = deliver(slot_payload(back_project(stream, squared)))
        pair_values, pair_rows = (
            lax.all_gather(got_values, "rep", axis=0, tiled=True),
            lax.all_gather(got_rows, "rep", axis=0, tiled=True),
        )
        target_rows = pair_rows.reshape(-1).astype(jnp.int32)
        summed = (
            jnp.zeros((owner_rows, block_width), jnp.float32)
            .at[target_rows]
            .add(pair_values.reshape(-1, block_width))
        )
        return (summed, got_rows.astype(jnp.int32))

    def remove_common(stream):
        local_sums = jnp.einsum("dg,dt->gt", member, stream, precision=highest)
        group_sums, group_counts = lax.psum((local_sums, member_count), "det")
        group_means = group_sums / jnp.maximum(group_counts, 1.0)[:, None]
        return stream - jnp.einsum("dg,gt->dt", member, group_means, precision=highest)

    def band_filter(stream):
        padded = with_halo(stream, (("rep", 1),), LAG)
        result = base_weight[:, None] * stream
        for offset in range(1, LAG + 1):
            later = padded[:, LAG + offset : LAG + offset + time_count]
            earlier = padded[:, LAG - offset : LAG - offset + time_count]
            result = result + lag_weight[:, offset - 1 : offset] * (later + earlier)
        return result

    def weigh_stream(stream):
        return remove_common(band_filter(remove_common(stream)))

    weight_stream = jnp.broadcast_to(base_weight[:, None], (det_count, time_count))
    diag_sum, serve_rows = to_owners(weight_stream, True)
    inverse_diag = 1.0 / (diag_sum + prior_weight)
    right_side = to_owners(weigh_stream(samples), False)[0]
    solution = jnp.zeros_like(right_side)
    residual = right_side

    def inner(left_map, right_map):
        return lax.psum(jnp.sum(left_map * right_map), ("det", "wafer"))

    precond = inverse_diag * residual
    direction = precond
    energy = inner(residual, precond)
    for iteration in range(ITERS):
        from_blocks = direction[serve_rows.reshape(-1)].reshape(owner_count, capacity, block_width)
        return_width = from_blocks.shape[-1]
        returned = lax.all_to_all(
            from_blocks, ("det", "wafer"), split_axis=0, concat_axis=0, tiled=True
        )
        return_placed = jnp.zeros((block_count + 1, return_width), jnp.float32)
        return_placed = return_placed.at[slot_ids].set(returned.reshape(-1, return_width))
        blocks = return_placed[:block_count].reshape(det_count, time_blocks, 3, PBLOCK)
        project_stokes = jnp.einsum("dkcp,dsp->dkcs", blocks, pixel_table, precision=highest)
        project_stream = (
            project_stokes[:, :, 0]
            + cosine_two * project_stokes[:, :, 1]
            + sine_two * project_stokes[:, :, 2]
        )
        seen_stream = project_stream.reshape(det_count, time_count)
        image_map = to_owners(weigh_stream(seen_stream), False)[0] + prior_weight * direction
        step_size = energy / inner(direction, image_map)
        solution = solution + step_size * direction
        residual = residual - step_size * image_map
        precond = inverse_diag * residual
        energy_next = inner(residual, precond)
        direction = precond + energy_next / energy * direction
        energy = energy_next
    return (solution, residual)


LANES = 128
ROWS = 8
OUT_TILES = 8
PAIR_BATCH = 4
BIG = float(1 << 24)
VMEM_BYTES = 60 << 20


def wide(values):
    return jnp.broadcast_to(values, (ROWS, LANES))


def tile_iotas():
    lane = lax.broadcasted_iota(jnp.int32, (ROWS, LANES), 1)
    sub = lax.broadcasted_iota(jnp.int32, (ROWS, LANES), 0)
    return lane, sub


def cosine_sine_double(angle):
    turns = jnp.floor(angle * 1.2732395447351628 + 0.5)
    reduced = 2.0 * angle - turns * 1.5703125
    reduced = reduced - turns * 4.837512969970703125e-4
    reduced = reduced - turns * 7.54978995489188216e-8
    square = reduced * reduced
    sine = (-1.9515295891e-4 * square + 8.3321608736e-3) * square - 1.6666654611e-1
    sine = sine * square * reduced + reduced
    cosine = (2.443315711809948e-5 * square - 1.388731625493765e-3) * square
    cosine = (cosine + 4.166664568298827e-2) * square * square - 0.5 * square + 1.0
    quarter = turns.astype(jnp.int32)
    odd = (quarter & 1) == 1
    first = jnp.where(odd, sine, cosine)
    second = jnp.where(odd, cosine, sine)
    first = jnp.where(((quarter + 1) & 2) == 2, -first, first)
    second = jnp.where((quarter & 2) == 2, -second, second)
    return first, second


def pack_kernel(
    shape, angle_ref, tod_ref, row_ref, hit_ref, group_ref, base_ref, coef_ref, lag_ref,
    table_ref, angle_rows_ref, tod_rows_ref,
):
    wafers, dets, reps, tiles, owners, capacity, owner_rows, lag_count = shape
    lane, sub = tile_iotas()
    lists = hit_ref[...]
    owner_hits = jnp.zeros((ROWS, LANES), jnp.float32)
    for c in range(capacity):
        owner_hits = owner_hits + jnp.where(wide(lists[:, c : c + 1]) == lane, 1.0, 0.0)
    owner_of = jnp.sum(owner_hits * sub.astype(jnp.float32), axis=0, keepdims=True)

    def spread(values, width):
        return jnp.concatenate(
            [values, jnp.zeros((values.shape[0], LANES - width), values.dtype)], axis=1
        )

    rows = spread(row_ref[...].astype(jnp.float32), tiles)
    ids = owner_of * float(owner_rows) + rows[0:1]
    for k in range(1, ROWS):
        ids = ids + pltpu.roll(rows[k : k + 1], k * tiles, 1)
    floats = spread(base_ref[...], ROWS)
    whole = spread(group_ref[...].astype(jnp.float32), ROWS)
    for j in range(lag_count):
        at = (j + 1) * ROWS
        floats = floats + pltpu.roll(spread(coef_ref[j : j + 1, :], ROWS), at, 1)
        lag = lag_ref[j : j + 1, :].astype(jnp.float32)
        whole = whole + pltpu.roll(spread(lag, ROWS), at, 1)
    table = jnp.where(sub == 0, wide(ids), jnp.where(sub == 1, wide(floats), wide(whole)))
    table_ref[:, 0:LANES] = table
    table_ref[:, LANES : 2 * LANES] = spread(lists.astype(jnp.float32), capacity)
    for b in range(tiles):
        angle_rows_ref[:, b, :] = angle_ref[:, b * LANES : (b + 1) * LANES]
        tod_rows_ref[:, b, :] = tod_ref[:, b * LANES : (b + 1) * LANES]


def part_copies(shape, self_ref, refs, target, sem):
    wafers, dets, reps = shape[:3]
    here_ref, across_ref, other_ref = refs
    copies = []
    for swap_rep in range(reps):
        for swap_wafer in range(wafers):
            for shift in range(dets):
                if swap_rep:
                    source = other_ref.at[swap_wafer, shift]
                else:
                    source = (across_ref if swap_wafer else here_ref).at[shift]
                wafer = self_ref[0] ^ swap_wafer
                det = self_ref[1] - shift
                det = jnp.where(det < 0, det + dets, det)
                device = (wafer * dets + det) * reps + (self_ref[2] ^ swap_rep)
                copies.append(
                    pltpu.make_async_copy(source, target(device), sem.at[len(copies)])
                )
    return copies


def table_copies(shape, self_ref, refs, part_ref, sem):
    wafers, dets, reps = shape[:3]
    chips = wafers * dets
    here = self_ref[1] * wafers + self_ref[0]
    copies = []
    for shift, ref in enumerate(refs):
        chip = here - shift
        chip = jnp.where(chip < 0, chip + chips, chip)
        team = lax.rem(chip, wafers) * dets + lax.div(chip, wafers)
        to = part_ref.at[pl.ds(team * reps, reps)]
        copies.append(pltpu.make_async_copy(ref, to, sem.at[shift]))
    for copy in copies:
        copy.start()
    for copy in copies:
        copy.wait()


def exact_dot(left, right, dims=((1,), (0,))):
    return lax.dot_general(
        left.astype(jnp.bfloat16), right.astype(jnp.bfloat16), (dims, ((), ())),
        preferred_element_type=jnp.float32,
    )


def twin_kernel(shape, self_ref, *refs):
    wafers, dets, reps, tiles, owners, capacity, owner_rows, lag_count = shape
    devices = wafers * dets * reps
    total = devices * LANES
    table_refs, refs = refs[: wafers * dets], refs[wafers * dets :]
    weight_ref, float_ref, whole_ref, size_ref, pair_ref, group_ref = refs[:6]
    part_ref, code_ref, lead_ref, part_sem = refs[6:]
    lane, sub = tile_iotas()
    lane_f = lane.astype(jnp.float32)
    table_copies(shape, self_ref, table_refs, part_ref, part_sem)

    def survey(device, carry):
        float_ref[pl.ds(device, 1), :] = part_ref[device, 1:2, 0:LANES]
        whole_ref[pl.ds(device, 1), :] = part_ref[device, 2:3, 0:LANES].astype(jnp.int32)
        ids = jnp.broadcast_to(part_ref[device, 0:1, 0:LANES], (LANES, LANES)).T
        ids = [ids[j * ROWS : (j + 1) * ROWS] for j in range(tiles)]

        def compare(other, state):
            key, least = state
            row = wide(part_ref[other, 0:1, 0:LANES])
            least = [
                jnp.minimum(least[j], jnp.where(ids[j] == row, key, BIG)) for j in range(tiles)
            ]
            return key + LANES, least

        none = jnp.full((ROWS, LANES), BIG, jnp.float32)
        _, least = lax.fori_loop(0, device + 1, compare, (lane_f, [none] * tiles))
        codes, leads = none, none
        for j in range(tiles):
            lead = jnp.min(least[j], axis=1, keepdims=True)
            mine = (device * LANES + j * ROWS + sub[:, 0:1]).astype(jnp.float32)
            weight_ref[device * tiles + j] = wide(jnp.where(lead == mine, 0.5, 0.0))
            later = lead < mine
            leads = jnp.where(lane == j, jnp.where(later, lead, BIG), leads)
            codes = jnp.where(lane == j, jnp.where(later, mine * float(total) + lead, BIG), codes)
        code_ref[device] = codes
        lead_ref[device] = leads
        return carry

    lax.fori_loop(0, devices, survey, 0)

    def next_code(last):
        found = jnp.full((ROWS, LANES), BIG, jnp.float32)
        for device in range(devices):
            codes = code_ref[device]
            found = jnp.minimum(found, jnp.where(codes > last, codes, BIG))
        return jnp.min(found)

    def detector(key):
        team = lax.rem(lax.div(key, reps * LANES), dets)
        return team * ROWS + lax.rem(lax.div(key, tiles), ROWS)

    def take(state):
        pairs, grouped, code = state
        number = code.astype(jnp.int32)
        key = lax.div(number, total)
        lead = lax.rem(number, total)
        shift = (3 * (detector(key) - detector(lead))) & (PBLOCK - 1)
        wanted = lead.astype(jnp.float32)
        same = jnp.zeros((ROWS, LANES), jnp.float32)
        for device in range(devices):
            same = same + jnp.where(lead_ref[device] == wanted, 1.0, 0.0)
        alone = jnp.sum(same) < 1.5
        entry = twin_entry(key, lead, shift)
        pair_ref[pairs] = entry
        group_ref[grouped] = entry
        return (
            pairs + jnp.where(alone, 1, 0), grouped + jnp.where(alone, 0, 1), next_code(code)
        )

    pairs, grouped, _ = lax.while_loop(
        lambda state: state[2] < BIG, take,
        (jnp.int32(0), jnp.int32(0), next_code(jnp.float32(-1.0))),
    )
    batches = lax.div(pairs + PAIR_BATCH - 1, PAIR_BATCH)

    def fill(n, carry):
        pair_ref[n] = twin_entry(total, total + 1, 0)
        return carry

    lax.fori_loop(pairs, batches * PAIR_BATCH, fill, 0)
    size_ref[0] = batches
    size_ref[1] = grouped


def twin_entry(key, lead, shift):
    return key * (1 << 19) + lead * (1 << 6) + shift


def twin_of(entry):
    return entry >> 19, (entry >> 6) & ((1 << 13) - 1), entry & (PBLOCK - 1)


def place_kernel(shape, self_ref, *refs):
    wafers, dets, reps, tiles, owners, capacity, owner_rows, lag_count = shape
    devices = wafers * dets * reps
    slots = devices * capacity
    table_refs, refs = refs[: wafers * dets], refs[wafers * dets :]
    place_ref, start_ref, move_ref = refs[:3]
    part_ref, rank_ref, hits_ref, rank_smem, hits_smem, part_sem, table_sem = refs[3:]
    lane, sub = tile_iotas()
    own = self_ref[1] * wafers + self_ref[0]
    first_row = (own * owner_rows).astype(jnp.float32)
    table_copies(shape, self_ref, table_refs, part_ref, part_sem)
    depth = 2 * LANES
    tall = lax.broadcasted_iota(jnp.int32, (depth, LANES), 0).astype(jnp.float32)

    def one_hots(device):
        local_row = part_ref[device, 0:1, 0:LANES] - first_row
        high = jnp.floor(local_row * (1.0 / LANES))
        low = local_row - high * LANES
        high = (jnp.broadcast_to(high, (depth, LANES)) == tall).astype(jnp.float32)
        low = (jnp.broadcast_to(low, (LANES, LANES)) == tall[0:LANES]).astype(jnp.float32)
        return high, low

    def survey(pair, hits):
        for k in range(2):
            device = 2 * pair + k
            own_hits = jnp.where(sub == own, part_ref[device, :, LANES : 2 * LANES], 0.0)
            own_hits = jnp.sum(own_hits, axis=0, keepdims=True)
            hits_ref[pl.ds(device, 1), :] = own_hits.astype(jnp.int32)
            high, low = one_hots(device)
            hits = hits + exact_dot(high, low, ((1,), (1,)))
        return hits

    hits = lax.fori_loop(0, devices // 2, survey, jnp.zeros((depth, LANES), jnp.float32))
    full = jnp.minimum(hits, 1.0)

    def ordered(size, axis):
        first = lax.broadcasted_iota(jnp.int32, (size, size), axis)
        second = lax.broadcasted_iota(jnp.int32, (size, size), 1 - axis)
        return (first < second).astype(jnp.float32)

    counts = exact_dot(jnp.ones((ROWS, LANES), jnp.float32), full, ((1,), (1,)))
    start_ref[...] = exact_dot(counts, ordered(depth, 0)).astype(jnp.int32)
    sums = exact_dot(full, jnp.ones((LANES, LANES), jnp.float32))
    place = exact_dot(full, ordered(LANES, 0)) + exact_dot(ordered(depth, 1), sums)
    place_ref[...] = jnp.where(full > 0.0, place, -1.0).astype(jnp.int32)
    place_high = jnp.floor(place * (1.0 / LANES))
    place_parts = jnp.concatenate([place_high, place - place_high * LANES], axis=0)

    def rank_of(pair, carry):
        for k in range(2):
            device = 2 * pair + k
            high, low = one_hots(device)
            parts = exact_dot(place_parts, low)
            rank = high * (parts[0:depth] * LANES + parts[depth : 2 * depth])
            rank = jnp.sum(rank, axis=0, keepdims=True)
            rank_ref[pl.ds(device, 1), :] = rank.astype(jnp.int32)
        return carry

    lax.fori_loop(0, devices // 2, rank_of, 0)
    copies = (
        pltpu.make_async_copy(rank_ref, rank_smem, table_sem.at[0]),
        pltpu.make_async_copy(hits_ref, hits_smem, table_sem.at[1]),
    )
    for copy in copies:
        copy.start()
    for copy in copies:
        copy.wait()

    def pick(device, carry):
        for c in range(capacity):
            number = hits_smem[device, c]
            valid = number < LANES
            number = number & (LANES - 1)
            target = jnp.where(valid, rank_smem[device, number], slots + LANES)
            move_ref[device * capacity + c] = target * (1 << 16) + device * LANES + number
        return carry

    lax.fori_loop(0, devices, pick, 0)


def map_kernel(
    shape, self_ref, size_ref, pair_ref, group_ref, move_ref, float_smem, whole_smem,
    angle_here_ref, angle_across_ref, angle_other_ref, tod_here_ref, tod_across_ref, tod_other_ref,
    weight_ref, column_ref,
    angle_ref, tod_ref, cos_ref, sin_ref, clean_ref, noise_ref,
    inverse_ref, r_map, image_map, share_ref, rows_ref, sorted_ref, angle_sem, tod_sem, *more_refs,
):
    wafers, dets, reps, tiles, owners, capacity, owner_rows, lag_count = shape
    devices = wafers * dets * reps
    halves = tiles // ROWS
    octets = reps * halves
    wafer_dets = dets * ROWS
    count = devices * tiles
    lane, sub = tile_iotas()
    zero = jnp.zeros((ROWS, LANES), jnp.float32)
    d_maps, sum_refs = more_refs[:ITERS], more_refs[ITERS:]
    first_sums, second_sums = sum_refs[:wafers], sum_refs[wafers:]

    def copies_of(refs, to_ref, sem):
        return part_copies(
            shape, self_ref, refs, lambda d: to_ref.at[pl.ds(d * tiles, tiles)], sem
        )

    angle_moves = copies_of((angle_here_ref, angle_across_ref, angle_other_ref), angle_ref, angle_sem)
    tod_moves = copies_of((tod_here_ref, tod_across_ref, tod_other_ref), tod_ref, tod_sem)
    for copy in angle_moves + tod_moves:
        copy.start()

    def fold(block):
        return block + pltpu.roll(block, LANES // 2, 1)

    def whole_sum(values):
        values = jnp.sum(values, axis=0, keepdims=True)
        return wide(jnp.sum(values, axis=1, keepdims=True))

    def loop(times, body, carry, unroll):
        def several(n, carry):
            for k in range(unroll):
                carry = body(n * unroll + k, carry)
            return carry

        return lax.fori_loop(0, times // unroll, several, carry)

    def device_of(wafer, n):
        return (wafer * dets + lax.shift_right_logical(n, 3)) * reps

    def register_of(wafer, n, octet):
        device = device_of(wafer, n) + octet // halves
        return device * tiles + (n & (ROWS - 1)) * halves + octet % halves

    def group_of(wafer, n):
        return whole_smem[device_of(wafer, n), n & (ROWS - 1)]

    def rows_of(octet):
        return pl.ds(octet * ROWS, ROWS)

    def count_members(n, counts):
        result = []
        for wafer in range(wafers):
            group = group_of(wafer, n)
            result += [
                counts[wafer * NSUB + g] + jnp.where(group == g, 1, 0) for g in range(NSUB)
            ]
        return tuple(result)

    members = lax.fori_loop(0, wafer_dets, count_members, (jnp.int32(0),) * (wafers * NSUB))
    for k, member in enumerate(members):
        share_ref[k] = 1.0 / jnp.maximum(zero + member.astype(jnp.float32), 1.0)
    for c in range(3):
        image_map[count, c] = zero
        r_map[count, c] = zero

    def clear_sorted(n, carry):
        at = pl.ds(pl.multiple_of(n * ROWS, ROWS), ROWS)
        sorted_ref[at, :] = jnp.zeros((ROWS, 6 * PBLOCK), jnp.float32)
        return carry

    lax.fori_loop(0, sorted_ref.shape[0] // ROWS, clear_sorted, 0)
    for copy in angle_moves:
        copy.wait()

    def survey(at, carry):
        first, second = cosine_sine_double(angle_ref[at])
        inside = lax.shift_right_logical(at, halves.bit_length() - 1) & (ROWS - 1)
        base = float_smem[lax.div(at, tiles), inside]
        cos_ref[at] = first
        sin_ref[at] = second
        image_map[at, 0] = zero + (base + base)
        image_map[at, 1] = fold(base * (first * first))
        image_map[at, 2] = fold(base * (second * second))
        return carry

    loop(count, survey, 0, 8)

    def merge_twins(target):
        def pair_batch(n, carry):
            found = []
            for k in range(PAIR_BATCH):
                key, lead, shift = twin_of(pair_ref[n * PAIR_BATCH + k])
                spots = [
                    (lax.shift_right_logical(spot, 3), pl.ds(spot & (ROWS - 1), 1))
                    for spot in (key, lead)
                ]
                values = [[target[at, c, row, :] for c in range(3)] for at, row in spots]
                found.append((spots, shift, values))
            for spots, shift, values in found:
                turns = (shift, (LANES - shift) & (LANES - 1))
                for (at, row), own, other, turn in zip(
                    spots, values, values[::-1], turns[::-1]
                ):
                    for c in range(3):
                        target[at, c, row, :] = own[c] + pltpu.roll(wide(other[c]), turn, 1)[0:1]
            return carry

        def gather_one(n, carry):
            key, lead, shift = twin_of(group_ref[n])
            at, row = lax.shift_right_logical(key, 3), key & (ROWS - 1)
            lead_at, lead_row = lax.shift_right_logical(lead, 3), lead & (ROWS - 1)
            for c in range(3):
                moved = pltpu.roll(wide(target[at, c, pl.ds(row, 1), :]), shift, 1)
                target[lead_at, c, pl.ds(lead_row, 1), :] += moved[0:1]
            return carry

        def spread_one(n, carry):
            key, lead, shift = twin_of(group_ref[n])
            at, row = lax.shift_right_logical(key, 3), key & (ROWS - 1)
            lead_at, lead_row = lax.shift_right_logical(lead, 3), lead & (ROWS - 1)
            turn = (LANES - shift) & (LANES - 1)
            for c in range(3):
                moved = pltpu.roll(wide(target[lead_at, c, pl.ds(lead_row, 1), :]), turn, 1)
                target[at, c, pl.ds(row, 1), :] = moved[0:1]
            return carry

        lax.fori_loop(0, size_ref[0], pair_batch, 0)
        lax.fori_loop(0, size_ref[1], gather_one, 0)
        lax.fori_loop(0, size_ref[1], spread_one, 0)

    def clear_sums(refs):
        for ref in refs:
            for group in range(NSUB):
                for octet in range(octets):
                    ref[group, rows_of(octet), :] = zero

    def average(refs):
        for wafer, ref in enumerate(refs):
            for group in range(NSUB):
                for octet in range(octets):
                    ref[group, rows_of(octet), :] *= share_ref[wafer * NSUB + group]

    def sum_streams(stream_of, carry):
        clear_sums(first_sums)

        def one_detector(n, carry):
            for wafer in range(wafers):
                group = group_of(wafer, n)
                for octet in range(octets):
                    stream, carry = stream_of(register_of(wafer, n, octet), carry)
                    clean_ref[wafer * wafer_dets + n, rows_of(octet), :] = stream
                    first_sums[wafer][group, rows_of(octet), :] += stream
            return carry

        carry = loop(wafer_dets, one_detector, carry, 2)
        average(first_sums)
        return carry

    def filter_streams():
        clear_sums(second_sums)

        def one_filter(n, carry):
            for wafer in range(wafers):
                device, inside = device_of(wafer, n), n & (ROWS - 1)
                detector = wafer * wafer_dets + n
                group = group_of(wafer, n)
                base = float_smem[device, inside]
                coefs = [float_smem[device, (j + 1) * ROWS + inside] for j in range(lag_count)]
                lags = [whole_smem[device, (j + 1) * ROWS + inside] for j in range(lag_count)]
                clean = [
                    clean_ref[detector, rows_of(octet), :] - first_sums[wafer][group, rows_of(octet), :]
                    for octet in range(octets)
                ]
                up = [pltpu.roll(here, ROWS - 1, 0) for here in clean] + [zero]
                down = [zero] + [pltpu.roll(here, 1, 0) for here in clean]
                for octet, here in enumerate(clean):
                    after = jnp.where(sub == ROWS - 1, up[octet + 1], up[octet])
                    ahead = jnp.where(sub == 0, down[octet], down[octet + 1])
                    result = base * here
                    for coef, lag in zip(coefs, lags):
                        later = pltpu.roll(jnp.where(lane < lag, after, here), LANES - lag, 1)
                        earlier = pltpu.roll(jnp.where(lane >= LANES - lag, ahead, here), lag, 1)
                        result = result + coef * (later + earlier)
                    noise_ref[detector, rows_of(octet), :] = result
                    second_sums[wafer][group, rows_of(octet), :] += result
                    carry = carry + here * result
            return carry

        product = loop(wafer_dets, one_filter, zero, 1)
        average(second_sums)
        return product

    def return_streams(target):
        def one_return(n, carry):
            for wafer in range(wafers):
                group = group_of(wafer, n)
                for octet in range(octets):
                    at = register_of(wafer, n, octet)
                    stream = noise_ref[wafer * wafer_dets + n, rows_of(octet), :]
                    stream = stream - second_sums[wafer][group, rows_of(octet), :]
                    target[at, 0] = fold(stream)
                    target[at, 1] = fold(cos_ref[at] * stream)
                    target[at, 2] = fold(sin_ref[at] * stream)
            return carry

        loop(wafer_dets, one_return, 0, 2)
        merge_twins(target)

    merge_twins(image_map)
    for copy in tod_moves:
        copy.wait()
    sum_streams(lambda at, carry: (tod_ref[at], carry), 0)
    filter_streams()
    return_streams(r_map)

    def begin(at, carry):
        parts = zero
        for c in range(3):
            inverse = 1.0 / (image_map[at, c] + prior_weight)
            inverse_ref[at, c] = inverse
            residual = r_map[at, c]
            parts = parts + residual * (inverse * residual)
        return carry + weight_ref[at] * parts

    energy = whole_sum(loop(count, begin, zero, 8))
    factor = zero
    steps = []
    for iteration, d_map in enumerate(d_maps):
        last = iteration == ITERS - 1

        def seen_stream(at, carry):
            parts = []
            for c in range(3):
                part = inverse_ref[at, c] * r_map[at, c]
                if iteration:
                    part = part + factor * d_maps[iteration - 1][at, c]
                d_map[at, c] = part
                parts.append(part)
            squares = parts[0] * parts[0] + parts[1] * parts[1] + parts[2] * parts[2]
            stream = parts[0] + cos_ref[at] * parts[1] + sin_ref[at] * parts[2]
            return stream, carry + weight_ref[at] * squares

        prior = sum_streams(seen_stream, zero)
        product = filter_streams()
        return_streams(image_map)
        step = energy / whole_sum(product + prior_weight * prior)
        steps.append(step)

        def new_residual(at, c):
            return r_map[at, c] - step * (image_map[at, c] + prior_weight * d_map[at, c])

        if not last:

            def update(at, carry):
                parts = zero
                for c in range(3):
                    residual = new_residual(at, c)
                    r_map[at, c] = residual
                    parts = parts + residual * (inverse_ref[at, c] * residual)
                return carry + weight_ref[at] * parts

            next_energy = whole_sum(loop(count, update, zero, 8))
            factor = next_energy / energy
            energy = next_energy
        else:

            def place_pixels(at, carry):
                team = lax.rem(lax.div(at, reps * tiles), dets)
                inside = lax.shift_right_logical(at, halves.bit_length() - 1) & (ROWS - 1)
                turn = (3 * (team * ROWS + inside)) & (PBLOCK - 1)
                values = []
                for c in range(3):
                    value = steps[0] * d_maps[0][at, c]
                    for k in range(1, ITERS):
                        value = value + steps[k] * d_maps[k][at, c]
                    values.append(value)
                values += [new_residual(at, c) for c in range(3)]
                values = [pltpu.roll(value, turn, 1) for value in values]
                rows = pl.ds(pl.multiple_of(at * ROWS, ROWS), ROWS)
                for c in range(3):
                    rows_ref[rows, c * LANES : (c + 1) * LANES] = jnp.where(
                        lane < PBLOCK, values[2 * c], values[2 * c + 1]
                    )
                return carry

            loop(count, place_pixels, 0, 8)

    def pick(device, carry):
        for c in range(capacity):
            move = move_ref[device * capacity + c]
            source, target = move & ((1 << 16) - 1), move >> 16
            sorted_ref[pl.ds(target, 1), :] = rows_ref[pl.ds(source, 1), :]
        return carry

    lax.fori_loop(0, devices, pick, 0)

    def turn_tile(tile, carry):
        columns = sorted_ref[pl.ds(pl.multiple_of(tile * LANES, LANES), LANES), :].T
        high = columns.astype(jnp.bfloat16)
        column_ref[tile, :, 0:LANES] = high
        column_ref[tile, :, LANES : 2 * LANES] = (columns - high.astype(jnp.float32)).astype(
            jnp.bfloat16
        )
        return carry

    lax.fori_loop(0, column_ref.shape[0], turn_tile, 0)


def write_kernel(start_ref, column_ref, place_ref, x_ref, r_ref):
    height = 3 * PBLOCK
    depth = lax.broadcasted_iota(jnp.int32, (LANES, LANES), 0)
    step = pl.program_id(0) * OUT_TILES

    def spread(group, tile):
        chosen = []
        for k in range(2):
            place = jnp.broadcast_to(place_ref[pl.ds(group + k, 1), :], (LANES, LANES))
            chosen.append(jnp.where(place == depth + tile * LANES, 1.0, 0.0).astype(jnp.bfloat16))
        chosen = jnp.concatenate(chosen, axis=1)
        chosen = jnp.concatenate([chosen, chosen], axis=0)
        return jnp.dot(column_ref[tile], chosen, preferred_element_type=jnp.float32)

    def tiles_of(group):
        start, end = start_ref[0, group], start_ref[0, group + 2]
        first = lax.shift_right_logical(start, 7)
        return first, lax.shift_right_logical(jnp.maximum(end - 1, start), 7)

    further = 0
    for pair in range(OUT_TILES // 2):
        first, last = tiles_of(step + 2 * pair)
        further = further + (last - first)
        values = spread(step + 2 * pair, first)
        columns = slice(pair * 2 * LANES, (pair + 1) * 2 * LANES)
        x_ref[:, columns] = values[:height]
        r_ref[:, columns] = values[height:]

    @pl.when(further > 0)
    def _():
        for pair in range(OUT_TILES // 2):
            first, last = tiles_of(step + 2 * pair)
            columns = slice(pair * 2 * LANES, (pair + 1) * 2 * LANES)

            def add_tile(tile, carry):
                values = spread(step + 2 * pair, tile)
                x_ref[:, columns] += values[:height]
                r_ref[:, columns] += values[height:]
                return carry

            lax.fori_loop(first + 1, last + 1, add_tile, 0)


def part_shape(sizes, tod, hit_list, band_lag):
    det_count, time_count = tod.shape[1:]
    owners, capacity = hit_list.shape[3:]
    return (
        sizes["wafer"], sizes["det"], sizes["rep"], time_count // SBLOCK,
        owners, capacity, BLOCKS // owners, band_lag.shape[2],
    ), det_count


def fits_one_device(shape, det_count):
    wafers, dets, reps, tiles, owners, capacity, owner_rows, lag_count = shape
    devices = wafers * dets * reps
    total = devices * tiles * det_count
    groups = owner_rows // LANES
    return (
        det_count == ROWS
        and owners == ROWS
        and tiles * ROWS == LANES
        and tiles % ROWS == 0
        and (wafers, reps) == (2, 2)
        and (1 + lag_count) * ROWS <= LANES
        and capacity <= LANES
        and devices * capacity % LANES == 0
        and owner_rows % (LANES * OUT_TILES) == 0
        and groups + 2 <= 2 * LANES
        and total * total < BIG
    )


def whole_part(shape, tod, psi, point_row, hit_list, group_id, a_zero, band_coef, band_lag):
    wafers, dets, reps, tiles, owners, capacity, owner_rows, lag_count = shape
    devices = wafers * dets * reps
    octets = reps * tiles // ROWS
    detectors = wafers * dets * ROWS
    count = devices * tiles
    total = count * ROWS
    slots = devices * capacity
    height = 3 * PBLOCK
    f32, i32 = jnp.float32, jnp.int32
    vmem, smem = pl.BlockSpec(memory_space=pltpu.VMEM), pl.BlockSpec(memory_space=pltpu.SMEM)
    anywhere = pl.BlockSpec(memory_space=pl.ANY)
    params = pltpu.CompilerParams(vmem_limit_bytes=VMEM_BYTES)
    swap = [(0, 1), (1, 0)]

    def along_det(block):
        moved = [
            lax.ppermute(block, "det", [(i, (i + shift) % dets) for i in range(dets)])
            for shift in range(1, dets)
        ]
        return [block] + moved

    def other_wafer(here):
        return lax.ppermute(here, "wafer", swap)

    def other_rep(here, across):
        return here, across, lax.ppermute(jnp.stack([here, across]), "rep", swap)

    tables, angles, samples = pl.pallas_call(
        functools.partial(pack_kernel, shape),
        out_shape=[
            jax.ShapeDtypeStruct((ROWS, 2 * LANES), f32),
            jax.ShapeDtypeStruct((ROWS, tiles, LANES), f32),
            jax.ShapeDtypeStruct((ROWS, tiles, LANES), f32),
        ],
        in_specs=[vmem] * 8,
        out_specs=[vmem] * 3,
        compiler_params=params,
        name="pack",
    )(
        psi[0], tod[0], point_row[0], hit_list[0, 0, 0], group_id, a_zero, band_coef[0].T,
        band_lag[0].T,
    )
    angles, samples = (stream.reshape(tiles, ROWS, LANES) for stream in (angles, samples))
    place_here = jnp.stack([lax.axis_index(axis) for axis in ("wafer", "det", "rep")]).astype(i32)
    chips = wafers * dets
    tables = lax.all_gather(tables, "rep", axis=0, tiled=False)
    angles, tables = lax.optimization_barrier((angles, tables))
    tables = [tables] + [
        lax.ppermute(tables, ("det", "wafer"), [(i, (i + shift) % chips) for i in range(chips)])
        for shift in range(1, chips)
    ]
    samples, angles, *tables = lax.optimization_barrier(
        (samples, jnp.stack(along_det(angles)), *tables)
    )
    angles_across = other_wafer(angles)
    samples = jnp.stack(along_det(samples))
    table_scratch = pltpu.VMEM((devices, ROWS, 2 * LANES), f32)
    table_sem = pltpu.SemaphoreType.DMA((chips,))
    twins = pl.pallas_call(
        functools.partial(twin_kernel, shape),
        out_shape=[
            jax.ShapeDtypeStruct((count, ROWS, LANES), f32),
            jax.ShapeDtypeStruct((devices, LANES), f32),
            jax.ShapeDtypeStruct((devices, LANES), i32),
            jax.ShapeDtypeStruct((2,), i32),
            jax.ShapeDtypeStruct((total,), i32),
            jax.ShapeDtypeStruct((total,), i32),
        ],
        in_specs=[smem] + [anywhere] * chips,
        out_specs=[vmem] * 3 + [smem] * 3,
        scratch_shapes=[
            table_scratch,
            pltpu.VMEM((devices, ROWS, LANES), f32),
            pltpu.VMEM((devices, ROWS, LANES), f32),
            table_sem,
        ],
        compiler_params=params,
        cost_estimate=pl.CostEstimate(flops=10**9, bytes_accessed=3 * 10**7, transcendentals=0),
        name="twins",
    )(place_here, *tables)
    angles, angles_across, samples, tables, twins = lax.optimization_barrier(
        (angles, angles_across, samples, tables, twins)
    )
    weight, floats, whole, size, pair, group = twins
    samples_across = other_wafer(samples)
    place, start, moves = pl.pallas_call(
        functools.partial(place_kernel, shape),
        out_shape=[
            jax.ShapeDtypeStruct((2 * LANES, LANES), i32),
            jax.ShapeDtypeStruct((ROWS, 2 * LANES), i32),
            jax.ShapeDtypeStruct((slots,), i32),
        ],
        in_specs=[smem] + [anywhere] * chips,
        out_specs=[vmem, vmem, smem],
        scratch_shapes=[
            table_scratch,
            pltpu.VMEM((devices, LANES), i32),
            pltpu.VMEM((devices, LANES), i32),
            pltpu.SMEM((devices, LANES), i32),
            pltpu.SMEM((devices, LANES), i32),
            table_sem,
            pltpu.SemaphoreType.DMA((2,)),
        ],
        compiler_params=params,
        cost_estimate=pl.CostEstimate(flops=10**9, bytes_accessed=2 * 10**7, transcendentals=0),
        name="places",
    )(place_here, *tables)
    angle_blocks = other_rep(angles, angles_across)
    samples, samples_across, place, start, moves = lax.optimization_barrier(
        (samples, samples_across, place, start, moves)
    )
    sample_blocks = other_rep(samples, samples_across)
    stream = pltpu.VMEM((count, ROWS, LANES), f32)
    sky = pltpu.VMEM((count, 3, ROWS, LANES), f32)
    sky_and_spare = pltpu.VMEM((count + 1, 3, ROWS, LANES), f32)
    group_sums = pltpu.VMEM((NSUB, octets * ROWS, LANES), f32)
    columns = pl.pallas_call(
        functools.partial(map_kernel, shape),
        out_shape=jax.ShapeDtypeStruct((slots // LANES + 1, 2 * height, 2 * LANES), jnp.bfloat16),
        in_specs=[smem] * 7 + [anywhere] * 6 + [vmem],
        out_specs=vmem,
        scratch_shapes=[
            stream, stream, stream, stream,
            pltpu.VMEM((detectors, octets * ROWS, LANES), f32),
            pltpu.VMEM((detectors, octets * ROWS, LANES), f32),
            sky, sky_and_spare, sky_and_spare,
            pltpu.VMEM((wafers * NSUB, ROWS, LANES), f32),
            pltpu.VMEM((total, 2 * height), f32),
            pltpu.VMEM((slots + LANES + ROWS, 2 * height), f32),
            pltpu.SemaphoreType.DMA((devices,)),
            pltpu.SemaphoreType.DMA((devices,)),
        ] + [sky] * ITERS + [group_sums] * (2 * wafers),
        compiler_params=params,
        name="map_maker",
    )(
        place_here, size, pair, group, moves, floats, whole, *angle_blocks,
        *sample_blocks, weight,
    )
    out_block = pl.BlockSpec((height, OUT_TILES * LANES), lambda n: (0, n))
    x_turned, r_turned = pl.pallas_call(
        write_kernel,
        grid=(owner_rows // (OUT_TILES * LANES),),
        out_shape=[jax.ShapeDtypeStruct((height, owner_rows), f32)] * 2,
        in_specs=[smem, vmem, vmem],
        out_specs=[out_block, out_block],
        compiler_params=params,
        name="write",
    )(start, columns, place)
    return x_turned.T, r_turned.T


def local(sizes, *arguments):
    tod, hit_list, band_lag = arguments[0], arguments[3], arguments[7]
    shape, det_count = part_shape(sizes, tod, hit_list, band_lag)
    if fits_one_device(shape, det_count):
        return whole_part(shape, *arguments)
    return distributed(*arguments)


def solution(mesh):
    placed = (
        P(("groups", "wafer"), "det", "rep"),
        P(("groups", "wafer"), "det", "rep"),
        P(("groups", "wafer"), "det", "rep"),
        P(("groups", "wafer"), "det", "rep", None, None),
        P(("groups", "wafer"), "det"),
        P(("groups", "wafer"), "det"),
        P(("groups", "wafer"), "det", None),
        P(("groups", "wafer"), "det", None),
    )
    return jax.shard_map(
        functools.partial(local, mesh.shape),
        mesh=mesh,
        in_specs=placed,
        out_specs=(P(("groups", "det", "wafer"), None), P(("groups", "det", "wafer"), None)),
        check_vma=False,
    )
```

```python
import functools

import jax
import jax.numpy as jnp
from jax import lax
from jax.experimental import pallas as pl
from jax.experimental.pallas import tpu as pltpu
from jax.sharding import PartitionSpec as P

BLOCKS = 196608
PBLOCK = 64
SBLOCK = 128
NSUB = 4
LAG = 16
ITERS = 3


prior_weight = 1.0


def with_halo(block, sides, width):
    for axis, dim in sides:
        count = lax.axis_size(axis)
        forward = [(i, i + 1) for i in range(count - 1)]
        backward = [(target, source) for source, target in forward]
        low = lax.ppermute(
            lax.slice_in_dim(block, block.shape[dim] - width, None, axis=dim), axis, forward
        )
        high = lax.ppermute(lax.slice_in_dim(block, 0, width, axis=dim), axis, backward)
        block = jnp.concatenate([low, block, high], axis=dim)
    return block


def distributed(tod, psi, point_row, hit_list, group_id, a_zero, band_coef, band_lag):
    highest = lax.Precision.HIGHEST
    samples = tod[0]
    angles = psi[0]
    det_count, time_count = samples.shape
    time_blocks = time_count // SBLOCK
    block_count = det_count * time_blocks
    send_table = hit_list[0, 0, 0]
    owner_count, capacity = send_table.shape
    owner_rows = BLOCKS // owner_count
    block_width = 3 * PBLOCK
    detector = lax.axis_index("det") * det_count + jnp.arange(det_count, dtype=jnp.int32)
    within = (jnp.arange(SBLOCK, dtype=jnp.int32)[None, :] + 3 * detector[:, None]) % PBLOCK
    pixel_table = (within[:, :, None] == jnp.arange(PBLOCK, dtype=jnp.int32)[None, None, :]).astype(
        jnp.float32
    )
    cosine_two = jnp.cos(2.0 * angles).reshape(det_count, time_blocks, SBLOCK)
    sine_two = jnp.sin(2.0 * angles).reshape(det_count, time_blocks, SBLOCK)
    slot_ids = send_table.reshape(-1)
    row_source = jnp.concatenate([point_row[0].reshape(-1), jnp.zeros((1,), jnp.int32)])
    slot_rows = row_source[slot_ids].astype(jnp.float32).reshape(owner_count, capacity)
    member = (group_id[0][:, None] == jnp.arange(NSUB, dtype=jnp.int32)[None, :]).astype(
        jnp.float32
    )
    member_count = jnp.sum(member, axis=0)
    lag_table = (
        band_lag[0][:, :, None] == jnp.arange(1, LAG + 1, dtype=jnp.int32)[None, None, :]
    ).astype(jnp.float32)
    lag_weight = jnp.einsum("dj,djl->dl", band_coef[0], lag_table, precision=highest)
    base_weight = a_zero[0]

    def slot_payload(by_block):
        width = by_block.shape[1]
        extended = jnp.concatenate([by_block, jnp.zeros((1, width), by_block.dtype)])
        return extended[slot_ids].reshape(owner_count, capacity, width)

    def deliver(payload):
        width = payload.shape[-1]
        got_values, got_rows = (
            lax.all_to_all(payload, ("det", "wafer"), split_axis=0, concat_axis=0, tiled=True),
            lax.all_to_all(slot_rows, ("det", "wafer"), split_axis=0, concat_axis=0, tiled=True),
        )
        return (got_values, got_rows)

    def back_project(stream, squared):
        shaped = stream.reshape(det_count, time_blocks, SBLOCK)
        first = cosine_two * cosine_two if squared else cosine_two
        second = sine_two * sine_two if squared else sine_two
        stacked = jnp.stack([shaped, first * shaped, second * shaped], axis=2)
        stokes = jnp.einsum("dkcs,dsp->dkcp", stacked, pixel_table, precision=highest)
        return stokes.reshape(block_count, block_width)

    def to_owners(stream, squared):
        got_values, got_rows = deliver(slot_payload(back_project(stream, squared)))
        pair_values, pair_rows = (
            lax.all_gather(got_values, "rep", axis=0, tiled=True),
            lax.all_gather(got_rows, "rep", axis=0, tiled=True),
        )
        target_rows = pair_rows.reshape(-1).astype(jnp.int32)
        summed = (
            jnp.zeros((owner_rows, block_width), jnp.float32)
            .at[target_rows]
            .add(pair_values.reshape(-1, block_width))
        )
        return (summed, got_rows.astype(jnp.int32))

    def remove_common(stream):
        local_sums = jnp.einsum("dg,dt->gt", member, stream, precision=highest)
        group_sums, group_counts = lax.psum((local_sums, member_count), "det")
        group_means = group_sums / jnp.maximum(group_counts, 1.0)[:, None]
        return stream - jnp.einsum("dg,gt->dt", member, group_means, precision=highest)

    def band_filter(stream):
        padded = with_halo(stream, (("rep", 1),), LAG)
        result = base_weight[:, None] * stream
        for offset in range(1, LAG + 1):
            later = padded[:, LAG + offset : LAG + offset + time_count]
            earlier = padded[:, LAG - offset : LAG - offset + time_count]
            result = result + lag_weight[:, offset - 1 : offset] * (later + earlier)
        return result

    def weigh_stream(stream):
        return remove_common(band_filter(remove_common(stream)))

    weight_stream = jnp.broadcast_to(base_weight[:, None], (det_count, time_count))
    diag_sum, serve_rows = to_owners(weight_stream, True)
    inverse_diag = 1.0 / (diag_sum + prior_weight)
    right_side = to_owners(weigh_stream(samples), False)[0]
    solution = jnp.zeros_like(right_side)
    residual = right_side

    def inner(left_map, right_map):
        return lax.psum(jnp.sum(left_map * right_map), ("det", "wafer"))

    precond = inverse_diag * residual
    direction = precond
    energy = inner(residual, precond)
    for iteration in range(ITERS):
        from_blocks = direction[serve_rows.reshape(-1)].reshape(owner_count, capacity, block_width)
        return_width = from_blocks.shape[-1]
        returned = lax.all_to_all(
            from_blocks, ("det", "wafer"), split_axis=0, concat_axis=0, tiled=True
        )
        return_placed = jnp.zeros((block_count + 1, return_width), jnp.float32)
        return_placed = return_placed.at[slot_ids].set(returned.reshape(-1, return_width))
        blocks = return_placed[:block_count].reshape(det_count, time_blocks, 3, PBLOCK)
        project_stokes = jnp.einsum("dkcp,dsp->dkcs", blocks, pixel_table, precision=highest)
        project_stream = (
            project_stokes[:, :, 0]
            + cosine_two * project_stokes[:, :, 1]
            + sine_two * project_stokes[:, :, 2]
        )
        seen_stream = project_stream.reshape(det_count, time_count)
        image_map = to_owners(weigh_stream(seen_stream), False)[0] + prior_weight * direction
        step_size = energy / inner(direction, image_map)
        solution = solution + step_size * direction
        residual = residual - step_size * image_map
        precond = inverse_diag * residual
        energy_next = inner(residual, precond)
        direction = precond + energy_next / energy * direction
        energy = energy_next
    return (solution, residual)


LANES = 128
ROWS = 8
OUT_TILES = 8
PAIR_BATCH = 4
BIG = float(1 << 24)
VMEM_BYTES = 60 << 20


def wide(values):
    return jnp.broadcast_to(values, (ROWS, LANES))


def tile_iotas():
    lane = lax.broadcasted_iota(jnp.int32, (ROWS, LANES), 1)
    sub = lax.broadcasted_iota(jnp.int32, (ROWS, LANES), 0)
    return lane, sub


def cosine_sine_double(angle):
    turns = jnp.floor(angle * 1.2732395447351628 + 0.5)
    reduced = 2.0 * angle - turns * 1.5703125
    reduced = reduced - turns * 4.837512969970703125e-4
    reduced = reduced - turns * 7.54978995489188216e-8
    square = reduced * reduced
    sine = (-1.9515295891e-4 * square + 8.3321608736e-3) * square - 1.6666654611e-1
    sine = sine * square * reduced + reduced
    cosine = (2.443315711809948e-5 * square - 1.388731625493765e-3) * square
    cosine = (cosine + 4.166664568298827e-2) * square * square - 0.5 * square + 1.0
    quarter = turns.astype(jnp.int32)
    odd = (quarter & 1) == 1
    first = jnp.where(odd, sine, cosine)
    second = jnp.where(odd, cosine, sine)
    first = jnp.where(((quarter + 1) & 2) == 2, -first, first)
    second = jnp.where((quarter & 2) == 2, -second, second)
    return first, second


def pack_kernel(
    shape, angle_ref, tod_ref, row_ref, hit_ref, group_ref, base_ref, coef_ref, lag_ref,
    angle_rows_ref, tod_rows_ref,
):
    wafers, dets, reps, tiles, owners, capacity, owner_rows, lag_count = shape
    lane, sub = tile_iotas()
    lists = hit_ref[...]
    owner_hits = jnp.zeros((ROWS, LANES), jnp.float32)
    for c in range(capacity):
        owner_hits = owner_hits + jnp.where(wide(lists[:, c : c + 1]) == lane, 1.0, 0.0)
    owner_of = jnp.sum(owner_hits * sub.astype(jnp.float32), axis=0, keepdims=True)

    def spread(values, width):
        return jnp.concatenate(
            [values, jnp.zeros((values.shape[0], LANES - width), values.dtype)], axis=1
        )

    rows = spread(row_ref[...].astype(jnp.float32), tiles)
    ids = owner_of * float(owner_rows) + rows[0:1]
    for k in range(1, ROWS):
        ids = ids + pltpu.roll(rows[k : k + 1], k * tiles, 1)
    floats = spread(base_ref[...], ROWS)
    whole = spread(group_ref[...].astype(jnp.float32), ROWS)
    for j in range(lag_count):
        at = (j + 1) * ROWS
        floats = floats + pltpu.roll(spread(coef_ref[j : j + 1, :], ROWS), at, 1)
        lag = lag_ref[j : j + 1, :].astype(jnp.float32)
        whole = whole + pltpu.roll(spread(lag, ROWS), at, 1)
    table = jnp.where(sub == 0, wide(ids), jnp.where(sub == 1, wide(floats), wide(whole)))
    angle_rows_ref[ROWS, 0:ROWS, :] = table
    angle_rows_ref[ROWS, ROWS : 2 * ROWS, :] = spread(lists.astype(jnp.float32), capacity)
    for b in range(tiles):
        angle_rows_ref[0:ROWS, b, :] = angle_ref[:, b * LANES : (b + 1) * LANES]
        tod_rows_ref[:, b, :] = tod_ref[:, b * LANES : (b + 1) * LANES]


def part_copies(shape, self_ref, refs, target, sem):
    wafers, dets, reps = shape[:3]
    here_ref, across_ref, other_ref = refs
    copies = []
    for swap_rep in range(reps):
        for swap_wafer in range(wafers):
            for shift in range(dets):
                if swap_rep:
                    source = other_ref.at[swap_wafer, shift]
                else:
                    source = (across_ref if swap_wafer else here_ref).at[shift]
                wafer = self_ref[0] ^ swap_wafer
                det = self_ref[1] - shift
                det = jnp.where(det < 0, det + dets, det)
                device = (wafer * dets + det) * reps + (self_ref[2] ^ swap_rep)
                copies.append(
                    pltpu.make_async_copy(source, target(device), sem.at[len(copies)])
                )
    return copies


def table_copies(shape, self_ref, source_ref, part_ref, sem):
    wafers, dets, reps = shape[:3]
    copies = []
    for rep in range(reps):
        for swap_wafer in range(wafers):
            for shift in range(dets):
                det = self_ref[1] - shift
                det = jnp.where(det < 0, det + dets, det)
                device = ((self_ref[0] ^ swap_wafer) * dets + det) * reps + rep
                copies.append(
                    pltpu.make_async_copy(
                        source_ref.at[rep, swap_wafer, shift], part_ref.at[device],
                        sem.at[len(copies)],
                    )
                )
    for copy in copies:
        copy.start()
    for copy in copies:
        copy.wait()


def exact_dot(left, right, dims=((1,), (0,))):
    return lax.dot_general(
        left.astype(jnp.bfloat16), right.astype(jnp.bfloat16), (dims, ((), ())),
        preferred_element_type=jnp.float32,
    )


def twin_kernel(
    shape, self_ref, table_ref, weight_ref, float_ref, whole_ref, size_ref, pair_ref, group_ref,
    part_ref, code_ref, lead_ref, part_sem,
):
    wafers, dets, reps, tiles, owners, capacity, owner_rows, lag_count = shape
    devices = wafers * dets * reps
    total = devices * LANES
    per_tile = LANES // tiles
    lane, sub = tile_iotas()
    lane_f = lane.astype(jnp.float32)
    table_copies(shape, self_ref, table_ref, part_ref, part_sem)
    none = jnp.full((ROWS, LANES), BIG, jnp.float32)
    for tile in range(devices // per_tile):
        code_ref[tile] = none
        lead_ref[tile] = none

    def survey(device, carry):
        float_ref[pl.ds(device, 1), :] = part_ref[device, 0, 1:2, :]
        whole_ref[pl.ds(device, 1), :] = part_ref[device, 0, 2:3, :].astype(jnp.int32)
        ids = jnp.broadcast_to(part_ref[device, 0, 0:1, :], (LANES, LANES)).T
        ids = [ids[j * ROWS : (j + 1) * ROWS] for j in range(tiles)]

        def compare(step, state):
            key, least = state
            for k in range(2):
                row = wide(part_ref[2 * step + k, 0, 0:1, :])
                least = [
                    jnp.minimum(least[j], jnp.where(ids[j] == row, key, BIG)) for j in range(tiles)
                ]
                key = key + LANES
            return key, least

        steps = lax.shift_right_logical(device, 1) + 1
        _, least = lax.fori_loop(0, steps, compare, (lane_f, [none] * tiles))
        codes, leads = none, none
        for j in range(tiles):
            lead = jnp.min(least[j], axis=1, keepdims=True)
            mine = (device * LANES + j * ROWS + sub[:, 0:1]).astype(jnp.float32)
            weight_ref[device * tiles + j] = wide(jnp.where(lead == mine, 0.5, 0.0))
            later = lead < mine
            leads = jnp.where(lane == j, jnp.where(later, lead, BIG), leads)
            codes = jnp.where(lane == j, jnp.where(later, mine * float(total) + lead, BIG), codes)
        tile, part = lax.div(device, per_tile), lax.rem(device, per_tile)
        inside = lax.shift_right_logical(lane, tiles.bit_length() - 1) == part
        for ref, found in ((code_ref, codes), (lead_ref, leads)):
            ref[tile] = jnp.where(inside, pltpu.roll(found, part * tiles, 1), ref[tile])
        return carry

    lax.fori_loop(0, devices, survey, 0)

    def next_code(last):
        found = jnp.full((ROWS, LANES), BIG, jnp.float32)
        for tile in range(devices // per_tile):
            codes = code_ref[tile]
            found = jnp.minimum(found, jnp.where(codes > last, codes, BIG))
        return jnp.min(found)

    def detector(key):
        team = lax.rem(lax.div(key, reps * LANES), dets)
        return team * ROWS + lax.rem(lax.div(key, tiles), ROWS)

    def take(state):
        pairs, grouped, code = state
        number = code.astype(jnp.int32)
        key = lax.div(number, total)
        lead = lax.rem(number, total)
        shift = (3 * (detector(key) - detector(lead))) & (PBLOCK - 1)
        wanted = lead.astype(jnp.float32)
        same = jnp.zeros((ROWS, LANES), jnp.float32)
        for tile in range(devices // per_tile):
            same = same + jnp.where(lead_ref[tile] == wanted, 1.0, 0.0)
        alone = jnp.sum(same) < 1.5
        entry = twin_entry(key, lead, shift)
        pair_ref[pairs] = entry
        group_ref[grouped] = entry
        return (
            pairs + jnp.where(alone, 1, 0), grouped + jnp.where(alone, 0, 1), next_code(code)
        )

    pairs, grouped, _ = lax.while_loop(
        lambda state: state[2] < BIG, take,
        (jnp.int32(0), jnp.int32(0), next_code(jnp.float32(-1.0))),
    )
    batches = lax.div(pairs + PAIR_BATCH - 1, PAIR_BATCH)

    def fill(n, carry):
        pair_ref[n] = twin_entry(total, total + 1, 0)
        return carry

    lax.fori_loop(pairs, batches * PAIR_BATCH, fill, 0)
    size_ref[0] = batches
    size_ref[1] = grouped


def twin_entry(key, lead, shift):
    return key * (1 << 19) + lead * (1 << 6) + shift


def twin_of(entry):
    return entry >> 19, (entry >> 6) & ((1 << 13) - 1), entry & (PBLOCK - 1)


def place_kernel(
    shape, self_ref, table_ref, place_ref, start_ref, move_ref, part_ref, rank_ref, hits_ref,
    part_sem,
):
    wafers, dets, reps, tiles, owners, capacity, owner_rows, lag_count = shape
    devices = wafers * dets * reps
    slots = devices * capacity
    lane, sub = tile_iotas()
    own = self_ref[1] * wafers + self_ref[0]
    first_row = (own * owner_rows).astype(jnp.float32)
    table_copies(shape, self_ref, table_ref, part_ref, part_sem)
    depth = 2 * LANES
    tall = lax.broadcasted_iota(jnp.int32, (depth, LANES), 0).astype(jnp.float32)

    def one_hots(device):
        local_row = part_ref[device, 0, 0:1, :] - first_row
        high = jnp.floor(local_row * (1.0 / LANES))
        low = local_row - high * LANES
        high = (jnp.broadcast_to(high, (depth, LANES)) == tall).astype(jnp.float32)
        low = (jnp.broadcast_to(low, (LANES, LANES)) == tall[0:LANES]).astype(jnp.float32)
        return high, low

    def survey(batch, hits):
        for k in range(4):
            device = 4 * batch + k
            own_hits = jnp.where(sub == own, part_ref[device, 1], 0.0)
            own_hits = jnp.sum(own_hits, axis=0, keepdims=True)
            hits_ref[pl.ds(device, 1), :] = own_hits.astype(jnp.int32)
            high, low = one_hots(device)
            hits = hits + exact_dot(high, low, ((1,), (1,)))
        return hits

    hits = lax.fori_loop(0, devices // 4, survey, jnp.zeros((depth, LANES), jnp.float32))
    full = jnp.minimum(hits, 1.0)

    def ordered(size, axis):
        first = lax.broadcasted_iota(jnp.int32, (size, size), axis)
        second = lax.broadcasted_iota(jnp.int32, (size, size), 1 - axis)
        return (first < second).astype(jnp.float32)

    counts = exact_dot(jnp.ones((ROWS, LANES), jnp.float32), full, ((1,), (1,)))
    start_ref[...] = exact_dot(counts, ordered(depth, 0)).astype(jnp.int32)
    sums = exact_dot(full, jnp.ones((LANES, LANES), jnp.float32))
    place = exact_dot(full, ordered(LANES, 0)) + exact_dot(ordered(depth, 1), sums)
    place_ref[...] = jnp.where(full > 0.0, place, -1.0).astype(jnp.int32)
    place_high = jnp.floor(place * (1.0 / LANES))
    place_parts = jnp.concatenate([place_high, place - place_high * LANES], axis=0)

    def rank_of(batch, carry):
        for k in range(4):
            device = 4 * batch + k
            high, low = one_hots(device)
            parts = exact_dot(place_parts, low)
            rank = high * (parts[0:depth] * LANES + parts[depth : 2 * depth])
            rank = jnp.sum(rank, axis=0, keepdims=True)
            rank_ref[pl.ds(device, 1), :] = rank.astype(jnp.int32)
        return carry

    lax.fori_loop(0, devices // 4, rank_of, 0)
    for tile in range(devices // ROWS):
        rows = slice(tile * ROWS, (tile + 1) * ROWS)
        number = hits_ref[rows, :]
        valid = number < LANES
        number = number & (LANES - 1)
        rank = jnp.take_along_axis(rank_ref[rows, :], number, axis=1, mode="promise_in_bounds")
        target = jnp.where(valid, rank, slots + LANES)
        move_ref[rows, :] = target * (1 << 16) + (tile * ROWS + sub) * LANES + number


def map_kernel(
    shape, self_ref, size_ref, pair_ref, group_ref, move_ref, float_smem, whole_smem,
    angle_here_ref, angle_across_ref, angle_other_ref, tod_here_ref, tod_across_ref, tod_other_ref,
    weight_ref, column_ref,
    angle_ref, tod_ref, cos_ref, sin_ref, clean_ref, noise_ref,
    inverse_ref, r_map, image_map, share_ref, rows_ref, sorted_ref, angle_sem, tod_sem, *more_refs,
):
    wafers, dets, reps, tiles, owners, capacity, owner_rows, lag_count = shape
    devices = wafers * dets * reps
    halves = tiles // ROWS
    octets = reps * halves
    wafer_dets = dets * ROWS
    count = devices * tiles
    lane, sub = tile_iotas()
    zero = jnp.zeros((ROWS, LANES), jnp.float32)
    d_maps, sum_refs = more_refs[:ITERS], more_refs[ITERS:]
    first_sums, second_sums = sum_refs[:wafers], sum_refs[wafers:]

    def copies_of(refs, to_ref, sem):
        return part_copies(
            shape, self_ref, refs, lambda d: to_ref.at[pl.ds(d * tiles, tiles)], sem
        )

    angle_moves = copies_of((angle_here_ref, angle_across_ref, angle_other_ref), angle_ref, angle_sem)
    tod_moves = copies_of((tod_here_ref, tod_across_ref, tod_other_ref), tod_ref, tod_sem)
    for copy in angle_moves + tod_moves:
        copy.start()

    def fold(block):
        return block + pltpu.roll(block, LANES // 2, 1)

    def whole_sum(values):
        values = jnp.sum(values, axis=0, keepdims=True)
        return wide(jnp.sum(values, axis=1, keepdims=True))

    def loop(times, body, carry, unroll):
        def several(n, carry):
            for k in range(unroll):
                carry = body(n * unroll + k, carry)
            return carry

        return lax.fori_loop(0, times // unroll, several, carry)

    def device_of(wafer, n):
        return (wafer * dets + lax.shift_right_logical(n, 3)) * reps

    def register_of(wafer, n, octet):
        device = device_of(wafer, n) + octet // halves
        return device * tiles + (n & (ROWS - 1)) * halves + octet % halves

    def group_of(wafer, n):
        return whole_smem[device_of(wafer, n), n & (ROWS - 1)]

    def rows_of(octet):
        return pl.ds(octet * ROWS, ROWS)

    def count_members(n, counts):
        result = []
        for wafer in range(wafers):
            group = group_of(wafer, n)
            result += [
                counts[wafer * NSUB + g] + jnp.where(group == g, 1, 0) for g in range(NSUB)
            ]
        return tuple(result)

    members = lax.fori_loop(0, wafer_dets, count_members, (jnp.int32(0),) * (wafers * NSUB))
    for k, member in enumerate(members):
        share_ref[k] = 1.0 / jnp.maximum(zero + member.astype(jnp.float32), 1.0)
    for c in range(3):
        image_map[count, c] = zero
        r_map[count, c] = zero

    def clear_sorted(n, carry):
        at = pl.ds(pl.multiple_of(n * ROWS, ROWS), ROWS)
        sorted_ref[at, :] = jnp.zeros((ROWS, 6 * PBLOCK), jnp.float32)
        return carry

    lax.fori_loop(0, sorted_ref.shape[0] // ROWS, clear_sorted, 0)
    for copy in angle_moves:
        copy.wait()

    def survey(at, carry):
        first, second = cosine_sine_double(angle_ref[at])
        inside = lax.shift_right_logical(at, halves.bit_length() - 1) & (ROWS - 1)
        base = float_smem[lax.div(at, tiles), inside]
        cos_ref[at] = first
        sin_ref[at] = second
        image_map[at, 0] = zero + (base + base)
        image_map[at, 1] = fold(base * (first * first))
        image_map[at, 2] = fold(base * (second * second))
        return carry

    loop(count, survey, 0, 8)

    def merge_twins(target):
        def pair_batch(n, carry):
            found = []
            for k in range(PAIR_BATCH):
                key, lead, shift = twin_of(pair_ref[n * PAIR_BATCH + k])
                spots = [
                    (lax.shift_right_logical(spot, 3), pl.ds(spot & (ROWS - 1), 1))
                    for spot in (key, lead)
                ]
                values = [[target[at, c, row, :] for c in range(3)] for at, row in spots]
                found.append((spots, shift, values))
            for spots, shift, values in found:
                turns = (shift, (LANES - shift) & (LANES - 1))
                for (at, row), own, other, turn in zip(
                    spots, values, values[::-1], turns[::-1]
                ):
                    for c in range(3):
                        target[at, c, row, :] = own[c] + pltpu.roll(wide(other[c]), turn, 1)[0:1]
            return carry

        def gather_one(n, carry):
            key, lead, shift = twin_of(group_ref[n])
            at, row = lax.shift_right_logical(key, 3), key & (ROWS - 1)
            lead_at, lead_row = lax.shift_right_logical(lead, 3), lead & (ROWS - 1)
            for c in range(3):
                moved = pltpu.roll(wide(target[at, c, pl.ds(row, 1), :]), shift, 1)
                target[lead_at, c, pl.ds(lead_row, 1), :] += moved[0:1]
            return carry

        def spread_one(n, carry):
            key, lead, shift = twin_of(group_ref[n])
            at, row = lax.shift_right_logical(key, 3), key & (ROWS - 1)
            lead_at, lead_row = lax.shift_right_logical(lead, 3), lead & (ROWS - 1)
            turn = (LANES - shift) & (LANES - 1)
            for c in range(3):
                moved = pltpu.roll(wide(target[lead_at, c, pl.ds(lead_row, 1), :]), turn, 1)
                target[at, c, pl.ds(row, 1), :] = moved[0:1]
            return carry

        lax.fori_loop(0, size_ref[0], pair_batch, 0)
        lax.fori_loop(0, size_ref[1], gather_one, 0)
        lax.fori_loop(0, size_ref[1], spread_one, 0)

    def clear_sums(refs):
        for ref in refs:
            for group in range(NSUB):
                for octet in range(octets):
                    ref[group, rows_of(octet), :] = zero

    def average(refs):
        for wafer, ref in enumerate(refs):
            for group in range(NSUB):
                for octet in range(octets):
                    ref[group, rows_of(octet), :] *= share_ref[wafer * NSUB + group]

    def sum_streams(stream_of, carry):
        clear_sums(first_sums)

        def one_detector(n, carry):
            for wafer in range(wafers):
                group = group_of(wafer, n)
                for octet in range(octets):
                    stream, carry = stream_of(register_of(wafer, n, octet), carry)
                    clean_ref[wafer * wafer_dets + n, rows_of(octet), :] = stream
                    first_sums[wafer][group, rows_of(octet), :] += stream
            return carry

        carry = loop(wafer_dets, one_detector, carry, 4)
        average(first_sums)
        return carry

    def filter_streams():
        clear_sums(second_sums)

        def one_filter(n, carry):
            for wafer in range(wafers):
                device, inside = device_of(wafer, n), n & (ROWS - 1)
                detector = wafer * wafer_dets + n
                group = group_of(wafer, n)
                base = float_smem[device, inside]
                coefs = [float_smem[device, (j + 1) * ROWS + inside] for j in range(lag_count)]
                lags = [whole_smem[device, (j + 1) * ROWS + inside] for j in range(lag_count)]
                clean = [
                    clean_ref[detector, rows_of(octet), :] - first_sums[wafer][group, rows_of(octet), :]
                    for octet in range(octets)
                ]
                up = [pltpu.roll(here, ROWS - 1, 0) for here in clean] + [zero]
                down = [zero] + [pltpu.roll(here, 1, 0) for here in clean]
                for octet, here in enumerate(clean):
                    after = jnp.where(sub == ROWS - 1, up[octet + 1], up[octet])
                    ahead = jnp.where(sub == 0, down[octet], down[octet + 1])
                    result = base * here
                    for coef, lag in zip(coefs, lags):
                        later = pltpu.roll(jnp.where(lane < lag, after, here), LANES - lag, 1)
                        earlier = pltpu.roll(jnp.where(lane >= LANES - lag, ahead, here), lag, 1)
                        result = result + coef * (later + earlier)
                    noise_ref[detector, rows_of(octet), :] = result
                    second_sums[wafer][group, rows_of(octet), :] += result
                    carry = carry + here * result
            return carry

        product = loop(wafer_dets, one_filter, zero, 2)
        average(second_sums)
        return product

    def return_streams(target):
        def one_return(n, carry):
            for wafer in range(wafers):
                group = group_of(wafer, n)
                for octet in range(octets):
                    at = register_of(wafer, n, octet)
                    stream = noise_ref[wafer * wafer_dets + n, rows_of(octet), :]
                    stream = stream - second_sums[wafer][group, rows_of(octet), :]
                    target[at, 0] = fold(stream)
                    target[at, 1] = fold(cos_ref[at] * stream)
                    target[at, 2] = fold(sin_ref[at] * stream)
            return carry

        loop(wafer_dets, one_return, 0, 4)
        merge_twins(target)

    merge_twins(image_map)
    for copy in tod_moves:
        copy.wait()
    sum_streams(lambda at, carry: (tod_ref[at], carry), 0)
    filter_streams()
    return_streams(r_map)

    def begin(at, carry):
        parts = zero
        for c in range(3):
            inverse = 1.0 / (image_map[at, c] + prior_weight)
            inverse_ref[at, c] = inverse
            residual = r_map[at, c]
            parts = parts + residual * (inverse * residual)
        return carry + weight_ref[at] * parts

    energy = whole_sum(loop(count, begin, zero, 8))
    factor = zero
    steps = []
    for iteration, d_map in enumerate(d_maps):
        last = iteration == ITERS - 1

        def seen_stream(at, carry):
            parts = []
            for c in range(3):
                part = inverse_ref[at, c] * r_map[at, c]
                if iteration:
                    part = part + factor * d_maps[iteration - 1][at, c]
                d_map[at, c] = part
                parts.append(part)
            squares = parts[0] * parts[0] + parts[1] * parts[1] + parts[2] * parts[2]
            stream = parts[0] + cos_ref[at] * parts[1] + sin_ref[at] * parts[2]
            return stream, carry + weight_ref[at] * squares

        prior = sum_streams(seen_stream, zero)
        product = filter_streams()
        return_streams(image_map)
        step = energy / whole_sum(product + prior_weight * prior)
        steps.append(step)

        def new_residual(at, c):
            return r_map[at, c] - step * (image_map[at, c] + prior_weight * d_map[at, c])

        if not last:

            def update(at, carry):
                parts = zero
                for c in range(3):
                    residual = new_residual(at, c)
                    r_map[at, c] = residual
                    parts = parts + residual * (inverse_ref[at, c] * residual)
                return carry + weight_ref[at] * parts

            next_energy = whole_sum(loop(count, update, zero, 16))
            factor = next_energy / energy
            energy = next_energy
        else:

            def place_pixels(at, carry):
                team = lax.rem(lax.div(at, reps * tiles), dets)
                inside = lax.shift_right_logical(at, halves.bit_length() - 1) & (ROWS - 1)
                turn = (3 * (team * ROWS + inside)) & (PBLOCK - 1)
                values = []
                for c in range(3):
                    value = steps[0] * d_maps[0][at, c]
                    for k in range(1, ITERS):
                        value = value + steps[k] * d_maps[k][at, c]
                    values.append(value)
                values += [new_residual(at, c) for c in range(3)]
                values = [pltpu.roll(value, turn, 1) for value in values]
                rows = pl.ds(pl.multiple_of(at * ROWS, ROWS), ROWS)
                for c in range(3):
                    rows_ref[rows, c * LANES : (c + 1) * LANES] = jnp.where(
                        lane < PBLOCK, values[2 * c], values[2 * c + 1]
                    )
                return carry

            loop(count, place_pixels, 0, 8)

    def pick(device, carry):
        for c in range(capacity):
            move = move_ref[device, c]
            source, target = move & ((1 << 16) - 1), move >> 16
            sorted_ref[pl.ds(target, 1), :] = rows_ref[pl.ds(source, 1), :]
        return carry

    lax.fori_loop(0, devices, pick, 0)

    def turn_tile(tile, carry):
        columns = sorted_ref[pl.ds(pl.multiple_of(tile * LANES, LANES), LANES), :].T
        high = columns.astype(jnp.bfloat16)
        column_ref[tile, :, 0:LANES] = high
        column_ref[tile, :, LANES : 2 * LANES] = (columns - high.astype(jnp.float32)).astype(
            jnp.bfloat16
        )
        return carry

    lax.fori_loop(0, column_ref.shape[0], turn_tile, 0)


def write_kernel(start_ref, column_ref, place_ref, x_ref, r_ref):
    height = 3 * PBLOCK
    depth = lax.broadcasted_iota(jnp.int32, (LANES, LANES), 0)
    group = pl.program_id(0) * OUT_TILES
    start, end = start_ref[0, group], start_ref[0, group + OUT_TILES]
    first = lax.shift_right_logical(start, 7)
    last = lax.shift_right_logical(jnp.maximum(end - 1, start), 7)

    def spread(tile):
        chosen = []
        for k in range(OUT_TILES):
            place = jnp.broadcast_to(place_ref[pl.ds(group + k, 1), :], (LANES, LANES))
            chosen.append(jnp.where(place == depth + tile * LANES, 1.0, 0.0).astype(jnp.bfloat16))
        chosen = jnp.concatenate(chosen, axis=1)
        chosen = jnp.concatenate([chosen, chosen], axis=0)
        return jnp.dot(column_ref[tile], chosen, preferred_element_type=jnp.float32)

    values = spread(first)
    x_ref[...] = values[:height]
    r_ref[...] = values[height:]

    def add_tile(tile, carry):
        values = spread(tile)
        x_ref[...] += values[:height]
        r_ref[...] += values[height:]
        return carry

    lax.fori_loop(first + 1, last + 1, add_tile, 0)


def part_shape(sizes, tod, hit_list, band_lag):
    det_count, time_count = tod.shape[1:]
    owners, capacity = hit_list.shape[3:]
    return (
        sizes["wafer"], sizes["det"], sizes["rep"], time_count // SBLOCK,
        owners, capacity, BLOCKS // owners, band_lag.shape[2],
    ), det_count


def fits_one_device(shape, det_count):
    wafers, dets, reps, tiles, owners, capacity, owner_rows, lag_count = shape
    devices = wafers * dets * reps
    total = devices * tiles * det_count
    groups = owner_rows // LANES
    return (
        det_count == ROWS
        and owners == ROWS
        and tiles * ROWS == LANES
        and tiles % ROWS == 0
        and (wafers, reps) == (2, 2)
        and (1 + lag_count) * ROWS <= LANES
        and capacity <= LANES
        and devices * capacity % LANES == 0
        and owner_rows % (LANES * OUT_TILES) == 0
        and groups + 1 <= 2 * LANES
        and devices % ROWS == 0
        and total * total < BIG
    )


def whole_part(shape, tod, psi, point_row, hit_list, group_id, a_zero, band_coef, band_lag):
    wafers, dets, reps, tiles, owners, capacity, owner_rows, lag_count = shape
    devices = wafers * dets * reps
    octets = reps * tiles // ROWS
    detectors = wafers * dets * ROWS
    count = devices * tiles
    total = count * ROWS
    slots = devices * capacity
    height = 3 * PBLOCK
    f32, i32 = jnp.float32, jnp.int32
    vmem, smem = pl.BlockSpec(memory_space=pltpu.VMEM), pl.BlockSpec(memory_space=pltpu.SMEM)
    anywhere = pl.BlockSpec(memory_space=pl.ANY)
    params = pltpu.CompilerParams(vmem_limit_bytes=VMEM_BYTES)
    swap = [(0, 1), (1, 0)]

    def along_det(block):
        moved = [
            lax.ppermute(block, "det", [(i, (i + shift) % dets) for i in range(dets)])
            for shift in range(1, dets)
        ]
        return [block] + moved

    def other_wafer(here):
        return lax.ppermute(here, "wafer", swap)

    def other_rep(here, across):
        return here, across, lax.ppermute(jnp.stack([here, across]), "rep", swap)

    angles, samples = pl.pallas_call(
        functools.partial(pack_kernel, shape),
        out_shape=[
            jax.ShapeDtypeStruct((ROWS + 1, tiles, LANES), f32),
            jax.ShapeDtypeStruct((ROWS, tiles, LANES), f32),
        ],
        in_specs=[vmem] * 8,
        out_specs=[vmem] * 2,
        compiler_params=params,
        name="pack",
    )(
        psi[0], tod[0], point_row[0], hit_list[0, 0, 0], group_id, a_zero, band_coef[0].T,
        band_lag[0].T,
    )
    angles = angles.reshape(tiles + 2, ROWS, LANES)
    samples = samples.reshape(tiles, ROWS, LANES)
    place_here = jnp.stack([lax.axis_index(axis) for axis in ("wafer", "det", "rep")]).astype(i32)
    angles = along_det(angles)
    tables = jnp.stack([block[tiles:] for block in angles])
    angles = jnp.stack([block[:tiles] for block in angles])
    tables = jnp.stack([tables, other_wafer(tables)])
    samples, angles, tables = lax.optimization_barrier((samples, angles, tables))
    angles_across = other_wafer(angles)
    samples = jnp.stack(along_det(samples))
    tables = lax.all_gather(tables, "rep", axis=0, tiled=False)
    table_scratch = pltpu.VMEM((devices, 2, ROWS, LANES), f32)
    table_sem = pltpu.SemaphoreType.DMA((devices,))
    twins = pl.pallas_call(
        functools.partial(twin_kernel, shape),
        out_shape=[
            jax.ShapeDtypeStruct((count, ROWS, LANES), f32),
            jax.ShapeDtypeStruct((devices, LANES), f32),
            jax.ShapeDtypeStruct((devices, LANES), i32),
            jax.ShapeDtypeStruct((2,), i32),
            jax.ShapeDtypeStruct((total,), i32),
            jax.ShapeDtypeStruct((total,), i32),
        ],
        in_specs=[smem, anywhere],
        out_specs=[vmem] * 3 + [smem] * 3,
        scratch_shapes=[
            table_scratch,
            pltpu.VMEM((devices * tiles // LANES, ROWS, LANES), f32),
            pltpu.VMEM((devices * tiles // LANES, ROWS, LANES), f32),
            table_sem,
        ],
        compiler_params=params,
        cost_estimate=pl.CostEstimate(flops=10**9, bytes_accessed=3 * 10**7, transcendentals=0),
        name="twins",
    )(place_here, tables)
    angles, angles_across, samples, tables, twins = lax.optimization_barrier(
        (angles, angles_across, samples, tables, twins)
    )
    weight, floats, whole, size, pair, group = twins
    samples_across = other_wafer(samples)
    place, start, moves = pl.pallas_call(
        functools.partial(place_kernel, shape),
        out_shape=[
            jax.ShapeDtypeStruct((2 * LANES, LANES), i32),
            jax.ShapeDtypeStruct((ROWS, 2 * LANES), i32),
            jax.ShapeDtypeStruct((devices, LANES), i32),
        ],
        in_specs=[smem, anywhere],
        out_specs=[vmem, vmem, vmem],
        scratch_shapes=[
            table_scratch,
            pltpu.VMEM((devices, LANES), i32),
            pltpu.VMEM((devices, LANES), i32),
            table_sem,
        ],
        compiler_params=params,
        cost_estimate=pl.CostEstimate(flops=10**9, bytes_accessed=2 * 10**7, transcendentals=0),
        name="places",
    )(place_here, tables)
    angles, angles_across, samples, samples_across, place, start, moves = lax.optimization_barrier(
        (angles, angles_across, samples, samples_across, place, start, moves)
    )
    angle_blocks = other_rep(angles, angles_across)
    sample_blocks = other_rep(samples, samples_across)
    stream = pltpu.VMEM((count, ROWS, LANES), f32)
    sky = pltpu.VMEM((count, 3, ROWS, LANES), f32)
    sky_and_spare = pltpu.VMEM((count + 1, 3, ROWS, LANES), f32)
    group_sums = pltpu.VMEM((NSUB, octets * ROWS, LANES), f32)
    columns = pl.pallas_call(
        functools.partial(map_kernel, shape),
        out_shape=jax.ShapeDtypeStruct((slots // LANES + 1, 2 * height, 2 * LANES), jnp.bfloat16),
        in_specs=[smem] * 7 + [anywhere] * 6 + [vmem],
        out_specs=vmem,
        scratch_shapes=[
            stream, stream, stream, stream,
            pltpu.VMEM((detectors, octets * ROWS, LANES), f32),
            pltpu.VMEM((detectors, octets * ROWS, LANES), f32),
            sky, sky_and_spare, sky_and_spare,
            pltpu.VMEM((wafers * NSUB, ROWS, LANES), f32),
            pltpu.VMEM((total, 2 * height), f32),
            pltpu.VMEM((slots + LANES + ROWS, 2 * height), f32),
            pltpu.SemaphoreType.DMA((devices,)),
            pltpu.SemaphoreType.DMA((devices,)),
        ] + [sky] * ITERS + [group_sums] * (2 * wafers),
        compiler_params=params,
        name="map_maker",
    )(
        place_here, size, pair, group, moves, floats, whole, *angle_blocks,
        *sample_blocks, weight,
    )
    out_block = pl.BlockSpec((height, OUT_TILES * LANES), lambda n: (0, n))
    x_turned, r_turned = pl.pallas_call(
        write_kernel,
        grid=(owner_rows // (OUT_TILES * LANES),),
        out_shape=[jax.ShapeDtypeStruct((height, owner_rows), f32)] * 2,
        in_specs=[smem, vmem, vmem],
        out_specs=[out_block, out_block],
        compiler_params=params,
        name="write",
    )(start, columns, place)
    return x_turned.T, r_turned.T


def local(sizes, *arguments):
    tod, hit_list, band_lag = arguments[0], arguments[3], arguments[7]
    shape, det_count = part_shape(sizes, tod, hit_list, band_lag)
    if fits_one_device(shape, det_count):
        return whole_part(shape, *arguments)
    return distributed(*arguments)


def solution(mesh):
    placed = (
        P(("groups", "wafer"), "det", "rep"),
        P(("groups", "wafer"), "det", "rep"),
        P(("groups", "wafer"), "det", "rep"),
        P(("groups", "wafer"), "det", "rep", None, None),
        P(("groups", "wafer"), "det"),
        P(("groups", "wafer"), "det"),
        P(("groups", "wafer"), "det", None),
        P(("groups", "wafer"), "det", None),
    )
    return jax.shard_map(
        functools.partial(local, mesh.shape),
        mesh=mesh,
        in_specs=placed,
        out_specs=(P(("groups", "det", "wafer"), None), P(("groups", "det", "wafer"), None)),
        check_vma=False,
    )
```

```python
import functools

import jax
import jax.numpy as jnp
from jax import lax
from jax.experimental import pallas as pl
from jax.experimental.pallas import tpu as pltpu
from jax.sharding import PartitionSpec as P

BLOCKS = 196608
PBLOCK = 64
SBLOCK = 128
NSUB = 4
LAG = 16
ITERS = 3


prior_weight = 1.0


def with_halo(block, sides, width):
    for axis, dim in sides:
        count = lax.axis_size(axis)
        forward = [(i, i + 1) for i in range(count - 1)]
        backward = [(target, source) for source, target in forward]
        low = lax.ppermute(
            lax.slice_in_dim(block, block.shape[dim] - width, None, axis=dim), axis, forward
        )
        high = lax.ppermute(lax.slice_in_dim(block, 0, width, axis=dim), axis, backward)
        block = jnp.concatenate([low, block, high], axis=dim)
    return block


def distributed(tod, psi, point_row, hit_list, group_id, a_zero, band_coef, band_lag):
    highest = lax.Precision.HIGHEST
    samples = tod[0]
    angles = psi[0]
    det_count, time_count = samples.shape
    time_blocks = time_count // SBLOCK
    block_count = det_count * time_blocks
    send_table = hit_list[0, 0, 0]
    owner_count, capacity = send_table.shape
    owner_rows = BLOCKS // owner_count
    block_width = 3 * PBLOCK
    detector = lax.axis_index("det") * det_count + jnp.arange(det_count, dtype=jnp.int32)
    within = (jnp.arange(SBLOCK, dtype=jnp.int32)[None, :] + 3 * detector[:, None]) % PBLOCK
    pixel_table = (within[:, :, None] == jnp.arange(PBLOCK, dtype=jnp.int32)[None, None, :]).astype(
        jnp.float32
    )
    cosine_two = jnp.cos(2.0 * angles).reshape(det_count, time_blocks, SBLOCK)
    sine_two = jnp.sin(2.0 * angles).reshape(det_count, time_blocks, SBLOCK)
    slot_ids = send_table.reshape(-1)
    row_source = jnp.concatenate([point_row[0].reshape(-1), jnp.zeros((1,), jnp.int32)])
    slot_rows = row_source[slot_ids].astype(jnp.float32).reshape(owner_count, capacity)
    member = (group_id[0][:, None] == jnp.arange(NSUB, dtype=jnp.int32)[None, :]).astype(
        jnp.float32
    )
    member_count = jnp.sum(member, axis=0)
    lag_table = (
        band_lag[0][:, :, None] == jnp.arange(1, LAG + 1, dtype=jnp.int32)[None, None, :]
    ).astype(jnp.float32)
    lag_weight = jnp.einsum("dj,djl->dl", band_coef[0], lag_table, precision=highest)
    base_weight = a_zero[0]

    def slot_payload(by_block):
        width = by_block.shape[1]
        extended = jnp.concatenate([by_block, jnp.zeros((1, width), by_block.dtype)])
        return extended[slot_ids].reshape(owner_count, capacity, width)

    def deliver(payload):
        width = payload.shape[-1]
        got_values, got_rows = (
            lax.all_to_all(payload, ("det", "wafer"), split_axis=0, concat_axis=0, tiled=True),
            lax.all_to_all(slot_rows, ("det", "wafer"), split_axis=0, concat_axis=0, tiled=True),
        )
        return (got_values, got_rows)

    def back_project(stream, squared):
        shaped = stream.reshape(det_count, time_blocks, SBLOCK)
        first = cosine_two * cosine_two if squared else cosine_two
        second = sine_two * sine_two if squared else sine_two
        stacked = jnp.stack([shaped, first * shaped, second * shaped], axis=2)
        stokes = jnp.einsum("dkcs,dsp->dkcp", stacked, pixel_table, precision=highest)
        return stokes.reshape(block_count, block_width)

    def to_owners(stream, squared):
        got_values, got_rows = deliver(slot_payload(back_project(stream, squared)))
        pair_values, pair_rows = (
            lax.all_gather(got_values, "rep", axis=0, tiled=True),
            lax.all_gather(got_rows, "rep", axis=0, tiled=True),
        )
        target_rows = pair_rows.reshape(-1).astype(jnp.int32)
        summed = (
            jnp.zeros((owner_rows, block_width), jnp.float32)
            .at[target_rows]
            .add(pair_values.reshape(-1, block_width))
        )
        return (summed, got_rows.astype(jnp.int32))

    def remove_common(stream):
        local_sums = jnp.einsum("dg,dt->gt", member, stream, precision=highest)
        group_sums, group_counts = lax.psum((local_sums, member_count), "det")
        group_means = group_sums / jnp.maximum(group_counts, 1.0)[:, None]
        return stream - jnp.einsum("dg,gt->dt", member, group_means, precision=highest)

    def band_filter(stream):
        padded = with_halo(stream, (("rep", 1),), LAG)
        result = base_weight[:, None] * stream
        for offset in range(1, LAG + 1):
            later = padded[:, LAG + offset : LAG + offset + time_count]
            earlier = padded[:, LAG - offset : LAG - offset + time_count]
            result = result + lag_weight[:, offset - 1 : offset] * (later + earlier)
        return result

    def weigh_stream(stream):
        return remove_common(band_filter(remove_common(stream)))

    weight_stream = jnp.broadcast_to(base_weight[:, None], (det_count, time_count))
    diag_sum, serve_rows = to_owners(weight_stream, True)
    inverse_diag = 1.0 / (diag_sum + prior_weight)
    right_side = to_owners(weigh_stream(samples), False)[0]
    solution = jnp.zeros_like(right_side)
    residual = right_side

    def inner(left_map, right_map):
        return lax.psum(jnp.sum(left_map * right_map), ("det", "wafer"))

    precond = inverse_diag * residual
    direction = precond
    energy = inner(residual, precond)
    for iteration in range(ITERS):
        from_blocks = direction[serve_rows.reshape(-1)].reshape(owner_count, capacity, block_width)
        return_width = from_blocks.shape[-1]
        returned = lax.all_to_all(
            from_blocks, ("det", "wafer"), split_axis=0, concat_axis=0, tiled=True
        )
        return_placed = jnp.zeros((block_count + 1, return_width), jnp.float32)
        return_placed = return_placed.at[slot_ids].set(returned.reshape(-1, return_width))
        blocks = return_placed[:block_count].reshape(det_count, time_blocks, 3, PBLOCK)
        project_stokes = jnp.einsum("dkcp,dsp->dkcs", blocks, pixel_table, precision=highest)
        project_stream = (
            project_stokes[:, :, 0]
            + cosine_two * project_stokes[:, :, 1]
            + sine_two * project_stokes[:, :, 2]
        )
        seen_stream = project_stream.reshape(det_count, time_count)
        image_map = to_owners(weigh_stream(seen_stream), False)[0] + prior_weight * direction
        step_size = energy / inner(direction, image_map)
        solution = solution + step_size * direction
        residual = residual - step_size * image_map
        precond = inverse_diag * residual
        energy_next = inner(residual, precond)
        direction = precond + energy_next / energy * direction
        energy = energy_next
    return (solution, residual)


LANES = 128
ROWS = 8
OUT_TILES = 8
PAIR_BATCH = 4
BIG = float(1 << 24)
VMEM_BYTES = 60 << 20


def wide(values):
    return jnp.broadcast_to(values, (ROWS, LANES))


def tile_iotas():
    lane = lax.broadcasted_iota(jnp.int32, (ROWS, LANES), 1)
    sub = lax.broadcasted_iota(jnp.int32, (ROWS, LANES), 0)
    return lane, sub


def cosine_sine_double(angle):
    turns = jnp.floor(angle * 1.2732395447351628 + 0.5)
    reduced = 2.0 * angle - turns * 1.5703125
    reduced = reduced - turns * 4.837512969970703125e-4
    reduced = reduced - turns * 7.54978995489188216e-8
    square = reduced * reduced
    sine = (-1.9515295891e-4 * square + 8.3321608736e-3) * square - 1.6666654611e-1
    sine = sine * square * reduced + reduced
    cosine = (2.443315711809948e-5 * square - 1.388731625493765e-3) * square
    cosine = (cosine + 4.166664568298827e-2) * square * square - 0.5 * square + 1.0
    quarter = turns.astype(jnp.int32)
    odd = (quarter & 1) == 1
    first = jnp.where(odd, sine, cosine)
    second = jnp.where(odd, cosine, sine)
    first = jnp.where(((quarter + 1) & 2) == 2, -first, first)
    second = jnp.where((quarter & 2) == 2, -second, second)
    return first, second


def pack_kernel(
    shape, angle_ref, tod_ref, row_ref, hit_ref, group_ref, base_ref, coef_ref, lag_ref,
    table_ref, angle_rows_ref, tod_rows_ref,
):
    wafers, dets, reps, tiles, owners, capacity, owner_rows, lag_count = shape
    lane, sub = tile_iotas()
    lists = hit_ref[...]
    owner_hits = jnp.zeros((ROWS, LANES), jnp.float32)
    for c in range(capacity):
        owner_hits = owner_hits + jnp.where(wide(lists[:, c : c + 1]) == lane, 1.0, 0.0)
    owner_of = jnp.sum(owner_hits * sub.astype(jnp.float32), axis=0, keepdims=True)

    def spread(values, width):
        return jnp.concatenate(
            [values, jnp.zeros((values.shape[0], LANES - width), values.dtype)], axis=1
        )

    rows = spread(row_ref[...].astype(jnp.float32), tiles)
    ids = owner_of * float(owner_rows) + rows[0:1]
    for k in range(1, ROWS):
        ids = ids + pltpu.roll(rows[k : k + 1], k * tiles, 1)
    floats = spread(base_ref[...], ROWS)
    whole = spread(group_ref[...].astype(jnp.float32), ROWS)
    for j in range(lag_count):
        at = (j + 1) * ROWS
        floats = floats + pltpu.roll(spread(coef_ref[j : j + 1, :], ROWS), at, 1)
        lag = lag_ref[j : j + 1, :].astype(jnp.float32)
        whole = whole + pltpu.roll(spread(lag, ROWS), at, 1)
    table = jnp.where(sub == 0, wide(ids), jnp.where(sub == 1, wide(floats), wide(whole)))
    table_ref[0] = table
    table_ref[1] = spread(lists.astype(jnp.float32), capacity)
    for b in range(tiles):
        angle_rows_ref[:, b, :] = angle_ref[:, b * LANES : (b + 1) * LANES]
        tod_rows_ref[:, b, :] = tod_ref[:, b * LANES : (b + 1) * LANES]


def part_copies(shape, self_ref, source, target, sem):
    wafers, dets, reps = shape[:3]
    copies = []
    for swap_rep in range(reps):
        for swap_wafer in range(wafers):
            for shift in range(dets):
                det = self_ref[1] - shift
                det = jnp.where(det < 0, det + dets, det)
                device = ((self_ref[0] ^ swap_wafer) * dets + det) * reps
                device = device + (self_ref[2] ^ swap_rep)
                copies.append(
                    pltpu.make_async_copy(
                        source(swap_rep, swap_wafer, shift), target(device), sem.at[len(copies)]
                    )
                )
    return copies


def table_copies(shape, self_ref, source_ref, part_ref, sem):
    wafers, dets, reps = shape[:3]
    copies = []
    for swap_wafer in range(wafers):
        for shift in range(dets):
            det = self_ref[1] - shift
            det = jnp.where(det < 0, det + dets, det)
            device = ((self_ref[0] ^ swap_wafer) * dets + det) * reps
            copies.append(
                pltpu.make_async_copy(
                    source_ref.at[swap_wafer, shift], part_ref.at[pl.ds(device, reps)],
                    sem.at[len(copies)],
                )
            )
    for copy in copies:
        copy.start()
    for copy in copies:
        copy.wait()


def exact_dot(left, right, dims=((1,), (0,))):
    return lax.dot_general(
        left.astype(jnp.bfloat16), right.astype(jnp.bfloat16), (dims, ((), ())),
        preferred_element_type=jnp.float32,
    )


def twin_kernel(
    shape, self_ref, table_ref, float_ref, whole_ref, size_ref, pair_ref, group_ref,
    part_ref, column_ref, code_ref, lead_ref, part_sem,
):
    wafers, dets, reps, tiles, owners, capacity, owner_rows, lag_count = shape
    devices = wafers * dets * reps
    total = devices * LANES
    lane, sub = tile_iotas()
    sub_f = sub.astype(jnp.float32)
    none = jnp.full((ROWS, LANES), BIG, jnp.float32)
    along = lax.broadcasted_iota(jnp.int32, (1, LANES), 1).astype(jnp.float32)
    table_copies(shape, self_ref, table_ref, part_ref, part_sem)

    def turn(batch, carry):
        for k in range(4):
            device = 4 * batch + k
            float_ref[pl.ds(device, 1), :] = part_ref[device, 0, 1:2, :]
            whole_ref[pl.ds(device, 1), :] = part_ref[device, 0, 2:3, :].astype(jnp.int32)
            column_ref[device] = jnp.broadcast_to(part_ref[device, 0, 0:1, :], (LANES, LANES)).T
        return carry

    lax.fori_loop(0, devices // 4, turn, 0)

    def survey(device, carry):
        row = wide(part_ref[device, 0, 0:1, :])

        def compare(other, least):
            found = [none] * 4
            for j in range(tiles):
                same = column_ref[other, j * ROWS : (j + 1) * ROWS, :] == row
                found[j % 4] = jnp.minimum(found[j % 4], jnp.where(same, sub_f + float(j * ROWS), BIG))
            here = jnp.minimum(jnp.minimum(found[0], found[1]), jnp.minimum(found[2], found[3]))
            return jnp.minimum(least, here + (other * LANES).astype(jnp.float32))

        least = lax.fori_loop(0, device + 1, compare, none)
        lead = jnp.min(least, axis=0, keepdims=True)
        mine = (device * LANES).astype(jnp.float32) + along
        later = lead < mine
        code_ref[pl.ds(device, 1), :] = jnp.where(later, mine * float(total) + lead, BIG)
        lead_ref[pl.ds(device, 1), :] = jnp.where(later, lead, BIG)
        return carry

    lax.fori_loop(0, devices, survey, 0)

    def next_code(last):
        found = none
        for tile in range(devices // ROWS):
            codes = code_ref[tile * ROWS : (tile + 1) * ROWS, :]
            found = jnp.minimum(found, jnp.where(codes > last, codes, BIG))
        return jnp.min(found)

    def detector(key):
        team = lax.rem(lax.div(key, reps * LANES), dets)
        return team * ROWS + lax.rem(lax.div(key, tiles), ROWS)

    def take(state):
        pairs, grouped, code = state
        number = code.astype(jnp.int32)
        key = lax.div(number, total)
        lead = lax.rem(number, total)
        shift = (3 * (detector(key) - detector(lead))) & (PBLOCK - 1)
        wanted = lead.astype(jnp.float32)
        same = jnp.zeros((ROWS, LANES), jnp.float32)
        for tile in range(devices // ROWS):
            leads = lead_ref[tile * ROWS : (tile + 1) * ROWS, :]
            same = same + jnp.where(leads == wanted, 1.0, 0.0)
        alone = jnp.sum(same) < 1.5
        entry = twin_entry(key, lead, shift)
        pair_ref[pairs] = entry
        group_ref[grouped] = entry
        return (
            pairs + jnp.where(alone, 1, 0), grouped + jnp.where(alone, 0, 1), next_code(code)
        )

    pairs, grouped, _ = lax.while_loop(
        lambda state: state[2] < BIG, take,
        (jnp.int32(0), jnp.int32(0), next_code(jnp.float32(-1.0))),
    )
    batches = lax.div(pairs + PAIR_BATCH - 1, PAIR_BATCH)

    def fill(n, carry):
        pair_ref[n] = twin_entry(total, total + 1, 0)
        return carry

    lax.fori_loop(pairs, batches * PAIR_BATCH, fill, 0)
    size_ref[0] = batches
    size_ref[1] = grouped


def twin_entry(key, lead, shift):
    return key * (1 << 19) + lead * (1 << 6) + shift


def twin_of(entry):
    return entry >> 19, (entry >> 6) & ((1 << 13) - 1), entry & (PBLOCK - 1)


def place_kernel(
    shape, self_ref, table_ref, place_ref, start_ref, move_ref, part_ref, rank_ref, hits_ref,
    part_sem,
):
    wafers, dets, reps, tiles, owners, capacity, owner_rows, lag_count = shape
    devices = wafers * dets * reps
    slots = devices * capacity
    lane, sub = tile_iotas()
    own = self_ref[1] * wafers + self_ref[0]
    first_row = (own * owner_rows).astype(jnp.float32)
    table_copies(shape, self_ref, table_ref, part_ref, part_sem)
    depth = 2 * LANES
    tall = lax.broadcasted_iota(jnp.int32, (depth, LANES), 0).astype(jnp.float32)

    def one_hots(device):
        local_row = part_ref[device, 0, 0:1, :] - first_row
        high = jnp.floor(local_row * (1.0 / LANES))
        low = local_row - high * LANES
        high = (jnp.broadcast_to(high, (depth, LANES)) == tall).astype(jnp.float32)
        low = (jnp.broadcast_to(low, (LANES, LANES)) == tall[0:LANES]).astype(jnp.float32)
        return high, low

    def survey(batch, hits):
        for k in range(4):
            device = 4 * batch + k
            own_hits = jnp.where(sub == own, part_ref[device, 1], 0.0)
            own_hits = jnp.sum(own_hits, axis=0, keepdims=True)
            hits_ref[pl.ds(device, 1), :] = own_hits.astype(jnp.int32)
            high, low = one_hots(device)
            hits = hits + exact_dot(high, low, ((1,), (1,)))
        return hits

    hits = lax.fori_loop(0, devices // 4, survey, jnp.zeros((depth, LANES), jnp.float32))
    full = jnp.minimum(hits, 1.0)

    def ordered(size, axis):
        first = lax.broadcasted_iota(jnp.int32, (size, size), axis)
        second = lax.broadcasted_iota(jnp.int32, (size, size), 1 - axis)
        return (first < second).astype(jnp.float32)

    counts = exact_dot(jnp.ones((ROWS, LANES), jnp.float32), full, ((1,), (1,)))
    start_ref[...] = exact_dot(counts, ordered(depth, 0)).astype(jnp.int32)
    sums = exact_dot(full, jnp.ones((LANES, LANES), jnp.float32))
    place = exact_dot(full, ordered(LANES, 0)) + exact_dot(ordered(depth, 1), sums)
    place_ref[...] = jnp.where(full > 0.0, place, -1.0).astype(jnp.int32)
    place_high = jnp.floor(place * (1.0 / LANES))
    place_parts = jnp.concatenate([place_high, place - place_high * LANES], axis=0)

    def rank_of(batch, carry):
        for k in range(4):
            device = 4 * batch + k
            high, low = one_hots(device)
            parts = exact_dot(place_parts, low)
            rank = high * (parts[0:depth] * LANES + parts[depth : 2 * depth])
            rank = jnp.sum(rank, axis=0, keepdims=True)
            rank_ref[pl.ds(device, 1), :] = rank.astype(jnp.int32)
        return carry

    lax.fori_loop(0, devices // 4, rank_of, 0)
    for tile in range(devices // ROWS):
        rows = slice(tile * ROWS, (tile + 1) * ROWS)
        number = hits_ref[rows, :]
        valid = number < LANES
        number = number & (LANES - 1)
        rank = jnp.take_along_axis(rank_ref[rows, :], number, axis=1, mode="promise_in_bounds")
        target = jnp.where(valid, rank, slots + LANES)
        move_ref[rows, :] = target * (1 << 16) + (tile * ROWS + sub) * LANES + number


def map_kernel(
    shape, self_ref, size_ref, pair_ref, group_ref, move_ref, float_smem, whole_smem,
    angle_here_ref, angle_across_ref, angle_other_ref, tod_here_ref, tod_other_ref, column_ref,
    angle_ref, tod_ref, cos_ref, sin_ref, clean_ref, noise_ref, weight_ref,
    inverse_ref, r_map, image_map, share_ref, rows_ref, sorted_ref, angle_sem, tod_sem, *more_refs,
):
    wafers, dets, reps, tiles, owners, capacity, owner_rows, lag_count = shape
    devices = wafers * dets * reps
    octets = 2 * reps
    wafer_dets = dets * ROWS
    count = devices * ROWS
    lane, sub = tile_iotas()
    zero = jnp.zeros((ROWS, LANES), jnp.float32)
    low = lane < PBLOCK
    d_maps, sum_refs = more_refs[:ITERS], more_refs[ITERS:]
    first_sums, second_sums = sum_refs[:wafers], sum_refs[wafers:]

    def copies_of(source, to_ref, sem):
        return part_copies(
            shape, self_ref, source, lambda d: to_ref.at[pl.ds(d * tiles, tiles)], sem
        )

    def angle_source(swap_rep, swap_wafer, shift):
        if swap_rep:
            return angle_other_ref.at[swap_wafer, shift]
        return (angle_across_ref if swap_wafer else angle_here_ref).at[shift]

    def tod_source(swap_rep, swap_wafer, shift):
        return (tod_other_ref if swap_rep else tod_here_ref).at[shift, swap_wafer]

    angle_moves = copies_of(angle_source, angle_ref, angle_sem)
    tod_moves = copies_of(tod_source, tod_ref, tod_sem)
    for copy in angle_moves + tod_moves:
        copy.start()

    def turn_half(block):
        return pltpu.roll(block, PBLOCK, 1)

    def fold(first, second):
        return jnp.where(low, first, second) + turn_half(jnp.where(low, second, first))

    def unfold(block):
        turned = turn_half(block)
        return jnp.where(low, block, turned), jnp.where(low, turned, block)

    def whole_sum(values):
        values = jnp.sum(values, axis=0, keepdims=True)
        return wide(jnp.sum(values, axis=1, keepdims=True))

    def loop(times, body, carry, unroll):
        def several(n, carry):
            for k in range(unroll):
                carry = body(n * unroll + k, carry)
            return carry

        return lax.fori_loop(0, times // unroll, several, carry)

    def device_of(wafer, n):
        return (wafer * dets + lax.shift_right_logical(n, 3)) * reps

    def group_of(wafer, n):
        return whole_smem[device_of(wafer, n), n & (ROWS - 1)]

    def rows_of(octet):
        return pl.ds(octet * ROWS, ROWS)

    def count_members(n, counts):
        result = []
        for wafer in range(wafers):
            group = group_of(wafer, n)
            result += [
                counts[wafer * NSUB + g] + jnp.where(group == g, 1, 0) for g in range(NSUB)
            ]
        return tuple(result)

    members = lax.fori_loop(0, wafer_dets, count_members, (jnp.int32(0),) * (wafers * NSUB))
    for k, member in enumerate(members):
        share_ref[k] = 1.0 / jnp.maximum(zero + member.astype(jnp.float32), 1.0)
    for c in range(3):
        image_map[count, c] = zero
        r_map[count, c] = zero

    def clear_sorted(n, carry):
        at = pl.ds(pl.multiple_of(n * ROWS, ROWS), ROWS)
        sorted_ref[at, :] = jnp.zeros((ROWS, 6 * PBLOCK), jnp.float32)
        return carry

    lax.fori_loop(0, sorted_ref.shape[0] // ROWS, clear_sorted, 0)

    def spot_of(key):
        return lax.shift_right_logical(key, 4), (key >> 3) & 1, pl.ds(key & (ROWS - 1), 1)

    def in_half(half):
        return (lane[0:1] >> 6) == half

    def set_weight(at, carry):
        weight_ref[at] = zero + 1.0
        return carry

    loop(count, set_weight, 0, 16)

    def drop(list_ref):
        def one(n, carry):
            at, half, row = spot_of(twin_of(list_ref[n])[0])
            weight_ref[at, row, :] = jnp.where(in_half(half), 0.0, weight_ref[at, row, :])
            return carry

        return one

    lax.fori_loop(0, size_ref[0] * PAIR_BATCH, drop(pair_ref), 0)
    lax.fori_loop(0, size_ref[1], drop(group_ref), 0)

    def moved_from(target, spot, shift):
        at, half, row = spot
        result = []
        for c in range(3):
            values = wide(target[at, c, row, :])
            values = jnp.where((lane >> 6) == half, values, turn_half(values))
            result.append(pltpu.roll(values, shift, 1)[0:1])
        return result

    def merge_twins(target):
        def add(spot, values):
            at, half, row = spot
            for c in range(3):
                target[at, c, row, :] += jnp.where(in_half(half), values[c], 0.0)

        def pair_batch(n, carry):
            found = []
            for k in range(PAIR_BATCH):
                key, lead, shift = twin_of(pair_ref[n * PAIR_BATCH + k])
                key, lead = spot_of(key), spot_of(lead)
                back = (PBLOCK - shift) & (PBLOCK - 1)
                found.append((lead, moved_from(target, key, shift)))
                found.append((key, moved_from(target, lead, back)))
            for spot, values in found:
                add(spot, values)
            return carry

        def gather_one(n, carry):
            key, lead, shift = twin_of(group_ref[n])
            add(spot_of(lead), moved_from(target, spot_of(key), shift))
            return carry

        def spread_one(n, carry):
            key, lead, shift = twin_of(group_ref[n])
            values = moved_from(target, spot_of(lead), (PBLOCK - shift) & (PBLOCK - 1))
            at, half, row = spot_of(key)
            for c in range(3):
                target[at, c, row, :] = jnp.where(in_half(half), values[c], target[at, c, row, :])
            return carry

        lax.fori_loop(0, size_ref[0], pair_batch, 0)
        lax.fori_loop(0, size_ref[1], gather_one, 0)
        lax.fori_loop(0, size_ref[1], spread_one, 0)

    for copy in angle_moves:
        copy.wait()

    def survey(at, carry):
        base = float_smem[lax.shift_right_logical(at, 3), at & (ROWS - 1)]
        squares = []
        for half in range(2):
            first, second = cosine_sine_double(angle_ref[2 * at + half])
            cos_ref[2 * at + half] = first
            sin_ref[2 * at + half] = second
            squares.append((base * (first * first), base * (second * second)))
        image_map[at, 0] = zero + (base + base)
        for c in range(2):
            image_map[at, c + 1] = fold(squares[0][c], squares[1][c])
        return carry

    loop(count, survey, 0, 8)

    def clear_sums(refs):
        for ref in refs:
            for group in range(NSUB):
                for octet in range(octets):
                    ref[group, rows_of(octet), :] = zero

    def average(refs):
        for wafer, ref in enumerate(refs):
            for group in range(NSUB):
                for octet in range(octets):
                    ref[group, rows_of(octet), :] *= share_ref[wafer * NSUB + group]

    def sum_streams(streams_of, carry):
        clear_sums(first_sums)

        def one_detector(n, carry):
            for wafer in range(wafers):
                group = group_of(wafer, n)
                for rep in range(reps):
                    at = (device_of(wafer, n) + rep) * ROWS + (n & (ROWS - 1))
                    streams, carry = streams_of(at, carry)
                    for half, stream in enumerate(streams):
                        rows = rows_of(2 * rep + half)
                        clean_ref[wafer * wafer_dets + n, rows, :] = stream
                        first_sums[wafer][group, rows, :] += stream
            return carry

        carry = loop(wafer_dets, one_detector, carry, 4)
        average(first_sums)
        return carry

    def filter_streams():
        clear_sums(second_sums)

        def one_filter(n, carry):
            for wafer in range(wafers):
                device, inside = device_of(wafer, n), n & (ROWS - 1)
                detector = wafer * wafer_dets + n
                group = group_of(wafer, n)
                base = float_smem[device, inside]
                coefs = [float_smem[device, (j + 1) * ROWS + inside] for j in range(lag_count)]
                lags = [whole_smem[device, (j + 1) * ROWS + inside] for j in range(lag_count)]
                clean = [
                    clean_ref[detector, rows_of(octet), :] - first_sums[wafer][group, rows_of(octet), :]
                    for octet in range(octets)
                ]
                up = [pltpu.roll(here, ROWS - 1, 0) for here in clean] + [zero]
                down = [zero] + [pltpu.roll(here, 1, 0) for here in clean]
                for octet, here in enumerate(clean):
                    after = jnp.where(sub == ROWS - 1, up[octet + 1], up[octet])
                    ahead = jnp.where(sub == 0, down[octet], down[octet + 1])
                    result = base * here
                    for coef, lag in zip(coefs, lags):
                        later = pltpu.roll(jnp.where(lane < lag, after, here), LANES - lag, 1)
                        earlier = pltpu.roll(jnp.where(lane >= LANES - lag, ahead, here), lag, 1)
                        result = result + coef * (later + earlier)
                    noise_ref[detector, rows_of(octet), :] = result
                    second_sums[wafer][group, rows_of(octet), :] += result
                    carry = carry + here * result
            return carry

        product = loop(wafer_dets, one_filter, zero, 4)
        average(second_sums)
        return product

    def return_streams(target):
        def one_return(n, carry):
            for wafer in range(wafers):
                group = group_of(wafer, n)
                for rep in range(reps):
                    at = (device_of(wafer, n) + rep) * ROWS + (n & (ROWS - 1))
                    streams = []
                    for half in range(2):
                        rows = rows_of(2 * rep + half)
                        stream = noise_ref[wafer * wafer_dets + n, rows, :]
                        streams.append(stream - second_sums[wafer][group, rows, :])
                    target[at, 0] = fold(*streams)
                    for c, ref in ((1, cos_ref), (2, sin_ref)):
                        target[at, c] = fold(*(ref[2 * at + h] * streams[h] for h in range(2)))
            return carry

        loop(wafer_dets, one_return, 0, 4)
        merge_twins(target)

    merge_twins(image_map)
    for copy in tod_moves:
        copy.wait()
    sum_streams(lambda at, carry: ([tod_ref[2 * at + half] for half in range(2)], carry), 0)
    filter_streams()
    return_streams(r_map)

    def begin(at, carry):
        parts = zero
        for c in range(3):
            inverse = 1.0 / (image_map[at, c] + prior_weight)
            inverse_ref[at, c] = inverse
            residual = r_map[at, c]
            parts = parts + residual * (inverse * residual)
        return carry + weight_ref[at] * parts

    energy = whole_sum(loop(count, begin, zero, 8))
    factor = zero
    steps = []
    for iteration, d_map in enumerate(d_maps):
        last = iteration == ITERS - 1

        def seen_streams(at, carry):
            squares = zero
            streams = [None, None]
            for c in range(3):
                part = inverse_ref[at, c] * r_map[at, c]
                if iteration:
                    part = part + factor * d_maps[iteration - 1][at, c]
                d_map[at, c] = part
                squares = squares + part * part
                for half, seen in enumerate(unfold(part)):
                    if c == 0:
                        streams[half] = seen
                    else:
                        ref = cos_ref if c == 1 else sin_ref
                        streams[half] = streams[half] + ref[2 * at + half] * seen
            return streams, carry + weight_ref[at] * squares

        prior = sum_streams(seen_streams, zero)
        product = filter_streams()
        return_streams(image_map)
        step = energy / whole_sum(product + prior_weight * prior)
        steps.append(step)

        def new_residual(at, c):
            return r_map[at, c] - step * (image_map[at, c] + prior_weight * d_map[at, c])

        if not last:

            def update(at, carry):
                parts = zero
                for c in range(3):
                    residual = new_residual(at, c)
                    r_map[at, c] = residual
                    parts = parts + residual * (inverse_ref[at, c] * residual)
                return carry + weight_ref[at] * parts

            next_energy = whole_sum(loop(count, update, zero, 16))
            factor = next_energy / energy
            energy = next_energy
        else:

            def place_pixels(at, carry):
                team = lax.rem(lax.div(at, reps * ROWS), dets)
                turn = (3 * (team * ROWS + (at & (ROWS - 1)))) & (PBLOCK - 1)
                inside = (lane & (PBLOCK - 1)) >= turn
                values = []
                for c in range(3):
                    value = steps[0] * d_maps[0][at, c]
                    for k in range(1, ITERS):
                        value = value + steps[k] * d_maps[k][at, c]
                    values.append(value)
                values += [new_residual(at, c) for c in range(3)]
                for c in range(3):
                    left, right = values[2 * c], values[2 * c + 1]
                    halves = (
                        jnp.where(low, left, turn_half(right)), jnp.where(low, turn_half(left), right)
                    )
                    for half, value in enumerate(halves):
                        value = jnp.where(
                            inside, pltpu.roll(value, turn, 1), pltpu.roll(value, turn + PBLOCK, 1)
                        )
                        rows = pl.ds(pl.multiple_of((2 * at + half) * ROWS, ROWS), ROWS)
                        rows_ref[rows, c * LANES : (c + 1) * LANES] = value
                return carry

            loop(count, place_pixels, 0, 8)

    def pick(device, carry):
        for c in range(capacity):
            move = move_ref[device, c]
            source, target = move & ((1 << 16) - 1), move >> 16
            sorted_ref[pl.ds(target, 1), :] = rows_ref[pl.ds(source, 1), :]
        return carry

    lax.fori_loop(0, devices, pick, 0)

    def turn_tile(tile, carry):
        columns = sorted_ref[pl.ds(pl.multiple_of(tile * LANES, LANES), LANES), :].T
        high = columns.astype(jnp.bfloat16)
        column_ref[tile, :, 0:LANES] = high
        column_ref[tile, :, LANES : 2 * LANES] = (columns - high.astype(jnp.float32)).astype(
            jnp.bfloat16
        )
        return carry

    lax.fori_loop(0, column_ref.shape[0], turn_tile, 0)


def write_kernel(start_ref, column_ref, place_ref, x_ref, r_ref):
    height = 3 * PBLOCK
    depth = lax.broadcasted_iota(jnp.int32, (LANES, LANES), 0)
    group = pl.program_id(0) * OUT_TILES
    start, end = start_ref[0, group], start_ref[0, group + OUT_TILES]
    first = lax.shift_right_logical(start, 7)
    last = lax.shift_right_logical(jnp.maximum(end - 1, start), 7)

    def spread(tile):
        chosen = []
        for k in range(OUT_TILES):
            place = jnp.broadcast_to(place_ref[pl.ds(group + k, 1), :], (LANES, LANES))
            chosen.append(jnp.where(place == depth + tile * LANES, 1.0, 0.0).astype(jnp.bfloat16))
        chosen = jnp.concatenate(chosen, axis=1)
        chosen = jnp.concatenate([chosen, chosen], axis=0)
        return jnp.dot(column_ref[tile], chosen, preferred_element_type=jnp.float32)

    values = spread(first)
    x_ref[...] = values[:height]
    r_ref[...] = values[height:]

    def add_tile(tile, carry):
        values = spread(tile)
        x_ref[...] += values[:height]
        r_ref[...] += values[height:]
        return carry

    lax.fori_loop(first + 1, last + 1, add_tile, 0)


def part_shape(sizes, tod, hit_list, band_lag):
    det_count, time_count = tod.shape[1:]
    owners, capacity = hit_list.shape[3:]
    return (
        sizes["wafer"], sizes["det"], sizes["rep"], time_count // SBLOCK,
        owners, capacity, BLOCKS // owners, band_lag.shape[2],
    ), det_count


def fits_one_device(shape, det_count):
    wafers, dets, reps, tiles, owners, capacity, owner_rows, lag_count = shape
    devices = wafers * dets * reps
    total = devices * tiles * det_count
    groups = owner_rows // LANES
    return (
        det_count == ROWS
        and owners == ROWS
        and tiles * ROWS == LANES
        and tiles == 2 * ROWS
        and (wafers, reps) == (2, 2)
        and (1 + lag_count) * ROWS <= LANES
        and capacity <= LANES
        and devices * capacity % LANES == 0
        and owner_rows % (LANES * OUT_TILES) == 0
        and groups + 1 <= 2 * LANES
        and devices % ROWS == 0
        and total * total < BIG
    )


def whole_part(shape, tod, psi, point_row, hit_list, group_id, a_zero, band_coef, band_lag):
    wafers, dets, reps, tiles, owners, capacity, owner_rows, lag_count = shape
    devices = wafers * dets * reps
    octets = reps * tiles // ROWS
    detectors = wafers * dets * ROWS
    count = devices * tiles
    total = count * ROWS
    slots = devices * capacity
    height = 3 * PBLOCK
    f32, i32 = jnp.float32, jnp.int32
    vmem, smem = pl.BlockSpec(memory_space=pltpu.VMEM), pl.BlockSpec(memory_space=pltpu.SMEM)
    anywhere = pl.BlockSpec(memory_space=pl.ANY)
    params = pltpu.CompilerParams(vmem_limit_bytes=VMEM_BYTES)
    swap = [(0, 1), (1, 0)]

    def along_det(block):
        moved = [
            lax.ppermute(block, "det", [(i, (i + shift) % dets) for i in range(dets)])
            for shift in range(1, dets)
        ]
        return [block] + moved

    def other_wafer(here):
        return lax.ppermute(here, "wafer", swap)

    def other_rep(here, across):
        return here, across, lax.ppermute(jnp.stack([here, across]), "rep", swap)

    tables, angles, samples = pl.pallas_call(
        functools.partial(pack_kernel, shape),
        out_shape=[
            jax.ShapeDtypeStruct((2, ROWS, LANES), f32),
            jax.ShapeDtypeStruct((ROWS, tiles, LANES), f32),
            jax.ShapeDtypeStruct((ROWS, tiles, LANES), f32),
        ],
        in_specs=[vmem] * 8,
        out_specs=[vmem] * 3,
        compiler_params=params,
        name="pack",
    )(
        psi[0], tod[0], point_row[0], hit_list[0, 0, 0], group_id, a_zero, band_coef[0].T,
        band_lag[0].T,
    )
    angles, samples = (stream.reshape(tiles, ROWS, LANES) for stream in (angles, samples))
    place_here = jnp.stack([lax.axis_index(axis) for axis in ("wafer", "det", "rep")]).astype(i32)
    tables = lax.all_gather(tables, "rep", axis=0, tiled=False)
    riders = jnp.concatenate([angles, tables.reshape(2 * reps, ROWS, LANES)])
    samples, riders = lax.optimization_barrier((samples, riders))
    samples = jnp.stack([samples, other_wafer(samples)])
    blocks = along_det(riders)
    tables = jnp.stack([block[tiles:] for block in blocks])
    angles = jnp.stack([block[:tiles] for block in blocks])
    tables = jnp.stack([tables, other_wafer(tables)])
    tables = tables.reshape(wafers, dets, reps, 2, ROWS, LANES)
    samples, angles, tables = lax.optimization_barrier((samples, angles, tables))
    angles_across = other_wafer(angles)
    samples = along_det(samples)
    table_scratch = pltpu.VMEM((devices, 2, ROWS, LANES), f32)
    table_sem = pltpu.SemaphoreType.DMA((devices,))
    twins = pl.pallas_call(
        functools.partial(twin_kernel, shape),
        out_shape=[
            jax.ShapeDtypeStruct((devices, LANES), f32),
            jax.ShapeDtypeStruct((devices, LANES), i32),
            jax.ShapeDtypeStruct((2,), i32),
            jax.ShapeDtypeStruct((total,), i32),
            jax.ShapeDtypeStruct((total,), i32),
        ],
        in_specs=[smem, anywhere],
        out_specs=[vmem] * 2 + [smem] * 3,
        scratch_shapes=[
            table_scratch,
            pltpu.VMEM((devices, LANES, LANES), f32),
            pltpu.VMEM((devices, LANES), f32),
            pltpu.VMEM((devices, LANES), f32),
            table_sem,
        ],
        compiler_params=params,
        cost_estimate=pl.CostEstimate(flops=10**9, bytes_accessed=3 * 10**7, transcendentals=0),
        name="twins",
    )(place_here, tables)
    place, start, moves = pl.pallas_call(
        functools.partial(place_kernel, shape),
        out_shape=[
            jax.ShapeDtypeStruct((2 * LANES, LANES), i32),
            jax.ShapeDtypeStruct((ROWS, 2 * LANES), i32),
            jax.ShapeDtypeStruct((devices, LANES), i32),
        ],
        in_specs=[smem, anywhere],
        out_specs=[vmem, vmem, vmem],
        scratch_shapes=[
            table_scratch,
            pltpu.VMEM((devices, LANES), i32),
            pltpu.VMEM((devices, LANES), i32),
            table_sem,
        ],
        compiler_params=params,
        cost_estimate=pl.CostEstimate(flops=10**9, bytes_accessed=2 * 10**7, transcendentals=0),
        name="places",
    )(place_here, tables)
    angles, angles_across, samples, twins, place, start, moves = lax.optimization_barrier(
        (angles, angles_across, samples, twins, place, start, moves)
    )
    floats, whole, size, pair, group = twins
    angle_blocks = other_rep(angles, angles_across)
    samples = jnp.stack(samples)
    sample_blocks = samples, lax.ppermute(samples, "rep", swap)
    stream = pltpu.VMEM((count, ROWS, LANES), f32)
    sky = pltpu.VMEM((devices * ROWS, 3, ROWS, LANES), f32)
    sky_and_spare = pltpu.VMEM((devices * ROWS + 1, 3, ROWS, LANES), f32)
    group_sums = pltpu.VMEM((NSUB, octets * ROWS, LANES), f32)
    columns = pl.pallas_call(
        functools.partial(map_kernel, shape),
        out_shape=jax.ShapeDtypeStruct((slots // LANES + 1, 2 * height, 2 * LANES), jnp.bfloat16),
        in_specs=[smem] * 7 + [anywhere] * 5,
        out_specs=vmem,
        scratch_shapes=[
            stream, stream, stream, stream,
            pltpu.VMEM((detectors, octets * ROWS, LANES), f32),
            pltpu.VMEM((detectors, octets * ROWS, LANES), f32),
            pltpu.VMEM((devices * ROWS + 1, ROWS, LANES), f32),
            sky, sky_and_spare, sky_and_spare,
            pltpu.VMEM((wafers * NSUB, ROWS, LANES), f32),
            pltpu.VMEM((total, 2 * height), f32),
            pltpu.VMEM((slots + LANES + ROWS, 2 * height), f32),
            pltpu.SemaphoreType.DMA((devices,)),
            pltpu.SemaphoreType.DMA((devices,)),
        ] + [sky] * ITERS + [group_sums] * (2 * wafers),
        compiler_params=params,
        name="map_maker",
    )(
        place_here, size, pair, group, moves, floats, whole, *angle_blocks,
        *sample_blocks,
    )
    out_block = pl.BlockSpec((height, OUT_TILES * LANES), lambda n: (0, n))
    x_turned, r_turned = pl.pallas_call(
        write_kernel,
        grid=(owner_rows // (OUT_TILES * LANES),),
        out_shape=[jax.ShapeDtypeStruct((height, owner_rows), f32)] * 2,
        in_specs=[smem, vmem, vmem],
        out_specs=[out_block, out_block],
        compiler_params=params,
        name="write",
    )(start, columns, place)
    return x_turned.T, r_turned.T


def local(sizes, *arguments):
    tod, hit_list, band_lag = arguments[0], arguments[3], arguments[7]
    shape, det_count = part_shape(sizes, tod, hit_list, band_lag)
    if fits_one_device(shape, det_count):
        return whole_part(shape, *arguments)
    return distributed(*arguments)


def solution(mesh):
    placed = (
        P(("groups", "wafer"), "det", "rep"),
        P(("groups", "wafer"), "det", "rep"),
        P(("groups", "wafer"), "det", "rep"),
        P(("groups", "wafer"), "det", "rep", None, None),
        P(("groups", "wafer"), "det"),
        P(("groups", "wafer"), "det"),
        P(("groups", "wafer"), "det", None),
        P(("groups", "wafer"), "det", None),
    )
    return jax.shard_map(
        functools.partial(local, mesh.shape),
        mesh=mesh,
        in_specs=placed,
        out_specs=(P(("groups", "det", "wafer"), None), P(("groups", "det", "wafer"), None)),
        check_vma=False,
    )
```

```python
import functools

import jax
import jax.numpy as jnp
from jax import lax
from jax.experimental import pallas as pl
from jax.experimental.pallas import tpu as pltpu
from jax.sharding import PartitionSpec as P

BLOCKS = 196608
PBLOCK = 64
SBLOCK = 128
NSUB = 4
LAG = 16
ITERS = 3


prior_weight = 1.0


def with_halo(block, sides, width):
    for axis, dim in sides:
        count = lax.axis_size(axis)
        forward = [(i, i + 1) for i in range(count - 1)]
        backward = [(target, source) for source, target in forward]
        low = lax.ppermute(
            lax.slice_in_dim(block, block.shape[dim] - width, None, axis=dim), axis, forward
        )
        high = lax.ppermute(lax.slice_in_dim(block, 0, width, axis=dim), axis, backward)
        block = jnp.concatenate([low, block, high], axis=dim)
    return block


def distributed(tod, psi, point_row, hit_list, group_id, a_zero, band_coef, band_lag):
    highest = lax.Precision.HIGHEST
    samples = tod[0]
    angles = psi[0]
    det_count, time_count = samples.shape
    time_blocks = time_count // SBLOCK
    block_count = det_count * time_blocks
    send_table = hit_list[0, 0, 0]
    owner_count, capacity = send_table.shape
    owner_rows = BLOCKS // owner_count
    block_width = 3 * PBLOCK
    detector = lax.axis_index("det") * det_count + jnp.arange(det_count, dtype=jnp.int32)
    within = (jnp.arange(SBLOCK, dtype=jnp.int32)[None, :] + 3 * detector[:, None]) % PBLOCK
    pixel_table = (within[:, :, None] == jnp.arange(PBLOCK, dtype=jnp.int32)[None, None, :]).astype(
        jnp.float32
    )
    cosine_two = jnp.cos(2.0 * angles).reshape(det_count, time_blocks, SBLOCK)
    sine_two = jnp.sin(2.0 * angles).reshape(det_count, time_blocks, SBLOCK)
    slot_ids = send_table.reshape(-1)
    row_source = jnp.concatenate([point_row[0].reshape(-1), jnp.zeros((1,), jnp.int32)])
    slot_rows = row_source[slot_ids].astype(jnp.float32).reshape(owner_count, capacity)
    member = (group_id[0][:, None] == jnp.arange(NSUB, dtype=jnp.int32)[None, :]).astype(
        jnp.float32
    )
    member_count = jnp.sum(member, axis=0)
    lag_table = (
        band_lag[0][:, :, None] == jnp.arange(1, LAG + 1, dtype=jnp.int32)[None, None, :]
    ).astype(jnp.float32)
    lag_weight = jnp.einsum("dj,djl->dl", band_coef[0], lag_table, precision=highest)
    base_weight = a_zero[0]

    def slot_payload(by_block):
        width = by_block.shape[1]
        extended = jnp.concatenate([by_block, jnp.zeros((1, width), by_block.dtype)])
        return extended[slot_ids].reshape(owner_count, capacity, width)

    def deliver(payload):
        width = payload.shape[-1]
        got_values, got_rows = (
            lax.all_to_all(payload, ("det", "wafer"), split_axis=0, concat_axis=0, tiled=True),
            lax.all_to_all(slot_rows, ("det", "wafer"), split_axis=0, concat_axis=0, tiled=True),
        )
        return (got_values, got_rows)

    def back_project(stream, squared):
        shaped = stream.reshape(det_count, time_blocks, SBLOCK)
        first = cosine_two * cosine_two if squared else cosine_two
        second = sine_two * sine_two if squared else sine_two
        stacked = jnp.stack([shaped, first * shaped, second * shaped], axis=2)
        stokes = jnp.einsum("dkcs,dsp->dkcp", stacked, pixel_table, precision=highest)
        return stokes.reshape(block_count, block_width)

    def to_owners(stream, squared):
        got_values, got_rows = deliver(slot_payload(back_project(stream, squared)))
        pair_values, pair_rows = (
            lax.all_gather(got_values, "rep", axis=0, tiled=True),
            lax.all_gather(got_rows, "rep", axis=0, tiled=True),
        )
        target_rows = pair_rows.reshape(-1).astype(jnp.int32)
        summed = (
            jnp.zeros((owner_rows, block_width), jnp.float32)
            .at[target_rows]
            .add(pair_values.reshape(-1, block_width))
        )
        return (summed, got_rows.astype(jnp.int32))

    def remove_common(stream):
        local_sums = jnp.einsum("dg,dt->gt", member, stream, precision=highest)
        group_sums, group_counts = lax.psum((local_sums, member_count), "det")
        group_means = group_sums / jnp.maximum(group_counts, 1.0)[:, None]
        return stream - jnp.einsum("dg,gt->dt", member, group_means, precision=highest)

    def band_filter(stream):
        padded = with_halo(stream, (("rep", 1),), LAG)
        result = base_weight[:, None] * stream
        for offset in range(1, LAG + 1):
            later = padded[:, LAG + offset : LAG + offset + time_count]
            earlier = padded[:, LAG - offset : LAG - offset + time_count]
            result = result + lag_weight[:, offset - 1 : offset] * (later + earlier)
        return result

    def weigh_stream(stream):
        return remove_common(band_filter(remove_common(stream)))

    weight_stream = jnp.broadcast_to(base_weight[:, None], (det_count, time_count))
    diag_sum, serve_rows = to_owners(weight_stream, True)
    inverse_diag = 1.0 / (diag_sum + prior_weight)
    right_side = to_owners(weigh_stream(samples), False)[0]
    solution = jnp.zeros_like(right_side)
    residual = right_side

    def inner(left_map, right_map):
        return lax.psum(jnp.sum(left_map * right_map), ("det", "wafer"))

    precond = inverse_diag * residual
    direction = precond
    energy = inner(residual, precond)
    for iteration in range(ITERS):
        from_blocks = direction[serve_rows.reshape(-1)].reshape(owner_count, capacity, block_width)
        return_width = from_blocks.shape[-1]
        returned = lax.all_to_all(
            from_blocks, ("det", "wafer"), split_axis=0, concat_axis=0, tiled=True
        )
        return_placed = jnp.zeros((block_count + 1, return_width), jnp.float32)
        return_placed = return_placed.at[slot_ids].set(returned.reshape(-1, return_width))
        blocks = return_placed[:block_count].reshape(det_count, time_blocks, 3, PBLOCK)
        project_stokes = jnp.einsum("dkcp,dsp->dkcs", blocks, pixel_table, precision=highest)
        project_stream = (
            project_stokes[:, :, 0]
            + cosine_two * project_stokes[:, :, 1]
            + sine_two * project_stokes[:, :, 2]
        )
        seen_stream = project_stream.reshape(det_count, time_count)
        image_map = to_owners(weigh_stream(seen_stream), False)[0] + prior_weight * direction
        step_size = energy / inner(direction, image_map)
        solution = solution + step_size * direction
        residual = residual - step_size * image_map
        precond = inverse_diag * residual
        energy_next = inner(residual, precond)
        direction = precond + energy_next / energy * direction
        energy = energy_next
    return (solution, residual)


LANES = 128
ROWS = 8
OUT_TILES = 8
PAIR_BATCH = 4
DET_BATCH = 8
SUM_SETS = 2
MAP_BATCH = 8
BIG = float(1 << 24)
VMEM_BYTES = 60 << 20


def wide(values):
    return jnp.broadcast_to(values, (ROWS, LANES))


def tile_iotas():
    lane = lax.broadcasted_iota(jnp.int32, (ROWS, LANES), 1)
    sub = lax.broadcasted_iota(jnp.int32, (ROWS, LANES), 0)
    return lane, sub


def cosine_sine_double(angle):
    turns = jnp.floor(angle * 1.2732395447351628 + 0.5)
    reduced = 2.0 * angle - turns * 1.5703125
    reduced = reduced - turns * 4.837512969970703125e-4
    reduced = reduced - turns * 7.54978995489188216e-8
    square = reduced * reduced
    sine = (-1.9515295891e-4 * square + 8.3321608736e-3) * square - 1.6666654611e-1
    sine = sine * square * reduced + reduced
    cosine = (2.443315711809948e-5 * square - 1.388731625493765e-3) * square
    cosine = (cosine + 4.166664568298827e-2) * square * square - 0.5 * square + 1.0
    quarter = turns.astype(jnp.int32)
    odd = (quarter & 1) == 1
    first = jnp.where(odd, sine, cosine)
    second = jnp.where(odd, cosine, sine)
    first = jnp.where(((quarter + 1) & 2) == 2, -first, first)
    second = jnp.where((quarter & 2) == 2, -second, second)
    return first, second


def pack_kernel(
    shape, angle_ref, tod_ref, row_ref, hit_ref, group_ref, base_ref, coef_ref, lag_ref,
    table_ref, angle_rows_ref, tod_rows_ref,
):
    wafers, dets, reps, tiles, owners, capacity, owner_rows, lag_count = shape
    lane, sub = tile_iotas()
    lists = hit_ref[...]
    owner_hits = jnp.zeros((ROWS, LANES), jnp.float32)
    for c in range(capacity):
        owner_hits = owner_hits + jnp.where(wide(lists[:, c : c + 1]) == lane, 1.0, 0.0)
    owner_of = jnp.sum(owner_hits * sub.astype(jnp.float32), axis=0, keepdims=True)

    def spread(values, width):
        return jnp.concatenate(
            [values, jnp.zeros((values.shape[0], LANES - width), values.dtype)], axis=1
        )

    rows = spread(row_ref[...].astype(jnp.float32), tiles)
    ids = owner_of * float(owner_rows) + rows[0:1]
    for k in range(1, ROWS):
        ids = ids + pltpu.roll(rows[k : k + 1], k * tiles, 1)
    floats = spread(base_ref[...], ROWS)
    whole = spread(group_ref[...].astype(jnp.float32), ROWS)
    for j in range(lag_count):
        at = (j + 1) * ROWS
        floats = floats + pltpu.roll(spread(coef_ref[j : j + 1, :], ROWS), at, 1)
        lag = lag_ref[j : j + 1, :].astype(jnp.float32)
        whole = whole + pltpu.roll(spread(lag, ROWS), at, 1)
    table = jnp.where(sub == 0, wide(ids), jnp.where(sub == 1, wide(floats), wide(whole)))
    table_ref[0] = table
    table_ref[1] = spread(lists.astype(jnp.float32), capacity)
    for b in range(tiles):
        angle_rows_ref[:, b, :] = angle_ref[:, b * LANES : (b + 1) * LANES]
        tod_rows_ref[:, b, :] = tod_ref[:, b * LANES : (b + 1) * LANES]


def part_copies(shape, self_ref, source, target, sem):
    wafers, dets, reps = shape[:3]
    copies = []
    for swap_rep in range(reps):
        for swap_wafer in range(wafers):
            for shift in range(dets):
                det = self_ref[1] - shift
                det = jnp.where(det < 0, det + dets, det)
                device = ((self_ref[0] ^ swap_wafer) * dets + det) * reps
                device = device + (self_ref[2] ^ swap_rep)
                copies.append(
                    pltpu.make_async_copy(
                        source(swap_rep, swap_wafer, shift), target(device), sem.at[len(copies)]
                    )
                )
    return copies


def table_copies(shape, self_ref, source_ref, part_ref, sem):
    wafers, dets, reps = shape[:3]
    copies = []
    for shift in range(dets):
        for wafer in range(wafers):
            det = self_ref[1] - shift
            det = jnp.where(det < 0, det + dets, det)
            device = (wafer * dets + det) * reps
            copies.append(
                pltpu.make_async_copy(
                    source_ref.at[shift, wafer], part_ref.at[pl.ds(device, reps)],
                    sem.at[len(copies)],
                )
            )
    for copy in copies:
        copy.start()
    for copy in copies:
        copy.wait()


def exact_dot(left, right, dims=((1,), (0,))):
    return lax.dot_general(
        left.astype(jnp.bfloat16), right.astype(jnp.bfloat16), (dims, ((), ())),
        preferred_element_type=jnp.float32,
    )


def twin_kernel(
    shape, self_ref, table_ref, float_ref, whole_ref, size_ref, pair_ref, group_ref,
    part_ref, column_ref, code_ref, lead_ref, used_ref, part_sem,
):
    wafers, dets, reps, tiles, owners, capacity, owner_rows, lag_count = shape
    devices = wafers * dets * reps
    total = devices * LANES
    lane, sub = tile_iotas()
    sub_f = sub.astype(jnp.float32)
    none = jnp.full((ROWS, LANES), BIG, jnp.float32)
    along = lax.broadcasted_iota(jnp.int32, (1, LANES), 1).astype(jnp.float32)
    table_copies(shape, self_ref, table_ref, part_ref, part_sem)

    def turn(batch, carry):
        for k in range(4):
            device = 4 * batch + k
            float_ref[pl.ds(device, 1), :] = part_ref[device, 0, 1:2, :]
            whole_ref[pl.ds(device, 1), :] = part_ref[device, 0, 2:3, :].astype(jnp.int32)
            column_ref[device] = jnp.broadcast_to(part_ref[device, 0, 0:1, :], (LANES, LANES)).T
        return carry

    lax.fori_loop(0, devices // 4, turn, 0)

    def survey(device, carry):
        row = wide(part_ref[device, 0, 0:1, :])

        def compare(other, least):
            found = [none] * 4
            for j in range(tiles):
                same = column_ref[other, j * ROWS : (j + 1) * ROWS, :] == row
                found[j % 4] = jnp.minimum(found[j % 4], jnp.where(same, sub_f + float(j * ROWS), BIG))
            here = jnp.minimum(jnp.minimum(found[0], found[1]), jnp.minimum(found[2], found[3]))
            return jnp.minimum(least, here + (other * LANES).astype(jnp.float32))

        least = lax.fori_loop(0, device + 1, compare, none)
        lead = jnp.min(least, axis=0, keepdims=True)
        mine = (device * LANES).astype(jnp.float32) + along
        later = lead < mine
        code_ref[pl.ds(device, 1), :] = jnp.where(later, mine * float(total) + lead, BIG)
        lead_ref[pl.ds(device, 1), :] = jnp.where(later, lead, BIG)
        return carry

    lax.fori_loop(0, devices, survey, 0)

    def next_code(last):
        found = none
        for tile in range(devices // ROWS):
            codes = code_ref[tile * ROWS : (tile + 1) * ROWS, :]
            found = jnp.minimum(found, jnp.where(codes > last, codes, BIG))
        return jnp.min(found)

    def detector(key):
        team = lax.rem(lax.div(key, reps * LANES), dets)
        return team * ROWS + lax.rem(lax.div(key, tiles), ROWS)

    number_of = [lane + (sub + tile * ROWS) * LANES for tile in range(devices // ROWS)]
    tile_rows = [slice(tile * ROWS, (tile + 1) * ROWS) for tile in range(devices // ROWS)]
    for rows in tile_rows:
        used_ref[rows, :] = jnp.zeros((ROWS, LANES), jnp.int32)

    def take(as_pairs, state):
        pairs, grouped, code = state
        number = code.astype(jnp.int32)
        key = lax.div(number, total)
        lead = lax.rem(number, total)
        shift = (3 * (detector(key) - detector(lead))) & (PBLOCK - 1)
        alone = False
        if as_pairs:
            wanted = lead.astype(jnp.float32)
            same = jnp.zeros((ROWS, LANES), jnp.float32)
            for rows, numbers in zip(tile_rows, number_of):
                same = same + jnp.where(lead_ref[rows, :] == wanted, 1.0, 0.0)
                used = (numbers == key) | (numbers == lead)
                used_ref[rows, :] = jnp.where(used, 1, used_ref[rows, :])
            alone = jnp.sum(same) < 1.5
        entry = twin_entry(key, lead, shift)
        pair_ref[pairs] = entry
        group_ref[grouped] = entry
        return (
            pairs + jnp.where(alone, 1, 0), grouped + jnp.where(alone, 0, 1), next_code(code)
        )

    def more(state):
        return state[2] < BIG

    none_yet = (jnp.int32(0), jnp.int32(0))
    first_code = next_code(jnp.float32(-1.0))
    pairs, grouped, _ = lax.while_loop(
        more, functools.partial(take, True), none_yet + (first_code,)
    )
    shared = jnp.zeros((ROWS, LANES), jnp.int32)
    for rows in tile_rows:
        used = used_ref[rows, :]
        shared = shared + jnp.where((lane & ROWS) == 0, used * pltpu.roll(used, LANES - ROWS, 1), 0)
    shared = jnp.sum(shared.astype(jnp.float32)) > 0.5
    pairs, grouped = jnp.where(shared, 0, pairs), jnp.where(shared, 0, grouped)
    _, grouped, _ = lax.while_loop(
        more, functools.partial(take, False),
        (pairs, grouped, jnp.where(shared, first_code, BIG)),
    )
    batches = lax.div(pairs + PAIR_BATCH - 1, PAIR_BATCH)

    def fill(n, carry):
        pair_ref[n] = twin_entry(total, total + 1, 0)
        return carry

    lax.fori_loop(pairs, batches * PAIR_BATCH, fill, 0)
    size_ref[0] = batches
    size_ref[1] = grouped


def twin_entry(key, lead, shift):
    return key * (1 << 19) + lead * (1 << 6) + shift


def twin_of(entry):
    return entry >> 19, (entry >> 6) & ((1 << 13) - 1), entry & (PBLOCK - 1)


def place_kernel(
    shape, self_ref, table_ref, place_ref, start_ref, move_ref, part_ref, rank_ref, hits_ref,
    part_sem,
):
    wafers, dets, reps, tiles, owners, capacity, owner_rows, lag_count = shape
    devices = wafers * dets * reps
    slots = devices * capacity
    lane, sub = tile_iotas()
    own = self_ref[1] * wafers + self_ref[0]
    first_row = (own * owner_rows).astype(jnp.float32)
    table_copies(shape, self_ref, table_ref, part_ref, part_sem)
    depth = 2 * LANES
    tall = lax.broadcasted_iota(jnp.int32, (depth, LANES), 0).astype(jnp.float32)

    def one_hots(device):
        local_row = part_ref[device, 0, 0:1, :] - first_row
        high = jnp.floor(local_row * (1.0 / LANES))
        low = local_row - high * LANES
        high = (jnp.broadcast_to(high, (depth, LANES)) == tall).astype(jnp.float32)
        low = (jnp.broadcast_to(low, (LANES, LANES)) == tall[0:LANES]).astype(jnp.float32)
        return high, low

    def survey(batch, hits):
        for k in range(4):
            device = 4 * batch + k
            own_hits = jnp.where(sub == own, part_ref[device, 1], 0.0)
            own_hits = jnp.sum(own_hits, axis=0, keepdims=True)
            hits_ref[pl.ds(device, 1), :] = own_hits.astype(jnp.int32)
            high, low = one_hots(device)
            hits = hits + exact_dot(high, low, ((1,), (1,)))
        return hits

    hits = lax.fori_loop(0, devices // 4, survey, jnp.zeros((depth, LANES), jnp.float32))
    full = jnp.minimum(hits, 1.0)

    def ordered(size, axis):
        first = lax.broadcasted_iota(jnp.int32, (size, size), axis)
        second = lax.broadcasted_iota(jnp.int32, (size, size), 1 - axis)
        return (first < second).astype(jnp.float32)

    counts = exact_dot(jnp.ones((ROWS, LANES), jnp.float32), full, ((1,), (1,)))
    start_ref[...] = exact_dot(counts, ordered(depth, 0)).astype(jnp.int32)
    sums = exact_dot(full, jnp.ones((LANES, LANES), jnp.float32))
    place = exact_dot(full, ordered(LANES, 0)) + exact_dot(ordered(depth, 1), sums)
    place_ref[...] = jnp.where(full > 0.0, place, -1.0).astype(jnp.int32)
    place_high = jnp.floor(place * (1.0 / LANES))
    place_parts = jnp.concatenate([place_high, place - place_high * LANES], axis=0)

    def rank_of(batch, carry):
        for k in range(4):
            device = 4 * batch + k
            high, low = one_hots(device)
            parts = exact_dot(place_parts, low)
            rank = high * (parts[0:depth] * LANES + parts[depth : 2 * depth])
            rank = jnp.sum(rank, axis=0, keepdims=True)
            rank_ref[pl.ds(device, 1), :] = rank.astype(jnp.int32)
        return carry

    lax.fori_loop(0, devices // 4, rank_of, 0)
    for tile in range(devices // ROWS):
        rows = slice(tile * ROWS, (tile + 1) * ROWS)
        number = hits_ref[rows, :]
        valid = number < LANES
        number = number & (LANES - 1)
        rank = jnp.take_along_axis(rank_ref[rows, :], number, axis=1, mode="promise_in_bounds")
        target = jnp.where(valid, rank, slots + LANES)
        move_ref[rows, :] = target * (1 << 16) + (tile * ROWS + sub) * LANES + number


def map_kernel(
    shape, self_ref, size_ref, pair_ref, group_ref, move_ref, float_smem, whole_smem,
    angle_here_ref, angle_across_ref, angle_other_ref, tod_here_ref, tod_other_ref, column_ref,
    angle_ref, tod_ref, cos_ref, sin_ref, clean_ref, noise_ref, weight_ref,
    share_ref, rows_ref, sorted_ref, angle_sem, tod_sem, *more_refs,
):
    wafers, dets, reps, tiles, owners, capacity, owner_rows, lag_count = shape
    devices = wafers * dets * reps
    octets = 2 * reps
    wafer_dets = dets * ROWS
    count = devices * ROWS
    lane, sub = tile_iotas()
    zero = jnp.zeros((ROWS, LANES), jnp.float32)
    low = lane < PBLOCK
    skies = [more_refs[3 * k : 3 * k + 3] for k in range(3 + ITERS)]
    inverse_ref, r_map, image_map, *d_maps = skies
    sum_refs = more_refs[3 * len(skies) :]
    first_sums = [sum_refs[SUM_SETS * wafer : SUM_SETS * (wafer + 1)] for wafer in range(wafers)]
    sum_refs = sum_refs[SUM_SETS * wafers :]
    second_sums = [sum_refs[SUM_SETS * wafer : SUM_SETS * (wafer + 1)] for wafer in range(wafers)]

    def copies_of(source, to_ref, sem):
        return part_copies(
            shape, self_ref, source, lambda d: to_ref.at[pl.ds(d * tiles, tiles)], sem
        )

    def angle_source(swap_rep, swap_wafer, shift):
        if swap_rep:
            return angle_other_ref.at[swap_wafer, shift]
        return (angle_across_ref if swap_wafer else angle_here_ref).at[shift]

    def tod_source(swap_rep, swap_wafer, shift):
        return (tod_other_ref if swap_rep else tod_here_ref).at[shift, swap_wafer]

    angle_moves = copies_of(angle_source, angle_ref, angle_sem)
    tod_moves = copies_of(tod_source, tod_ref, tod_sem)
    for copy in angle_moves + tod_moves:
        copy.start()

    def turn_half(block):
        return pltpu.roll(block, PBLOCK, 1)

    def fold(first, second):
        return jnp.where(low, first, second) + turn_half(jnp.where(low, second, first))

    def unfold(block):
        turned = turn_half(block)
        return jnp.where(low, block, turned), jnp.where(low, turned, block)

    def whole_sum(values):
        values = jnp.sum(values, axis=0, keepdims=True)
        return wide(jnp.sum(values, axis=1, keepdims=True))

    def loop(times, body, carry, unroll):
        def several(n, carry):
            for k in range(unroll):
                carry = body(n * unroll + k, carry)
            return carry

        return lax.fori_loop(0, times // unroll, several, carry)

    def device_of(wafer, n):
        return (wafer * dets + lax.shift_right_logical(n, 3)) * reps

    def group_of(wafer, n):
        return whole_smem[device_of(wafer, n), n & (ROWS - 1)]

    def rows_of(octet):
        return pl.ds(octet * ROWS, ROWS)

    def count_members(n, counts):
        result = []
        for wafer in range(wafers):
            group = group_of(wafer, n)
            result += [
                counts[wafer * NSUB + g] + jnp.where(group == g, 1, 0) for g in range(NSUB)
            ]
        return tuple(result)

    members = lax.fori_loop(0, wafer_dets, count_members, (jnp.int32(0),) * (wafers * NSUB))
    for k, member in enumerate(members):
        share_ref[k] = 1.0 / jnp.maximum(zero + member.astype(jnp.float32), 1.0)
    for c in range(3):
        image_map[c][count] = zero
        r_map[c][count] = zero

    def clear_sorted(n, carry):
        at = pl.ds(pl.multiple_of(n * ROWS, ROWS), ROWS)
        sorted_ref[at, :] = jnp.zeros((ROWS, 6 * PBLOCK), jnp.float32)
        return carry

    lax.fori_loop(0, sorted_ref.shape[0] // ROWS, clear_sorted, 0)

    def spot_of(key):
        return lax.shift_right_logical(key, 4), (key >> 3) & 1, pl.ds(key & (ROWS - 1), 1)

    def in_half(half):
        return (lane[0:1] >> 6) == half

    def set_weight(at, carry):
        weight_ref[at] = zero + 1.0
        return carry

    loop(count, set_weight, 0, 16)

    def drop(list_ref):
        def one(n, carry):
            at, half, row = spot_of(twin_of(list_ref[n])[0])
            weight_ref[at, row, :] = jnp.where(in_half(half), 0.0, weight_ref[at, row, :])
            return carry

        return one

    lax.fori_loop(0, size_ref[0] * PAIR_BATCH, drop(pair_ref), 0)
    lax.fori_loop(0, size_ref[1], drop(group_ref), 0)

    def moved_from(target, spot, shift):
        at, half, row = spot
        result = []
        for ref in target:
            values = wide(ref[at, row, :])
            values = jnp.where((lane >> 6) == half, values, turn_half(values))
            result.append(pltpu.roll(values, shift, 1)[0:1])
        return result

    def merge_twins(target):
        def pair_batch(n, carry):
            found = []
            for k in range(PAIR_BATCH):
                key, lead, shift = twin_of(pair_ref[n * PAIR_BATCH + k])
                key, lead = spot_of(key), spot_of(lead)
                back = (PBLOCK - shift) & (PBLOCK - 1)
                for spot, values in (
                    (lead, moved_from(target, key, shift)), (key, moved_from(target, lead, back))
                ):
                    at, half, row = spot
                    for c in range(3):
                        values[c] = target[c][at, row, :] + jnp.where(in_half(half), values[c], 0.0)
                    found.append((at, row, values))
            for at, row, values in found:
                for c in range(3):
                    target[c][at, row, :] = values[c]
            return carry

        def gather_one(n, carry):
            key, lead, shift = twin_of(group_ref[n])
            values = moved_from(target, spot_of(key), shift)
            at, half, row = spot_of(lead)
            for c in range(3):
                target[c][at, row, :] += jnp.where(in_half(half), values[c], 0.0)
            return carry

        def spread_one(n, carry):
            key, lead, shift = twin_of(group_ref[n])
            values = moved_from(target, spot_of(lead), (PBLOCK - shift) & (PBLOCK - 1))
            at, half, row = spot_of(key)
            for c in range(3):
                target[c][at, row, :] = jnp.where(in_half(half), values[c], target[c][at, row, :])
            return carry

        lax.fori_loop(0, size_ref[0], pair_batch, 0)
        lax.fori_loop(0, size_ref[1], gather_one, 0)
        lax.fori_loop(0, size_ref[1], spread_one, 0)

    for copy in angle_moves:
        copy.wait()

    def survey(at, carry):
        base = float_smem[lax.shift_right_logical(at, 3), at & (ROWS - 1)]
        squares = []
        for half in range(2):
            first, second = cosine_sine_double(angle_ref[2 * at + half])
            cos_ref[2 * at + half] = first
            sin_ref[2 * at + half] = second
            squares.append((base * (first * first), base * (second * second)))
        image_map[0][at] = zero + (base + base)
        for c in range(2):
            image_map[c + 1][at] = fold(squares[0][c], squares[1][c])
        return carry

    loop(count, survey, 0, 8)

    def clear_sums(refs):
        for sets in refs:
            for ref in sets:
                for group in range(NSUB):
                    for octet in range(octets):
                        ref[group, rows_of(octet), :] = zero

    def average(refs):
        for wafer, sets in enumerate(refs):
            for group in range(NSUB):
                for octet in range(octets):
                    total = sets[0][group, rows_of(octet), :]
                    for ref in sets[1:]:
                        total = total + ref[group, rows_of(octet), :]
                    sets[0][group, rows_of(octet), :] = total * share_ref[wafer * NSUB + group]

    def over_detectors(body, carry):
        def several(step, carry):
            for k in range(DET_BATCH):
                carry = body(step * DET_BATCH + k, k % SUM_SETS, carry)
            return carry

        return lax.fori_loop(0, wafer_dets // DET_BATCH, several, carry)

    def sum_streams(streams_of, carry):
        clear_sums(first_sums)

        def one_detector(n, part, carry):
            for wafer in range(wafers):
                group = group_of(wafer, n)
                for rep in range(reps):
                    at = (device_of(wafer, n) + rep) * ROWS + (n & (ROWS - 1))
                    streams, carry = streams_of(at, carry)
                    for half, stream in enumerate(streams):
                        rows = rows_of(2 * rep + half)
                        clean_ref[wafer * wafer_dets + n, rows, :] = stream
                        first_sums[wafer][part][group, rows, :] += stream
            return carry

        carry = over_detectors(one_detector, carry)
        average(first_sums)
        return carry

    def filter_streams():
        clear_sums(second_sums)

        def one_filter(n, part, carry):
            for wafer in range(wafers):
                device, inside = device_of(wafer, n), n & (ROWS - 1)
                detector = wafer * wafer_dets + n
                group = group_of(wafer, n)
                base = float_smem[device, inside]
                coefs = [float_smem[device, (j + 1) * ROWS + inside] for j in range(lag_count)]
                lags = [whole_smem[device, (j + 1) * ROWS + inside] for j in range(lag_count)]
                clean = [
                    clean_ref[detector, rows_of(octet), :]
                    - first_sums[wafer][0][group, rows_of(octet), :]
                    for octet in range(octets)
                ]
                up = [pltpu.roll(here, ROWS - 1, 0) for here in clean] + [zero]
                down = [zero] + [pltpu.roll(here, 1, 0) for here in clean]
                for octet, here in enumerate(clean):
                    after = jnp.where(sub == ROWS - 1, up[octet + 1], up[octet])
                    ahead = jnp.where(sub == 0, down[octet], down[octet + 1])
                    result = base * here
                    for coef, lag in zip(coefs, lags):
                        later = pltpu.roll(jnp.where(lane < lag, after, here), LANES - lag, 1)
                        earlier = pltpu.roll(jnp.where(lane >= LANES - lag, ahead, here), lag, 1)
                        result = result + coef * (later + earlier)
                    noise_ref[detector, rows_of(octet), :] = result
                    second_sums[wafer][part][group, rows_of(octet), :] += result
                    carry = carry + here * result
            return carry

        product = over_detectors(one_filter, zero)
        average(second_sums)
        return product

    def return_streams(target):
        def one_return(n, part, carry):
            for wafer in range(wafers):
                group = group_of(wafer, n)
                for rep in range(reps):
                    at = (device_of(wafer, n) + rep) * ROWS + (n & (ROWS - 1))
                    streams = []
                    for half in range(2):
                        rows = rows_of(2 * rep + half)
                        stream = noise_ref[wafer * wafer_dets + n, rows, :]
                        streams.append(stream - second_sums[wafer][0][group, rows, :])
                    target[0][at] = fold(*streams)
                    for c, ref in ((1, cos_ref), (2, sin_ref)):
                        target[c][at] = fold(*(ref[2 * at + h] * streams[h] for h in range(2)))
            return carry

        over_detectors(one_return, 0)
        merge_twins(target)

    merge_twins(image_map)
    for copy in tod_moves:
        copy.wait()
    sum_streams(lambda at, carry: ([tod_ref[2 * at + half] for half in range(2)], carry), 0)
    filter_streams()
    return_streams(r_map)

    def begin(at, carry):
        parts = zero
        for c in range(3):
            inverse = 1.0 / (image_map[c][at] + prior_weight)
            inverse_ref[c][at] = inverse
            residual = r_map[c][at]
            parts = parts + residual * (inverse * residual)
        return carry + weight_ref[at] * parts

    energy = whole_sum(loop(count, begin, zero, 16))
    factor = zero
    steps = []
    for iteration, d_map in enumerate(d_maps):
        last = iteration == ITERS - 1

        def seen_streams(at, carry):
            squares = zero
            streams = [None, None]
            for c in range(3):
                part = inverse_ref[c][at] * r_map[c][at]
                if iteration:
                    part = part + factor * d_maps[iteration - 1][c][at]
                d_map[c][at] = part
                squares = squares + part * part
                for half, seen in enumerate(unfold(part)):
                    if c == 0:
                        streams[half] = seen
                    else:
                        ref = cos_ref if c == 1 else sin_ref
                        streams[half] = streams[half] + ref[2 * at + half] * seen
            return streams, carry + weight_ref[at] * squares

        prior = sum_streams(seen_streams, zero)
        product = filter_streams()
        return_streams(image_map)
        step = energy / whole_sum(product + prior_weight * prior)
        steps.append(step)

        def new_residual(at, c):
            return r_map[c][at] - step * (image_map[c][at] + prior_weight * d_map[c][at])

        if not last:

            def update(batch, carry):
                found = []
                for k in range(MAP_BATCH):
                    at = batch * MAP_BATCH + k
                    residual = [new_residual(at, c) for c in range(3)]
                    parts = zero
                    for c in range(3):
                        parts = parts + residual[c] * (inverse_ref[c][at] * residual[c])
                    carry = carry + weight_ref[at] * parts
                    found.append((at, residual))
                for at, residual in found:
                    for c in range(3):
                        r_map[c][at] = residual[c]
                return carry

            next_energy = whole_sum(loop(count // MAP_BATCH, update, zero, 2))
            factor = next_energy / energy
            energy = next_energy
        else:

            def place_pixels(at, carry):
                team = lax.rem(lax.div(at, reps * ROWS), dets)
                turn = (3 * (team * ROWS + (at & (ROWS - 1)))) & (PBLOCK - 1)
                inside = (lane & (PBLOCK - 1)) >= turn
                values = []
                for c in range(3):
                    value = steps[0] * d_maps[0][c][at]
                    for k in range(1, ITERS):
                        value = value + steps[k] * d_maps[k][c][at]
                    values.append(value)
                values += [new_residual(at, c) for c in range(3)]
                for c in range(3):
                    left, right = values[2 * c], values[2 * c + 1]
                    halves = (
                        jnp.where(low, left, turn_half(right)), jnp.where(low, turn_half(left), right)
                    )
                    for half, value in enumerate(halves):
                        value = jnp.where(
                            inside, pltpu.roll(value, turn, 1), pltpu.roll(value, turn + PBLOCK, 1)
                        )
                        rows = pl.ds(pl.multiple_of((2 * at + half) * ROWS, ROWS), ROWS)
                        rows_ref[rows, c * LANES : (c + 1) * LANES] = value
                return carry

            loop(count, place_pixels, 0, 8)

    def pick(device, carry):
        for c in range(capacity):
            move = move_ref[device, c]
            source, target = move & ((1 << 16) - 1), move >> 16
            sorted_ref[pl.ds(target, 1), :] = rows_ref[pl.ds(source, 1), :]
        return carry

    lax.fori_loop(0, devices, pick, 0)

    def turn_tile(tile, carry):
        columns = sorted_ref[pl.ds(pl.multiple_of(tile * LANES, LANES), LANES), :].T
        high = columns.astype(jnp.bfloat16)
        column_ref[tile, :, 0:LANES] = high
        column_ref[tile, :, LANES : 2 * LANES] = (columns - high.astype(jnp.float32)).astype(
            jnp.bfloat16
        )
        return carry

    lax.fori_loop(0, column_ref.shape[0], turn_tile, 0)


def write_kernel(start_ref, column_ref, place_ref, x_ref, r_ref):
    height = 3 * PBLOCK
    depth = lax.broadcasted_iota(jnp.int32, (LANES, LANES), 0)
    group = pl.program_id(0) * OUT_TILES
    start, end = start_ref[0, group], start_ref[0, group + OUT_TILES]
    first = lax.shift_right_logical(start, 7)
    last = lax.shift_right_logical(jnp.maximum(end - 1, start), 7)

    def spread(tile):
        chosen = []
        for k in range(OUT_TILES):
            place = jnp.broadcast_to(place_ref[pl.ds(group + k, 1), :], (LANES, LANES))
            chosen.append(jnp.where(place == depth + tile * LANES, 1.0, 0.0).astype(jnp.bfloat16))
        chosen = jnp.concatenate(chosen, axis=1)
        chosen = jnp.concatenate([chosen, chosen], axis=0)
        return jnp.dot(column_ref[tile], chosen, preferred_element_type=jnp.float32)

    values = spread(first)
    x_ref[...] = values[:height]
    r_ref[...] = values[height:]

    def add_tile(tile, carry):
        values = spread(tile)
        x_ref[...] += values[:height]
        r_ref[...] += values[height:]
        return carry

    lax.fori_loop(first + 1, last + 1, add_tile, 0)


def part_shape(sizes, tod, hit_list, band_lag):
    det_count, time_count = tod.shape[1:]
    owners, capacity = hit_list.shape[3:]
    return (
        sizes["wafer"], sizes["det"], sizes["rep"], time_count // SBLOCK,
        owners, capacity, BLOCKS // owners, band_lag.shape[2],
    ), det_count


def fits_one_device(shape, det_count):
    wafers, dets, reps, tiles, owners, capacity, owner_rows, lag_count = shape
    devices = wafers * dets * reps
    total = devices * tiles * det_count
    groups = owner_rows // LANES
    return (
        det_count == ROWS
        and owners == ROWS
        and tiles * ROWS == LANES
        and tiles == 2 * ROWS
        and (wafers, reps) == (2, 2)
        and (1 + lag_count) * ROWS <= LANES
        and capacity <= LANES
        and devices * capacity % LANES == 0
        and owner_rows % (LANES * OUT_TILES) == 0
        and groups + 1 <= 2 * LANES
        and devices % ROWS == 0
        and dets % (DET_BATCH // ROWS) == 0
        and total * total < BIG
    )


def whole_part(shape, tod, psi, point_row, hit_list, group_id, a_zero, band_coef, band_lag):
    wafers, dets, reps, tiles, owners, capacity, owner_rows, lag_count = shape
    devices = wafers * dets * reps
    octets = reps * tiles // ROWS
    detectors = wafers * dets * ROWS
    count = devices * tiles
    total = count * ROWS
    slots = devices * capacity
    height = 3 * PBLOCK
    f32, i32 = jnp.float32, jnp.int32
    vmem, smem = pl.BlockSpec(memory_space=pltpu.VMEM), pl.BlockSpec(memory_space=pltpu.SMEM)
    anywhere = pl.BlockSpec(memory_space=pl.ANY)
    params = pltpu.CompilerParams(vmem_limit_bytes=VMEM_BYTES)
    swap = [(0, 1), (1, 0)]

    def along_det(block):
        moved = [
            lax.ppermute(block, "det", [(i, (i + shift) % dets) for i in range(dets)])
            for shift in range(1, dets)
        ]
        return [block] + moved

    def other_wafer(here):
        return lax.ppermute(here, "wafer", swap)

    def other_rep(here, across):
        return here, across, lax.ppermute(jnp.stack([here, across]), "rep", swap)

    tables, angles, samples = pl.pallas_call(
        functools.partial(pack_kernel, shape),
        out_shape=[
            jax.ShapeDtypeStruct((2, ROWS, LANES), f32),
            jax.ShapeDtypeStruct((ROWS, tiles, LANES), f32),
            jax.ShapeDtypeStruct((ROWS, tiles, LANES), f32),
        ],
        in_specs=[vmem] * 8,
        out_specs=[vmem] * 3,
        compiler_params=params,
        name="pack",
    )(
        psi[0], tod[0], point_row[0], hit_list[0, 0, 0], group_id, a_zero, band_coef[0].T,
        band_lag[0].T,
    )
    angles, samples = (stream.reshape(tiles, ROWS, LANES) for stream in (angles, samples))
    place_here = jnp.stack([lax.axis_index(axis) for axis in ("wafer", "det", "rep")]).astype(i32)
    tables = lax.all_gather(tables, ("wafer", "rep"), axis=0, tiled=False)
    riders = jnp.concatenate([angles, tables.reshape(2 * wafers * reps, ROWS, LANES)])
    samples, riders = lax.optimization_barrier((samples, riders))
    samples = jnp.stack([samples, other_wafer(samples)])
    blocks = along_det(riders)
    tables = jnp.stack([block[tiles:] for block in blocks])
    tables = tables.reshape(dets, wafers, reps, 2, ROWS, LANES)
    angles = jnp.stack([block[:tiles] for block in blocks])
    samples, angles, tables = lax.optimization_barrier((samples, angles, tables))
    angles_across = other_wafer(angles)
    samples = along_det(samples)
    table_scratch = pltpu.VMEM((devices, 2, ROWS, LANES), f32)
    table_sem = pltpu.SemaphoreType.DMA((devices,))
    twins = pl.pallas_call(
        functools.partial(twin_kernel, shape),
        out_shape=[
            jax.ShapeDtypeStruct((devices, LANES), f32),
            jax.ShapeDtypeStruct((devices, LANES), i32),
            jax.ShapeDtypeStruct((2,), i32),
            jax.ShapeDtypeStruct((total,), i32),
            jax.ShapeDtypeStruct((total,), i32),
        ],
        in_specs=[smem, anywhere],
        out_specs=[vmem] * 2 + [smem] * 3,
        scratch_shapes=[
            table_scratch,
            pltpu.VMEM((devices, LANES, LANES), f32),
            pltpu.VMEM((devices, LANES), f32),
            pltpu.VMEM((devices, LANES), f32),
            pltpu.VMEM((devices, LANES), i32),
            table_sem,
        ],
        compiler_params=params,
        cost_estimate=pl.CostEstimate(flops=10**9, bytes_accessed=3 * 10**7, transcendentals=0),
        name="twins",
    )(place_here, tables)
    place, start, moves = pl.pallas_call(
        functools.partial(place_kernel, shape),
        out_shape=[
            jax.ShapeDtypeStruct((2 * LANES, LANES), i32),
            jax.ShapeDtypeStruct((ROWS, 2 * LANES), i32),
            jax.ShapeDtypeStruct((devices, LANES), i32),
        ],
        in_specs=[smem, anywhere],
        out_specs=[vmem, vmem, vmem],
        scratch_shapes=[
            table_scratch,
            pltpu.VMEM((devices, LANES), i32),
            pltpu.VMEM((devices, LANES), i32),
            table_sem,
        ],
        compiler_params=params,
        cost_estimate=pl.CostEstimate(flops=10**9, bytes_accessed=2 * 10**7, transcendentals=0),
        name="places",
    )(place_here, tables)
    angles, angles_across, samples, twins, place, start, moves = lax.optimization_barrier(
        (angles, angles_across, samples, twins, place, start, moves)
    )
    floats, whole, size, pair, group = twins
    angle_blocks = other_rep(angles, angles_across)
    samples = jnp.stack(samples)
    sample_blocks = samples, lax.ppermute(samples, "rep", swap)
    stream = pltpu.VMEM((count, ROWS, LANES), f32)
    sky = pltpu.VMEM((devices * ROWS + 1, ROWS, LANES), f32)
    group_sums = pltpu.VMEM((NSUB, octets * ROWS, LANES), f32)
    columns = pl.pallas_call(
        functools.partial(map_kernel, shape),
        out_shape=jax.ShapeDtypeStruct((slots // LANES + 1, 2 * height, 2 * LANES), jnp.bfloat16),
        in_specs=[smem] * 7 + [anywhere] * 5,
        out_specs=vmem,
        scratch_shapes=[
            stream, stream, stream, stream,
            pltpu.VMEM((detectors, octets * ROWS, LANES), f32),
            pltpu.VMEM((detectors, octets * ROWS, LANES), f32),
            sky,
            pltpu.VMEM((wafers * NSUB, ROWS, LANES), f32),
            pltpu.VMEM((total, 2 * height), f32),
            pltpu.VMEM((slots + LANES + ROWS, 2 * height), f32),
            pltpu.SemaphoreType.DMA((devices,)),
            pltpu.SemaphoreType.DMA((devices,)),
        ] + [sky] * (3 * (3 + ITERS)) + [group_sums] * (2 * wafers * SUM_SETS),
        compiler_params=params,
        name="map_maker",
    )(
        place_here, size, pair, group, moves, floats, whole, *angle_blocks,
        *sample_blocks,
    )
    out_block = pl.BlockSpec((height, OUT_TILES * LANES), lambda n: (0, n))
    x_turned, r_turned = pl.pallas_call(
        write_kernel,
        grid=(owner_rows // (OUT_TILES * LANES),),
        out_shape=[jax.ShapeDtypeStruct((height, owner_rows), f32)] * 2,
        in_specs=[smem, vmem, vmem],
        out_specs=[out_block, out_block],
        compiler_params=params,
        name="write",
    )(start, columns, place)
    return x_turned.T, r_turned.T


def local(sizes, *arguments):
    tod, hit_list, band_lag = arguments[0], arguments[3], arguments[7]
    shape, det_count = part_shape(sizes, tod, hit_list, band_lag)
    if fits_one_device(shape, det_count):
        return whole_part(shape, *arguments)
    return distributed(*arguments)


def solution(mesh):
    placed = (
        P(("groups", "wafer"), "det", "rep"),
        P(("groups", "wafer"), "det", "rep"),
        P(("groups", "wafer"), "det", "rep"),
        P(("groups", "wafer"), "det", "rep", None, None),
        P(("groups", "wafer"), "det"),
        P(("groups", "wafer"), "det"),
        P(("groups", "wafer"), "det", None),
        P(("groups", "wafer"), "det", None),
    )
    return jax.shard_map(
        functools.partial(local, mesh.shape),
        mesh=mesh,
        in_specs=placed,
        out_specs=(P(("groups", "det", "wafer"), None), P(("groups", "det", "wafer"), None)),
        check_vma=False,
    )
```

```python
import functools

import jax
import jax.numpy as jnp
from jax import lax
from jax.experimental import pallas as pl
from jax.experimental.pallas import tpu as pltpu
from jax.sharding import PartitionSpec as P

BLOCKS = 196608
PBLOCK = 64
SBLOCK = 128
NSUB = 4
LAG = 16
ITERS = 3


prior_weight = 1.0


def with_halo(block, sides, width):
    for axis, dim in sides:
        count = lax.axis_size(axis)
        forward = [(i, i + 1) for i in range(count - 1)]
        backward = [(target, source) for source, target in forward]
        low = lax.ppermute(
            lax.slice_in_dim(block, block.shape[dim] - width, None, axis=dim), axis, forward
        )
        high = lax.ppermute(lax.slice_in_dim(block, 0, width, axis=dim), axis, backward)
        block = jnp.concatenate([low, block, high], axis=dim)
    return block


def distributed(tod, psi, point_row, hit_list, group_id, a_zero, band_coef, band_lag):
    highest = lax.Precision.HIGHEST
    samples = tod[0]
    angles = psi[0]
    det_count, time_count = samples.shape
    time_blocks = time_count // SBLOCK
    block_count = det_count * time_blocks
    send_table = hit_list[0, 0, 0]
    owner_count, capacity = send_table.shape
    owner_rows = BLOCKS // owner_count
    block_width = 3 * PBLOCK
    detector = lax.axis_index("det") * det_count + jnp.arange(det_count, dtype=jnp.int32)
    within = (jnp.arange(SBLOCK, dtype=jnp.int32)[None, :] + 3 * detector[:, None]) % PBLOCK
    pixel_table = (within[:, :, None] == jnp.arange(PBLOCK, dtype=jnp.int32)[None, None, :]).astype(
        jnp.float32
    )
    cosine_two = jnp.cos(2.0 * angles).reshape(det_count, time_blocks, SBLOCK)
    sine_two = jnp.sin(2.0 * angles).reshape(det_count, time_blocks, SBLOCK)
    slot_ids = send_table.reshape(-1)
    row_source = jnp.concatenate([point_row[0].reshape(-1), jnp.zeros((1,), jnp.int32)])
    slot_rows = row_source[slot_ids].astype(jnp.float32).reshape(owner_count, capacity)
    member = (group_id[0][:, None] == jnp.arange(NSUB, dtype=jnp.int32)[None, :]).astype(
        jnp.float32
    )
    member_count = jnp.sum(member, axis=0)
    lag_table = (
        band_lag[0][:, :, None] == jnp.arange(1, LAG + 1, dtype=jnp.int32)[None, None, :]
    ).astype(jnp.float32)
    lag_weight = jnp.einsum("dj,djl->dl", band_coef[0], lag_table, precision=highest)
    base_weight = a_zero[0]

    def slot_payload(by_block):
        width = by_block.shape[1]
        extended = jnp.concatenate([by_block, jnp.zeros((1, width), by_block.dtype)])
        return extended[slot_ids].reshape(owner_count, capacity, width)

    def deliver(payload):
        width = payload.shape[-1]
        got_values, got_rows = (
            lax.all_to_all(payload, ("det", "wafer"), split_axis=0, concat_axis=0, tiled=True),
            lax.all_to_all(slot_rows, ("det", "wafer"), split_axis=0, concat_axis=0, tiled=True),
        )
        return (got_values, got_rows)

    def back_project(stream, squared):
        shaped = stream.reshape(det_count, time_blocks, SBLOCK)
        first = cosine_two * cosine_two if squared else cosine_two
        second = sine_two * sine_two if squared else sine_two
        stacked = jnp.stack([shaped, first * shaped, second * shaped], axis=2)
        stokes = jnp.einsum("dkcs,dsp->dkcp", stacked, pixel_table, precision=highest)
        return stokes.reshape(block_count, block_width)

    def to_owners(stream, squared):
        got_values, got_rows = deliver(slot_payload(back_project(stream, squared)))
        pair_values, pair_rows = (
            lax.all_gather(got_values, "rep", axis=0, tiled=True),
            lax.all_gather(got_rows, "rep", axis=0, tiled=True),
        )
        target_rows = pair_rows.reshape(-1).astype(jnp.int32)
        summed = (
            jnp.zeros((owner_rows, block_width), jnp.float32)
            .at[target_rows]
            .add(pair_values.reshape(-1, block_width))
        )
        return (summed, got_rows.astype(jnp.int32))

    def remove_common(stream):
        local_sums = jnp.einsum("dg,dt->gt", member, stream, precision=highest)
        group_sums, group_counts = lax.psum((local_sums, member_count), "det")
        group_means = group_sums / jnp.maximum(group_counts, 1.0)[:, None]
        return stream - jnp.einsum("dg,gt->dt", member, group_means, precision=highest)

    def band_filter(stream):
        padded = with_halo(stream, (("rep", 1),), LAG)
        result = base_weight[:, None] * stream
        for offset in range(1, LAG + 1):
            later = padded[:, LAG + offset : LAG + offset + time_count]
            earlier = padded[:, LAG - offset : LAG - offset + time_count]
            result = result + lag_weight[:, offset - 1 : offset] * (later + earlier)
        return result

    def weigh_stream(stream):
        return remove_common(band_filter(remove_common(stream)))

    weight_stream = jnp.broadcast_to(base_weight[:, None], (det_count, time_count))
    diag_sum, serve_rows = to_owners(weight_stream, True)
    inverse_diag = 1.0 / (diag_sum + prior_weight)
    right_side = to_owners(weigh_stream(samples), False)[0]
    solution = jnp.zeros_like(right_side)
    residual = right_side

    def inner(left_map, right_map):
        return lax.psum(jnp.sum(left_map * right_map), ("det", "wafer"))

    precond = inverse_diag * residual
    direction = precond
    energy = inner(residual, precond)
    for iteration in range(ITERS):
        from_blocks = direction[serve_rows.reshape(-1)].reshape(owner_count, capacity, block_width)
        return_width = from_blocks.shape[-1]
        returned = lax.all_to_all(
            from_blocks, ("det", "wafer"), split_axis=0, concat_axis=0, tiled=True
        )
        return_placed = jnp.zeros((block_count + 1, return_width), jnp.float32)
        return_placed = return_placed.at[slot_ids].set(returned.reshape(-1, return_width))
        blocks = return_placed[:block_count].reshape(det_count, time_blocks, 3, PBLOCK)
        project_stokes = jnp.einsum("dkcp,dsp->dkcs", blocks, pixel_table, precision=highest)
        project_stream = (
            project_stokes[:, :, 0]
            + cosine_two * project_stokes[:, :, 1]
            + sine_two * project_stokes[:, :, 2]
        )
        seen_stream = project_stream.reshape(det_count, time_count)
        image_map = to_owners(weigh_stream(seen_stream), False)[0] + prior_weight * direction
        step_size = energy / inner(direction, image_map)
        solution = solution + step_size * direction
        residual = residual - step_size * image_map
        precond = inverse_diag * residual
        energy_next = inner(residual, precond)
        direction = precond + energy_next / energy * direction
        energy = energy_next
    return (solution, residual)


LANES = 128
ROWS = 8
OUT_TILES = 8
PAIR_BATCH = 8
WRITES = 6
DET_BATCH = 8
SUM_SETS = 2
MAP_BATCH = 8
BIG = float(1 << 24)
VMEM_BYTES = 60 << 20


def wide(values):
    return jnp.broadcast_to(values, (ROWS, LANES))


def tile_iotas():
    lane = lax.broadcasted_iota(jnp.int32, (ROWS, LANES), 1)
    sub = lax.broadcasted_iota(jnp.int32, (ROWS, LANES), 0)
    return lane, sub


def cosine_sine_double(angle):
    turns = jnp.floor(angle * 1.2732395447351628 + 0.5)
    reduced = 2.0 * angle - turns * 1.5703125
    reduced = reduced - turns * 4.837512969970703125e-4
    reduced = reduced - turns * 7.54978995489188216e-8
    square = reduced * reduced
    sine = (-1.9515295891e-4 * square + 8.3321608736e-3) * square - 1.6666654611e-1
    sine = sine * square * reduced + reduced
    cosine = (2.443315711809948e-5 * square - 1.388731625493765e-3) * square
    cosine = (cosine + 4.166664568298827e-2) * square * square - 0.5 * square + 1.0
    quarter = turns.astype(jnp.int32)
    odd = (quarter & 1) == 1
    first = jnp.where(odd, sine, cosine)
    second = jnp.where(odd, cosine, sine)
    first = jnp.where(((quarter + 1) & 2) == 2, -first, first)
    second = jnp.where((quarter & 2) == 2, -second, second)
    return first, second


def pack_kernel(
    shape, angle_ref, tod_ref, row_ref, hit_ref, group_ref, base_ref, coef_ref, lag_ref,
    table_ref, angle_rows_ref, tod_rows_ref,
):
    wafers, dets, reps, tiles, owners, capacity, owner_rows, lag_count = shape
    lane, sub = tile_iotas()
    lists = hit_ref[...]
    owner_hits = jnp.zeros((ROWS, LANES), jnp.float32)
    for c in range(capacity):
        owner_hits = owner_hits + jnp.where(wide(lists[:, c : c + 1]) == lane, 1.0, 0.0)
    owner_of = jnp.sum(owner_hits * sub.astype(jnp.float32), axis=0, keepdims=True)

    def spread(values, width):
        return jnp.concatenate(
            [values, jnp.zeros((values.shape[0], LANES - width), values.dtype)], axis=1
        )

    rows = spread(row_ref[...].astype(jnp.float32), tiles)
    ids = owner_of * float(owner_rows) + rows[0:1]
    for k in range(1, ROWS):
        ids = ids + pltpu.roll(rows[k : k + 1], k * tiles, 1)
    floats = spread(base_ref[...], ROWS)
    whole = spread(group_ref[...].astype(jnp.float32), ROWS)
    for j in range(lag_count):
        at = (j + 1) * ROWS
        floats = floats + pltpu.roll(spread(coef_ref[j : j + 1, :], ROWS), at, 1)
        lag = lag_ref[j : j + 1, :].astype(jnp.float32)
        whole = whole + pltpu.roll(spread(lag, ROWS), at, 1)
    table = jnp.where(sub == 0, wide(ids), jnp.where(sub == 1, wide(floats), wide(whole)))
    table_ref[0] = table
    table_ref[1] = spread(lists.astype(jnp.float32), capacity)
    for b in range(tiles):
        angle_rows_ref[:, b, :] = angle_ref[:, b * LANES : (b + 1) * LANES]
        tod_rows_ref[:, b, :] = tod_ref[:, b * LANES : (b + 1) * LANES]


def part_copies(shape, self_ref, source, target, sem):
    wafers, dets, reps = shape[:3]
    copies = []
    for swap_rep in range(reps):
        for swap_wafer in range(wafers):
            for shift in range(dets):
                det = self_ref[1] - shift
                det = jnp.where(det < 0, det + dets, det)
                device = ((self_ref[0] ^ swap_wafer) * dets + det) * reps
                device = device + (self_ref[2] ^ swap_rep)
                copies.append(
                    pltpu.make_async_copy(
                        source(swap_rep, swap_wafer, shift), target(device), sem.at[len(copies)]
                    )
                )
    return copies


def table_copies(shape, self_ref, source_ref, part_ref, sem):
    wafers, dets, reps = shape[:3]
    copies = []
    for swap_wafer in range(wafers):
        for shift in range(dets):
            det = self_ref[1] - shift
            det = jnp.where(det < 0, det + dets, det)
            device = ((self_ref[0] ^ swap_wafer) * dets + det) * reps
            copies.append(
                pltpu.make_async_copy(
                    source_ref.at[swap_wafer, shift], part_ref.at[pl.ds(device, reps)],
                    sem.at[len(copies)],
                )
            )
    for copy in copies:
        copy.start()
    for copy in copies:
        copy.wait()


def exact_dot(left, right, dims=((1,), (0,))):
    return lax.dot_general(
        left.astype(jnp.bfloat16), right.astype(jnp.bfloat16), (dims, ((), ())),
        preferred_element_type=jnp.float32,
    )


def list_kernel(
    shape, wafer_ref, det_ref, table_ref, float_ref, whole_ref, place_ref, start_ref, move_ref,
    size_ref, pair_ref, group_ref,
    part_ref, column_ref, code_ref, lead_ref, used_ref, rank_ref, hits_ref, part_sem,
):
    self_ref = wafer_ref[0], det_ref[0]
    table_copies(shape, self_ref, table_ref, part_ref, part_sem)
    list_twins(
        shape, float_ref, whole_ref, size_ref, pair_ref, group_ref, part_ref, column_ref, code_ref,
        lead_ref, used_ref,
    )
    list_places(shape, self_ref, place_ref, start_ref, move_ref, part_ref, rank_ref, hits_ref)


def list_twins(
    shape, float_ref, whole_ref, size_ref, pair_ref, group_ref, part_ref, column_ref, code_ref,
    lead_ref, used_ref,
):
    wafers, dets, reps, tiles, owners, capacity, owner_rows, lag_count = shape
    devices = wafers * dets * reps
    total = devices * LANES
    lane, sub = tile_iotas()
    sub_f = sub.astype(jnp.float32)
    none = jnp.full((ROWS, LANES), BIG, jnp.float32)
    along = lax.broadcasted_iota(jnp.int32, (1, LANES), 1).astype(jnp.float32)

    def turn(batch, carry):
        for k in range(4):
            device = 4 * batch + k
            float_ref[pl.ds(device, 1), :] = part_ref[device, 0, 1:2, :]
            whole_ref[pl.ds(device, 1), :] = part_ref[device, 0, 2:3, :].astype(jnp.int32)
            column_ref[device] = jnp.broadcast_to(part_ref[device, 0, 0:1, :], (LANES, LANES)).T
        return carry

    lax.fori_loop(0, devices // 4, turn, 0)

    def survey(device, carry):
        row = wide(part_ref[device, 0, 0:1, :])

        def compare(step, least):
            for k in range(2):
                other = 2 * step + k
                found = [none] * 4
                for j in range(tiles):
                    same = column_ref[other, j * ROWS : (j + 1) * ROWS, :] == row
                    at = jnp.where(same, sub_f + float(j * ROWS), BIG)
                    found[j % 4] = jnp.minimum(found[j % 4], at)
                here = jnp.minimum(jnp.minimum(found[0], found[1]), jnp.minimum(found[2], found[3]))
                least = jnp.minimum(least, here + (other * LANES).astype(jnp.float32))
            return least

        least = lax.fori_loop(0, lax.shift_right_logical(device, 1) + 1, compare, none)
        lead = jnp.min(least, axis=0, keepdims=True)
        mine = (device * LANES).astype(jnp.float32) + along
        later = lead < mine
        code_ref[pl.ds(device, 1), :] = jnp.where(later, mine * float(total) + lead, BIG)
        lead_ref[pl.ds(device, 1), :] = jnp.where(later, lead, BIG)
        return carry

    lax.fori_loop(0, devices, survey, 0)

    def next_code(last):
        found = none
        for tile in range(devices // ROWS):
            codes = code_ref[tile * ROWS : (tile + 1) * ROWS, :]
            found = jnp.minimum(found, jnp.where(codes > last, codes, BIG))
        return jnp.min(found)

    def detector(key):
        team = lax.rem(lax.div(key, reps * LANES), dets)
        return team * ROWS + lax.rem(lax.div(key, tiles), ROWS)

    number_of = [lane + (sub + tile * ROWS) * LANES for tile in range(devices // ROWS)]
    tile_rows = [slice(tile * ROWS, (tile + 1) * ROWS) for tile in range(devices // ROWS)]
    for rows in tile_rows:
        used_ref[rows, :] = jnp.zeros((ROWS, LANES), jnp.int32)

    def take(state):
        pairs, grouped, code = state
        number = code.astype(jnp.int32)
        key = lax.div(number, total)
        lead = lax.rem(number, total)
        shift = (3 * (detector(key) - detector(lead))) & (PBLOCK - 1)
        wanted = lead.astype(jnp.float32)
        same = jnp.zeros((ROWS, LANES), jnp.float32)
        for rows, numbers in zip(tile_rows, number_of):
            same = same + jnp.where(lead_ref[rows, :] == wanted, 1.0, 0.0)
            beside = numbers ^ ROWS
            beside = (beside == key) | (beside == lead)
            same = same + jnp.where(beside & (used_ref[rows, :] > 0), 2.0, 0.0)
        alone = jnp.sum(same) + jnp.where((key ^ lead) == ROWS, 2.0, 0.0) < 1.5
        mark = jnp.where(alone, 1, 0)
        for rows, numbers in zip(tile_rows, number_of):
            listed = (numbers == key) | (numbers == lead)
            used_ref[rows, :] = jnp.where(listed, mark, used_ref[rows, :])
        entry = twin_entry(key, lead, shift)
        pair_ref[pairs] = entry
        group_ref[grouped] = entry
        return (
            pairs + jnp.where(alone, 1, 0), grouped + jnp.where(alone, 0, 1), next_code(code)
        )

    pairs, grouped, _ = lax.while_loop(
        lambda state: state[2] < BIG, take,
        (jnp.int32(0), jnp.int32(0), next_code(jnp.float32(-1.0))),
    )
    batches = lax.div(pairs + PAIR_BATCH - 1, PAIR_BATCH)

    def fill(n, carry):
        pair_ref[n] = twin_entry(total, total + 1, 0)
        return carry

    lax.fori_loop(pairs, batches * PAIR_BATCH, fill, 0)
    size_ref[0] = batches
    size_ref[1] = grouped


def twin_entry(key, lead, shift):
    return key * (1 << 19) + lead * (1 << 6) + shift


def twin_of(entry):
    return entry >> 19, (entry >> 6) & ((1 << 13) - 1), entry & (PBLOCK - 1)


def list_places(shape, self_ref, place_ref, start_ref, move_ref, part_ref, rank_ref, hits_ref):
    wafers, dets, reps, tiles, owners, capacity, owner_rows, lag_count = shape
    devices = wafers * dets * reps
    slots = devices * capacity
    lane, sub = tile_iotas()
    own = self_ref[1] * wafers + self_ref[0]
    first_row = (own * owner_rows).astype(jnp.float32)
    depth = 2 * LANES
    tall = lax.broadcasted_iota(jnp.int32, (depth, LANES), 0).astype(jnp.float32)

    def one_hots(device):
        local_row = part_ref[device, 0, 0:1, :] - first_row
        high = jnp.floor(local_row * (1.0 / LANES))
        low = local_row - high * LANES
        high = (jnp.broadcast_to(high, (depth, LANES)) == tall).astype(jnp.float32)
        low = (jnp.broadcast_to(low, (LANES, LANES)) == tall[0:LANES]).astype(jnp.float32)
        return high, low

    def survey(batch, hits):
        for k in range(4):
            device = 4 * batch + k
            own_hits = jnp.where(sub == own, part_ref[device, 1], 0.0)
            own_hits = jnp.sum(own_hits, axis=0, keepdims=True)
            hits_ref[pl.ds(device, 1), :] = own_hits.astype(jnp.int32)
            high, low = one_hots(device)
            hits = hits + exact_dot(high, low, ((1,), (1,)))
        return hits

    hits = lax.fori_loop(0, devices // 4, survey, jnp.zeros((depth, LANES), jnp.float32))
    full = jnp.minimum(hits, 1.0)

    def ordered(size, axis):
        first = lax.broadcasted_iota(jnp.int32, (size, size), axis)
        second = lax.broadcasted_iota(jnp.int32, (size, size), 1 - axis)
        return (first < second).astype(jnp.float32)

    counts = exact_dot(jnp.ones((ROWS, LANES), jnp.float32), full, ((1,), (1,)))
    start_ref[...] = exact_dot(counts, ordered(depth, 0)).astype(jnp.int32)
    sums = exact_dot(full, jnp.ones((LANES, LANES), jnp.float32))
    place = exact_dot(full, ordered(LANES, 0)) + exact_dot(ordered(depth, 1), sums)
    place_ref[...] = jnp.where(full > 0.0, place, -1.0).astype(jnp.int32)
    place_high = jnp.floor(place * (1.0 / LANES))
    place_parts = jnp.concatenate([place_high, place - place_high * LANES], axis=0)

    def rank_of(batch, carry):
        for k in range(4):
            device = 4 * batch + k
            high, low = one_hots(device)
            parts = exact_dot(place_parts, low)
            rank = high * (parts[0:depth] * LANES + parts[depth : 2 * depth])
            rank = jnp.sum(rank, axis=0, keepdims=True)
            rank_ref[pl.ds(device, 1), :] = rank.astype(jnp.int32)
        return carry

    lax.fori_loop(0, devices // 4, rank_of, 0)
    for tile in range(devices // ROWS):
        rows = slice(tile * ROWS, (tile + 1) * ROWS)
        number = hits_ref[rows, :]
        valid = number < LANES
        number = number & (LANES - 1)
        rank = jnp.take_along_axis(rank_ref[rows, :], number, axis=1, mode="promise_in_bounds")
        target = jnp.where(valid, rank, slots + LANES)
        move_ref[rows, :] = target * (1 << 16) + (tile * ROWS + sub) * LANES + number


def map_kernel(
    shape, wafer_ref, det_ref, rep_ref, size_ref, pair_ref, group_ref, move_ref, float_smem, whole_smem,
    angle_here_ref, angle_across_ref, angle_other_ref, tod_here_ref, tod_other_ref, column_ref,
    angle_ref, tod_ref, cos_ref, sin_ref, clean_ref, noise_ref, weight_ref,
    share_ref, rows_ref, sorted_ref, angle_sem, tod_sem, *more_refs,
):
    wafers, dets, reps, tiles, owners, capacity, owner_rows, lag_count = shape
    devices = wafers * dets * reps
    octets = 2 * reps
    wafer_dets = dets * ROWS
    self_ref = wafer_ref[0], det_ref[0], rep_ref[0]
    count = devices * ROWS
    lane, sub = tile_iotas()
    zero = jnp.zeros((ROWS, LANES), jnp.float32)
    low = lane < PBLOCK
    skies = [more_refs[3 * k : 3 * k + 3] for k in range(3 + ITERS)]
    inverse_ref, r_map, image_map, *d_maps = skies
    sum_refs = more_refs[3 * len(skies) :]
    first_sums = [sum_refs[SUM_SETS * wafer : SUM_SETS * (wafer + 1)] for wafer in range(wafers)]
    sum_refs = sum_refs[SUM_SETS * wafers :]
    second_sums = [sum_refs[SUM_SETS * wafer : SUM_SETS * (wafer + 1)] for wafer in range(wafers)]

    def copies_of(source, to_ref, sem):
        return part_copies(
            shape, self_ref, source, lambda d: to_ref.at[pl.ds(d * tiles, tiles)], sem
        )

    def angle_source(swap_rep, swap_wafer, shift):
        if swap_rep:
            return angle_other_ref.at[swap_wafer, shift]
        return (angle_across_ref if swap_wafer else angle_here_ref).at[shift]

    def tod_source(swap_rep, swap_wafer, shift):
        return (tod_other_ref if swap_rep else tod_here_ref).at[shift, swap_wafer]

    angle_moves = copies_of(angle_source, angle_ref, angle_sem)
    tod_moves = copies_of(tod_source, tod_ref, tod_sem)
    for copy in angle_moves + tod_moves:
        copy.start()

    def turn_half(block):
        return pltpu.roll(block, PBLOCK, 1)

    def fold(first, second):
        return jnp.where(low, first, second) + turn_half(jnp.where(low, second, first))

    def unfold(block):
        turned = turn_half(block)
        return jnp.where(low, block, turned), jnp.where(low, turned, block)

    def whole_sum(values):
        values = jnp.sum(values, axis=0, keepdims=True)
        return wide(jnp.sum(values, axis=1, keepdims=True))

    def loop(times, body, carry, unroll):
        def several(n, carry):
            for k in range(unroll):
                carry = body(n * unroll + k, carry)
            return carry

        return lax.fori_loop(0, times // unroll, several, carry)

    def device_of(wafer, n):
        return (wafer * dets + lax.shift_right_logical(n, 3)) * reps

    def group_of(wafer, n):
        return whole_smem[device_of(wafer, n), n & (ROWS - 1)]

    def rows_of(octet):
        return pl.ds(octet * ROWS, ROWS)

    def count_members(n, counts):
        result = []
        for wafer in range(wafers):
            group = group_of(wafer, n)
            result += [
                counts[wafer * NSUB + g] + jnp.where(group == g, 1, 0) for g in range(NSUB)
            ]
        return tuple(result)

    members = lax.fori_loop(0, wafer_dets, count_members, (jnp.int32(0),) * (wafers * NSUB))
    for k, member in enumerate(members):
        share_ref[k] = 1.0 / jnp.maximum(zero + member.astype(jnp.float32), 1.0)
    for c in range(3):
        image_map[c][count] = zero
        r_map[c][count] = zero

    def clear_sorted(n, carry):
        at = pl.ds(pl.multiple_of(n * ROWS, ROWS), ROWS)
        sorted_ref[at, :] = jnp.zeros((ROWS, 6 * PBLOCK), jnp.float32)
        return carry

    lax.fori_loop(0, sorted_ref.shape[0] // ROWS, clear_sorted, 0)

    def spot_of(key):
        return lax.shift_right_logical(key, 4), (key >> 3) & 1, pl.ds(key & (ROWS - 1), 1)

    def in_half(half):
        return (lane[0:1] >> 6) == half

    def set_weight(at, carry):
        weight_ref[at] = zero + 1.0
        return carry

    loop(count, set_weight, 0, 16)

    def drop(list_ref):
        def one(n, carry):
            at, half, row = spot_of(twin_of(list_ref[n])[0])
            weight_ref[at, row, :] = jnp.where(in_half(half), 0.0, weight_ref[at, row, :])
            return carry

        return one

    lax.fori_loop(0, size_ref[0] * PAIR_BATCH, drop(pair_ref), 0)
    lax.fori_loop(0, size_ref[1], drop(group_ref), 0)

    def moved_from(target, spot, shift):
        at, half, row = spot
        result = []
        for ref in target:
            values = wide(ref[at, row, :])
            values = jnp.where((lane >> 6) == half, values, turn_half(values))
            result.append(pltpu.roll(values, shift, 1)[0:1])
        return result

    def merge_twins(target):
        def pair_batch(n, carry):
            found = []
            for k in range(PAIR_BATCH):
                key, lead, shift = twin_of(pair_ref[n * PAIR_BATCH + k])
                key, lead = spot_of(key), spot_of(lead)
                back = (PBLOCK - shift) & (PBLOCK - 1)
                for spot, values in (
                    (lead, moved_from(target, key, shift)), (key, moved_from(target, lead, back))
                ):
                    at, half, row = spot
                    for c in range(3):
                        values[c] = target[c][at, row, :] + jnp.where(in_half(half), values[c], 0.0)
                    found.append((at, row, values))
            for at, row, values in found:
                for c in range(3):
                    target[c][at, row, :] = values[c]
            return carry

        def gather_one(n, carry):
            key, lead, shift = twin_of(group_ref[n])
            values = moved_from(target, spot_of(key), shift)
            at, half, row = spot_of(lead)
            for c in range(3):
                target[c][at, row, :] += jnp.where(in_half(half), values[c], 0.0)
            return carry

        def spread_one(n, carry):
            key, lead, shift = twin_of(group_ref[n])
            values = moved_from(target, spot_of(lead), (PBLOCK - shift) & (PBLOCK - 1))
            at, half, row = spot_of(key)
            for c in range(3):
                target[c][at, row, :] = jnp.where(in_half(half), values[c], target[c][at, row, :])
            return carry

        lax.fori_loop(0, size_ref[0], pair_batch, 0)
        lax.fori_loop(0, size_ref[1], gather_one, 0)
        lax.fori_loop(0, size_ref[1], spread_one, 0)

    for copy in angle_moves:
        copy.wait()

    def survey(at, carry):
        base = float_smem[lax.shift_right_logical(at, 3), at & (ROWS - 1)]
        squares = []
        for half in range(2):
            first, second = cosine_sine_double(angle_ref[2 * at + half])
            cos_ref[2 * at + half] = first
            sin_ref[2 * at + half] = second
            squares.append((base * (first * first), base * (second * second)))
        image_map[0][at] = zero + (base + base)
        for c in range(2):
            image_map[c + 1][at] = fold(squares[0][c], squares[1][c])
        return carry

    loop(count, survey, 0, 8)

    def clear_sums(refs):
        for sets in refs:
            for ref in sets:
                for group in range(NSUB):
                    for octet in range(octets):
                        ref[group, rows_of(octet), :] = zero

    def average(refs):
        for wafer, sets in enumerate(refs):
            for group in range(NSUB):
                for octet in range(octets):
                    total = sets[0][group, rows_of(octet), :]
                    for ref in sets[1:]:
                        total = total + ref[group, rows_of(octet), :]
                    sets[0][group, rows_of(octet), :] = total * share_ref[wafer * NSUB + group]

    def over_detectors(body, carry):
        def several(step, carry):
            for k in range(DET_BATCH):
                carry = body(step * DET_BATCH + k, k % SUM_SETS, carry)
            return carry

        return lax.fori_loop(0, wafer_dets // DET_BATCH, several, carry)

    def sum_streams(streams_of, carry):
        clear_sums(first_sums)

        def one_detector(n, part, carry):
            for wafer in range(wafers):
                group = group_of(wafer, n)
                for rep in range(reps):
                    at = (device_of(wafer, n) + rep) * ROWS + (n & (ROWS - 1))
                    streams, carry = streams_of(at, carry)
                    for half, stream in enumerate(streams):
                        rows = rows_of(2 * rep + half)
                        clean_ref[wafer * wafer_dets + n, rows, :] = stream
                        first_sums[wafer][part][group, rows, :] += stream
            return carry

        carry = over_detectors(one_detector, carry)
        average(first_sums)
        return carry

    def filter_streams():
        clear_sums(second_sums)

        def one_filter(n, part, carry):
            for wafer in range(wafers):
                device, inside = device_of(wafer, n), n & (ROWS - 1)
                detector = wafer * wafer_dets + n
                group = group_of(wafer, n)
                base = float_smem[device, inside]
                coefs = [float_smem[device, (j + 1) * ROWS + inside] for j in range(lag_count)]
                lags = [whole_smem[device, (j + 1) * ROWS + inside] for j in range(lag_count)]
                clean = [
                    clean_ref[detector, rows_of(octet), :]
                    - first_sums[wafer][0][group, rows_of(octet), :]
                    for octet in range(octets)
                ]
                up = [pltpu.roll(here, ROWS - 1, 0) for here in clean] + [zero]
                down = [zero] + [pltpu.roll(here, 1, 0) for here in clean]
                for octet, here in enumerate(clean):
                    after = jnp.where(sub == ROWS - 1, up[octet + 1], up[octet])
                    ahead = jnp.where(sub == 0, down[octet], down[octet + 1])
                    result = base * here
                    for coef, lag in zip(coefs, lags):
                        later = pltpu.roll(jnp.where(lane < lag, after, here), LANES - lag, 1)
                        earlier = pltpu.roll(jnp.where(lane >= LANES - lag, ahead, here), lag, 1)
                        result = result + coef * (later + earlier)
                    noise_ref[detector, rows_of(octet), :] = result
                    second_sums[wafer][part][group, rows_of(octet), :] += result
                    carry = carry + here * result
            return carry

        product = over_detectors(one_filter, zero)
        average(second_sums)
        return product

    def return_streams(target):
        def one_return(n, part, carry):
            for wafer in range(wafers):
                group = group_of(wafer, n)
                for rep in range(reps):
                    at = (device_of(wafer, n) + rep) * ROWS + (n & (ROWS - 1))
                    streams = []
                    for half in range(2):
                        rows = rows_of(2 * rep + half)
                        stream = noise_ref[wafer * wafer_dets + n, rows, :]
                        streams.append(stream - second_sums[wafer][0][group, rows, :])
                    target[0][at] = fold(*streams)
                    for c, ref in ((1, cos_ref), (2, sin_ref)):
                        target[c][at] = fold(*(ref[2 * at + h] * streams[h] for h in range(2)))
            return carry

        over_detectors(one_return, 0)
        merge_twins(target)

    merge_twins(image_map)
    for copy in tod_moves:
        copy.wait()
    sum_streams(lambda at, carry: ([tod_ref[2 * at + half] for half in range(2)], carry), 0)
    filter_streams()
    return_streams(r_map)

    def begin(at, carry):
        parts = zero
        for c in range(3):
            inverse = 1.0 / (image_map[c][at] + prior_weight)
            inverse_ref[c][at] = inverse
            residual = r_map[c][at]
            parts = parts + residual * (inverse * residual)
        return carry + weight_ref[at] * parts

    energy = whole_sum(loop(count, begin, zero, 16))
    factor = zero
    steps = []
    for iteration, d_map in enumerate(d_maps):
        last = iteration == ITERS - 1

        def seen_streams(at, carry):
            squares = zero
            streams = [None, None]
            for c in range(3):
                part = inverse_ref[c][at] * r_map[c][at]
                if iteration:
                    part = part + factor * d_maps[iteration - 1][c][at]
                d_map[c][at] = part
                squares = squares + part * part
                for half, seen in enumerate(unfold(part)):
                    if c == 0:
                        streams[half] = seen
                    else:
                        ref = cos_ref if c == 1 else sin_ref
                        streams[half] = streams[half] + ref[2 * at + half] * seen
            return streams, carry + weight_ref[at] * squares

        prior = sum_streams(seen_streams, zero)
        product = filter_streams()
        return_streams(image_map)
        step = energy / whole_sum(product + prior_weight * prior)
        steps.append(step)

        def new_residual(at, c):
            return r_map[c][at] - step * (image_map[c][at] + prior_weight * d_map[c][at])

        if not last:

            def update(batch, carry):
                found = []
                for k in range(MAP_BATCH):
                    at = batch * MAP_BATCH + k
                    residual = [new_residual(at, c) for c in range(3)]
                    parts = zero
                    for c in range(3):
                        parts = parts + residual[c] * (inverse_ref[c][at] * residual[c])
                    carry = carry + weight_ref[at] * parts
                    found.append((at, residual))
                for at, residual in found:
                    for c in range(3):
                        r_map[c][at] = residual[c]
                return carry

            next_energy = whole_sum(loop(count // MAP_BATCH, update, zero, 2))
            factor = next_energy / energy
            energy = next_energy
        else:

            def place_pixels(at, carry):
                team = lax.rem(lax.div(at, reps * ROWS), dets)
                turn = (3 * (team * ROWS + (at & (ROWS - 1)))) & (PBLOCK - 1)
                inside = (lane & (PBLOCK - 1)) >= turn
                values = []
                for c in range(3):
                    value = steps[0] * d_maps[0][c][at]
                    for k in range(1, ITERS):
                        value = value + steps[k] * d_maps[k][c][at]
                    values.append(value)
                values += [new_residual(at, c) for c in range(3)]
                for c in range(3):
                    left, right = values[2 * c], values[2 * c + 1]
                    halves = (
                        jnp.where(low, left, turn_half(right)), jnp.where(low, turn_half(left), right)
                    )
                    for half, value in enumerate(halves):
                        value = jnp.where(
                            inside, pltpu.roll(value, turn, 1), pltpu.roll(value, turn + PBLOCK, 1)
                        )
                        rows = pl.ds(pl.multiple_of((2 * at + half) * ROWS, ROWS), ROWS)
                        rows_ref[rows, c * LANES : (c + 1) * LANES] = value
                return carry

            loop(count, place_pixels, 0, 8)

    def pick(device, carry):
        for c in range(capacity):
            move = move_ref[device, c]
            source, target = move & ((1 << 16) - 1), move >> 16
            sorted_ref[pl.ds(target, 1), :] = rows_ref[pl.ds(source, 1), :]
        return carry

    lax.fori_loop(0, devices, pick, 0)

    def turn_tile(tile, carry):
        columns = sorted_ref[pl.ds(pl.multiple_of(tile * LANES, LANES), LANES), :].T
        high = columns.astype(jnp.bfloat16)
        column_ref[tile, :, 0:LANES] = high
        column_ref[tile, :, LANES : 2 * LANES] = (columns - high.astype(jnp.float32)).astype(
            jnp.bfloat16
        )
        return carry

    lax.fori_loop(0, column_ref.shape[0], turn_tile, 0)


def write_kernel(start_ref, column_ref, place_ref, x_ref, r_ref, x_buffer, r_buffer, x_sem, r_sem):
    height = 3 * PBLOCK
    width = OUT_TILES * LANES
    steps = x_ref.shape[1] // width
    depth = lax.broadcasted_iota(jnp.int32, (LANES, LANES), 0)

    def copies(step, slot):
        to = pl.ds(pl.multiple_of(step * width, width), width)
        return (
            pltpu.make_async_copy(x_buffer.at[slot], x_ref.at[:, to], x_sem.at[slot]),
            pltpu.make_async_copy(r_buffer.at[slot], r_ref.at[:, to], r_sem.at[slot]),
        )

    def spread(group, tile):
        chosen = []
        for k in range(OUT_TILES):
            place = jnp.broadcast_to(place_ref[pl.ds(group + k, 1), :], (LANES, LANES))
            chosen.append(jnp.where(place == depth + tile * LANES, 1.0, 0.0).astype(jnp.bfloat16))
        chosen = jnp.concatenate(chosen, axis=1)
        chosen = jnp.concatenate([chosen, chosen], axis=0)
        return jnp.dot(column_ref[tile], chosen, preferred_element_type=jnp.float32)

    def one_step(step, carry):
        slot = lax.rem(step, WRITES)

        @pl.when(step >= WRITES)
        def _():
            for copy in copies(step - WRITES, slot):
                copy.wait()

        group = step * OUT_TILES
        start, end = start_ref[0, group], start_ref[0, group + OUT_TILES]
        first = lax.shift_right_logical(start, 7)
        last = lax.shift_right_logical(jnp.maximum(end - 1, start), 7)
        values = spread(group, first)
        x_buffer[slot] = values[:height]
        r_buffer[slot] = values[height:]

        def add_tile(tile, carry):
            values = spread(group, tile)
            x_buffer[slot] += values[:height]
            r_buffer[slot] += values[height:]
            return carry

        lax.fori_loop(first + 1, last + 1, add_tile, 0)
        for copy in copies(step, slot):
            copy.start()
        return carry

    lax.fori_loop(0, steps, one_step, 0)
    for step in range(steps - WRITES, steps):
        for copy in copies(step, step % WRITES):
            copy.wait()


def part_shape(sizes, tod, hit_list, band_lag):
    det_count, time_count = tod.shape[1:]
    owners, capacity = hit_list.shape[3:]
    return (
        sizes["wafer"], sizes["det"], sizes["rep"], time_count // SBLOCK,
        owners, capacity, BLOCKS // owners, band_lag.shape[2],
    ), det_count


def fits_one_device(shape, det_count):
    wafers, dets, reps, tiles, owners, capacity, owner_rows, lag_count = shape
    devices = wafers * dets * reps
    total = devices * tiles * det_count
    groups = owner_rows // LANES
    return (
        det_count == ROWS
        and owners == ROWS
        and tiles * ROWS == LANES
        and tiles == 2 * ROWS
        and (wafers, reps) == (2, 2)
        and (1 + lag_count) * ROWS <= LANES
        and capacity <= LANES
        and devices * capacity % LANES == 0
        and owner_rows % (LANES * OUT_TILES) == 0
        and owner_rows >= LANES * OUT_TILES * WRITES
        and groups + 1 <= 2 * LANES
        and devices % ROWS == 0
        and dets % (DET_BATCH // ROWS) == 0
        and total * total < BIG
    )


def whole_part(shape, tod, psi, point_row, hit_list, group_id, a_zero, band_coef, band_lag):
    wafers, dets, reps, tiles, owners, capacity, owner_rows, lag_count = shape
    devices = wafers * dets * reps
    octets = reps * tiles // ROWS
    detectors = wafers * dets * ROWS
    count = devices * tiles
    total = count * ROWS
    slots = devices * capacity
    height = 3 * PBLOCK
    f32, i32 = jnp.float32, jnp.int32
    vmem, smem = pl.BlockSpec(memory_space=pltpu.VMEM), pl.BlockSpec(memory_space=pltpu.SMEM)
    anywhere = pl.BlockSpec(memory_space=pl.ANY)
    params = pltpu.CompilerParams(vmem_limit_bytes=VMEM_BYTES)
    swap = [(0, 1), (1, 0)]

    def along_det(block):
        moved = [
            lax.ppermute(block, "det", [(i, (i + shift) % dets) for i in range(dets)])
            for shift in range(1, dets)
        ]
        return [block] + moved

    def other_wafer(here):
        return lax.ppermute(here, "wafer", swap)

    def other_rep(here, across):
        return here, across, lax.ppermute(jnp.stack([here, across]), "rep", swap)

    tables, angles, samples = pl.pallas_call(
        functools.partial(pack_kernel, shape),
        out_shape=[
            jax.ShapeDtypeStruct((2, ROWS, LANES), f32),
            jax.ShapeDtypeStruct((ROWS, tiles, LANES), f32),
            jax.ShapeDtypeStruct((ROWS, tiles, LANES), f32),
        ],
        in_specs=[vmem] * 8,
        out_specs=[vmem] * 3,
        compiler_params=params,
        name="pack",
    )(
        psi[0], tod[0], point_row[0], hit_list[0, 0, 0], group_id, a_zero, band_coef[0].T,
        band_lag[0].T,
    )
    angles, samples = (stream.reshape(tiles, ROWS, LANES) for stream in (angles, samples))
    place_here = [
        lax.axis_index(axis).astype(i32).reshape(1) for axis in ("wafer", "det", "rep")
    ]
    tables = lax.all_gather(tables, "rep", axis=0, tiled=False)
    riders = jnp.concatenate([angles, tables.reshape(2 * reps, ROWS, LANES)])
    samples, riders = lax.optimization_barrier((samples, riders))
    samples = jnp.stack([samples, other_wafer(samples)])
    blocks = along_det(riders)
    tables = jnp.stack([block[tiles:] for block in blocks])
    angles = jnp.stack([block[:tiles] for block in blocks])
    tables = jnp.stack([tables, other_wafer(tables)])
    tables = tables.reshape(wafers, dets, reps, 2, ROWS, LANES)
    samples, angles, tables = lax.optimization_barrier((samples, angles, tables))
    angles_across = other_wafer(angles)
    samples = along_det(samples)
    table_rows = jax.ShapeDtypeStruct((devices, LANES), i32)
    lists = pl.pallas_call(
        functools.partial(list_kernel, shape),
        out_shape=[
            jax.ShapeDtypeStruct((devices, LANES), f32),
            table_rows,
            jax.ShapeDtypeStruct((2 * LANES, LANES), i32),
            jax.ShapeDtypeStruct((ROWS, 2 * LANES), i32),
            table_rows,
            jax.ShapeDtypeStruct((2,), i32),
            jax.ShapeDtypeStruct((total,), i32),
            jax.ShapeDtypeStruct((total,), i32),
        ],
        in_specs=[smem, smem, anywhere],
        out_specs=[vmem] * 5 + [smem] * 3,
        scratch_shapes=[
            pltpu.VMEM((devices, 2, ROWS, LANES), f32),
            pltpu.VMEM((devices, LANES, LANES), f32),
            pltpu.VMEM((devices, LANES), f32),
            pltpu.VMEM((devices, LANES), f32),
            pltpu.VMEM((devices, LANES), i32),
            pltpu.VMEM((devices, LANES), i32),
            pltpu.VMEM((devices, LANES), i32),
            pltpu.SemaphoreType.DMA((devices,)),
        ],
        compiler_params=params,
        cost_estimate=pl.CostEstimate(flops=10**9, bytes_accessed=5 * 10**7, transcendentals=0),
        name="lists",
    )(*place_here[:2], tables)
    angles, angles_across, samples, lists = lax.optimization_barrier(
        (angles, angles_across, samples, lists)
    )
    floats, whole, place, start, moves, size, pair, group = lists
    angle_blocks = other_rep(angles, angles_across)
    samples = jnp.stack(samples)
    sample_blocks = samples, lax.ppermute(samples, "rep", swap)
    stream = pltpu.VMEM((count, ROWS, LANES), f32)
    sky = pltpu.VMEM((devices * ROWS + 1, ROWS, LANES), f32)
    group_sums = pltpu.VMEM((NSUB, octets * ROWS, LANES), f32)
    columns = pl.pallas_call(
        functools.partial(map_kernel, shape),
        out_shape=jax.ShapeDtypeStruct((slots // LANES + 1, 2 * height, 2 * LANES), jnp.bfloat16),
        in_specs=[smem] * 9 + [anywhere] * 5,
        out_specs=vmem,
        scratch_shapes=[
            stream, stream, stream, stream,
            pltpu.VMEM((detectors, octets * ROWS, LANES), f32),
            pltpu.VMEM((detectors, octets * ROWS, LANES), f32),
            sky,
            pltpu.VMEM((wafers * NSUB, ROWS, LANES), f32),
            pltpu.VMEM((total, 2 * height), f32),
            pltpu.VMEM((slots + LANES + ROWS, 2 * height), f32),
            pltpu.SemaphoreType.DMA((devices,)),
            pltpu.SemaphoreType.DMA((devices,)),
        ] + [sky] * (3 * (3 + ITERS)) + [group_sums] * (2 * wafers * SUM_SETS),
        compiler_params=params,
        name="map_maker",
    )(
        *place_here, size, pair, group, moves, floats, whole, *angle_blocks,
        *sample_blocks,
    )
    buffers = pltpu.VMEM((WRITES, height, OUT_TILES * LANES), f32)
    x_turned, r_turned = pl.pallas_call(
        write_kernel,
        out_shape=[jax.ShapeDtypeStruct((height, owner_rows), f32)] * 2,
        in_specs=[smem, vmem, vmem],
        out_specs=[anywhere] * 2,
        scratch_shapes=[buffers, buffers] + [pltpu.SemaphoreType.DMA((WRITES,))] * 2,
        compiler_params=params,
        name="write",
    )(start, columns, place)
    return x_turned.T, r_turned.T


def local(sizes, *arguments):
    tod, hit_list, band_lag = arguments[0], arguments[3], arguments[7]
    shape, det_count = part_shape(sizes, tod, hit_list, band_lag)
    if fits_one_device(shape, det_count):
        return whole_part(shape, *arguments)
    return distributed(*arguments)


def solution(mesh):
    placed = (
        P(("groups", "wafer"), "det", "rep"),
        P(("groups", "wafer"), "det", "rep"),
        P(("groups", "wafer"), "det", "rep"),
        P(("groups", "wafer"), "det", "rep", None, None),
        P(("groups", "wafer"), "det"),
        P(("groups", "wafer"), "det"),
        P(("groups", "wafer"), "det", None),
        P(("groups", "wafer"), "det", None),
    )
    return jax.shard_map(
        functools.partial(local, mesh.shape),
        mesh=mesh,
        in_specs=placed,
        out_specs=(P(("groups", "det", "wafer"), None), P(("groups", "det", "wafer"), None)),
        check_vma=False,
    )
```

```python
import functools

import jax
import jax.numpy as jnp
from jax import lax
from jax.experimental import pallas as pl
from jax.experimental.pallas import tpu as pltpu
from jax.sharding import PartitionSpec as P

BLOCKS = 196608
PBLOCK = 64
SBLOCK = 128
NSUB = 4
LAG = 16
ITERS = 3


prior_weight = 1.0


def with_halo(block, sides, width):
    for axis, dim in sides:
        count = lax.axis_size(axis)
        forward = [(i, i + 1) for i in range(count - 1)]
        backward = [(target, source) for source, target in forward]
        low = lax.ppermute(
            lax.slice_in_dim(block, block.shape[dim] - width, None, axis=dim), axis, forward
        )
        high = lax.ppermute(lax.slice_in_dim(block, 0, width, axis=dim), axis, backward)
        block = jnp.concatenate([low, block, high], axis=dim)
    return block


def distributed(tod, psi, point_row, hit_list, group_id, a_zero, band_coef, band_lag):
    highest = lax.Precision.HIGHEST
    samples = tod[0]
    angles = psi[0]
    det_count, time_count = samples.shape
    time_blocks = time_count // SBLOCK
    block_count = det_count * time_blocks
    send_table = hit_list[0, 0, 0]
    owner_count, capacity = send_table.shape
    owner_rows = BLOCKS // owner_count
    block_width = 3 * PBLOCK
    detector = lax.axis_index("det") * det_count + jnp.arange(det_count, dtype=jnp.int32)
    within = (jnp.arange(SBLOCK, dtype=jnp.int32)[None, :] + 3 * detector[:, None]) % PBLOCK
    pixel_table = (within[:, :, None] == jnp.arange(PBLOCK, dtype=jnp.int32)[None, None, :]).astype(
        jnp.float32
    )
    cosine_two = jnp.cos(2.0 * angles).reshape(det_count, time_blocks, SBLOCK)
    sine_two = jnp.sin(2.0 * angles).reshape(det_count, time_blocks, SBLOCK)
    slot_ids = send_table.reshape(-1)
    row_source = jnp.concatenate([point_row[0].reshape(-1), jnp.zeros((1,), jnp.int32)])
    slot_rows = row_source[slot_ids].astype(jnp.float32).reshape(owner_count, capacity)
    member = (group_id[0][:, None] == jnp.arange(NSUB, dtype=jnp.int32)[None, :]).astype(
        jnp.float32
    )
    member_count = jnp.sum(member, axis=0)
    lag_table = (
        band_lag[0][:, :, None] == jnp.arange(1, LAG + 1, dtype=jnp.int32)[None, None, :]
    ).astype(jnp.float32)
    lag_weight = jnp.einsum("dj,djl->dl", band_coef[0], lag_table, precision=highest)
    base_weight = a_zero[0]

    def slot_payload(by_block):
        width = by_block.shape[1]
        extended = jnp.concatenate([by_block, jnp.zeros((1, width), by_block.dtype)])
        return extended[slot_ids].reshape(owner_count, capacity, width)

    def deliver(payload):
        width = payload.shape[-1]
        got_values, got_rows = (
            lax.all_to_all(payload, ("det", "wafer"), split_axis=0, concat_axis=0, tiled=True),
            lax.all_to_all(slot_rows, ("det", "wafer"), split_axis=0, concat_axis=0, tiled=True),
        )
        return (got_values, got_rows)

    def back_project(stream, squared):
        shaped = stream.reshape(det_count, time_blocks, SBLOCK)
        first = cosine_two * cosine_two if squared else cosine_two
        second = sine_two * sine_two if squared else sine_two
        stacked = jnp.stack([shaped, first * shaped, second * shaped], axis=2)
        stokes = jnp.einsum("dkcs,dsp->dkcp", stacked, pixel_table, precision=highest)
        return stokes.reshape(block_count, block_width)

    def to_owners(stream, squared):
        got_values, got_rows = deliver(slot_payload(back_project(stream, squared)))
        pair_values, pair_rows = (
            lax.all_gather(got_values, "rep", axis=0, tiled=True),
            lax.all_gather(got_rows, "rep", axis=0, tiled=True),
        )
        target_rows = pair_rows.reshape(-1).astype(jnp.int32)
        summed = (
            jnp.zeros((owner_rows, block_width), jnp.float32)
            .at[target_rows]
            .add(pair_values.reshape(-1, block_width))
        )
        return (summed, got_rows.astype(jnp.int32))

    def remove_common(stream):
        local_sums = jnp.einsum("dg,dt->gt", member, stream, precision=highest)
        group_sums, group_counts = lax.psum((local_sums, member_count), "det")
        group_means = group_sums / jnp.maximum(group_counts, 1.0)[:, None]
        return stream - jnp.einsum("dg,gt->dt", member, group_means, precision=highest)

    def band_filter(stream):
        padded = with_halo(stream, (("rep", 1),), LAG)
        result = base_weight[:, None] * stream
        for offset in range(1, LAG + 1):
            later = padded[:, LAG + offset : LAG + offset + time_count]
            earlier = padded[:, LAG - offset : LAG - offset + time_count]
            result = result + lag_weight[:, offset - 1 : offset] * (later + earlier)
        return result

    def weigh_stream(stream):
        return remove_common(band_filter(remove_common(stream)))

    weight_stream = jnp.broadcast_to(base_weight[:, None], (det_count, time_count))
    diag_sum, serve_rows = to_owners(weight_stream, True)
    inverse_diag = 1.0 / (diag_sum + prior_weight)
    right_side = to_owners(weigh_stream(samples), False)[0]
    solution = jnp.zeros_like(right_side)
    residual = right_side

    def inner(left_map, right_map):
        return lax.psum(jnp.sum(left_map * right_map), ("det", "wafer"))

    precond = inverse_diag * residual
    direction = precond
    energy = inner(residual, precond)
    for iteration in range(ITERS):
        from_blocks = direction[serve_rows.reshape(-1)].reshape(owner_count, capacity, block_width)
        return_width = from_blocks.shape[-1]
        returned = lax.all_to_all(
            from_blocks, ("det", "wafer"), split_axis=0, concat_axis=0, tiled=True
        )
        return_placed = jnp.zeros((block_count + 1, return_width), jnp.float32)
        return_placed = return_placed.at[slot_ids].set(returned.reshape(-1, return_width))
        blocks = return_placed[:block_count].reshape(det_count, time_blocks, 3, PBLOCK)
        project_stokes = jnp.einsum("dkcp,dsp->dkcs", blocks, pixel_table, precision=highest)
        project_stream = (
            project_stokes[:, :, 0]
            + cosine_two * project_stokes[:, :, 1]
            + sine_two * project_stokes[:, :, 2]
        )
        seen_stream = project_stream.reshape(det_count, time_count)
        image_map = to_owners(weigh_stream(seen_stream), False)[0] + prior_weight * direction
        step_size = energy / inner(direction, image_map)
        solution = solution + step_size * direction
        residual = residual - step_size * image_map
        precond = inverse_diag * residual
        energy_next = inner(residual, precond)
        direction = precond + energy_next / energy * direction
        energy = energy_next
    return (solution, residual)


LANES = 128
ROWS = 8
OUT_TILES = 8
PAIR_BATCH = 8
WRITES = 6
DET_BATCH = 16
SUM_SETS = 2
MAP_BATCH = 8
BIG = float(1 << 24)


def wide(values):
    return jnp.broadcast_to(values, (ROWS, LANES))


def tile_iotas():
    lane = lax.broadcasted_iota(jnp.int32, (ROWS, LANES), 1)
    sub = lax.broadcasted_iota(jnp.int32, (ROWS, LANES), 0)
    return lane, sub


def cosine_sine_double(angle):
    turns = jnp.floor(angle * 1.2732395447351628 + 0.5)
    reduced = 2.0 * angle - turns * 1.5703125
    reduced = reduced - turns * 4.837512969970703125e-4
    reduced = reduced - turns * 7.54978995489188216e-8
    square = reduced * reduced
    sine = (-1.9515295891e-4 * square + 8.3321608736e-3) * square - 1.6666654611e-1
    sine = sine * square * reduced + reduced
    cosine = (2.443315711809948e-5 * square - 1.388731625493765e-3) * square
    cosine = (cosine + 4.166664568298827e-2) * square * square - 0.5 * square + 1.0
    quarter = turns.astype(jnp.int32)
    odd = (quarter & 1) == 1
    first = jnp.where(odd, sine, cosine)
    second = jnp.where(odd, cosine, sine)
    first = jnp.where(((quarter + 1) & 2) == 2, -first, first)
    second = jnp.where((quarter & 2) == 2, -second, second)
    return first, second


def pack_kernel(
    shape, angle_ref, tod_ref, row_ref, hit_ref, group_ref, base_ref, coef_ref, lag_ref,
    table_ref, angle_rows_ref, tod_rows_ref,
):
    wafers, dets, reps, tiles, owners, capacity, owner_rows, lag_count = shape
    lane, sub = tile_iotas()
    lists = hit_ref[...]
    owner_hits = jnp.zeros((ROWS, LANES), jnp.float32)
    for c in range(capacity):
        owner_hits = owner_hits + jnp.where(wide(lists[:, c : c + 1]) == lane, 1.0, 0.0)
    owner_of = jnp.sum(owner_hits * sub.astype(jnp.float32), axis=0, keepdims=True)

    def spread(values, width):
        return jnp.concatenate(
            [values, jnp.zeros((values.shape[0], LANES - width), values.dtype)], axis=1
        )

    rows = spread(row_ref[...].astype(jnp.float32), tiles)
    ids = owner_of * float(owner_rows) + rows[0:1]
    for k in range(1, ROWS):
        ids = ids + pltpu.roll(rows[k : k + 1], k * tiles, 1)
    floats = spread(base_ref[...], ROWS)
    whole = spread(group_ref[...].astype(jnp.float32), ROWS)
    for j in range(lag_count):
        at = (j + 1) * ROWS
        floats = floats + pltpu.roll(spread(coef_ref[j : j + 1, :], ROWS), at, 1)
        lag = lag_ref[j : j + 1, :].astype(jnp.float32)
        whole = whole + pltpu.roll(spread(lag, ROWS), at, 1)
    table = jnp.where(sub == 0, wide(ids), jnp.where(sub == 1, wide(floats), wide(whole)))
    table_ref[0] = table
    table_ref[1] = spread(lists.astype(jnp.float32), capacity)
    for b in range(tiles):
        angle_rows_ref[:, b, :] = angle_ref[:, b * LANES : (b + 1) * LANES]
        tod_rows_ref[:, b, :] = tod_ref[:, b * LANES : (b + 1) * LANES]


def part_copies(shape, self_ref, source, target, sem):
    wafers, dets, reps = shape[:3]
    copies = []
    for swap_rep in range(reps):
        for swap_wafer in range(wafers):
            for shift in range(dets):
                det = self_ref[1] - shift
                det = jnp.where(det < 0, det + dets, det)
                device = ((self_ref[0] ^ swap_wafer) * dets + det) * reps
                device = device + (self_ref[2] ^ swap_rep)
                copies.append(
                    pltpu.make_async_copy(
                        source(swap_rep, swap_wafer, shift), target(device), sem.at[len(copies)]
                    )
                )
    return copies


def table_copies(shape, self_ref, source_ref, part_ref, sem):
    wafers, dets, reps = shape[:3]
    copies = []
    for swap_wafer in range(wafers):
        for shift in range(dets):
            det = self_ref[1] - shift
            det = jnp.where(det < 0, det + dets, det)
            device = ((self_ref[0] ^ swap_wafer) * dets + det) * reps
            copies.append(
                pltpu.make_async_copy(
                    source_ref.at[swap_wafer, shift], part_ref.at[pl.ds(device, reps)],
                    sem.at[len(copies)],
                )
            )
    for copy in copies:
        copy.start()
    for copy in copies:
        copy.wait()


def exact_dot(left, right, dims=((1,), (0,))):
    return lax.dot_general(
        left.astype(jnp.bfloat16), right.astype(jnp.bfloat16), (dims, ((), ())),
        preferred_element_type=jnp.float32,
    )


def list_kernel(
    shape, wafer_ref, det_ref, table_ref, float_ref, whole_ref, place_ref, start_ref, move_ref,
    size_ref, pair_ref, group_ref,
    part_ref, column_ref, code_ref, lead_ref, used_ref, rank_ref, hits_ref, part_sem,
):
    self_ref = wafer_ref[0], det_ref[0]
    table_copies(shape, self_ref, table_ref, part_ref, part_sem)
    list_twins(
        shape, float_ref, whole_ref, size_ref, pair_ref, group_ref, part_ref, column_ref, code_ref,
        lead_ref, used_ref,
    )
    list_places(shape, self_ref, place_ref, start_ref, move_ref, part_ref, rank_ref, hits_ref)


def list_twins(
    shape, float_ref, whole_ref, size_ref, pair_ref, group_ref, part_ref, column_ref, code_ref,
    lead_ref, used_ref,
):
    wafers, dets, reps, tiles, owners, capacity, owner_rows, lag_count = shape
    devices = wafers * dets * reps
    total = devices * LANES
    lane, sub = tile_iotas()
    sub_f = sub.astype(jnp.float32)
    none = jnp.full((ROWS, LANES), BIG, jnp.float32)
    along = lax.broadcasted_iota(jnp.int32, (1, LANES), 1).astype(jnp.float32)

    def turn(batch, carry):
        for k in range(4):
            device = 4 * batch + k
            float_ref[pl.ds(device, 1), :] = part_ref[device, 0, 1:2, :]
            whole_ref[pl.ds(device, 1), :] = part_ref[device, 0, 2:3, :].astype(jnp.int32)
            column_ref[device] = jnp.broadcast_to(part_ref[device, 0, 0:1, :], (LANES, LANES)).T
        return carry

    lax.fori_loop(0, devices // 4, turn, 0)

    def survey(device, carry):
        row = wide(part_ref[device, 0, 0:1, :])

        def compare(step, least):
            for k in range(2):
                other = 2 * step + k
                found = [none] * 4
                for j in range(tiles):
                    same = column_ref[other, j * ROWS : (j + 1) * ROWS, :] == row
                    at = jnp.where(same, sub_f + float(j * ROWS), BIG)
                    found[j % 4] = jnp.minimum(found[j % 4], at)
                here = jnp.minimum(jnp.minimum(found[0], found[1]), jnp.minimum(found[2], found[3]))
                least = jnp.minimum(least, here + (other * LANES).astype(jnp.float32))
            return least

        least = lax.fori_loop(0, lax.shift_right_logical(device, 1) + 1, compare, none)
        lead = jnp.min(least, axis=0, keepdims=True)
        mine = (device * LANES).astype(jnp.float32) + along
        later = lead < mine
        code_ref[pl.ds(device, 1), :] = jnp.where(later, mine * float(total) + lead, BIG)
        lead_ref[pl.ds(device, 1), :] = jnp.where(later, lead, BIG)
        return carry

    lax.fori_loop(0, devices, survey, 0)

    def next_code(last):
        found = none
        for tile in range(devices // ROWS):
            codes = code_ref[tile * ROWS : (tile + 1) * ROWS, :]
            found = jnp.minimum(found, jnp.where(codes > last, codes, BIG))
        return jnp.min(found)

    def detector(key):
        team = lax.rem(lax.div(key, reps * LANES), dets)
        return team * ROWS + lax.rem(lax.div(key, tiles), ROWS)

    number_of = [lane + (sub + tile * ROWS) * LANES for tile in range(devices // ROWS)]
    tile_rows = [slice(tile * ROWS, (tile + 1) * ROWS) for tile in range(devices // ROWS)]
    for rows in tile_rows:
        used_ref[rows, :] = jnp.zeros((ROWS, LANES), jnp.int32)

    def take(state):
        pairs, grouped, code = state
        number = code.astype(jnp.int32)
        key = lax.div(number, total)
        lead = lax.rem(number, total)
        shift = (3 * (detector(key) - detector(lead))) & (PBLOCK - 1)
        wanted = lead.astype(jnp.float32)
        same = jnp.zeros((ROWS, LANES), jnp.float32)
        for rows, numbers in zip(tile_rows, number_of):
            same = same + jnp.where(lead_ref[rows, :] == wanted, 1.0, 0.0)
            beside = numbers ^ ROWS
            beside = (beside == key) | (beside == lead)
            same = same + jnp.where(beside & (used_ref[rows, :] > 0), 2.0, 0.0)
        alone = jnp.sum(same) + jnp.where((key ^ lead) == ROWS, 2.0, 0.0) < 1.5
        mark = jnp.where(alone, 1, 0)
        for rows, numbers in zip(tile_rows, number_of):
            listed = (numbers == key) | (numbers == lead)
            used_ref[rows, :] = jnp.where(listed, mark, used_ref[rows, :])
        entry = twin_entry(key, lead, shift)
        pair_ref[pairs] = entry
        group_ref[grouped] = entry
        return (
            pairs + jnp.where(alone, 1, 0), grouped + jnp.where(alone, 0, 1), next_code(code)
        )

    pairs, grouped, _ = lax.while_loop(
        lambda state: state[2] < BIG, take,
        (jnp.int32(0), jnp.int32(0), next_code(jnp.float32(-1.0))),
    )
    batches = lax.div(pairs + PAIR_BATCH - 1, PAIR_BATCH)

    def fill(n, carry):
        pair_ref[n] = twin_entry(total, total + 1, 0)
        return carry

    lax.fori_loop(pairs, batches * PAIR_BATCH, fill, 0)
    size_ref[0] = batches
    size_ref[1] = grouped


def twin_entry(key, lead, shift):
    return key * (1 << 19) + lead * (1 << 6) + shift


def twin_of(entry):
    return entry >> 19, (entry >> 6) & ((1 << 13) - 1), entry & (PBLOCK - 1)


def list_places(shape, self_ref, place_ref, start_ref, move_ref, part_ref, rank_ref, hits_ref):
    wafers, dets, reps, tiles, owners, capacity, owner_rows, lag_count = shape
    devices = wafers * dets * reps
    slots = devices * capacity
    lane, sub = tile_iotas()
    own = self_ref[1] * wafers + self_ref[0]
    first_row = (own * owner_rows).astype(jnp.float32)
    depth = 2 * LANES
    tall = lax.broadcasted_iota(jnp.int32, (depth, LANES), 0).astype(jnp.float32)

    def one_hots(device):
        local_row = part_ref[device, 0, 0:1, :] - first_row
        high = jnp.floor(local_row * (1.0 / LANES))
        low = local_row - high * LANES
        high = (jnp.broadcast_to(high, (depth, LANES)) == tall).astype(jnp.float32)
        low = (jnp.broadcast_to(low, (LANES, LANES)) == tall[0:LANES]).astype(jnp.float32)
        return high, low

    def survey(batch, hits):
        for k in range(4):
            device = 4 * batch + k
            own_hits = jnp.where(sub == own, part_ref[device, 1], 0.0)
            own_hits = jnp.sum(own_hits, axis=0, keepdims=True)
            hits_ref[pl.ds(device, 1), :] = own_hits.astype(jnp.int32)
            high, low = one_hots(device)
            hits = hits + exact_dot(high, low, ((1,), (1,)))
        return hits

    hits = lax.fori_loop(0, devices // 4, survey, jnp.zeros((depth, LANES), jnp.float32))
    full = jnp.minimum(hits, 1.0)

    def ordered(size, axis):
        first = lax.broadcasted_iota(jnp.int32, (size, size), axis)
        second = lax.broadcasted_iota(jnp.int32, (size, size), 1 - axis)
        return (first < second).astype(jnp.float32)

    counts = exact_dot(jnp.ones((ROWS, LANES), jnp.float32), full, ((1,), (1,)))
    start_ref[...] = exact_dot(counts, ordered(depth, 0)).astype(jnp.int32)
    sums = exact_dot(full, jnp.ones((LANES, LANES), jnp.float32))
    place = exact_dot(full, ordered(LANES, 0)) + exact_dot(ordered(depth, 1), sums)
    place_ref[...] = jnp.where(full > 0.0, place, -1.0).astype(jnp.int32)
    place_high = jnp.floor(place * (1.0 / LANES))
    place_parts = jnp.concatenate([place_high, place - place_high * LANES], axis=0)

    def rank_of(batch, carry):
        for k in range(4):
            device = 4 * batch + k
            high, low = one_hots(device)
            parts = exact_dot(place_parts, low)
            rank = high * (parts[0:depth] * LANES + parts[depth : 2 * depth])
            rank = jnp.sum(rank, axis=0, keepdims=True)
            rank_ref[pl.ds(device, 1), :] = rank.astype(jnp.int32)
        return carry

    lax.fori_loop(0, devices // 4, rank_of, 0)
    for tile in range(devices // ROWS):
        rows = slice(tile * ROWS, (tile + 1) * ROWS)
        number = hits_ref[rows, :]
        valid = number < LANES
        number = number & (LANES - 1)
        rank = jnp.take_along_axis(rank_ref[rows, :], number, axis=1, mode="promise_in_bounds")
        target = jnp.where(valid, rank, slots + LANES)
        move_ref[rows, :] = target * (1 << 16) + (tile * ROWS + sub) * LANES + number


def map_kernel(
    shape, wafer_ref, det_ref, rep_ref, size_ref, pair_ref, group_ref, move_ref, float_smem, whole_smem,
    angle_here_ref, angle_across_ref, angle_other_ref, tod_here_ref, tod_other_ref, column_ref,
    angle_ref, tod_ref, cos_ref, sin_ref, clean_ref, noise_ref, weight_ref,
    share_ref, rows_ref, sorted_ref, angle_sem, tod_sem, *more_refs,
):
    wafers, dets, reps, tiles, owners, capacity, owner_rows, lag_count = shape
    devices = wafers * dets * reps
    octets = 2 * reps
    wafer_dets = dets * ROWS
    self_ref = wafer_ref[0], det_ref[0], rep_ref[0]
    count = devices * ROWS
    lane, sub = tile_iotas()
    zero = jnp.zeros((ROWS, LANES), jnp.float32)
    low = lane < PBLOCK
    skies = [more_refs[3 * k : 3 * k + 3] for k in range(3 + ITERS)]
    inverse_ref, r_map, image_map, *d_maps = skies
    sum_refs = more_refs[3 * len(skies) :]
    first_sums = [sum_refs[SUM_SETS * wafer : SUM_SETS * (wafer + 1)] for wafer in range(wafers)]
    sum_refs = sum_refs[SUM_SETS * wafers :]
    second_sums = [sum_refs[SUM_SETS * wafer : SUM_SETS * (wafer + 1)] for wafer in range(wafers)]

    def copies_of(source, to_ref, sem):
        return part_copies(
            shape, self_ref, source, lambda d: to_ref.at[pl.ds(d * tiles, tiles)], sem
        )

    def angle_source(swap_rep, swap_wafer, shift):
        if swap_rep:
            return angle_other_ref.at[swap_wafer, shift]
        return (angle_across_ref if swap_wafer else angle_here_ref).at[shift]

    def tod_source(swap_rep, swap_wafer, shift):
        return (tod_other_ref if swap_rep else tod_here_ref).at[shift, swap_wafer]

    angle_moves = copies_of(angle_source, angle_ref, angle_sem)
    tod_moves = copies_of(tod_source, tod_ref, tod_sem)
    for copy in angle_moves + tod_moves:
        copy.start()

    def turn_half(block):
        return pltpu.roll(block, PBLOCK, 1)

    def fold(first, second):
        return jnp.where(low, first, second) + turn_half(jnp.where(low, second, first))

    def unfold(block):
        turned = turn_half(block)
        return jnp.where(low, block, turned), jnp.where(low, turned, block)

    def whole_sum(values):
        values = jnp.sum(values, axis=0, keepdims=True)
        return wide(jnp.sum(values, axis=1, keepdims=True))

    def loop(times, body, carry, unroll):
        def several(n, carry):
            for k in range(unroll):
                carry = body(n * unroll + k, carry)
            return carry

        return lax.fori_loop(0, times // unroll, several, carry)

    def device_of(wafer, n):
        return (wafer * dets + lax.shift_right_logical(n, 3)) * reps

    def group_of(wafer, n):
        return whole_smem[device_of(wafer, n), n & (ROWS - 1)]

    def rows_of(octet):
        return pl.ds(octet * ROWS, ROWS)

    def count_members(n, counts):
        result = []
        for wafer in range(wafers):
            group = group_of(wafer, n)
            result += [
                counts[wafer * NSUB + g] + jnp.where(group == g, 1, 0) for g in range(NSUB)
            ]
        return tuple(result)

    members = lax.fori_loop(0, wafer_dets, count_members, (jnp.int32(0),) * (wafers * NSUB))
    for k, member in enumerate(members):
        share_ref[k] = 1.0 / jnp.maximum(zero + member.astype(jnp.float32), 1.0)
    for c in range(3):
        image_map[c][count] = zero
        r_map[c][count] = zero

    def clear_sorted(n, carry):
        at = pl.ds(pl.multiple_of(n * ROWS, ROWS), ROWS)
        sorted_ref[at, :] = jnp.zeros((ROWS, 6 * PBLOCK), jnp.float32)
        return carry

    lax.fori_loop(0, sorted_ref.shape[0] // ROWS, clear_sorted, 0)

    def spot_of(key):
        return lax.shift_right_logical(key, 4), (key >> 3) & 1, pl.ds(key & (ROWS - 1), 1)

    def in_half(half):
        return (lane[0:1] >> 6) == half

    def set_weight(at, carry):
        weight_ref[at] = zero + 1.0
        return carry

    loop(count, set_weight, 0, 16)

    def drop(list_ref):
        def one(n, carry):
            at, half, row = spot_of(twin_of(list_ref[n])[0])
            weight_ref[at, row, :] = jnp.where(in_half(half), 0.0, weight_ref[at, row, :])
            return carry

        return one

    lax.fori_loop(0, size_ref[0] * PAIR_BATCH, drop(pair_ref), 0)
    lax.fori_loop(0, size_ref[1], drop(group_ref), 0)

    def moved_from(target, spot, shift):
        at, half, row = spot
        result = []
        for ref in target:
            values = wide(ref[at, row, :])
            values = jnp.where((lane >> 6) == half, values, turn_half(values))
            result.append(pltpu.roll(values, shift, 1)[0:1])
        return result

    def merge_twins(target):
        def pair_batch(n, carry):
            found = []
            for k in range(PAIR_BATCH):
                key, lead, shift = twin_of(pair_ref[n * PAIR_BATCH + k])
                key, lead = spot_of(key), spot_of(lead)
                back = (PBLOCK - shift) & (PBLOCK - 1)
                for spot, values in (
                    (lead, moved_from(target, key, shift)), (key, moved_from(target, lead, back))
                ):
                    at, half, row = spot
                    for c in range(3):
                        values[c] = target[c][at, row, :] + jnp.where(in_half(half), values[c], 0.0)
                    found.append((at, row, values))
            for at, row, values in found:
                for c in range(3):
                    target[c][at, row, :] = values[c]
            return carry

        def gather_one(n, carry):
            key, lead, shift = twin_of(group_ref[n])
            values = moved_from(target, spot_of(key), shift)
            at, half, row = spot_of(lead)
            for c in range(3):
                target[c][at, row, :] += jnp.where(in_half(half), values[c], 0.0)
            return carry

        def spread_one(n, carry):
            key, lead, shift = twin_of(group_ref[n])
            values = moved_from(target, spot_of(lead), (PBLOCK - shift) & (PBLOCK - 1))
            at, half, row = spot_of(key)
            for c in range(3):
                target[c][at, row, :] = jnp.where(in_half(half), values[c], target[c][at, row, :])
            return carry

        lax.fori_loop(0, size_ref[0], pair_batch, 0)
        lax.fori_loop(0, size_ref[1], gather_one, 0)
        lax.fori_loop(0, size_ref[1], spread_one, 0)

    for copy in angle_moves:
        copy.wait()

    def survey(at, carry):
        base = float_smem[lax.shift_right_logical(at, 3), at & (ROWS - 1)]
        squares = []
        for half in range(2):
            first, second = cosine_sine_double(angle_ref[2 * at + half])
            cos_ref[2 * at + half] = first
            sin_ref[2 * at + half] = second
            squares.append((base * (first * first), base * (second * second)))
        image_map[0][at] = zero + (base + base)
        for c in range(2):
            image_map[c + 1][at] = fold(squares[0][c], squares[1][c])
        return carry

    loop(count, survey, 0, 8)

    def clear_sums(refs):
        for sets in refs:
            for ref in sets:
                for group in range(NSUB):
                    for octet in range(octets):
                        ref[group, rows_of(octet), :] = zero

    def average(refs):
        for wafer, sets in enumerate(refs):
            for group in range(NSUB):
                for octet in range(octets):
                    total = sets[0][group, rows_of(octet), :]
                    for ref in sets[1:]:
                        total = total + ref[group, rows_of(octet), :]
                    sets[0][group, rows_of(octet), :] = total * share_ref[wafer * NSUB + group]

    def over_detectors(body, carry):
        def several(step, carry):
            for k in range(DET_BATCH):
                carry = body(step * DET_BATCH + k, k % SUM_SETS, carry)
            return carry

        return lax.fori_loop(0, wafer_dets // DET_BATCH, several, carry)

    def sum_streams(streams_of, carry):
        clear_sums(first_sums)

        def one_detector(n, part, carry):
            for wafer in range(wafers):
                group = group_of(wafer, n)
                for rep in range(reps):
                    at = (device_of(wafer, n) + rep) * ROWS + (n & (ROWS - 1))
                    streams, carry = streams_of(at, carry)
                    for half, stream in enumerate(streams):
                        rows = rows_of(2 * rep + half)
                        clean_ref[wafer * wafer_dets + n, rows, :] = stream
                        first_sums[wafer][part][group, rows, :] += stream
            return carry

        carry = over_detectors(one_detector, carry)
        average(first_sums)
        return carry

    def filter_streams():
        clear_sums(second_sums)

        def one_filter(n, part, carry):
            for wafer in range(wafers):
                device, inside = device_of(wafer, n), n & (ROWS - 1)
                detector = wafer * wafer_dets + n
                group = group_of(wafer, n)
                base = float_smem[device, inside]
                coefs = [float_smem[device, (j + 1) * ROWS + inside] for j in range(lag_count)]
                lags = [whole_smem[device, (j + 1) * ROWS + inside] for j in range(lag_count)]
                clean = [
                    clean_ref[detector, rows_of(octet), :]
                    - first_sums[wafer][0][group, rows_of(octet), :]
                    for octet in range(octets)
                ]
                up = [pltpu.roll(here, ROWS - 1, 0) for here in clean] + [zero]
                down = [zero] + [pltpu.roll(here, 1, 0) for here in clean]
                for octet, here in enumerate(clean):
                    after = jnp.where(sub == ROWS - 1, up[octet + 1], up[octet])
                    ahead = jnp.where(sub == 0, down[octet], down[octet + 1])
                    result = base * here
                    for coef, lag in zip(coefs, lags):
                        later = pltpu.roll(jnp.where(lane < lag, after, here), LANES - lag, 1)
                        earlier = pltpu.roll(jnp.where(lane >= LANES - lag, ahead, here), lag, 1)
                        result = result + coef * (later + earlier)
                    noise_ref[detector, rows_of(octet), :] = result
                    second_sums[wafer][part][group, rows_of(octet), :] += result
                    carry = carry + here * result
            return carry

        product = over_detectors(one_filter, zero)
        average(second_sums)
        return product

    def return_streams(target):
        def one_return(n, part, carry):
            for wafer in range(wafers):
                group = group_of(wafer, n)
                for rep in range(reps):
                    at = (device_of(wafer, n) + rep) * ROWS + (n & (ROWS - 1))
                    streams = []
                    for half in range(2):
                        rows = rows_of(2 * rep + half)
                        stream = noise_ref[wafer * wafer_dets + n, rows, :]
                        streams.append(stream - second_sums[wafer][0][group, rows, :])
                    target[0][at] = fold(*streams)
                    for c, ref in ((1, cos_ref), (2, sin_ref)):
                        target[c][at] = fold(*(ref[2 * at + h] * streams[h] for h in range(2)))
            return carry

        over_detectors(one_return, 0)
        merge_twins(target)

    merge_twins(image_map)
    for copy in tod_moves:
        copy.wait()
    sum_streams(lambda at, carry: ([tod_ref[2 * at + half] for half in range(2)], carry), 0)
    filter_streams()
    return_streams(r_map)

    factor = zero
    steps = []
    for iteration, d_map in enumerate(d_maps):
        last = iteration == ITERS - 1

        def seen_streams(at, carry):
            prior, energy = carry
            squares, products = zero, zero
            streams = [None, None]
            for c in range(3):
                residual = r_map[c][at]
                if iteration:
                    part = inverse_ref[c][at] * residual + factor * d_maps[iteration - 1][c][at]
                else:
                    inverse = 1.0 / (image_map[c][at] + prior_weight)
                    inverse_ref[c][at] = inverse
                    part = inverse * residual
                    products = products + residual * part
                d_map[c][at] = part
                squares = squares + part * part
                for half, seen in enumerate(unfold(part)):
                    if c == 0:
                        streams[half] = seen
                    else:
                        ref = cos_ref if c == 1 else sin_ref
                        streams[half] = streams[half] + ref[2 * at + half] * seen
            weight = weight_ref[at]
            if not iteration:
                energy = energy + weight * products
            return streams, (prior + weight * squares, energy)

        prior, first_energy = sum_streams(seen_streams, (zero, zero))
        if not iteration:
            energy = whole_sum(first_energy)
        product = filter_streams()
        return_streams(image_map)
        step = energy / whole_sum(product + prior_weight * prior)
        steps.append(step)

        def new_residual(at, c):
            return r_map[c][at] - step * (image_map[c][at] + prior_weight * d_map[c][at])

        if not last:

            def update(batch, carry):
                found = []
                for k in range(MAP_BATCH):
                    at = batch * MAP_BATCH + k
                    residual = [new_residual(at, c) for c in range(3)]
                    parts = zero
                    for c in range(3):
                        parts = parts + residual[c] * (inverse_ref[c][at] * residual[c])
                    carry = carry + weight_ref[at] * parts
                    found.append((at, residual))
                for at, residual in found:
                    for c in range(3):
                        r_map[c][at] = residual[c]
                return carry

            next_energy = whole_sum(loop(count // MAP_BATCH, update, zero, 2))
            factor = next_energy / energy
            energy = next_energy
        else:

            def place_pixels(at, carry):
                team = lax.rem(lax.div(at, reps * ROWS), dets)
                turn = (3 * (team * ROWS + (at & (ROWS - 1)))) & (PBLOCK - 1)
                inside = (lane & (PBLOCK - 1)) >= turn
                values = []
                for c in range(3):
                    value = steps[0] * d_maps[0][c][at]
                    for k in range(1, ITERS):
                        value = value + steps[k] * d_maps[k][c][at]
                    values.append(value)
                values += [new_residual(at, c) for c in range(3)]
                for c in range(3):
                    left, right = values[2 * c], values[2 * c + 1]
                    halves = (
                        jnp.where(low, left, turn_half(right)), jnp.where(low, turn_half(left), right)
                    )
                    for half, value in enumerate(halves):
                        value = jnp.where(
                            inside, pltpu.roll(value, turn, 1), pltpu.roll(value, turn + PBLOCK, 1)
                        )
                        rows = pl.ds(pl.multiple_of((2 * at + half) * ROWS, ROWS), ROWS)
                        rows_ref[rows, c * LANES : (c + 1) * LANES] = value
                return carry

            loop(count, place_pixels, 0, 8)

    def pick(device, carry):
        for c in range(capacity):
            move = move_ref[device, c]
            source, target = move & ((1 << 16) - 1), move >> 16
            sorted_ref[pl.ds(target, 1), :] = rows_ref[pl.ds(source, 1), :]
        return carry

    lax.fori_loop(0, devices, pick, 0)

    def turn_tile(tile, carry):
        columns = sorted_ref[pl.ds(pl.multiple_of(tile * LANES, LANES), LANES), :].T
        high = columns.astype(jnp.bfloat16)
        column_ref[tile, :, 0:LANES] = high
        column_ref[tile, :, LANES : 2 * LANES] = (columns - high.astype(jnp.float32)).astype(
            jnp.bfloat16
        )
        return carry

    lax.fori_loop(0, column_ref.shape[0], turn_tile, 0)


def write_kernel(start_ref, column_ref, place_ref, x_ref, r_ref, x_buffer, r_buffer, x_sem, r_sem):
    height = 3 * PBLOCK
    width = OUT_TILES * LANES
    steps = x_ref.shape[1] // width
    depth = lax.broadcasted_iota(jnp.int32, (LANES, LANES), 0)

    def copies(step, slot):
        to = pl.ds(pl.multiple_of(step * width, width), width)
        return (
            pltpu.make_async_copy(x_buffer.at[slot], x_ref.at[:, to], x_sem.at[slot]),
            pltpu.make_async_copy(r_buffer.at[slot], r_ref.at[:, to], r_sem.at[slot]),
        )

    def spread(group, tile):
        chosen = []
        for k in range(OUT_TILES):
            place = jnp.broadcast_to(place_ref[pl.ds(group + k, 1), :], (LANES, LANES))
            chosen.append(jnp.where(place == depth + tile * LANES, 1.0, 0.0).astype(jnp.bfloat16))
        chosen = jnp.concatenate(chosen, axis=1)
        chosen = jnp.concatenate([chosen, chosen], axis=0)
        return jnp.dot(column_ref[tile], chosen, preferred_element_type=jnp.float32)

    def one_step(step, carry):
        slot = lax.rem(step, WRITES)

        @pl.when(step >= WRITES)
        def _():
            for copy in copies(step - WRITES, slot):
                copy.wait()

        group = step * OUT_TILES
        start, end = start_ref[0, group], start_ref[0, group + OUT_TILES]
        first = lax.shift_right_logical(start, 7)
        last = lax.shift_right_logical(jnp.maximum(end - 1, start), 7)
        values = spread(group, first)
        x_buffer[slot] = values[:height]
        r_buffer[slot] = values[height:]

        def add_tile(tile, carry):
            values = spread(group, tile)
            x_buffer[slot] += values[:height]
            r_buffer[slot] += values[height:]
            return carry

        lax.fori_loop(first + 1, last + 1, add_tile, 0)
        for copy in copies(step, slot):
            copy.start()
        return carry

    lax.fori_loop(0, steps, one_step, 0)
    for step in range(steps - WRITES, steps):
        for copy in copies(step, step % WRITES):
            copy.wait()


def part_shape(sizes, tod, hit_list, band_lag):
    det_count, time_count = tod.shape[1:]
    owners, capacity = hit_list.shape[3:]
    return (
        sizes["wafer"], sizes["det"], sizes["rep"], time_count // SBLOCK,
        owners, capacity, BLOCKS // owners, band_lag.shape[2],
    ), det_count


def fits_one_device(shape, det_count):
    wafers, dets, reps, tiles, owners, capacity, owner_rows, lag_count = shape
    devices = wafers * dets * reps
    total = devices * tiles * det_count
    groups = owner_rows // LANES
    return (
        det_count == ROWS
        and owners == ROWS
        and tiles * ROWS == LANES
        and tiles == 2 * ROWS
        and (wafers, reps) == (2, 2)
        and (1 + lag_count) * ROWS <= LANES
        and capacity <= LANES
        and devices * capacity % LANES == 0
        and owner_rows % (LANES * OUT_TILES) == 0
        and owner_rows >= LANES * OUT_TILES * WRITES
        and groups + 1 <= 2 * LANES
        and devices % ROWS == 0
        and dets % (DET_BATCH // ROWS) == 0
        and total * total < BIG
    )


def whole_part(shape, tod, psi, point_row, hit_list, group_id, a_zero, band_coef, band_lag):
    wafers, dets, reps, tiles, owners, capacity, owner_rows, lag_count = shape
    devices = wafers * dets * reps
    octets = reps * tiles // ROWS
    detectors = wafers * dets * ROWS
    count = devices * tiles
    total = count * ROWS
    slots = devices * capacity
    height = 3 * PBLOCK
    f32, i32 = jnp.float32, jnp.int32
    vmem, smem = pl.BlockSpec(memory_space=pltpu.VMEM), pl.BlockSpec(memory_space=pltpu.SMEM)
    anywhere = pl.BlockSpec(memory_space=pl.ANY)

    def params(mebibytes):
        return pltpu.CompilerParams(vmem_limit_bytes=mebibytes << 20)

    swap = [(0, 1), (1, 0)]

    def along_det(block):
        moved = [
            lax.ppermute(block, "det", [(i, (i + shift) % dets) for i in range(dets)])
            for shift in range(1, dets)
        ]
        return [block] + moved

    def other_wafer(here):
        return lax.ppermute(here, "wafer", swap)

    def other_rep(here, across):
        return here, across, lax.ppermute(jnp.stack([here, across]), "rep", swap)

    tables, angles, samples = pl.pallas_call(
        functools.partial(pack_kernel, shape),
        out_shape=[
            jax.ShapeDtypeStruct((2, ROWS, LANES), f32),
            jax.ShapeDtypeStruct((ROWS, tiles, LANES), f32),
            jax.ShapeDtypeStruct((ROWS, tiles, LANES), f32),
        ],
        in_specs=[vmem] * 8,
        out_specs=[vmem] * 3,
        compiler_params=params(60),
        name="pack",
    )(
        psi[0], tod[0], point_row[0], hit_list[0, 0, 0], group_id, a_zero, band_coef[0].T,
        band_lag[0].T,
    )
    angles, samples = (stream.reshape(tiles, ROWS, LANES) for stream in (angles, samples))
    place_here = [
        lax.axis_index(axis).astype(i32).reshape(1) for axis in ("wafer", "det", "rep")
    ]
    tables = lax.all_gather(tables, "rep", axis=0, tiled=False)
    riders = jnp.concatenate([angles, tables.reshape(2 * reps, ROWS, LANES)])
    samples, riders = lax.optimization_barrier((samples, riders))
    samples = jnp.stack([samples, other_wafer(samples)])
    samples, *blocks = lax.optimization_barrier((samples, *along_det(riders)))
    samples = along_det(samples)
    tables = jnp.stack([block[tiles:] for block in blocks])
    angles = jnp.stack([block[:tiles] for block in blocks])
    tables = jnp.stack([tables, other_wafer(tables)])
    tables = tables.reshape(wafers, dets, reps, 2, ROWS, LANES)
    angles, tables = lax.optimization_barrier((angles, tables))
    angles_across = other_wafer(angles)
    table_rows = jax.ShapeDtypeStruct((devices, LANES), i32)
    lists = pl.pallas_call(
        functools.partial(list_kernel, shape),
        out_shape=[
            jax.ShapeDtypeStruct((devices, LANES), f32),
            table_rows,
            jax.ShapeDtypeStruct((2 * LANES, LANES), i32),
            jax.ShapeDtypeStruct((ROWS, 2 * LANES), i32),
            table_rows,
            jax.ShapeDtypeStruct((2,), i32),
            jax.ShapeDtypeStruct((total,), i32),
            jax.ShapeDtypeStruct((total,), i32),
        ],
        in_specs=[smem, smem, anywhere],
        out_specs=[vmem] * 5 + [smem] * 3,
        scratch_shapes=[
            pltpu.VMEM((devices, 2, ROWS, LANES), f32),
            pltpu.VMEM((devices, LANES, LANES), f32),
            pltpu.VMEM((devices, LANES), f32),
            pltpu.VMEM((devices, LANES), f32),
            pltpu.VMEM((devices, LANES), i32),
            pltpu.VMEM((devices, LANES), i32),
            pltpu.VMEM((devices, LANES), i32),
            pltpu.SemaphoreType.DMA((devices,)),
        ],
        compiler_params=params(8),
        cost_estimate=pl.CostEstimate(flops=10**9, bytes_accessed=5 * 10**7, transcendentals=0),
        name="lists",
    )(*place_here[:2], tables)
    angles, angles_across, samples, lists = lax.optimization_barrier(
        (angles, angles_across, samples, lists)
    )
    floats, whole, place, start, moves, size, pair, group = lists
    angle_blocks = other_rep(angles, angles_across)
    samples = jnp.stack(samples)
    sample_blocks = samples, lax.ppermute(samples, "rep", swap)
    stream = pltpu.VMEM((count, ROWS, LANES), f32)
    sky = pltpu.VMEM((devices * ROWS + 1, ROWS, LANES), f32)
    group_sums = pltpu.VMEM((NSUB, octets * ROWS, LANES), f32)
    columns = pl.pallas_call(
        functools.partial(map_kernel, shape),
        out_shape=jax.ShapeDtypeStruct((slots // LANES + 1, 2 * height, 2 * LANES), jnp.bfloat16),
        in_specs=[smem] * 9 + [anywhere] * 5,
        out_specs=vmem,
        scratch_shapes=[
            stream, stream, stream, stream,
            pltpu.VMEM((detectors, octets * ROWS, LANES), f32),
            pltpu.VMEM((detectors, octets * ROWS, LANES), f32),
            sky,
            pltpu.VMEM((wafers * NSUB, ROWS, LANES), f32),
            pltpu.VMEM((total, 2 * height), f32),
            pltpu.VMEM((slots + LANES + ROWS, 2 * height), f32),
            pltpu.SemaphoreType.DMA((devices,)),
            pltpu.SemaphoreType.DMA((devices,)),
        ] + [sky] * (3 * (3 + ITERS)) + [group_sums] * (2 * wafers * SUM_SETS),
        compiler_params=params(30),
        name="map_maker",
    )(
        *place_here, size, pair, group, moves, floats, whole, *angle_blocks,
        *sample_blocks,
    )
    buffers = pltpu.VMEM((WRITES, height, OUT_TILES * LANES), f32)
    x_turned, r_turned = pl.pallas_call(
        write_kernel,
        out_shape=[jax.ShapeDtypeStruct((height, owner_rows), f32)] * 2,
        in_specs=[smem, vmem, vmem],
        out_specs=[anywhere] * 2,
        scratch_shapes=[buffers, buffers] + [pltpu.SemaphoreType.DMA((WRITES,))] * 2,
        compiler_params=params(16),
        name="write",
    )(start, columns, place)
    return x_turned.T, r_turned.T


def local(sizes, *arguments):
    tod, hit_list, band_lag = arguments[0], arguments[3], arguments[7]
    shape, det_count = part_shape(sizes, tod, hit_list, band_lag)
    if fits_one_device(shape, det_count):
        return whole_part(shape, *arguments)
    return distributed(*arguments)


def solution(mesh):
    placed = (
        P(("groups", "wafer"), "det", "rep"),
        P(("groups", "wafer"), "det", "rep"),
        P(("groups", "wafer"), "det", "rep"),
        P(("groups", "wafer"), "det", "rep", None, None),
        P(("groups", "wafer"), "det"),
        P(("groups", "wafer"), "det"),
        P(("groups", "wafer"), "det", None),
        P(("groups", "wafer"), "det", None),
    )
    return jax.shard_map(
        functools.partial(local, mesh.shape),
        mesh=mesh,
        in_specs=placed,
        out_specs=(P(("groups", "det", "wafer"), None), P(("groups", "det", "wafer"), None)),
        check_vma=False,
    )
```

```python
import functools

import jax
import jax.numpy as jnp
from jax import lax
from jax.experimental import pallas as pl
from jax.experimental.pallas import tpu as pltpu
from jax.sharding import PartitionSpec as P

BLOCKS = 196608
PBLOCK = 64
SBLOCK = 128
NSUB = 4
LAG = 16
ITERS = 3


prior_weight = 1.0


def with_halo(block, sides, width):
    for axis, dim in sides:
        count = lax.axis_size(axis)
        forward = [(i, i + 1) for i in range(count - 1)]
        backward = [(target, source) for source, target in forward]
        low = lax.ppermute(
            lax.slice_in_dim(block, block.shape[dim] - width, None, axis=dim), axis, forward
        )
        high = lax.ppermute(lax.slice_in_dim(block, 0, width, axis=dim), axis, backward)
        block = jnp.concatenate([low, block, high], axis=dim)
    return block


def distributed(tod, psi, point_row, hit_list, group_id, a_zero, band_coef, band_lag):
    highest = lax.Precision.HIGHEST
    samples = tod[0]
    angles = psi[0]
    det_count, time_count = samples.shape
    time_blocks = time_count // SBLOCK
    block_count = det_count * time_blocks
    send_table = hit_list[0, 0, 0]
    owner_count, capacity = send_table.shape
    owner_rows = BLOCKS // owner_count
    block_width = 3 * PBLOCK
    detector = lax.axis_index("det") * det_count + jnp.arange(det_count, dtype=jnp.int32)
    within = (jnp.arange(SBLOCK, dtype=jnp.int32)[None, :] + 3 * detector[:, None]) % PBLOCK
    pixel_table = (within[:, :, None] == jnp.arange(PBLOCK, dtype=jnp.int32)[None, None, :]).astype(
        jnp.float32
    )
    cosine_two = jnp.cos(2.0 * angles).reshape(det_count, time_blocks, SBLOCK)
    sine_two = jnp.sin(2.0 * angles).reshape(det_count, time_blocks, SBLOCK)
    slot_ids = send_table.reshape(-1)
    row_source = jnp.concatenate([point_row[0].reshape(-1), jnp.zeros((1,), jnp.int32)])
    slot_rows = row_source[slot_ids].astype(jnp.float32).reshape(owner_count, capacity)
    member = (group_id[0][:, None] == jnp.arange(NSUB, dtype=jnp.int32)[None, :]).astype(
        jnp.float32
    )
    member_count = jnp.sum(member, axis=0)
    lag_table = (
        band_lag[0][:, :, None] == jnp.arange(1, LAG + 1, dtype=jnp.int32)[None, None, :]
    ).astype(jnp.float32)
    lag_weight = jnp.einsum("dj,djl->dl", band_coef[0], lag_table, precision=highest)
    base_weight = a_zero[0]

    def slot_payload(by_block):
        width = by_block.shape[1]
        extended = jnp.concatenate([by_block, jnp.zeros((1, width), by_block.dtype)])
        return extended[slot_ids].reshape(owner_count, capacity, width)

    def deliver(payload):
        width = payload.shape[-1]
        got_values, got_rows = (
            lax.all_to_all(payload, ("det", "wafer"), split_axis=0, concat_axis=0, tiled=True),
            lax.all_to_all(slot_rows, ("det", "wafer"), split_axis=0, concat_axis=0, tiled=True),
        )
        return (got_values, got_rows)

    def back_project(stream, squared):
        shaped = stream.reshape(det_count, time_blocks, SBLOCK)
        first = cosine_two * cosine_two if squared else cosine_two
        second = sine_two * sine_two if squared else sine_two
        stacked = jnp.stack([shaped, first * shaped, second * shaped], axis=2)
        stokes = jnp.einsum("dkcs,dsp->dkcp", stacked, pixel_table, precision=highest)
        return stokes.reshape(block_count, block_width)

    def to_owners(stream, squared):
        got_values, got_rows = deliver(slot_payload(back_project(stream, squared)))
        pair_values, pair_rows = (
            lax.all_gather(got_values, "rep", axis=0, tiled=True),
            lax.all_gather(got_rows, "rep", axis=0, tiled=True),
        )
        target_rows = pair_rows.reshape(-1).astype(jnp.int32)
        summed = (
            jnp.zeros((owner_rows, block_width), jnp.float32)
            .at[target_rows]
            .add(pair_values.reshape(-1, block_width))
        )
        return (summed, got_rows.astype(jnp.int32))

    def remove_common(stream):
        local_sums = jnp.einsum("dg,dt->gt", member, stream, precision=highest)
        group_sums, group_counts = lax.psum((local_sums, member_count), "det")
        group_means = group_sums / jnp.maximum(group_counts, 1.0)[:, None]
        return stream - jnp.einsum("dg,gt->dt", member, group_means, precision=highest)

    def band_filter(stream):
        padded = with_halo(stream, (("rep", 1),), LAG)
        result = base_weight[:, None] * stream
        for offset in range(1, LAG + 1):
            later = padded[:, LAG + offset : LAG + offset + time_count]
            earlier = padded[:, LAG - offset : LAG - offset + time_count]
            result = result + lag_weight[:, offset - 1 : offset] * (later + earlier)
        return result

    def weigh_stream(stream):
        return remove_common(band_filter(remove_common(stream)))

    weight_stream = jnp.broadcast_to(base_weight[:, None], (det_count, time_count))
    diag_sum, serve_rows = to_owners(weight_stream, True)
    inverse_diag = 1.0 / (diag_sum + prior_weight)
    right_side = to_owners(weigh_stream(samples), False)[0]
    solution = jnp.zeros_like(right_side)
    residual = right_side

    def inner(left_map, right_map):
        return lax.psum(jnp.sum(left_map * right_map), ("det", "wafer"))

    precond = inverse_diag * residual
    direction = precond
    energy = inner(residual, precond)
    for iteration in range(ITERS):
        from_blocks = direction[serve_rows.reshape(-1)].reshape(owner_count, capacity, block_width)
        return_width = from_blocks.shape[-1]
        returned = lax.all_to_all(
            from_blocks, ("det", "wafer"), split_axis=0, concat_axis=0, tiled=True
        )
        return_placed = jnp.zeros((block_count + 1, return_width), jnp.float32)
        return_placed = return_placed.at[slot_ids].set(returned.reshape(-1, return_width))
        blocks = return_placed[:block_count].reshape(det_count, time_blocks, 3, PBLOCK)
        project_stokes = jnp.einsum("dkcp,dsp->dkcs", blocks, pixel_table, precision=highest)
        project_stream = (
            project_stokes[:, :, 0]
            + cosine_two * project_stokes[:, :, 1]
            + sine_two * project_stokes[:, :, 2]
        )
        seen_stream = project_stream.reshape(det_count, time_count)
        image_map = to_owners(weigh_stream(seen_stream), False)[0] + prior_weight * direction
        step_size = energy / inner(direction, image_map)
        solution = solution + step_size * direction
        residual = residual - step_size * image_map
        precond = inverse_diag * residual
        energy_next = inner(residual, precond)
        direction = precond + energy_next / energy * direction
        energy = energy_next
    return (solution, residual)


LANES = 128
ROWS = 8
OUT_TILES = 8
PAIR_BATCH = 8
WRITES = 12
DET_BATCH = 8
SUM_SETS = 2
MAP_BATCH = 8
BIG = float(1 << 24)


def wide(values):
    return jnp.broadcast_to(values, (ROWS, LANES))


def tile_iotas():
    lane = lax.broadcasted_iota(jnp.int32, (ROWS, LANES), 1)
    sub = lax.broadcasted_iota(jnp.int32, (ROWS, LANES), 0)
    return lane, sub


def cosine_sine_double(angle):
    turns = jnp.floor(angle * 1.2732395447351628 + 0.5)
    reduced = 2.0 * angle - turns * 1.5703125
    reduced = reduced - turns * 4.837512969970703125e-4
    reduced = reduced - turns * 7.54978995489188216e-8
    square = reduced * reduced
    sine = (-1.9515295891e-4 * square + 8.3321608736e-3) * square - 1.6666654611e-1
    sine = sine * square * reduced + reduced
    cosine = (2.443315711809948e-5 * square - 1.388731625493765e-3) * square
    cosine = (cosine + 4.166664568298827e-2) * square * square - 0.5 * square + 1.0
    quarter = turns.astype(jnp.int32)
    odd = (quarter & 1) == 1
    first = jnp.where(odd, sine, cosine)
    second = jnp.where(odd, cosine, sine)
    first = jnp.where(((quarter + 1) & 2) == 2, -first, first)
    second = jnp.where((quarter & 2) == 2, -second, second)
    return first, second


def pack_kernel(
    shape, angle_ref, tod_ref, row_ref, hit_ref, group_ref, base_ref, coef_ref, lag_ref,
    table_ref, angle_rows_ref, tod_rows_ref,
):
    wafers, dets, reps, tiles, owners, capacity, owner_rows, lag_count = shape
    lane, sub = tile_iotas()
    lists = hit_ref[...]
    owner_hits = jnp.zeros((ROWS, LANES), jnp.float32)
    for c in range(capacity):
        owner_hits = owner_hits + jnp.where(wide(lists[:, c : c + 1]) == lane, 1.0, 0.0)
    owner_of = jnp.sum(owner_hits * sub.astype(jnp.float32), axis=0, keepdims=True)

    def spread(values, width):
        return jnp.concatenate(
            [values, jnp.zeros((values.shape[0], LANES - width), values.dtype)], axis=1
        )

    rows = spread(row_ref[...].astype(jnp.float32), tiles)
    ids = owner_of * float(owner_rows) + rows[0:1]
    for k in range(1, ROWS):
        ids = ids + pltpu.roll(rows[k : k + 1], k * tiles, 1)
    floats = spread(base_ref[...], ROWS)
    whole = spread(group_ref[...].astype(jnp.float32), ROWS)
    for j in range(lag_count):
        at = (j + 1) * ROWS
        floats = floats + pltpu.roll(spread(coef_ref[j : j + 1, :], ROWS), at, 1)
        lag = lag_ref[j : j + 1, :].astype(jnp.float32)
        whole = whole + pltpu.roll(spread(lag, ROWS), at, 1)
    table = jnp.where(sub == 0, wide(ids), jnp.where(sub == 1, wide(floats), wide(whole)))
    table_ref[0] = table
    table_ref[1] = spread(lists.astype(jnp.float32), capacity)
    for b in range(tiles):
        angle_rows_ref[:, b, :] = angle_ref[:, b * LANES : (b + 1) * LANES]
        tod_rows_ref[:, b, :] = tod_ref[:, b * LANES : (b + 1) * LANES]


def part_copies(shape, self_ref, source, target, sem):
    wafers, dets, reps = shape[:3]
    copies = []
    for swap_rep in range(reps):
        for swap_wafer in range(wafers):
            for shift in range(dets):
                det = self_ref[1] - shift
                det = jnp.where(det < 0, det + dets, det)
                device = ((self_ref[0] ^ swap_wafer) * dets + det) * reps
                device = device + (self_ref[2] ^ swap_rep)
                copies.append(
                    pltpu.make_async_copy(
                        source(swap_rep, swap_wafer, shift), target(device), sem.at[len(copies)]
                    )
                )
    return copies


def table_copies(shape, self_ref, source_ref, part_ref, sem):
    wafers, dets, reps = shape[:3]
    copies = []
    for swap_wafer in range(wafers):
        for shift in range(dets):
            det = self_ref[1] - shift
            det = jnp.where(det < 0, det + dets, det)
            device = ((self_ref[0] ^ swap_wafer) * dets + det) * reps
            copies.append(
                pltpu.make_async_copy(
                    source_ref.at[swap_wafer, shift], part_ref.at[pl.ds(device, reps)],
                    sem.at[len(copies)],
                )
            )
    for copy in copies:
        copy.start()
    for copy in copies:
        copy.wait()


def exact_dot(left, right, dims=((1,), (0,))):
    return lax.dot_general(
        left.astype(jnp.bfloat16), right.astype(jnp.bfloat16), (dims, ((), ())),
        preferred_element_type=jnp.float32,
    )


def list_kernel(
    shape, wafer_ref, det_ref, table_ref, float_ref, whole_ref, place_ref, start_ref, move_ref,
    size_ref, pair_ref, group_ref,
    part_ref, column_ref, code_ref, lead_ref, used_ref, rank_ref, hits_ref, part_sem,
):
    self_ref = wafer_ref[0], det_ref[0]
    table_copies(shape, self_ref, table_ref, part_ref, part_sem)
    list_twins(
        shape, float_ref, whole_ref, size_ref, pair_ref, group_ref, part_ref, column_ref, code_ref,
        lead_ref, used_ref,
    )
    list_places(shape, self_ref, place_ref, start_ref, move_ref, part_ref, rank_ref, hits_ref)


def list_twins(
    shape, float_ref, whole_ref, size_ref, pair_ref, group_ref, part_ref, column_ref, code_ref,
    lead_ref, used_ref,
):
    wafers, dets, reps, tiles, owners, capacity, owner_rows, lag_count = shape
    devices = wafers * dets * reps
    total = devices * LANES
    lane, sub = tile_iotas()
    sub_f = sub.astype(jnp.float32)
    none = jnp.full((ROWS, LANES), BIG, jnp.float32)
    along = lax.broadcasted_iota(jnp.int32, (1, LANES), 1).astype(jnp.float32)

    def turn(batch, carry):
        for k in range(4):
            device = 4 * batch + k
            float_ref[pl.ds(device, 1), :] = part_ref[device, 0, 1:2, :]
            whole_ref[pl.ds(device, 1), :] = part_ref[device, 0, 2:3, :].astype(jnp.int32)
            column_ref[device] = jnp.broadcast_to(part_ref[device, 0, 0:1, :], (LANES, LANES)).T
        return carry

    lax.fori_loop(0, devices // 4, turn, 0)

    def survey(device, carry):
        row = wide(part_ref[device, 0, 0:1, :])

        def compare(step, least):
            for k in range(2):
                other = 2 * step + k
                found = [none] * 4
                for j in range(tiles):
                    same = column_ref[other, j * ROWS : (j + 1) * ROWS, :] == row
                    at = jnp.where(same, sub_f + float(j * ROWS), BIG)
                    found[j % 4] = jnp.minimum(found[j % 4], at)
                here = jnp.minimum(jnp.minimum(found[0], found[1]), jnp.minimum(found[2], found[3]))
                least = jnp.minimum(least, here + (other * LANES).astype(jnp.float32))
            return least

        least = lax.fori_loop(0, lax.shift_right_logical(device, 1) + 1, compare, none)
        lead = jnp.min(least, axis=0, keepdims=True)
        mine = (device * LANES).astype(jnp.float32) + along
        later = lead < mine
        code_ref[pl.ds(device, 1), :] = jnp.where(later, mine * float(total) + lead, BIG)
        lead_ref[pl.ds(device, 1), :] = jnp.where(later, lead, BIG)
        return carry

    lax.fori_loop(0, devices, survey, 0)

    def next_code(last):
        found = none
        for tile in range(devices // ROWS):
            codes = code_ref[tile * ROWS : (tile + 1) * ROWS, :]
            found = jnp.minimum(found, jnp.where(codes > last, codes, BIG))
        return jnp.min(found)

    def detector(key):
        team = lax.rem(lax.div(key, reps * LANES), dets)
        return team * ROWS + lax.rem(lax.div(key, tiles), ROWS)

    number_of = [lane + (sub + tile * ROWS) * LANES for tile in range(devices // ROWS)]
    tile_rows = [slice(tile * ROWS, (tile + 1) * ROWS) for tile in range(devices // ROWS)]
    for rows in tile_rows:
        used_ref[rows, :] = jnp.zeros((ROWS, LANES), jnp.int32)

    def take(state):
        pairs, grouped, code = state
        number = code.astype(jnp.int32)
        key = lax.div(number, total)
        lead = lax.rem(number, total)
        shift = (3 * (detector(key) - detector(lead))) & (PBLOCK - 1)
        wanted = lead.astype(jnp.float32)
        same = jnp.zeros((ROWS, LANES), jnp.float32)
        for rows, numbers in zip(tile_rows, number_of):
            same = same + jnp.where(lead_ref[rows, :] == wanted, 1.0, 0.0)
            beside = numbers ^ ROWS
            beside = (beside == key) | (beside == lead)
            same = same + jnp.where(beside & (used_ref[rows, :] > 0), 2.0, 0.0)
        alone = jnp.sum(same) + jnp.where((key ^ lead) == ROWS, 2.0, 0.0) < 1.5
        mark = jnp.where(alone, 1, 0)
        for rows, numbers in zip(tile_rows, number_of):
            listed = (numbers == key) | (numbers == lead)
            used_ref[rows, :] = jnp.where(listed, mark, used_ref[rows, :])
        entry = twin_entry(key, lead, shift)
        pair_ref[pairs] = entry
        group_ref[grouped] = entry
        return (
            pairs + jnp.where(alone, 1, 0), grouped + jnp.where(alone, 0, 1), next_code(code)
        )

    pairs, grouped, _ = lax.while_loop(
        lambda state: state[2] < BIG, take,
        (jnp.int32(0), jnp.int32(0), next_code(jnp.float32(-1.0))),
    )
    batches = lax.div(pairs + PAIR_BATCH - 1, PAIR_BATCH)

    def fill(n, carry):
        pair_ref[n] = twin_entry(total, total + 1, 0)
        return carry

    lax.fori_loop(pairs, batches * PAIR_BATCH, fill, 0)
    size_ref[0] = batches
    size_ref[1] = grouped


def twin_entry(key, lead, shift):
    return key * (1 << 19) + lead * (1 << 6) + shift


def twin_of(entry):
    return entry >> 19, (entry >> 6) & ((1 << 13) - 1), entry & (PBLOCK - 1)


def list_places(shape, self_ref, place_ref, start_ref, move_ref, part_ref, rank_ref, hits_ref):
    wafers, dets, reps, tiles, owners, capacity, owner_rows, lag_count = shape
    devices = wafers * dets * reps
    slots = devices * capacity
    lane, sub = tile_iotas()
    own = self_ref[1] * wafers + self_ref[0]
    first_row = (own * owner_rows).astype(jnp.float32)
    depth = 2 * LANES
    tall = lax.broadcasted_iota(jnp.int32, (depth, LANES), 0).astype(jnp.float32)

    def one_hots(device):
        local_row = part_ref[device, 0, 0:1, :] - first_row
        high = jnp.floor(local_row * (1.0 / LANES))
        low = local_row - high * LANES
        high = (jnp.broadcast_to(high, (depth, LANES)) == tall).astype(jnp.float32)
        low = (jnp.broadcast_to(low, (LANES, LANES)) == tall[0:LANES]).astype(jnp.float32)
        return high, low

    def survey(batch, hits):
        for k in range(4):
            device = 4 * batch + k
            own_hits = jnp.where(sub == own, part_ref[device, 1], 0.0)
            own_hits = jnp.sum(own_hits, axis=0, keepdims=True)
            hits_ref[pl.ds(device, 1), :] = own_hits.astype(jnp.int32)
            high, low = one_hots(device)
            hits = hits + exact_dot(high, low, ((1,), (1,)))
        return hits

    hits = lax.fori_loop(0, devices // 4, survey, jnp.zeros((depth, LANES), jnp.float32))
    full = jnp.minimum(hits, 1.0)

    def ordered(size, axis):
        first = lax.broadcasted_iota(jnp.int32, (size, size), axis)
        second = lax.broadcasted_iota(jnp.int32, (size, size), 1 - axis)
        return (first < second).astype(jnp.float32)

    counts = exact_dot(jnp.ones((ROWS, LANES), jnp.float32), full, ((1,), (1,)))
    start_ref[...] = exact_dot(counts, ordered(depth, 0)).astype(jnp.int32)
    sums = exact_dot(full, jnp.ones((LANES, LANES), jnp.float32))
    place = exact_dot(full, ordered(LANES, 0)) + exact_dot(ordered(depth, 1), sums)
    place_ref[...] = jnp.where(full > 0.0, place, -1.0).astype(jnp.int32)
    place_high = jnp.floor(place * (1.0 / LANES))
    place_parts = jnp.concatenate([place_high, place - place_high * LANES], axis=0)

    def rank_of(batch, carry):
        for k in range(4):
            device = 4 * batch + k
            high, low = one_hots(device)
            parts = exact_dot(place_parts, low)
            rank = high * (parts[0:depth] * LANES + parts[depth : 2 * depth])
            rank = jnp.sum(rank, axis=0, keepdims=True)
            rank_ref[pl.ds(device, 1), :] = rank.astype(jnp.int32)
        return carry

    lax.fori_loop(0, devices // 4, rank_of, 0)
    for tile in range(devices // ROWS):
        rows = slice(tile * ROWS, (tile + 1) * ROWS)
        number = hits_ref[rows, :]
        valid = number < LANES
        number = number & (LANES - 1)
        rank = jnp.take_along_axis(rank_ref[rows, :], number, axis=1, mode="promise_in_bounds")
        target = jnp.where(valid, rank, slots + LANES)
        move_ref[rows, :] = target * (1 << 16) + (tile * ROWS + sub) * LANES + number


def map_kernel(
    shape, wafer_ref, det_ref, rep_ref, size_ref, pair_ref, group_ref, move_ref, float_smem, whole_smem,
    start_ref, angle_here_ref, angle_across_ref, angle_other_ref, tod_here_ref, tod_other_ref,
    place_ref, x_ref, r_ref,
    angle_ref, tod_ref, cos_ref, sin_ref, clean_ref, noise_ref, weight_ref,
    share_ref, rows_ref, sorted_ref, column_ref, write_ref, angle_sem, tod_sem, write_sem, *more_refs,
):
    wafers, dets, reps, tiles, owners, capacity, owner_rows, lag_count = shape
    devices = wafers * dets * reps
    octets = 2 * reps
    wafer_dets = dets * ROWS
    self_ref = wafer_ref[0], det_ref[0], rep_ref[0]
    count = devices * ROWS
    lane, sub = tile_iotas()
    zero = jnp.zeros((ROWS, LANES), jnp.float32)
    low = lane < PBLOCK
    skies = [more_refs[3 * k : 3 * k + 3] for k in range(3 + ITERS)]
    inverse_ref, r_map, image_map, *d_maps = skies
    sum_refs = more_refs[3 * len(skies) :]
    first_sums = [sum_refs[SUM_SETS * wafer : SUM_SETS * (wafer + 1)] for wafer in range(wafers)]
    sum_refs = sum_refs[SUM_SETS * wafers :]
    second_sums = [sum_refs[SUM_SETS * wafer : SUM_SETS * (wafer + 1)] for wafer in range(wafers)]

    def copies_of(source, to_ref, sem):
        return part_copies(
            shape, self_ref, source, lambda d: to_ref.at[pl.ds(d * tiles, tiles)], sem
        )

    def angle_source(swap_rep, swap_wafer, shift):
        if swap_rep:
            return angle_other_ref.at[swap_wafer, shift]
        return (angle_across_ref if swap_wafer else angle_here_ref).at[shift]

    def tod_source(swap_rep, swap_wafer, shift):
        return (tod_other_ref if swap_rep else tod_here_ref).at[shift, swap_wafer]

    angle_moves = copies_of(angle_source, angle_ref, angle_sem)
    tod_moves = copies_of(tod_source, tod_ref, tod_sem)
    for copy in angle_moves + tod_moves:
        copy.start()

    def turn_half(block):
        return pltpu.roll(block, PBLOCK, 1)

    def fold(first, second):
        return jnp.where(low, first, second) + turn_half(jnp.where(low, second, first))

    def unfold(block):
        turned = turn_half(block)
        return jnp.where(low, block, turned), jnp.where(low, turned, block)

    def whole_sum(values):
        values = jnp.sum(values, axis=0, keepdims=True)
        return wide(jnp.sum(values, axis=1, keepdims=True))

    def loop(times, body, carry, unroll):
        def several(n, carry):
            for k in range(unroll):
                carry = body(n * unroll + k, carry)
            return carry

        return lax.fori_loop(0, times // unroll, several, carry)

    def device_of(wafer, n):
        return (wafer * dets + lax.shift_right_logical(n, 3)) * reps

    def group_of(wafer, n):
        return whole_smem[device_of(wafer, n), n & (ROWS - 1)]

    def rows_of(octet):
        return pl.ds(octet * ROWS, ROWS)

    def count_members(n, counts):
        result = []
        for wafer in range(wafers):
            group = group_of(wafer, n)
            result += [
                counts[wafer * NSUB + g] + jnp.where(group == g, 1, 0) for g in range(NSUB)
            ]
        return tuple(result)

    members = lax.fori_loop(0, wafer_dets, count_members, (jnp.int32(0),) * (wafers * NSUB))
    for k, member in enumerate(members):
        share_ref[k] = 1.0 / jnp.maximum(zero + member.astype(jnp.float32), 1.0)
    for c in range(3):
        image_map[c][count] = zero
        r_map[c][count] = zero

    def clear_sorted(n, carry):
        at = pl.ds(pl.multiple_of(n * ROWS, ROWS), ROWS)
        sorted_ref[at, :] = jnp.zeros((ROWS, 2 * LANES), jnp.float32)
        return carry

    lax.fori_loop(0, sorted_ref.shape[0] // ROWS, clear_sorted, 0)

    def spot_of(key):
        return lax.shift_right_logical(key, 4), (key >> 3) & 1, pl.ds(key & (ROWS - 1), 1)

    def in_half(half):
        return (lane[0:1] >> 6) == half

    def set_weight(at, carry):
        weight_ref[at] = zero + 1.0
        return carry

    loop(count, set_weight, 0, 16)

    def drop(list_ref):
        def one(n, carry):
            at, half, row = spot_of(twin_of(list_ref[n])[0])
            weight_ref[at, row, :] = jnp.where(in_half(half), 0.0, weight_ref[at, row, :])
            return carry

        return one

    lax.fori_loop(0, size_ref[0] * PAIR_BATCH, drop(pair_ref), 0)
    lax.fori_loop(0, size_ref[1], drop(group_ref), 0)

    def moved_from(target, spot, shift):
        at, half, row = spot
        result = []
        for ref in target:
            values = wide(ref[at, row, :])
            values = jnp.where((lane >> 6) == half, values, turn_half(values))
            result.append(pltpu.roll(values, shift, 1)[0:1])
        return result

    def merge_twins(target):
        def pair_batch(n, carry):
            found = []
            for k in range(PAIR_BATCH):
                key, lead, shift = twin_of(pair_ref[n * PAIR_BATCH + k])
                key, lead = spot_of(key), spot_of(lead)
                back = (PBLOCK - shift) & (PBLOCK - 1)
                for spot, values in (
                    (lead, moved_from(target, key, shift)), (key, moved_from(target, lead, back))
                ):
                    at, half, row = spot
                    for c in range(3):
                        values[c] = target[c][at, row, :] + jnp.where(in_half(half), values[c], 0.0)
                    found.append((at, row, values))
            for at, row, values in found:
                for c in range(3):
                    target[c][at, row, :] = values[c]
            return carry

        def gather_one(n, carry):
            key, lead, shift = twin_of(group_ref[n])
            values = moved_from(target, spot_of(key), shift)
            at, half, row = spot_of(lead)
            for c in range(3):
                target[c][at, row, :] += jnp.where(in_half(half), values[c], 0.0)
            return carry

        def spread_one(n, carry):
            key, lead, shift = twin_of(group_ref[n])
            values = moved_from(target, spot_of(lead), (PBLOCK - shift) & (PBLOCK - 1))
            at, half, row = spot_of(key)
            for c in range(3):
                target[c][at, row, :] = jnp.where(in_half(half), values[c], target[c][at, row, :])
            return carry

        lax.fori_loop(0, size_ref[0], pair_batch, 0)
        lax.fori_loop(0, size_ref[1], gather_one, 0)
        lax.fori_loop(0, size_ref[1], spread_one, 0)

    for copy in angle_moves:
        copy.wait()

    def survey(at, carry):
        base = float_smem[lax.shift_right_logical(at, 3), at & (ROWS - 1)]
        squares = []
        for half in range(2):
            first, second = cosine_sine_double(angle_ref[2 * at + half])
            cos_ref[2 * at + half] = first
            sin_ref[2 * at + half] = second
            squares.append((base * (first * first), base * (second * second)))
        image_map[0][at] = zero + (base + base)
        for c in range(2):
            image_map[c + 1][at] = fold(squares[0][c], squares[1][c])
        return carry

    loop(count, survey, 0, 8)

    def clear_sums(refs):
        for sets in refs:
            for ref in sets:
                for group in range(NSUB):
                    for octet in range(octets):
                        ref[group, rows_of(octet), :] = zero

    def average(refs):
        for wafer, sets in enumerate(refs):
            for group in range(NSUB):
                for octet in range(octets):
                    total = sets[0][group, rows_of(octet), :]
                    for ref in sets[1:]:
                        total = total + ref[group, rows_of(octet), :]
                    sets[0][group, rows_of(octet), :] = total * share_ref[wafer * NSUB + group]

    def over_detectors(body, carry):
        def several(step, carry):
            for k in range(DET_BATCH):
                carry = body(step * DET_BATCH + k, k % SUM_SETS, carry)
            return carry

        return lax.fori_loop(0, wafer_dets // DET_BATCH, several, carry)

    def sum_streams(streams_of, carry):
        clear_sums(first_sums)

        def one_detector(n, part, carry):
            for wafer in range(wafers):
                group = group_of(wafer, n)
                for rep in range(reps):
                    at = (device_of(wafer, n) + rep) * ROWS + (n & (ROWS - 1))
                    streams, carry = streams_of(at, carry)
                    for half, stream in enumerate(streams):
                        rows = rows_of(2 * rep + half)
                        clean_ref[wafer * wafer_dets + n, rows, :] = stream
                        first_sums[wafer][part][group, rows, :] += stream
            return carry

        carry = over_detectors(one_detector, carry)
        average(first_sums)
        return carry

    def filter_streams():
        clear_sums(second_sums)

        def one_filter(n, part, carry):
            for wafer in range(wafers):
                device, inside = device_of(wafer, n), n & (ROWS - 1)
                detector = wafer * wafer_dets + n
                group = group_of(wafer, n)
                base = float_smem[device, inside]
                coefs = [float_smem[device, (j + 1) * ROWS + inside] for j in range(lag_count)]
                lags = [whole_smem[device, (j + 1) * ROWS + inside] for j in range(lag_count)]
                clean = [
                    clean_ref[detector, rows_of(octet), :]
                    - first_sums[wafer][0][group, rows_of(octet), :]
                    for octet in range(octets)
                ]
                up = [pltpu.roll(here, ROWS - 1, 0) for here in clean] + [zero]
                down = [zero] + [pltpu.roll(here, 1, 0) for here in clean]
                for octet, here in enumerate(clean):
                    after = jnp.where(sub == ROWS - 1, up[octet + 1], up[octet])
                    ahead = jnp.where(sub == 0, down[octet], down[octet + 1])
                    result = base * here
                    for coef, lag in zip(coefs, lags):
                        later = pltpu.roll(jnp.where(lane < lag, after, here), LANES - lag, 1)
                        earlier = pltpu.roll(jnp.where(lane >= LANES - lag, ahead, here), lag, 1)
                        result = result + coef * (later + earlier)
                    noise_ref[detector, rows_of(octet), :] = result
                    second_sums[wafer][part][group, rows_of(octet), :] += result
                    carry = carry + here * result
            return carry

        product = over_detectors(one_filter, zero)
        average(second_sums)
        return product

    def return_streams(target):
        def one_return(n, part, carry):
            for wafer in range(wafers):
                group = group_of(wafer, n)
                for rep in range(reps):
                    at = (device_of(wafer, n) + rep) * ROWS + (n & (ROWS - 1))
                    streams = []
                    for half in range(2):
                        rows = rows_of(2 * rep + half)
                        stream = noise_ref[wafer * wafer_dets + n, rows, :]
                        streams.append(stream - second_sums[wafer][0][group, rows, :])
                    target[0][at] = fold(*streams)
                    for c, ref in ((1, cos_ref), (2, sin_ref)):
                        target[c][at] = fold(*(ref[2 * at + h] * streams[h] for h in range(2)))
            return carry

        over_detectors(one_return, 0)
        merge_twins(target)

    merge_twins(image_map)
    for copy in tod_moves:
        copy.wait()
    sum_streams(lambda at, carry: ([tod_ref[2 * at + half] for half in range(2)], carry), 0)
    filter_streams()
    return_streams(r_map)

    factor = zero
    steps = []
    width = OUT_TILES * LANES
    out_steps = x_ref.shape[1] // width
    depth = lax.broadcasted_iota(jnp.int32, (LANES, LANES), 0)

    def solution_at(at):
        result = []
        for c in range(3):
            value = steps[0] * d_maps[0][c][at]
            for k in range(1, ITERS):
                value = value + steps[k] * d_maps[k][c][at]
            result.append(value)
        return result

    def copy_out(out_ref, block, slot):
        to = pl.ds(pl.multiple_of(block * width, width), width)
        return pltpu.make_async_copy(write_ref.at[slot], out_ref.at[:, to], write_sem.at[slot])

    def write_map(out_ref, order, values_of):
        def place_pixels(at, carry):
            team = lax.rem(lax.div(at, reps * ROWS), dets)
            turn = (3 * (team * ROWS + (at & (ROWS - 1)))) & (PBLOCK - 1)
            inside = (lane & (PBLOCK - 1)) >= turn
            left, right, third = values_of(at)
            halves = jnp.where(low, left, turn_half(right)), jnp.where(low, turn_half(left), right)
            for half, (value, other) in enumerate(zip(halves, unfold(third))):
                value = jnp.where(
                    inside, pltpu.roll(value, turn, 1), pltpu.roll(value, turn + PBLOCK, 1)
                )
                rows = pl.ds(pl.multiple_of((2 * at + half) * ROWS, ROWS), ROWS)
                rows_ref[rows, 0:LANES] = value
                rows_ref[rows, LANES : 2 * LANES] = pltpu.roll(other, turn, 1)
            return carry

        loop(count, place_pixels, 0, 16)

        def pick(device, carry):
            for c in range(capacity):
                move = move_ref[device, c]
                source, target = move & ((1 << 16) - 1), move >> 16
                sorted_ref[pl.ds(target, 1), :] = rows_ref[pl.ds(source, 1), :]
            return carry

        lax.fori_loop(0, devices, pick, 0)
        for tile in range(column_ref.shape[0]):
            columns = sorted_ref[tile * LANES : (tile + 1) * LANES, :].T[0 : 3 * PBLOCK]
            high = columns.astype(jnp.bfloat16)
            column_ref[tile, :, 0:LANES] = high
            column_ref[tile, :, LANES : 2 * LANES] = (columns - high.astype(jnp.float32)).astype(
                jnp.bfloat16
            )

        def spread(group, tile):
            chosen = []
            for k in range(OUT_TILES):
                place = jnp.broadcast_to(place_ref[pl.ds(group + k, 1), :], (LANES, LANES))
                place = jnp.where(place == depth + tile * LANES, 1.0, 0.0)
                chosen.append(place.astype(jnp.bfloat16))
            chosen = jnp.concatenate(chosen, axis=1)
            chosen = jnp.concatenate([chosen, chosen], axis=0)
            return jnp.dot(column_ref[tile], chosen, preferred_element_type=jnp.float32)

        def one_block(block, carry):
            number = order * out_steps + block
            slot = lax.rem(number, WRITES)

            @pl.when(number >= WRITES)
            def _():
                copy_out(out_ref, block, slot).wait()

            group = block * OUT_TILES
            start, end = start_ref[0, group], start_ref[0, group + OUT_TILES]
            first = lax.shift_right_logical(start, 7)
            last = lax.shift_right_logical(jnp.maximum(end - 1, start), 7)
            write_ref[slot] = spread(group, first)

            def add_tile(tile, carry):
                write_ref[slot] += spread(group, tile)
                return carry

            lax.fori_loop(first + 1, last + 1, add_tile, 0)
            copy_out(out_ref, block, slot).start()
            return carry

        lax.fori_loop(0, out_steps, one_block, 0)

    for iteration, d_map in enumerate(d_maps):
        last = iteration == ITERS - 1

        def seen_streams(at, carry):
            prior, energy = carry
            squares, products = zero, zero
            streams = [None, None]
            for c in range(3):
                residual = r_map[c][at]
                if iteration:
                    part = inverse_ref[c][at] * residual + factor * d_maps[iteration - 1][c][at]
                else:
                    inverse = 1.0 / (image_map[c][at] + prior_weight)
                    inverse_ref[c][at] = inverse
                    part = inverse * residual
                    products = products + residual * part
                d_map[c][at] = part
                squares = squares + part * part
                for half, seen in enumerate(unfold(part)):
                    if c == 0:
                        streams[half] = seen
                    else:
                        ref = cos_ref if c == 1 else sin_ref
                        streams[half] = streams[half] + ref[2 * at + half] * seen
            weight = weight_ref[at]
            if not iteration:
                energy = energy + weight * products
            return streams, (prior + weight * squares, energy)

        prior, first_energy = sum_streams(seen_streams, (zero, zero))
        if not iteration:
            energy = whole_sum(first_energy)
        product = filter_streams()
        step = energy / whole_sum(product + prior_weight * prior)
        steps.append(step)
        if last:
            write_map(x_ref, 0, solution_at)
        return_streams(image_map)

        def new_residual(at, c):
            return r_map[c][at] - step * (image_map[c][at] + prior_weight * d_map[c][at])

        if not last:

            def update(batch, carry):
                found = []
                for k in range(MAP_BATCH):
                    at = batch * MAP_BATCH + k
                    residual = [new_residual(at, c) for c in range(3)]
                    parts = zero
                    for c in range(3):
                        parts = parts + residual[c] * (inverse_ref[c][at] * residual[c])
                    carry = carry + weight_ref[at] * parts
                    found.append((at, residual))
                for at, residual in found:
                    for c in range(3):
                        r_map[c][at] = residual[c]
                return carry

            next_energy = whole_sum(loop(count // MAP_BATCH, update, zero, 2))
            factor = next_energy / energy
            energy = next_energy
        else:
            write_map(r_ref, 1, lambda at: [new_residual(at, c) for c in range(3)])
    for block in range(WRITES):
        copy_out(r_ref, out_steps - WRITES + block, (2 * out_steps - WRITES + block) % WRITES).wait()


def part_shape(sizes, tod, hit_list, band_lag):
    det_count, time_count = tod.shape[1:]
    owners, capacity = hit_list.shape[3:]
    return (
        sizes["wafer"], sizes["det"], sizes["rep"], time_count // SBLOCK,
        owners, capacity, BLOCKS // owners, band_lag.shape[2],
    ), det_count


def fits_one_device(shape, det_count):
    wafers, dets, reps, tiles, owners, capacity, owner_rows, lag_count = shape
    devices = wafers * dets * reps
    total = devices * tiles * det_count
    groups = owner_rows // LANES
    return (
        det_count == ROWS
        and owners == ROWS
        and tiles * ROWS == LANES
        and tiles == 2 * ROWS
        and (wafers, reps) == (2, 2)
        and (1 + lag_count) * ROWS <= LANES
        and capacity <= LANES
        and devices * capacity % LANES == 0
        and owner_rows % (LANES * OUT_TILES) == 0
        and owner_rows >= LANES * OUT_TILES * WRITES
        and groups + 1 <= 2 * LANES
        and devices % ROWS == 0
        and dets % (DET_BATCH // ROWS) == 0
        and total * total < BIG
    )


def whole_part(shape, tod, psi, point_row, hit_list, group_id, a_zero, band_coef, band_lag):
    wafers, dets, reps, tiles, owners, capacity, owner_rows, lag_count = shape
    devices = wafers * dets * reps
    octets = reps * tiles // ROWS
    detectors = wafers * dets * ROWS
    count = devices * tiles
    total = count * ROWS
    slots = devices * capacity
    height = 3 * PBLOCK
    f32, i32 = jnp.float32, jnp.int32
    vmem, smem = pl.BlockSpec(memory_space=pltpu.VMEM), pl.BlockSpec(memory_space=pltpu.SMEM)
    anywhere = pl.BlockSpec(memory_space=pl.ANY)

    def params(mebibytes):
        return pltpu.CompilerParams(vmem_limit_bytes=mebibytes << 20)

    swap = [(0, 1), (1, 0)]

    def along_det(block):
        moved = [
            lax.ppermute(block, "det", [(i, (i + shift) % dets) for i in range(dets)])
            for shift in range(1, dets)
        ]
        return [block] + moved

    def other_wafer(here):
        return lax.ppermute(here, "wafer", swap)

    def other_rep(here, across):
        return here, across, lax.ppermute(jnp.stack([here, across]), "rep", swap)

    tables, angles, samples = pl.pallas_call(
        functools.partial(pack_kernel, shape),
        out_shape=[
            jax.ShapeDtypeStruct((2, ROWS, LANES), f32),
            jax.ShapeDtypeStruct((ROWS, tiles, LANES), f32),
            jax.ShapeDtypeStruct((ROWS, tiles, LANES), f32),
        ],
        in_specs=[vmem] * 8,
        out_specs=[vmem] * 3,
        compiler_params=params(60),
        name="pack",
    )(
        psi[0], tod[0], point_row[0], hit_list[0, 0, 0], group_id, a_zero, band_coef[0].T,
        band_lag[0].T,
    )
    angles, samples = (stream.reshape(tiles, ROWS, LANES) for stream in (angles, samples))
    place_here = [
        lax.axis_index(axis).astype(i32).reshape(1) for axis in ("wafer", "det", "rep")
    ]
    tables = lax.all_gather(tables, "rep", axis=0, tiled=False)
    riders = jnp.concatenate([angles, tables.reshape(2 * reps, ROWS, LANES)])
    samples, riders = lax.optimization_barrier((samples, riders))
    samples = jnp.stack([samples, other_wafer(samples)])
    blocks = along_det(riders)
    samples = along_det(samples)
    tables = jnp.stack([block[tiles:] for block in blocks])
    angles = jnp.stack([block[:tiles] for block in blocks])
    tables = jnp.stack([tables, other_wafer(tables)])
    tables = tables.reshape(wafers, dets, reps, 2, ROWS, LANES)
    angles, tables = lax.optimization_barrier((angles, tables))
    angles_across = other_wafer(angles)
    table_rows = jax.ShapeDtypeStruct((devices, LANES), i32)
    lists = pl.pallas_call(
        functools.partial(list_kernel, shape),
        out_shape=[
            jax.ShapeDtypeStruct((devices, LANES), f32),
            table_rows,
            jax.ShapeDtypeStruct((2 * LANES, LANES), i32),
            jax.ShapeDtypeStruct((ROWS, 2 * LANES), i32),
            table_rows,
            jax.ShapeDtypeStruct((2,), i32),
            jax.ShapeDtypeStruct((total,), i32),
            jax.ShapeDtypeStruct((total,), i32),
        ],
        in_specs=[smem, smem, anywhere],
        out_specs=[vmem] * 5 + [smem] * 3,
        scratch_shapes=[
            pltpu.VMEM((devices, 2, ROWS, LANES), f32),
            pltpu.VMEM((devices, LANES, LANES), f32),
            pltpu.VMEM((devices, LANES), f32),
            pltpu.VMEM((devices, LANES), f32),
            pltpu.VMEM((devices, LANES), i32),
            pltpu.VMEM((devices, LANES), i32),
            pltpu.VMEM((devices, LANES), i32),
            pltpu.SemaphoreType.DMA((devices,)),
        ],
        compiler_params=params(8),
        cost_estimate=pl.CostEstimate(flops=10**6, bytes_accessed=10**6, transcendentals=0),
        name="lists",
    )(*place_here[:2], tables)
    angles, angles_across, samples, lists = lax.optimization_barrier(
        (angles, angles_across, samples, lists)
    )
    floats, whole, place, start, moves, size, pair, group = lists
    angle_blocks = other_rep(angles, angles_across)
    samples = jnp.stack(samples)
    sample_blocks = samples, lax.ppermute(samples, "rep", swap)
    stream = pltpu.VMEM((count, ROWS, LANES), f32)
    sky = pltpu.VMEM((devices * ROWS + 1, ROWS, LANES), f32)
    group_sums = pltpu.VMEM((NSUB, octets * ROWS, LANES), f32)
    x_turned, r_turned = pl.pallas_call(
        functools.partial(map_kernel, shape),
        out_shape=[jax.ShapeDtypeStruct((height, owner_rows), f32)] * 2,
        in_specs=[smem] * 10 + [anywhere] * 5 + [vmem],
        out_specs=[anywhere] * 2,
        scratch_shapes=[
            stream, stream, stream, stream,
            pltpu.VMEM((detectors, octets * ROWS, LANES), f32),
            pltpu.VMEM((detectors, octets * ROWS, LANES), f32),
            sky,
            pltpu.VMEM((wafers * NSUB, ROWS, LANES), f32),
            pltpu.VMEM((total, 2 * LANES), f32),
            pltpu.VMEM((slots + LANES + ROWS, 2 * LANES), f32),
            pltpu.VMEM((slots // LANES + 1, height, 2 * LANES), jnp.bfloat16),
            pltpu.VMEM((WRITES, height, OUT_TILES * LANES), f32),
            pltpu.SemaphoreType.DMA((devices,)),
            pltpu.SemaphoreType.DMA((devices,)),
            pltpu.SemaphoreType.DMA((WRITES,)),
        ] + [sky] * (3 * (3 + ITERS)) + [group_sums] * (2 * wafers * SUM_SETS),
        compiler_params=params(40),
        name="map_maker",
    )(
        *place_here, size, pair, group, moves, floats, whole, start, *angle_blocks,
        *sample_blocks, place,
    )
    return x_turned.T, r_turned.T


def local(sizes, *arguments):
    tod, hit_list, band_lag = arguments[0], arguments[3], arguments[7]
    shape, det_count = part_shape(sizes, tod, hit_list, band_lag)
    if fits_one_device(shape, det_count):
        return whole_part(shape, *arguments)
    return distributed(*arguments)


def solution(mesh):
    placed = (
        P(("groups", "wafer"), "det", "rep"),
        P(("groups", "wafer"), "det", "rep"),
        P(("groups", "wafer"), "det", "rep"),
        P(("groups", "wafer"), "det", "rep", None, None),
        P(("groups", "wafer"), "det"),
        P(("groups", "wafer"), "det"),
        P(("groups", "wafer"), "det", None),
        P(("groups", "wafer"), "det", None),
    )
    return jax.shard_map(
        functools.partial(local, mesh.shape),
        mesh=mesh,
        in_specs=placed,
        out_specs=(P(("groups", "det", "wafer"), None), P(("groups", "det", "wafer"), None)),
        check_vma=False,
    )
```

```python
import functools

import jax
import jax.numpy as jnp
from jax import lax
from jax.experimental import pallas as pl
from jax.experimental.pallas import tpu as pltpu
from jax.sharding import PartitionSpec as P

BLOCKS = 196608
PBLOCK = 64
SBLOCK = 128
NSUB = 4
LAG = 16
ITERS = 3


prior_weight = 1.0


def with_halo(block, sides, width):
    for axis, dim in sides:
        count = lax.axis_size(axis)
        forward = [(i, i + 1) for i in range(count - 1)]
        backward = [(target, source) for source, target in forward]
        low = lax.ppermute(
            lax.slice_in_dim(block, block.shape[dim] - width, None, axis=dim), axis, forward
        )
        high = lax.ppermute(lax.slice_in_dim(block, 0, width, axis=dim), axis, backward)
        block = jnp.concatenate([low, block, high], axis=dim)
    return block


def distributed(tod, psi, point_row, hit_list, group_id, a_zero, band_coef, band_lag):
    highest = lax.Precision.HIGHEST
    samples = tod[0]
    angles = psi[0]
    det_count, time_count = samples.shape
    time_blocks = time_count // SBLOCK
    block_count = det_count * time_blocks
    send_table = hit_list[0, 0, 0]
    owner_count, capacity = send_table.shape
    owner_rows = BLOCKS // owner_count
    block_width = 3 * PBLOCK
    detector = lax.axis_index("det") * det_count + jnp.arange(det_count, dtype=jnp.int32)
    within = (jnp.arange(SBLOCK, dtype=jnp.int32)[None, :] + 3 * detector[:, None]) % PBLOCK
    pixel_table = (within[:, :, None] == jnp.arange(PBLOCK, dtype=jnp.int32)[None, None, :]).astype(
        jnp.float32
    )
    cosine_two = jnp.cos(2.0 * angles).reshape(det_count, time_blocks, SBLOCK)
    sine_two = jnp.sin(2.0 * angles).reshape(det_count, time_blocks, SBLOCK)
    slot_ids = send_table.reshape(-1)
    row_source = jnp.concatenate([point_row[0].reshape(-1), jnp.zeros((1,), jnp.int32)])
    slot_rows = row_source[slot_ids].astype(jnp.float32).reshape(owner_count, capacity)
    member = (group_id[0][:, None] == jnp.arange(NSUB, dtype=jnp.int32)[None, :]).astype(
        jnp.float32
    )
    member_count = jnp.sum(member, axis=0)
    lag_table = (
        band_lag[0][:, :, None] == jnp.arange(1, LAG + 1, dtype=jnp.int32)[None, None, :]
    ).astype(jnp.float32)
    lag_weight = jnp.einsum("dj,djl->dl", band_coef[0], lag_table, precision=highest)
    base_weight = a_zero[0]

    def slot_payload(by_block):
        width = by_block.shape[1]
        extended = jnp.concatenate([by_block, jnp.zeros((1, width), by_block.dtype)])
        return extended[slot_ids].reshape(owner_count, capacity, width)

    def deliver(payload):
        width = payload.shape[-1]
        got_values, got_rows = (
            lax.all_to_all(payload, ("det", "wafer"), split_axis=0, concat_axis=0, tiled=True),
            lax.all_to_all(slot_rows, ("det", "wafer"), split_axis=0, concat_axis=0, tiled=True),
        )
        return (got_values, got_rows)

    def back_project(stream, squared):
        shaped = stream.reshape(det_count, time_blocks, SBLOCK)
        first = cosine_two * cosine_two if squared else cosine_two
        second = sine_two * sine_two if squared else sine_two
        stacked = jnp.stack([shaped, first * shaped, second * shaped], axis=2)
        stokes = jnp.einsum("dkcs,dsp->dkcp", stacked, pixel_table, precision=highest)
        return stokes.reshape(block_count, block_width)

    def to_owners(stream, squared):
        got_values, got_rows = deliver(slot_payload(back_project(stream, squared)))
        pair_values, pair_rows = (
            lax.all_gather(got_values, "rep", axis=0, tiled=True),
            lax.all_gather(got_rows, "rep", axis=0, tiled=True),
        )
        target_rows = pair_rows.reshape(-1).astype(jnp.int32)
        summed = (
            jnp.zeros((owner_rows, block_width), jnp.float32)
            .at[target_rows]
            .add(pair_values.reshape(-1, block_width))
        )
        return (summed, got_rows.astype(jnp.int32))

    def remove_common(stream):
        local_sums = jnp.einsum("dg,dt->gt", member, stream, precision=highest)
        group_sums, group_counts = lax.psum((local_sums, member_count), "det")
        group_means = group_sums / jnp.maximum(group_counts, 1.0)[:, None]
        return stream - jnp.einsum("dg,gt->dt", member, group_means, precision=highest)

    def band_filter(stream):
        padded = with_halo(stream, (("rep", 1),), LAG)
        result = base_weight[:, None] * stream
        for offset in range(1, LAG + 1):
            later = padded[:, LAG + offset : LAG + offset + time_count]
            earlier = padded[:, LAG - offset : LAG - offset + time_count]
            result = result + lag_weight[:, offset - 1 : offset] * (later + earlier)
        return result

    def weigh_stream(stream):
        return remove_common(band_filter(remove_common(stream)))

    weight_stream = jnp.broadcast_to(base_weight[:, None], (det_count, time_count))
    diag_sum, serve_rows = to_owners(weight_stream, True)
    inverse_diag = 1.0 / (diag_sum + prior_weight)
    right_side = to_owners(weigh_stream(samples), False)[0]
    solution = jnp.zeros_like(right_side)
    residual = right_side

    def inner(left_map, right_map):
        return lax.psum(jnp.sum(left_map * right_map), ("det", "wafer"))

    precond = inverse_diag * residual
    direction = precond
    energy = inner(residual, precond)
    for iteration in range(ITERS):
        from_blocks = direction[serve_rows.reshape(-1)].reshape(owner_count, capacity, block_width)
        return_width = from_blocks.shape[-1]
        returned = lax.all_to_all(
            from_blocks, ("det", "wafer"), split_axis=0, concat_axis=0, tiled=True
        )
        return_placed = jnp.zeros((block_count + 1, return_width), jnp.float32)
        return_placed = return_placed.at[slot_ids].set(returned.reshape(-1, return_width))
        blocks = return_placed[:block_count].reshape(det_count, time_blocks, 3, PBLOCK)
        project_stokes = jnp.einsum("dkcp,dsp->dkcs", blocks, pixel_table, precision=highest)
        project_stream = (
            project_stokes[:, :, 0]
            + cosine_two * project_stokes[:, :, 1]
            + sine_two * project_stokes[:, :, 2]
        )
        seen_stream = project_stream.reshape(det_count, time_count)
        image_map = to_owners(weigh_stream(seen_stream), False)[0] + prior_weight * direction
        step_size = energy / inner(direction, image_map)
        solution = solution + step_size * direction
        residual = residual - step_size * image_map
        precond = inverse_diag * residual
        energy_next = inner(residual, precond)
        direction = precond + energy_next / energy * direction
        energy = energy_next
    return (solution, residual)


LANES = 128
ROWS = 8
OUT_TILES = 8
PAIR_BATCH = 8
WRITES = 6
DET_BATCH = 8
SUM_SETS = 2
MAP_BATCH = 8
BIG = float(1 << 24)


def wide(values):
    return jnp.broadcast_to(values, (ROWS, LANES))


def tile_iotas():
    lane = lax.broadcasted_iota(jnp.int32, (ROWS, LANES), 1)
    sub = lax.broadcasted_iota(jnp.int32, (ROWS, LANES), 0)
    return lane, sub


def cosine_sine_double(angle):
    turns = jnp.floor(angle * 1.2732395447351628 + 0.5)
    reduced = 2.0 * angle - turns * 1.5703125
    reduced = reduced - turns * 4.837512969970703125e-4
    reduced = reduced - turns * 7.54978995489188216e-8
    square = reduced * reduced
    sine = (-1.9515295891e-4 * square + 8.3321608736e-3) * square - 1.6666654611e-1
    sine = sine * square * reduced + reduced
    cosine = (2.443315711809948e-5 * square - 1.388731625493765e-3) * square
    cosine = (cosine + 4.166664568298827e-2) * square * square - 0.5 * square + 1.0
    quarter = turns.astype(jnp.int32)
    odd = (quarter & 1) == 1
    first = jnp.where(odd, sine, cosine)
    second = jnp.where(odd, cosine, sine)
    first = jnp.where(((quarter + 1) & 2) == 2, -first, first)
    second = jnp.where((quarter & 2) == 2, -second, second)
    return first, second


def pack_kernel(
    shape, angle_ref, tod_ref, row_ref, hit_ref, group_ref, base_ref, coef_ref, lag_ref,
    table_ref, angle_rows_ref, tod_rows_ref,
):
    wafers, dets, reps, tiles, owners, capacity, owner_rows, lag_count = shape
    lane, sub = tile_iotas()
    lists = hit_ref[...]
    owner_hits = jnp.zeros((ROWS, LANES), jnp.float32)
    for c in range(capacity):
        owner_hits = owner_hits + jnp.where(wide(lists[:, c : c + 1]) == lane, 1.0, 0.0)
    owner_of = jnp.sum(owner_hits * sub.astype(jnp.float32), axis=0, keepdims=True)

    def spread(values, width):
        return jnp.concatenate(
            [values, jnp.zeros((values.shape[0], LANES - width), values.dtype)], axis=1
        )

    rows = spread(row_ref[...].astype(jnp.float32), tiles)
    ids = owner_of * float(owner_rows) + rows[0:1]
    for k in range(1, ROWS):
        ids = ids + pltpu.roll(rows[k : k + 1], k * tiles, 1)
    floats = spread(base_ref[...], ROWS)
    whole = spread(group_ref[...].astype(jnp.float32), ROWS)
    for j in range(lag_count):
        at = (j + 1) * ROWS
        floats = floats + pltpu.roll(spread(coef_ref[j : j + 1, :], ROWS), at, 1)
        lag = lag_ref[j : j + 1, :].astype(jnp.float32)
        whole = whole + pltpu.roll(spread(lag, ROWS), at, 1)
    table = jnp.where(sub == 0, wide(ids), jnp.where(sub == 1, wide(floats), wide(whole)))
    table_ref[0] = table
    table_ref[1] = spread(lists.astype(jnp.float32), capacity)
    for b in range(tiles):
        angle_rows_ref[:, b, :] = angle_ref[:, b * LANES : (b + 1) * LANES]
        tod_rows_ref[:, b, :] = tod_ref[:, b * LANES : (b + 1) * LANES]


def part_copies(shape, self_ref, source, target, sem):
    wafers, dets, reps = shape[:3]
    copies = []
    for swap_rep in range(reps):
        for swap_wafer in range(wafers):
            for shift in range(dets):
                det = self_ref[1] - shift
                det = jnp.where(det < 0, det + dets, det)
                device = ((self_ref[0] ^ swap_wafer) * dets + det) * reps
                device = device + (self_ref[2] ^ swap_rep)
                copies.append(
                    pltpu.make_async_copy(
                        source(swap_rep, swap_wafer, shift), target(device), sem.at[len(copies)]
                    )
                )
    return copies


def table_copies(shape, self_ref, source_ref, part_ref, sem):
    wafers, dets, reps = shape[:3]
    copies = []
    for swap_wafer in range(wafers):
        for shift in range(dets):
            det = self_ref[1] - shift
            det = jnp.where(det < 0, det + dets, det)
            device = ((self_ref[0] ^ swap_wafer) * dets + det) * reps
            copies.append(
                pltpu.make_async_copy(
                    source_ref.at[shift, swap_wafer], part_ref.at[pl.ds(device, reps)],
                    sem.at[len(copies)],
                )
            )
    for copy in copies:
        copy.start()
    for copy in copies:
        copy.wait()


def exact_dot(left, right, dims=((1,), (0,))):
    return lax.dot_general(
        left.astype(jnp.bfloat16), right.astype(jnp.bfloat16), (dims, ((), ())),
        preferred_element_type=jnp.float32,
    )


def list_kernel(
    shape, wafer_ref, det_ref, table_ref, float_ref, whole_ref, place_ref, start_ref, move_ref,
    size_ref, pair_ref, group_ref,
    part_ref, column_ref, code_ref, lead_ref, used_ref, rank_ref, hits_ref, part_sem,
):
    self_ref = wafer_ref[0], det_ref[0]
    table_copies(shape, self_ref, table_ref, part_ref, part_sem)
    list_twins(
        shape, float_ref, whole_ref, size_ref, pair_ref, group_ref, part_ref, column_ref, code_ref,
        lead_ref, used_ref,
    )
    list_places(shape, self_ref, place_ref, start_ref, move_ref, part_ref, rank_ref, hits_ref)


def list_twins(
    shape, float_ref, whole_ref, size_ref, pair_ref, group_ref, part_ref, column_ref, code_ref,
    lead_ref, used_ref,
):
    wafers, dets, reps, tiles, owners, capacity, owner_rows, lag_count = shape
    devices = wafers * dets * reps
    total = devices * LANES
    lane, sub = tile_iotas()
    sub_f = sub.astype(jnp.float32)
    none = jnp.full((ROWS, LANES), BIG, jnp.float32)
    along = lax.broadcasted_iota(jnp.int32, (1, LANES), 1).astype(jnp.float32)

    def turn(batch, carry):
        for k in range(4):
            device = 4 * batch + k
            float_ref[pl.ds(device, 1), :] = part_ref[device, 0, 1:2, :]
            whole_ref[pl.ds(device, 1), :] = part_ref[device, 0, 2:3, :].astype(jnp.int32)
            column_ref[device] = jnp.broadcast_to(part_ref[device, 0, 0:1, :], (LANES, LANES)).T
        return carry

    lax.fori_loop(0, devices // 4, turn, 0)

    def survey(device, carry):
        row = wide(part_ref[device, 0, 0:1, :])

        def compare(step, least):
            for k in range(2):
                other = 2 * step + k
                found = [none] * 4
                for j in range(tiles):
                    same = column_ref[other, j * ROWS : (j + 1) * ROWS, :] == row
                    at = jnp.where(same, sub_f + float(j * ROWS), BIG)
                    found[j % 4] = jnp.minimum(found[j % 4], at)
                here = jnp.minimum(jnp.minimum(found[0], found[1]), jnp.minimum(found[2], found[3]))
                least = jnp.minimum(least, here + (other * LANES).astype(jnp.float32))
            return least

        least = lax.fori_loop(0, lax.shift_right_logical(device, 1) + 1, compare, none)
        lead = jnp.min(least, axis=0, keepdims=True)
        mine = (device * LANES).astype(jnp.float32) + along
        later = lead < mine
        code_ref[pl.ds(device, 1), :] = jnp.where(later, mine * float(total) + lead, BIG)
        lead_ref[pl.ds(device, 1), :] = jnp.where(later, lead, BIG)
        return carry

    lax.fori_loop(0, devices, survey, 0)

    def next_code(last):
        found = none
        for tile in range(devices // ROWS):
            codes = code_ref[tile * ROWS : (tile + 1) * ROWS, :]
            found = jnp.minimum(found, jnp.where(codes > last, codes, BIG))
        return jnp.min(found)

    def detector(key):
        team = lax.rem(lax.div(key, reps * LANES), dets)
        return team * ROWS + lax.rem(lax.div(key, tiles), ROWS)

    number_of = [lane + (sub + tile * ROWS) * LANES for tile in range(devices // ROWS)]
    tile_rows = [slice(tile * ROWS, (tile + 1) * ROWS) for tile in range(devices // ROWS)]
    for rows in tile_rows:
        used_ref[rows, :] = jnp.zeros((ROWS, LANES), jnp.int32)

    def take(state):
        pairs, grouped, code = state
        number = code.astype(jnp.int32)
        key = lax.div(number, total)
        lead = lax.rem(number, total)
        shift = (3 * (detector(key) - detector(lead))) & (PBLOCK - 1)
        wanted = lead.astype(jnp.float32)
        same = jnp.zeros((ROWS, LANES), jnp.float32)
        for rows, numbers in zip(tile_rows, number_of):
            same = same + jnp.where(lead_ref[rows, :] == wanted, 1.0, 0.0)
            beside = numbers ^ ROWS
            beside = (beside == key) | (beside == lead)
            same = same + jnp.where(beside & (used_ref[rows, :] > 0), 2.0, 0.0)
        alone = jnp.sum(same) + jnp.where((key ^ lead) == ROWS, 2.0, 0.0) < 1.5
        mark = jnp.where(alone, 1, 0)
        for rows, numbers in zip(tile_rows, number_of):
            listed = (numbers == key) | (numbers == lead)
            used_ref[rows, :] = jnp.where(listed, mark, used_ref[rows, :])
        entry = twin_entry(key, lead, shift)
        pair_ref[pairs] = entry
        group_ref[grouped] = entry
        return (
            pairs + jnp.where(alone, 1, 0), grouped + jnp.where(alone, 0, 1), next_code(code)
        )

    pairs, grouped, _ = lax.while_loop(
        lambda state: state[2] < BIG, take,
        (jnp.int32(0), jnp.int32(0), next_code(jnp.float32(-1.0))),
    )
    batches = lax.div(pairs + PAIR_BATCH - 1, PAIR_BATCH)

    def fill(n, carry):
        pair_ref[n] = twin_entry(total, total + 1, 0)
        return carry

    lax.fori_loop(pairs, batches * PAIR_BATCH, fill, 0)
    size_ref[0] = batches
    size_ref[1] = grouped


def twin_entry(key, lead, shift):
    return key * (1 << 19) + lead * (1 << 6) + shift


def twin_of(entry):
    return entry >> 19, (entry >> 6) & ((1 << 13) - 1), entry & (PBLOCK - 1)


def list_places(shape, self_ref, place_ref, start_ref, move_ref, part_ref, rank_ref, hits_ref):
    wafers, dets, reps, tiles, owners, capacity, owner_rows, lag_count = shape
    devices = wafers * dets * reps
    slots = devices * capacity
    lane, sub = tile_iotas()
    own = self_ref[1] * wafers + self_ref[0]
    first_row = (own * owner_rows).astype(jnp.float32)
    depth = 2 * LANES
    tall = lax.broadcasted_iota(jnp.int32, (depth, LANES), 0).astype(jnp.float32)

    def one_hots(device):
        local_row = part_ref[device, 0, 0:1, :] - first_row
        high = jnp.floor(local_row * (1.0 / LANES))
        low = local_row - high * LANES
        high = (jnp.broadcast_to(high, (depth, LANES)) == tall).astype(jnp.float32)
        low = (jnp.broadcast_to(low, (LANES, LANES)) == tall[0:LANES]).astype(jnp.float32)
        return high, low

    def survey(batch, hits):
        for k in range(4):
            device = 4 * batch + k
            own_hits = jnp.where(sub == own, part_ref[device, 1], 0.0)
            own_hits = jnp.sum(own_hits, axis=0, keepdims=True)
            hits_ref[pl.ds(device, 1), :] = own_hits.astype(jnp.int32)
            high, low = one_hots(device)
            hits = hits + exact_dot(high, low, ((1,), (1,)))
        return hits

    hits = lax.fori_loop(0, devices // 4, survey, jnp.zeros((depth, LANES), jnp.float32))
    full = jnp.minimum(hits, 1.0)

    def ordered(size, axis):
        first = lax.broadcasted_iota(jnp.int32, (size, size), axis)
        second = lax.broadcasted_iota(jnp.int32, (size, size), 1 - axis)
        return (first < second).astype(jnp.float32)

    counts = exact_dot(jnp.ones((ROWS, LANES), jnp.float32), full, ((1,), (1,)))
    start_ref[...] = exact_dot(counts, ordered(depth, 0)).astype(jnp.int32)
    sums = exact_dot(full, jnp.ones((LANES, LANES), jnp.float32))
    place = exact_dot(full, ordered(LANES, 0)) + exact_dot(ordered(depth, 1), sums)
    place_ref[...] = jnp.where(full > 0.0, place, -1.0).astype(jnp.int32)
    place_high = jnp.floor(place * (1.0 / LANES))
    place_parts = jnp.concatenate([place_high, place - place_high * LANES], axis=0)

    def rank_of(batch, carry):
        for k in range(4):
            device = 4 * batch + k
            high, low = one_hots(device)
            parts = exact_dot(place_parts, low)
            rank = high * (parts[0:depth] * LANES + parts[depth : 2 * depth])
            rank = jnp.sum(rank, axis=0, keepdims=True)
            rank_ref[pl.ds(device, 1), :] = rank.astype(jnp.int32)
        return carry

    lax.fori_loop(0, devices // 4, rank_of, 0)
    for tile in range(devices // ROWS):
        rows = slice(tile * ROWS, (tile + 1) * ROWS)
        number = hits_ref[rows, :]
        valid = number < LANES
        number = number & (LANES - 1)
        rank = jnp.take_along_axis(rank_ref[rows, :], number, axis=1, mode="promise_in_bounds")
        target = jnp.where(valid, rank, slots + LANES)
        move_ref[rows, :] = target * (1 << 16) + (tile * ROWS + sub) * LANES + number


def map_kernel(
    shape, wafer_ref, det_ref, rep_ref, size_ref, pair_ref, group_ref, move_ref, float_smem, whole_smem,
    angle_here_ref, angle_across_ref, angle_other_ref, tod_here_ref, tod_other_ref, column_ref,
    angle_ref, tod_ref, cos_ref, sin_ref, clean_ref, noise_ref, weight_ref,
    share_ref, rows_ref, sorted_ref, angle_sem, tod_sem, *more_refs,
):
    wafers, dets, reps, tiles, owners, capacity, owner_rows, lag_count = shape
    devices = wafers * dets * reps
    octets = 2 * reps
    wafer_dets = dets * ROWS
    self_ref = wafer_ref[0], det_ref[0], rep_ref[0]
    count = devices * ROWS
    lane, sub = tile_iotas()
    zero = jnp.zeros((ROWS, LANES), jnp.float32)
    low = lane < PBLOCK
    skies = [more_refs[3 * k : 3 * k + 3] for k in range(3 + ITERS)]
    inverse_ref, r_map, image_map, *d_maps = skies
    sum_refs = more_refs[3 * len(skies) :]
    first_sums = [sum_refs[SUM_SETS * wafer : SUM_SETS * (wafer + 1)] for wafer in range(wafers)]
    sum_refs = sum_refs[SUM_SETS * wafers :]
    second_sums = [sum_refs[SUM_SETS * wafer : SUM_SETS * (wafer + 1)] for wafer in range(wafers)]

    def copies_of(source, to_ref, sem):
        return part_copies(
            shape, self_ref, source, lambda d: to_ref.at[pl.ds(d * tiles, tiles)], sem
        )

    def angle_source(swap_rep, swap_wafer, shift):
        if swap_rep:
            return angle_other_ref.at[swap_wafer, shift]
        return (angle_across_ref if swap_wafer else angle_here_ref).at[shift]

    def tod_source(swap_rep, swap_wafer, shift):
        return (tod_other_ref if swap_rep else tod_here_ref).at[shift, swap_wafer]

    angle_moves = copies_of(angle_source, angle_ref, angle_sem)
    tod_moves = copies_of(tod_source, tod_ref, tod_sem)
    for copy in angle_moves + tod_moves:
        copy.start()

    def turn_half(block):
        return pltpu.roll(block, PBLOCK, 1)

    def fold(first, second):
        return jnp.where(low, first, second) + turn_half(jnp.where(low, second, first))

    def unfold(block):
        turned = turn_half(block)
        return jnp.where(low, block, turned), jnp.where(low, turned, block)

    def whole_sum(values):
        values = jnp.sum(values, axis=0, keepdims=True)
        return wide(jnp.sum(values, axis=1, keepdims=True))

    def loop(times, body, carry, unroll):
        def several(n, carry):
            for k in range(unroll):
                carry = body(n * unroll + k, carry)
            return carry

        return lax.fori_loop(0, times // unroll, several, carry)

    def device_of(wafer, n):
        return (wafer * dets + lax.shift_right_logical(n, 3)) * reps

    def group_of(wafer, n):
        return whole_smem[device_of(wafer, n), n & (ROWS - 1)]

    def rows_of(octet):
        return pl.ds(octet * ROWS, ROWS)

    def count_members(n, counts):
        result = []
        for wafer in range(wafers):
            group = group_of(wafer, n)
            result += [
                counts[wafer * NSUB + g] + jnp.where(group == g, 1, 0) for g in range(NSUB)
            ]
        return tuple(result)

    members = lax.fori_loop(0, wafer_dets, count_members, (jnp.int32(0),) * (wafers * NSUB))
    for k, member in enumerate(members):
        share_ref[k] = 1.0 / jnp.maximum(zero + member.astype(jnp.float32), 1.0)
    for c in range(3):
        image_map[c][count] = zero
        r_map[c][count] = zero

    def clear_sorted(n, carry):
        at = pl.ds(pl.multiple_of(n * ROWS, ROWS), ROWS)
        sorted_ref[at, :] = jnp.zeros((ROWS, 6 * PBLOCK), jnp.float32)
        return carry

    lax.fori_loop(0, sorted_ref.shape[0] // ROWS, clear_sorted, 0)

    def spot_of(key):
        return lax.shift_right_logical(key, 4), (key >> 3) & 1, pl.ds(key & (ROWS - 1), 1)

    def in_half(half):
        return (lane[0:1] >> 6) == half

    def set_weight(at, carry):
        weight_ref[at] = zero + 1.0
        return carry

    loop(count, set_weight, 0, 16)

    def drop(list_ref):
        def one(n, carry):
            at, half, row = spot_of(twin_of(list_ref[n])[0])
            weight_ref[at, row, :] = jnp.where(in_half(half), 0.0, weight_ref[at, row, :])
            return carry

        return one

    lax.fori_loop(0, size_ref[0] * PAIR_BATCH, drop(pair_ref), 0)
    lax.fori_loop(0, size_ref[1], drop(group_ref), 0)

    def moved_from(target, spot, shift):
        at, half, row = spot
        result = []
        for ref in target:
            values = wide(ref[at, row, :])
            values = jnp.where((lane >> 6) == half, values, turn_half(values))
            result.append(pltpu.roll(values, shift, 1)[0:1])
        return result

    def merge_twins(target):
        def pair_batch(n, carry):
            found = []
            for k in range(PAIR_BATCH):
                key, lead, shift = twin_of(pair_ref[n * PAIR_BATCH + k])
                key, lead = spot_of(key), spot_of(lead)
                back = (PBLOCK - shift) & (PBLOCK - 1)
                for spot, values in (
                    (lead, moved_from(target, key, shift)), (key, moved_from(target, lead, back))
                ):
                    at, half, row = spot
                    for c in range(3):
                        values[c] = target[c][at, row, :] + jnp.where(in_half(half), values[c], 0.0)
                    found.append((at, row, values))
            for at, row, values in found:
                for c in range(3):
                    target[c][at, row, :] = values[c]
            return carry

        def gather_one(n, carry):
            key, lead, shift = twin_of(group_ref[n])
            values = moved_from(target, spot_of(key), shift)
            at, half, row = spot_of(lead)
            for c in range(3):
                target[c][at, row, :] += jnp.where(in_half(half), values[c], 0.0)
            return carry

        def spread_one(n, carry):
            key, lead, shift = twin_of(group_ref[n])
            values = moved_from(target, spot_of(lead), (PBLOCK - shift) & (PBLOCK - 1))
            at, half, row = spot_of(key)
            for c in range(3):
                target[c][at, row, :] = jnp.where(in_half(half), values[c], target[c][at, row, :])
            return carry

        lax.fori_loop(0, size_ref[0], pair_batch, 0)
        lax.fori_loop(0, size_ref[1], gather_one, 0)
        lax.fori_loop(0, size_ref[1], spread_one, 0)

    for copy in angle_moves:
        copy.wait()

    def survey(at, carry):
        base = float_smem[lax.shift_right_logical(at, 3), at & (ROWS - 1)]
        squares = []
        for half in range(2):
            first, second = cosine_sine_double(angle_ref[2 * at + half])
            cos_ref[2 * at + half] = first
            sin_ref[2 * at + half] = second
            squares.append((base * (first * first), base * (second * second)))
        image_map[0][at] = zero + (base + base)
        for c in range(2):
            image_map[c + 1][at] = fold(squares[0][c], squares[1][c])
        return carry

    loop(count, survey, 0, 8)

    def clear_sums(refs):
        for sets in refs:
            for ref in sets:
                for group in range(NSUB):
                    for octet in range(octets):
                        ref[group, rows_of(octet), :] = zero

    def average(refs):
        for wafer, sets in enumerate(refs):
            for group in range(NSUB):
                for octet in range(octets):
                    total = sets[0][group, rows_of(octet), :]
                    for ref in sets[1:]:
                        total = total + ref[group, rows_of(octet), :]
                    sets[0][group, rows_of(octet), :] = total * share_ref[wafer * NSUB + group]

    def over_detectors(body, carry):
        def several(step, carry):
            for k in range(DET_BATCH):
                carry = body(step * DET_BATCH + k, k % SUM_SETS, carry)
            return carry

        return lax.fori_loop(0, wafer_dets // DET_BATCH, several, carry)

    def sum_streams(streams_of, carry):
        clear_sums(first_sums)

        def one_detector(n, part, carry):
            for wafer in range(wafers):
                group = group_of(wafer, n)
                for rep in range(reps):
                    at = (device_of(wafer, n) + rep) * ROWS + (n & (ROWS - 1))
                    streams, carry = streams_of(at, carry)
                    for half, stream in enumerate(streams):
                        rows = rows_of(2 * rep + half)
                        clean_ref[wafer * wafer_dets + n, rows, :] = stream
                        first_sums[wafer][part][group, rows, :] += stream
            return carry

        carry = over_detectors(one_detector, carry)
        average(first_sums)
        return carry

    def filter_streams():
        clear_sums(second_sums)

        def one_filter(n, part, carry):
            for wafer in range(wafers):
                device, inside = device_of(wafer, n), n & (ROWS - 1)
                detector = wafer * wafer_dets + n
                group = group_of(wafer, n)
                base = float_smem[device, inside]
                coefs = [float_smem[device, (j + 1) * ROWS + inside] for j in range(lag_count)]
                lags = [whole_smem[device, (j + 1) * ROWS + inside] for j in range(lag_count)]
                clean = [
                    clean_ref[detector, rows_of(octet), :]
                    - first_sums[wafer][0][group, rows_of(octet), :]
                    for octet in range(octets)
                ]
                up = [pltpu.roll(here, ROWS - 1, 0) for here in clean] + [zero]
                down = [zero] + [pltpu.roll(here, 1, 0) for here in clean]
                for octet, here in enumerate(clean):
                    after = jnp.where(sub == ROWS - 1, up[octet + 1], up[octet])
                    ahead = jnp.where(sub == 0, down[octet], down[octet + 1])
                    result = base * here
                    for coef, lag in zip(coefs, lags):
                        later = pltpu.roll(jnp.where(lane < lag, after, here), LANES - lag, 1)
                        earlier = pltpu.roll(jnp.where(lane >= LANES - lag, ahead, here), lag, 1)
                        result = result + coef * (later + earlier)
                    noise_ref[detector, rows_of(octet), :] = result
                    second_sums[wafer][part][group, rows_of(octet), :] += result
                    carry = carry + here * result
            return carry

        product = over_detectors(one_filter, zero)
        average(second_sums)
        return product

    def return_streams(target):
        def one_return(n, part, carry):
            for wafer in range(wafers):
                group = group_of(wafer, n)
                for rep in range(reps):
                    at = (device_of(wafer, n) + rep) * ROWS + (n & (ROWS - 1))
                    streams = []
                    for half in range(2):
                        rows = rows_of(2 * rep + half)
                        stream = noise_ref[wafer * wafer_dets + n, rows, :]
                        streams.append(stream - second_sums[wafer][0][group, rows, :])
                    target[0][at] = fold(*streams)
                    for c, ref in ((1, cos_ref), (2, sin_ref)):
                        target[c][at] = fold(*(ref[2 * at + h] * streams[h] for h in range(2)))
            return carry

        over_detectors(one_return, 0)
        merge_twins(target)

    merge_twins(image_map)
    for copy in tod_moves:
        copy.wait()
    sum_streams(lambda at, carry: ([tod_ref[2 * at + half] for half in range(2)], carry), 0)
    filter_streams()
    return_streams(r_map)

    factor = zero
    steps = []
    for iteration, d_map in enumerate(d_maps):
        last = iteration == ITERS - 1

        def seen_streams(at, carry):
            prior, energy = carry
            squares, products = zero, zero
            streams = [None, None]
            for c in range(3):
                residual = r_map[c][at]
                if iteration:
                    part = inverse_ref[c][at] * residual + factor * d_maps[iteration - 1][c][at]
                else:
                    inverse = 1.0 / (image_map[c][at] + prior_weight)
                    inverse_ref[c][at] = inverse
                    part = inverse * residual
                    products = products + residual * part
                d_map[c][at] = part
                squares = squares + part * part
                for half, seen in enumerate(unfold(part)):
                    if c == 0:
                        streams[half] = seen
                    else:
                        ref = cos_ref if c == 1 else sin_ref
                        streams[half] = streams[half] + ref[2 * at + half] * seen
            weight = weight_ref[at]
            if not iteration:
                energy = energy + weight * products
            return streams, (prior + weight * squares, energy)

        prior, first_energy = sum_streams(seen_streams, (zero, zero))
        if not iteration:
            energy = whole_sum(first_energy)
        product = filter_streams()
        return_streams(image_map)
        step = energy / whole_sum(product + prior_weight * prior)
        steps.append(step)

        def new_residual(at, c):
            return r_map[c][at] - step * (image_map[c][at] + prior_weight * d_map[c][at])

        if not last:

            def update(batch, carry):
                found = []
                for k in range(MAP_BATCH):
                    at = batch * MAP_BATCH + k
                    residual = [new_residual(at, c) for c in range(3)]
                    parts = zero
                    for c in range(3):
                        parts = parts + residual[c] * (inverse_ref[c][at] * residual[c])
                    carry = carry + weight_ref[at] * parts
                    found.append((at, residual))
                for at, residual in found:
                    for c in range(3):
                        r_map[c][at] = residual[c]
                return carry

            next_energy = whole_sum(loop(count // MAP_BATCH, update, zero, 2))
            factor = next_energy / energy
            energy = next_energy
        else:

            def place_pixels(at, carry):
                team = lax.rem(lax.div(at, reps * ROWS), dets)
                turn = (3 * (team * ROWS + (at & (ROWS - 1)))) & (PBLOCK - 1)
                inside = (lane & (PBLOCK - 1)) >= turn
                values = []
                for c in range(3):
                    value = steps[0] * d_maps[0][c][at]
                    for k in range(1, ITERS):
                        value = value + steps[k] * d_maps[k][c][at]
                    values.append(value)
                values += [new_residual(at, c) for c in range(3)]
                for c in range(3):
                    left, right = values[2 * c], values[2 * c + 1]
                    halves = (
                        jnp.where(low, left, turn_half(right)), jnp.where(low, turn_half(left), right)
                    )
                    for half, value in enumerate(halves):
                        value = jnp.where(
                            inside, pltpu.roll(value, turn, 1), pltpu.roll(value, turn + PBLOCK, 1)
                        )
                        rows = pl.ds(pl.multiple_of((2 * at + half) * ROWS, ROWS), ROWS)
                        rows_ref[rows, c * LANES : (c + 1) * LANES] = value
                return carry

            loop(count, place_pixels, 0, 8)

    def pick(device, carry):
        for c in range(capacity):
            move = move_ref[device, c]
            source, target = move & ((1 << 16) - 1), move >> 16
            sorted_ref[pl.ds(target, 1), :] = rows_ref[pl.ds(source, 1), :]
        return carry

    lax.fori_loop(0, devices, pick, 0)

    def turn_tile(tile, carry):
        columns = sorted_ref[pl.ds(pl.multiple_of(tile * LANES, LANES), LANES), :].T
        high = columns.astype(jnp.bfloat16)
        column_ref[tile, :, 0:LANES] = high
        column_ref[tile, :, LANES : 2 * LANES] = (columns - high.astype(jnp.float32)).astype(
            jnp.bfloat16
        )
        return carry

    lax.fori_loop(0, column_ref.shape[0], turn_tile, 0)


def write_kernel(start_ref, column_ref, place_ref, x_ref, r_ref, x_buffer, r_buffer, x_sem, r_sem):
    height = 3 * PBLOCK
    width = OUT_TILES * LANES
    steps = x_ref.shape[1] // width
    depth = lax.broadcasted_iota(jnp.int32, (LANES, LANES), 0)

    def copies(step, slot):
        to = pl.ds(pl.multiple_of(step * width, width), width)
        return (
            pltpu.make_async_copy(x_buffer.at[slot], x_ref.at[:, to], x_sem.at[slot]),
            pltpu.make_async_copy(r_buffer.at[slot], r_ref.at[:, to], r_sem.at[slot]),
        )

    def spread(group, tile):
        chosen = []
        for k in range(OUT_TILES):
            place = jnp.broadcast_to(place_ref[pl.ds(group + k, 1), :], (LANES, LANES))
            chosen.append(jnp.where(place == depth + tile * LANES, 1.0, 0.0).astype(jnp.bfloat16))
        chosen = jnp.concatenate(chosen, axis=1)
        chosen = jnp.concatenate([chosen, chosen], axis=0)
        return jnp.dot(column_ref[tile], chosen, preferred_element_type=jnp.float32)

    def one_step(step, carry):
        slot = lax.rem(step, WRITES)

        @pl.when(step >= WRITES)
        def _():
            for copy in copies(step - WRITES, slot):
                copy.wait()

        group = step * OUT_TILES
        start, end = start_ref[0, group], start_ref[0, group + OUT_TILES]
        first = lax.shift_right_logical(start, 7)
        last = lax.shift_right_logical(jnp.maximum(end - 1, start), 7)
        values = spread(group, first)
        x_buffer[slot] = values[:height]
        r_buffer[slot] = values[height:]

        def add_tile(tile, carry):
            values = spread(group, tile)
            x_buffer[slot] += values[:height]
            r_buffer[slot] += values[height:]
            return carry

        lax.fori_loop(first + 1, last + 1, add_tile, 0)
        for copy in copies(step, slot):
            copy.start()
        return carry

    lax.fori_loop(0, steps, one_step, 0)
    for step in range(steps - WRITES, steps):
        for copy in copies(step, step % WRITES):
            copy.wait()


def part_shape(sizes, tod, hit_list, band_lag):
    det_count, time_count = tod.shape[1:]
    owners, capacity = hit_list.shape[3:]
    return (
        sizes["wafer"], sizes["det"], sizes["rep"], time_count // SBLOCK,
        owners, capacity, BLOCKS // owners, band_lag.shape[2],
    ), det_count


def fits_one_device(shape, det_count):
    wafers, dets, reps, tiles, owners, capacity, owner_rows, lag_count = shape
    devices = wafers * dets * reps
    total = devices * tiles * det_count
    groups = owner_rows // LANES
    return (
        det_count == ROWS
        and owners == ROWS
        and tiles * ROWS == LANES
        and tiles == 2 * ROWS
        and (wafers, reps) == (2, 2)
        and (1 + lag_count) * ROWS <= LANES
        and capacity <= LANES
        and devices * capacity % LANES == 0
        and owner_rows % (LANES * OUT_TILES) == 0
        and owner_rows >= LANES * OUT_TILES * WRITES
        and groups + 1 <= 2 * LANES
        and devices % ROWS == 0
        and dets % (DET_BATCH // ROWS) == 0
        and total * total < BIG
    )


def whole_part(shape, tod, psi, point_row, hit_list, group_id, a_zero, band_coef, band_lag):
    wafers, dets, reps, tiles, owners, capacity, owner_rows, lag_count = shape
    devices = wafers * dets * reps
    octets = reps * tiles // ROWS
    detectors = wafers * dets * ROWS
    count = devices * tiles
    total = count * ROWS
    slots = devices * capacity
    height = 3 * PBLOCK
    f32, i32 = jnp.float32, jnp.int32
    vmem, smem = pl.BlockSpec(memory_space=pltpu.VMEM), pl.BlockSpec(memory_space=pltpu.SMEM)
    anywhere = pl.BlockSpec(memory_space=pl.ANY)

    def params(mebibytes):
        return pltpu.CompilerParams(vmem_limit_bytes=mebibytes << 20)

    swap = [(0, 1), (1, 0)]

    def along_det(block):
        moved = [
            lax.ppermute(block, "det", [(i, (i + shift) % dets) for i in range(dets)])
            for shift in range(1, dets)
        ]
        return [block] + moved

    def other_wafer(here):
        return lax.ppermute(here, "wafer", swap)

    def other_rep(here, across):
        return here, across, lax.ppermute(jnp.stack([here, across]), "rep", swap)

    tables, angles, samples = pl.pallas_call(
        functools.partial(pack_kernel, shape),
        out_shape=[
            jax.ShapeDtypeStruct((2, ROWS, LANES), f32),
            jax.ShapeDtypeStruct((ROWS, tiles, LANES), f32),
            jax.ShapeDtypeStruct((ROWS, tiles, LANES), f32),
        ],
        in_specs=[vmem] * 8,
        out_specs=[vmem] * 3,
        compiler_params=params(60),
        name="pack",
    )(
        psi[0], tod[0], point_row[0], hit_list[0, 0, 0], group_id, a_zero, band_coef[0].T,
        band_lag[0].T,
    )
    angles, samples = (stream.reshape(tiles, ROWS, LANES) for stream in (angles, samples))
    place_here = [
        lax.axis_index(axis).astype(i32).reshape(1) for axis in ("wafer", "det", "rep")
    ]
    tables = lax.all_gather(tables, "rep", axis=0, tiled=False)
    angles, tables = lax.optimization_barrier((angles, tables))
    riders = jnp.concatenate([samples, tables.reshape(2 * reps, ROWS, LANES)])
    riders = jnp.stack([riders, other_wafer(riders)])
    angles = jnp.stack(along_det(angles))
    blocks = along_det(riders)
    tables = jnp.stack([block[:, tiles:] for block in blocks])
    tables = tables.reshape(dets, wafers, reps, 2, ROWS, LANES)
    samples = jnp.stack([block[:, :tiles] for block in blocks])
    angle_blocks = other_rep(angles, other_wafer(angles))
    sample_blocks = samples, lax.ppermute(samples, "rep", swap)
    table_rows = jax.ShapeDtypeStruct((devices, LANES), i32)
    lists = pl.pallas_call(
        functools.partial(list_kernel, shape),
        out_shape=[
            jax.ShapeDtypeStruct((devices, LANES), f32),
            table_rows,
            jax.ShapeDtypeStruct((2 * LANES, LANES), i32),
            jax.ShapeDtypeStruct((ROWS, 2 * LANES), i32),
            table_rows,
            jax.ShapeDtypeStruct((2,), i32),
            jax.ShapeDtypeStruct((total,), i32),
            jax.ShapeDtypeStruct((total,), i32),
        ],
        in_specs=[smem, smem, anywhere],
        out_specs=[vmem] * 5 + [smem] * 3,
        scratch_shapes=[
            pltpu.VMEM((devices, 2, ROWS, LANES), f32),
            pltpu.VMEM((devices, LANES, LANES), f32),
            pltpu.VMEM((devices, LANES), f32),
            pltpu.VMEM((devices, LANES), f32),
            pltpu.VMEM((devices, LANES), i32),
            pltpu.VMEM((devices, LANES), i32),
            pltpu.VMEM((devices, LANES), i32),
            pltpu.SemaphoreType.DMA((devices,)),
        ],
        compiler_params=params(8),
        cost_estimate=pl.CostEstimate(flops=10**9, bytes_accessed=5 * 10**7, transcendentals=0),
        name="lists",
    )(*place_here[:2], tables)
    floats, whole, place, start, moves, size, pair, group = lists
    stream = pltpu.VMEM((count, ROWS, LANES), f32)
    sky = pltpu.VMEM((devices * ROWS + 1, ROWS, LANES), f32)
    group_sums = pltpu.VMEM((NSUB, octets * ROWS, LANES), f32)
    columns = pl.pallas_call(
        functools.partial(map_kernel, shape),
        out_shape=jax.ShapeDtypeStruct((slots // LANES + 1, 2 * height, 2 * LANES), jnp.bfloat16),
        in_specs=[smem] * 9 + [anywhere] * 5,
        out_specs=vmem,
        scratch_shapes=[
            stream, stream, stream, stream,
            pltpu.VMEM((detectors, octets * ROWS, LANES), f32),
            pltpu.VMEM((detectors, octets * ROWS, LANES), f32),
            sky,
            pltpu.VMEM((wafers * NSUB, ROWS, LANES), f32),
            pltpu.VMEM((total, 2 * height), f32),
            pltpu.VMEM((slots + LANES + ROWS, 2 * height), f32),
            pltpu.SemaphoreType.DMA((devices,)),
            pltpu.SemaphoreType.DMA((devices,)),
        ] + [sky] * (3 * (3 + ITERS)) + [group_sums] * (2 * wafers * SUM_SETS),
        compiler_params=params(30),
        name="map_maker",
    )(
        *place_here, size, pair, group, moves, floats, whole, *angle_blocks,
        *sample_blocks,
    )
    buffers = pltpu.VMEM((WRITES, height, OUT_TILES * LANES), f32)
    x_turned, r_turned = pl.pallas_call(
        write_kernel,
        out_shape=[jax.ShapeDtypeStruct((height, owner_rows), f32)] * 2,
        in_specs=[smem, vmem, vmem],
        out_specs=[anywhere] * 2,
        scratch_shapes=[buffers, buffers] + [pltpu.SemaphoreType.DMA((WRITES,))] * 2,
        compiler_params=params(16),
        name="write",
    )(start, columns, place)
    return x_turned.T, r_turned.T


def local(sizes, *arguments):
    tod, hit_list, band_lag = arguments[0], arguments[3], arguments[7]
    shape, det_count = part_shape(sizes, tod, hit_list, band_lag)
    if fits_one_device(shape, det_count):
        return whole_part(shape, *arguments)
    return distributed(*arguments)


def solution(mesh):
    placed = (
        P(("groups", "wafer"), "det", "rep"),
        P(("groups", "wafer"), "det", "rep"),
        P(("groups", "wafer"), "det", "rep"),
        P(("groups", "wafer"), "det", "rep", None, None),
        P(("groups", "wafer"), "det"),
        P(("groups", "wafer"), "det"),
        P(("groups", "wafer"), "det", None),
        P(("groups", "wafer"), "det", None),
    )
    return jax.shard_map(
        functools.partial(local, mesh.shape),
        mesh=mesh,
        in_specs=placed,
        out_specs=(P(("groups", "det", "wafer"), None), P(("groups", "det", "wafer"), None)),
        check_vma=False,
    )
```

```python
import functools

import jax
import jax.numpy as jnp
from jax import lax
from jax.experimental import pallas as pl
from jax.experimental.pallas import tpu as pltpu
from jax.sharding import PartitionSpec as P

BLOCKS = 196608
PBLOCK = 64
SBLOCK = 128
NSUB = 4
LAG = 16
ITERS = 3


prior_weight = 1.0


def with_halo(block, sides, width):
    for axis, dim in sides:
        count = lax.axis_size(axis)
        forward = [(i, i + 1) for i in range(count - 1)]
        backward = [(target, source) for source, target in forward]
        low = lax.ppermute(
            lax.slice_in_dim(block, block.shape[dim] - width, None, axis=dim), axis, forward
        )
        high = lax.ppermute(lax.slice_in_dim(block, 0, width, axis=dim), axis, backward)
        block = jnp.concatenate([low, block, high], axis=dim)
    return block


def distributed(tod, psi, point_row, hit_list, group_id, a_zero, band_coef, band_lag):
    highest = lax.Precision.HIGHEST
    samples = tod[0]
    angles = psi[0]
    det_count, time_count = samples.shape
    time_blocks = time_count // SBLOCK
    block_count = det_count * time_blocks
    send_table = hit_list[0, 0, 0]
    owner_count, capacity = send_table.shape
    owner_rows = BLOCKS // owner_count
    block_width = 3 * PBLOCK
    detector = lax.axis_index("det") * det_count + jnp.arange(det_count, dtype=jnp.int32)
    within = (jnp.arange(SBLOCK, dtype=jnp.int32)[None, :] + 3 * detector[:, None]) % PBLOCK
    pixel_table = (within[:, :, None] == jnp.arange(PBLOCK, dtype=jnp.int32)[None, None, :]).astype(
        jnp.float32
    )
    cosine_two = jnp.cos(2.0 * angles).reshape(det_count, time_blocks, SBLOCK)
    sine_two = jnp.sin(2.0 * angles).reshape(det_count, time_blocks, SBLOCK)
    slot_ids = send_table.reshape(-1)
    row_source = jnp.concatenate([point_row[0].reshape(-1), jnp.zeros((1,), jnp.int32)])
    slot_rows = row_source[slot_ids].astype(jnp.float32).reshape(owner_count, capacity)
    member = (group_id[0][:, None] == jnp.arange(NSUB, dtype=jnp.int32)[None, :]).astype(
        jnp.float32
    )
    member_count = jnp.sum(member, axis=0)
    lag_table = (
        band_lag[0][:, :, None] == jnp.arange(1, LAG + 1, dtype=jnp.int32)[None, None, :]
    ).astype(jnp.float32)
    lag_weight = jnp.einsum("dj,djl->dl", band_coef[0], lag_table, precision=highest)
    base_weight = a_zero[0]

    def slot_payload(by_block):
        width = by_block.shape[1]
        extended = jnp.concatenate([by_block, jnp.zeros((1, width), by_block.dtype)])
        return extended[slot_ids].reshape(owner_count, capacity, width)

    def deliver(payload):
        width = payload.shape[-1]
        got_values, got_rows = (
            lax.all_to_all(payload, ("det", "wafer"), split_axis=0, concat_axis=0, tiled=True),
            lax.all_to_all(slot_rows, ("det", "wafer"), split_axis=0, concat_axis=0, tiled=True),
        )
        return (got_values, got_rows)

    def back_project(stream, squared):
        shaped = stream.reshape(det_count, time_blocks, SBLOCK)
        first = cosine_two * cosine_two if squared else cosine_two
        second = sine_two * sine_two if squared else sine_two
        stacked = jnp.stack([shaped, first * shaped, second * shaped], axis=2)
        stokes = jnp.einsum("dkcs,dsp->dkcp", stacked, pixel_table, precision=highest)
        return stokes.reshape(block_count, block_width)

    def to_owners(stream, squared):
        got_values, got_rows = deliver(slot_payload(back_project(stream, squared)))
        pair_values, pair_rows = (
            lax.all_gather(got_values, "rep", axis=0, tiled=True),
            lax.all_gather(got_rows, "rep", axis=0, tiled=True),
        )
        target_rows = pair_rows.reshape(-1).astype(jnp.int32)
        summed = (
            jnp.zeros((owner_rows, block_width), jnp.float32)
            .at[target_rows]
            .add(pair_values.reshape(-1, block_width))
        )
        return (summed, got_rows.astype(jnp.int32))

    def remove_common(stream):
        local_sums = jnp.einsum("dg,dt->gt", member, stream, precision=highest)
        group_sums, group_counts = lax.psum((local_sums, member_count), "det")
        group_means = group_sums / jnp.maximum(group_counts, 1.0)[:, None]
        return stream - jnp.einsum("dg,gt->dt", member, group_means, precision=highest)

    def band_filter(stream):
        padded = with_halo(stream, (("rep", 1),), LAG)
        result = base_weight[:, None] * stream
        for offset in range(1, LAG + 1):
            later = padded[:, LAG + offset : LAG + offset + time_count]
            earlier = padded[:, LAG - offset : LAG - offset + time_count]
            result = result + lag_weight[:, offset - 1 : offset] * (later + earlier)
        return result

    def weigh_stream(stream):
        return remove_common(band_filter(remove_common(stream)))

    weight_stream = jnp.broadcast_to(base_weight[:, None], (det_count, time_count))
    diag_sum, serve_rows = to_owners(weight_stream, True)
    inverse_diag = 1.0 / (diag_sum + prior_weight)
    right_side = to_owners(weigh_stream(samples), False)[0]
    solution = jnp.zeros_like(right_side)
    residual = right_side

    def inner(left_map, right_map):
        return lax.psum(jnp.sum(left_map * right_map), ("det", "wafer"))

    precond = inverse_diag * residual
    direction = precond
    energy = inner(residual, precond)
    for iteration in range(ITERS):
        from_blocks = direction[serve_rows.reshape(-1)].reshape(owner_count, capacity, block_width)
        return_width = from_blocks.shape[-1]
        returned = lax.all_to_all(
            from_blocks, ("det", "wafer"), split_axis=0, concat_axis=0, tiled=True
        )
        return_placed = jnp.zeros((block_count + 1, return_width), jnp.float32)
        return_placed = return_placed.at[slot_ids].set(returned.reshape(-1, return_width))
        blocks = return_placed[:block_count].reshape(det_count, time_blocks, 3, PBLOCK)
        project_stokes = jnp.einsum("dkcp,dsp->dkcs", blocks, pixel_table, precision=highest)
        project_stream = (
            project_stokes[:, :, 0]
            + cosine_two * project_stokes[:, :, 1]
            + sine_two * project_stokes[:, :, 2]
        )
        seen_stream = project_stream.reshape(det_count, time_count)
        image_map = to_owners(weigh_stream(seen_stream), False)[0] + prior_weight * direction
        step_size = energy / inner(direction, image_map)
        solution = solution + step_size * direction
        residual = residual - step_size * image_map
        precond = inverse_diag * residual
        energy_next = inner(residual, precond)
        direction = precond + energy_next / energy * direction
        energy = energy_next
    return (solution, residual)


LANES = 128
ROWS = 8
OUT_TILES = 8
PAIR_BATCH = 8
WRITES = 6
DET_BATCH = 16
SUM_SETS = 2
MAP_BATCH = 8
BIG = float(1 << 24)


def wide(values):
    return jnp.broadcast_to(values, (ROWS, LANES))


def tile_iotas():
    lane = lax.broadcasted_iota(jnp.int32, (ROWS, LANES), 1)
    sub = lax.broadcasted_iota(jnp.int32, (ROWS, LANES), 0)
    return lane, sub


def cosine_sine_double(angle):
    turns = jnp.floor(angle * 1.2732395447351628 + 0.5)
    reduced = 2.0 * angle - turns * 1.5703125
    reduced = reduced - turns * 4.837512969970703125e-4
    reduced = reduced - turns * 7.54978995489188216e-8
    square = reduced * reduced
    sine = (-1.9515295891e-4 * square + 8.3321608736e-3) * square - 1.6666654611e-1
    sine = sine * square * reduced + reduced
    cosine = (2.443315711809948e-5 * square - 1.388731625493765e-3) * square
    cosine = (cosine + 4.166664568298827e-2) * square * square - 0.5 * square + 1.0
    quarter = turns.astype(jnp.int32)
    odd = (quarter & 1) == 1
    first = jnp.where(odd, sine, cosine)
    second = jnp.where(odd, cosine, sine)
    first = jnp.where(((quarter + 1) & 2) == 2, -first, first)
    second = jnp.where((quarter & 2) == 2, -second, second)
    return first, second


def pack_kernel(
    shape, angle_ref, tod_ref, row_ref, hit_ref, group_ref, base_ref, coef_ref, lag_ref,
    angle_rows_ref, tod_rows_ref,
):
    wafers, dets, reps, tiles, owners, capacity, owner_rows, lag_count = shape
    lane, sub = tile_iotas()
    lists = hit_ref[...]
    owner_hits = jnp.zeros((ROWS, LANES), jnp.float32)
    for c in range(capacity):
        owner_hits = owner_hits + jnp.where(wide(lists[:, c : c + 1]) == lane, 1.0, 0.0)
    owner_of = jnp.sum(owner_hits * sub.astype(jnp.float32), axis=0, keepdims=True)

    def spread(values, width):
        return jnp.concatenate(
            [values, jnp.zeros((values.shape[0], LANES - width), values.dtype)], axis=1
        )

    rows = spread(row_ref[...].astype(jnp.float32), tiles)
    ids = owner_of * float(owner_rows) + rows[0:1]
    for k in range(1, ROWS):
        ids = ids + pltpu.roll(rows[k : k + 1], k * tiles, 1)
    floats = spread(base_ref[...], ROWS)
    whole = spread(group_ref[...].astype(jnp.float32), ROWS)
    for j in range(lag_count):
        at = (j + 1) * ROWS
        floats = floats + pltpu.roll(spread(coef_ref[j : j + 1, :], ROWS), at, 1)
        lag = lag_ref[j : j + 1, :].astype(jnp.float32)
        whole = whole + pltpu.roll(spread(lag, ROWS), at, 1)
    table = jnp.where(sub == 0, wide(ids), jnp.where(sub == 1, wide(floats), wide(whole)))
    angle_rows_ref[ROWS, 0:ROWS, :] = table
    angle_rows_ref[ROWS, ROWS : 2 * ROWS, :] = spread(lists.astype(jnp.float32), capacity)
    for b in range(tiles):
        angle_rows_ref[0:ROWS, b, :] = angle_ref[:, b * LANES : (b + 1) * LANES]
        tod_rows_ref[:, b, :] = tod_ref[:, b * LANES : (b + 1) * LANES]


def part_copies(shape, self_ref, source, target, sem):
    wafers, dets, reps = shape[:3]
    copies = []
    for swap_rep in range(reps):
        for swap_wafer in range(wafers):
            for shift in range(dets):
                det = self_ref[1] - shift
                det = jnp.where(det < 0, det + dets, det)
                device = ((self_ref[0] ^ swap_wafer) * dets + det) * reps
                device = device + (self_ref[2] ^ swap_rep)
                copies.append(
                    pltpu.make_async_copy(
                        source(swap_rep, swap_wafer, shift), target(device), sem.at[len(copies)]
                    )
                )
    return copies


def table_copies(shape, self_ref, source_ref, part_ref, sem):
    wafers, dets, reps = shape[:3]
    copies = []
    for rep in range(reps):
        for swap_wafer in range(wafers):
            for shift in range(dets):
                det = self_ref[1] - shift
                det = jnp.where(det < 0, det + dets, det)
                device = ((self_ref[0] ^ swap_wafer) * dets + det) * reps + rep
                copies.append(
                    pltpu.make_async_copy(
                        source_ref.at[rep, swap_wafer, shift], part_ref.at[device],
                        sem.at[len(copies)],
                    )
                )
    for copy in copies:
        copy.start()
    for copy in copies:
        copy.wait()


def exact_dot(left, right, dims=((1,), (0,))):
    return lax.dot_general(
        left.astype(jnp.bfloat16), right.astype(jnp.bfloat16), (dims, ((), ())),
        preferred_element_type=jnp.float32,
    )


def list_kernel(
    shape, wafer_ref, det_ref, table_ref, float_ref, whole_ref, place_ref, start_ref, move_ref,
    size_ref, pair_ref, group_ref,
    part_ref, column_ref, code_ref, lead_ref, used_ref, rank_ref, hits_ref, part_sem,
):
    self_ref = wafer_ref[0], det_ref[0]
    table_copies(shape, self_ref, table_ref, part_ref, part_sem)
    list_twins(
        shape, float_ref, whole_ref, size_ref, pair_ref, group_ref, part_ref, column_ref, code_ref,
        lead_ref, used_ref,
    )
    list_places(shape, self_ref, place_ref, start_ref, move_ref, part_ref, rank_ref, hits_ref)


def list_twins(
    shape, float_ref, whole_ref, size_ref, pair_ref, group_ref, part_ref, column_ref, code_ref,
    lead_ref, used_ref,
):
    wafers, dets, reps, tiles, owners, capacity, owner_rows, lag_count = shape
    devices = wafers * dets * reps
    total = devices * LANES
    lane, sub = tile_iotas()
    sub_f = sub.astype(jnp.float32)
    none = jnp.full((ROWS, LANES), BIG, jnp.float32)
    along = lax.broadcasted_iota(jnp.int32, (1, LANES), 1).astype(jnp.float32)

    def turn(batch, carry):
        for k in range(4):
            device = 4 * batch + k
            float_ref[pl.ds(device, 1), :] = part_ref[device, 0, 1:2, :]
            whole_ref[pl.ds(device, 1), :] = part_ref[device, 0, 2:3, :].astype(jnp.int32)
            column_ref[device] = jnp.broadcast_to(part_ref[device, 0, 0:1, :], (LANES, LANES)).T
        return carry

    lax.fori_loop(0, devices // 4, turn, 0)

    def survey(device, carry):
        row = wide(part_ref[device, 0, 0:1, :])

        def compare(step, least):
            for k in range(2):
                other = 2 * step + k
                found = [none] * 4
                for j in range(tiles):
                    same = column_ref[other, j * ROWS : (j + 1) * ROWS, :] == row
                    at = jnp.where(same, sub_f + float(j * ROWS), BIG)
                    found[j % 4] = jnp.minimum(found[j % 4], at)
                here = jnp.minimum(jnp.minimum(found[0], found[1]), jnp.minimum(found[2], found[3]))
                least = jnp.minimum(least, here + (other * LANES).astype(jnp.float32))
            return least

        least = lax.fori_loop(0, lax.shift_right_logical(device, 1) + 1, compare, none)
        lead = jnp.min(least, axis=0, keepdims=True)
        mine = (device * LANES).astype(jnp.float32) + along
        later = lead < mine
        code_ref[pl.ds(device, 1), :] = jnp.where(later, mine * float(total) + lead, BIG)
        lead_ref[pl.ds(device, 1), :] = jnp.where(later, lead, BIG)
        return carry

    lax.fori_loop(0, devices, survey, 0)

    def next_code(last):
        found = none
        for tile in range(devices // ROWS):
            codes = code_ref[tile * ROWS : (tile + 1) * ROWS, :]
            found = jnp.minimum(found, jnp.where(codes > last, codes, BIG))
        return jnp.min(found)

    def detector(key):
        team = lax.rem(lax.div(key, reps * LANES), dets)
        return team * ROWS + lax.rem(lax.div(key, tiles), ROWS)

    number_of = [lane + (sub + tile * ROWS) * LANES for tile in range(devices // ROWS)]
    tile_rows = [slice(tile * ROWS, (tile + 1) * ROWS) for tile in range(devices // ROWS)]
    for rows in tile_rows:
        used_ref[rows, :] = jnp.zeros((ROWS, LANES), jnp.int32)

    def take(state):
        pairs, grouped, code = state
        number = code.astype(jnp.int32)
        key = lax.div(number, total)
        lead = lax.rem(number, total)
        shift = (3 * (detector(key) - detector(lead))) & (PBLOCK - 1)
        wanted = lead.astype(jnp.float32)
        same = jnp.zeros((ROWS, LANES), jnp.float32)
        for rows, numbers in zip(tile_rows, number_of):
            same = same + jnp.where(lead_ref[rows, :] == wanted, 1.0, 0.0)
            beside = numbers ^ ROWS
            beside = (beside == key) | (beside == lead)
            same = same + jnp.where(beside & (used_ref[rows, :] > 0), 2.0, 0.0)
        alone = jnp.sum(same) + jnp.where((key ^ lead) == ROWS, 2.0, 0.0) < 1.5
        mark = jnp.where(alone, 1, 0)
        for rows, numbers in zip(tile_rows, number_of):
            listed = (numbers == key) | (numbers == lead)
            used_ref[rows, :] = jnp.where(listed, mark, used_ref[rows, :])
        entry = twin_entry(key, lead, shift)
        pair_ref[pairs] = entry
        group_ref[grouped] = entry
        return (
            pairs + jnp.where(alone, 1, 0), grouped + jnp.where(alone, 0, 1), next_code(code)
        )

    pairs, grouped, _ = lax.while_loop(
        lambda state: state[2] < BIG, take,
        (jnp.int32(0), jnp.int32(0), next_code(jnp.float32(-1.0))),
    )
    batches = lax.div(pairs + PAIR_BATCH - 1, PAIR_BATCH)

    def fill(n, carry):
        pair_ref[n] = twin_entry(total, total + 1, 0)
        return carry

    lax.fori_loop(pairs, batches * PAIR_BATCH, fill, 0)
    size_ref[0] = batches
    size_ref[1] = grouped


def twin_entry(key, lead, shift):
    return key * (1 << 19) + lead * (1 << 6) + shift


def twin_of(entry):
    return entry >> 19, (entry >> 6) & ((1 << 13) - 1), entry & (PBLOCK - 1)


def list_places(shape, self_ref, place_ref, start_ref, move_ref, part_ref, rank_ref, hits_ref):
    wafers, dets, reps, tiles, owners, capacity, owner_rows, lag_count = shape
    devices = wafers * dets * reps
    slots = devices * capacity
    lane, sub = tile_iotas()
    own = self_ref[1] * wafers + self_ref[0]
    first_row = (own * owner_rows).astype(jnp.float32)
    depth = 2 * LANES
    tall = lax.broadcasted_iota(jnp.int32, (depth, LANES), 0).astype(jnp.float32)

    def one_hots(device):
        local_row = part_ref[device, 0, 0:1, :] - first_row
        high = jnp.floor(local_row * (1.0 / LANES))
        low = local_row - high * LANES
        high = (jnp.broadcast_to(high, (depth, LANES)) == tall).astype(jnp.float32)
        low = (jnp.broadcast_to(low, (LANES, LANES)) == tall[0:LANES]).astype(jnp.float32)
        return high, low

    def survey(batch, hits):
        for k in range(4):
            device = 4 * batch + k
            own_hits = jnp.where(sub == own, part_ref[device, 1], 0.0)
            own_hits = jnp.sum(own_hits, axis=0, keepdims=True)
            hits_ref[pl.ds(device, 1), :] = own_hits.astype(jnp.int32)
            high, low = one_hots(device)
            hits = hits + exact_dot(high, low, ((1,), (1,)))
        return hits

    hits = lax.fori_loop(0, devices // 4, survey, jnp.zeros((depth, LANES), jnp.float32))
    full = jnp.minimum(hits, 1.0)

    def ordered(size, axis):
        first = lax.broadcasted_iota(jnp.int32, (size, size), axis)
        second = lax.broadcasted_iota(jnp.int32, (size, size), 1 - axis)
        return (first < second).astype(jnp.float32)

    counts = exact_dot(jnp.ones((ROWS, LANES), jnp.float32), full, ((1,), (1,)))
    start_ref[...] = exact_dot(counts, ordered(depth, 0)).astype(jnp.int32)
    sums = exact_dot(full, jnp.ones((LANES, LANES), jnp.float32))
    place = exact_dot(full, ordered(LANES, 0)) + exact_dot(ordered(depth, 1), sums)
    place_ref[...] = jnp.where(full > 0.0, place, -1.0).astype(jnp.int32)
    place_high = jnp.floor(place * (1.0 / LANES))
    place_parts = jnp.concatenate([place_high, place - place_high * LANES], axis=0)

    def rank_of(batch, carry):
        for k in range(4):
            device = 4 * batch + k
            high, low = one_hots(device)
            parts = exact_dot(place_parts, low)
            rank = high * (parts[0:depth] * LANES + parts[depth : 2 * depth])
            rank = jnp.sum(rank, axis=0, keepdims=True)
            rank_ref[pl.ds(device, 1), :] = rank.astype(jnp.int32)
        return carry

    lax.fori_loop(0, devices // 4, rank_of, 0)
    for tile in range(devices // ROWS):
        rows = slice(tile * ROWS, (tile + 1) * ROWS)
        number = hits_ref[rows, :]
        valid = number < LANES
        number = number & (LANES - 1)
        rank = jnp.take_along_axis(rank_ref[rows, :], number, axis=1, mode="promise_in_bounds")
        target = jnp.where(valid, rank, slots + LANES)
        move_ref[rows, :] = target * (1 << 16) + (tile * ROWS + sub) * LANES + number


def map_kernel(
    shape, wafer_ref, det_ref, rep_ref, size_ref, pair_ref, group_ref, move_ref, float_smem, whole_smem,
    angle_here_ref, angle_across_ref, angle_other_ref, tod_here_ref, tod_other_ref, column_ref,
    angle_ref, tod_ref, cos_ref, sin_ref, clean_ref, noise_ref, weight_ref,
    share_ref, rows_ref, sorted_ref, angle_sem, tod_sem, *more_refs,
):
    wafers, dets, reps, tiles, owners, capacity, owner_rows, lag_count = shape
    devices = wafers * dets * reps
    octets = 2 * reps
    wafer_dets = dets * ROWS
    self_ref = wafer_ref[0], det_ref[0], rep_ref[0]
    count = devices * ROWS
    lane, sub = tile_iotas()
    zero = jnp.zeros((ROWS, LANES), jnp.float32)
    low = lane < PBLOCK
    skies = [more_refs[3 * k : 3 * k + 3] for k in range(3 + ITERS)]
    inverse_ref, r_map, image_map, *d_maps = skies
    sum_refs = more_refs[3 * len(skies) :]
    first_sums = [sum_refs[SUM_SETS * wafer : SUM_SETS * (wafer + 1)] for wafer in range(wafers)]
    sum_refs = sum_refs[SUM_SETS * wafers :]
    second_sums = [sum_refs[SUM_SETS * wafer : SUM_SETS * (wafer + 1)] for wafer in range(wafers)]

    def copies_of(source, to_ref, sem):
        return part_copies(
            shape, self_ref, source, lambda d: to_ref.at[pl.ds(d * tiles, tiles)], sem
        )

    def angle_source(swap_rep, swap_wafer, shift):
        if swap_rep:
            return angle_other_ref.at[swap_wafer, shift]
        return (angle_across_ref if swap_wafer else angle_here_ref).at[shift]

    def tod_source(swap_rep, swap_wafer, shift):
        return (tod_other_ref if swap_rep else tod_here_ref).at[shift, swap_wafer]

    angle_moves = copies_of(angle_source, angle_ref, angle_sem)
    tod_moves = copies_of(tod_source, tod_ref, tod_sem)
    for copy in angle_moves + tod_moves:
        copy.start()

    def turn_half(block):
        return pltpu.roll(block, PBLOCK, 1)

    def fold(first, second):
        return jnp.where(low, first, second) + turn_half(jnp.where(low, second, first))

    def unfold(block):
        turned = turn_half(block)
        return jnp.where(low, block, turned), jnp.where(low, turned, block)

    def whole_sum(values):
        values = jnp.sum(values, axis=0, keepdims=True)
        return wide(jnp.sum(values, axis=1, keepdims=True))

    def loop(times, body, carry, unroll):
        def several(n, carry):
            for k in range(unroll):
                carry = body(n * unroll + k, carry)
            return carry

        return lax.fori_loop(0, times // unroll, several, carry)

    def device_of(wafer, n):
        return (wafer * dets + lax.shift_right_logical(n, 3)) * reps

    def group_of(wafer, n):
        return whole_smem[device_of(wafer, n), n & (ROWS - 1)]

    def rows_of(octet):
        return pl.ds(octet * ROWS, ROWS)

    def count_members(n, counts):
        result = []
        for wafer in range(wafers):
            group = group_of(wafer, n)
            result += [
                counts[wafer * NSUB + g] + jnp.where(group == g, 1, 0) for g in range(NSUB)
            ]
        return tuple(result)

    members = lax.fori_loop(0, wafer_dets, count_members, (jnp.int32(0),) * (wafers * NSUB))
    for k, member in enumerate(members):
        share_ref[k] = 1.0 / jnp.maximum(zero + member.astype(jnp.float32), 1.0)
    for c in range(3):
        image_map[c][count] = zero
        r_map[c][count] = zero

    def clear_sorted(n, carry):
        at = pl.ds(pl.multiple_of(n * ROWS, ROWS), ROWS)
        sorted_ref[at, :] = jnp.zeros((ROWS, 6 * PBLOCK), jnp.float32)
        return carry

    lax.fori_loop(0, sorted_ref.shape[0] // ROWS, clear_sorted, 0)

    def spot_of(key):
        return lax.shift_right_logical(key, 4), (key >> 3) & 1, pl.ds(key & (ROWS - 1), 1)

    def in_half(half):
        return (lane[0:1] >> 6) == half

    def set_weight(at, carry):
        weight_ref[at] = zero + 1.0
        return carry

    loop(count, set_weight, 0, 16)

    def drop(list_ref):
        def one(n, carry):
            at, half, row = spot_of(twin_of(list_ref[n])[0])
            weight_ref[at, row, :] = jnp.where(in_half(half), 0.0, weight_ref[at, row, :])
            return carry

        return one

    lax.fori_loop(0, size_ref[0] * PAIR_BATCH, drop(pair_ref), 0)
    lax.fori_loop(0, size_ref[1], drop(group_ref), 0)

    def moved_from(target, spot, shift):
        at, half, row = spot
        result = []
        for ref in target:
            values = wide(ref[at, row, :])
            values = jnp.where((lane >> 6) == half, values, turn_half(values))
            result.append(pltpu.roll(values, shift, 1)[0:1])
        return result

    def merge_twins(target):
        def pair_batch(n, carry):
            found = []
            for k in range(PAIR_BATCH):
                key, lead, shift = twin_of(pair_ref[n * PAIR_BATCH + k])
                key, lead = spot_of(key), spot_of(lead)
                back = (PBLOCK - shift) & (PBLOCK - 1)
                for spot, values in (
                    (lead, moved_from(target, key, shift)), (key, moved_from(target, lead, back))
                ):
                    at, half, row = spot
                    for c in range(3):
                        values[c] = target[c][at, row, :] + jnp.where(in_half(half), values[c], 0.0)
                    found.append((at, row, values))
            for at, row, values in found:
                for c in range(3):
                    target[c][at, row, :] = values[c]
            return carry

        def gather_one(n, carry):
            key, lead, shift = twin_of(group_ref[n])
            values = moved_from(target, spot_of(key), shift)
            at, half, row = spot_of(lead)
            for c in range(3):
                target[c][at, row, :] += jnp.where(in_half(half), values[c], 0.0)
            return carry

        def spread_one(n, carry):
            key, lead, shift = twin_of(group_ref[n])
            values = moved_from(target, spot_of(lead), (PBLOCK - shift) & (PBLOCK - 1))
            at, half, row = spot_of(key)
            for c in range(3):
                target[c][at, row, :] = jnp.where(in_half(half), values[c], target[c][at, row, :])
            return carry

        lax.fori_loop(0, size_ref[0], pair_batch, 0)
        lax.fori_loop(0, size_ref[1], gather_one, 0)
        lax.fori_loop(0, size_ref[1], spread_one, 0)

    for copy in angle_moves:
        copy.wait()

    def survey(at, carry):
        base = float_smem[lax.shift_right_logical(at, 3), at & (ROWS - 1)]
        squares = []
        for half in range(2):
            first, second = cosine_sine_double(angle_ref[2 * at + half])
            cos_ref[2 * at + half] = first
            sin_ref[2 * at + half] = second
            squares.append((base * (first * first), base * (second * second)))
        image_map[0][at] = zero + (base + base)
        for c in range(2):
            image_map[c + 1][at] = fold(squares[0][c], squares[1][c])
        return carry

    loop(count, survey, 0, 8)

    def clear_sums(refs):
        for sets in refs:
            for ref in sets:
                for group in range(NSUB):
                    for octet in range(octets):
                        ref[group, rows_of(octet), :] = zero

    def average(refs):
        for wafer, sets in enumerate(refs):
            for group in range(NSUB):
                for octet in range(octets):
                    total = sets[0][group, rows_of(octet), :]
                    for ref in sets[1:]:
                        total = total + ref[group, rows_of(octet), :]
                    sets[0][group, rows_of(octet), :] = total * share_ref[wafer * NSUB + group]

    def over_detectors(body, carry):
        def several(step, carry):
            for k in range(DET_BATCH):
                carry = body(step * DET_BATCH + k, k % SUM_SETS, carry)
            return carry

        return lax.fori_loop(0, wafer_dets // DET_BATCH, several, carry)

    def sum_streams(streams_of, carry):
        clear_sums(first_sums)

        def one_detector(n, part, carry):
            for wafer in range(wafers):
                group = group_of(wafer, n)
                for rep in range(reps):
                    at = (device_of(wafer, n) + rep) * ROWS + (n & (ROWS - 1))
                    streams, carry = streams_of(at, carry)
                    for half, stream in enumerate(streams):
                        rows = rows_of(2 * rep + half)
                        clean_ref[wafer * wafer_dets + n, rows, :] = stream
                        first_sums[wafer][part][group, rows, :] += stream
            return carry

        carry = over_detectors(one_detector, carry)
        average(first_sums)
        return carry

    def filter_streams():
        clear_sums(second_sums)

        def one_filter(n, part, carry):
            for wafer in range(wafers):
                device, inside = device_of(wafer, n), n & (ROWS - 1)
                detector = wafer * wafer_dets + n
                group = group_of(wafer, n)
                base = float_smem[device, inside]
                coefs = [float_smem[device, (j + 1) * ROWS + inside] for j in range(lag_count)]
                lags = [whole_smem[device, (j + 1) * ROWS + inside] for j in range(lag_count)]
                clean = [
                    clean_ref[detector, rows_of(octet), :]
                    - first_sums[wafer][0][group, rows_of(octet), :]
                    for octet in range(octets)
                ]
                up = [pltpu.roll(here, ROWS - 1, 0) for here in clean] + [zero]
                down = [zero] + [pltpu.roll(here, 1, 0) for here in clean]
                for octet, here in enumerate(clean):
                    after = jnp.where(sub == ROWS - 1, up[octet + 1], up[octet])
                    ahead = jnp.where(sub == 0, down[octet], down[octet + 1])
                    result = base * here
                    for coef, lag in zip(coefs, lags):
                        later = pltpu.roll(jnp.where(lane < lag, after, here), LANES - lag, 1)
                        earlier = pltpu.roll(jnp.where(lane >= LANES - lag, ahead, here), lag, 1)
                        result = result + coef * (later + earlier)
                    noise_ref[detector, rows_of(octet), :] = result
                    second_sums[wafer][part][group, rows_of(octet), :] += result
                    carry = carry + here * result
            return carry

        product = over_detectors(one_filter, zero)
        average(second_sums)
        return product

    def return_streams(target):
        def one_return(n, part, carry):
            for wafer in range(wafers):
                group = group_of(wafer, n)
                for rep in range(reps):
                    at = (device_of(wafer, n) + rep) * ROWS + (n & (ROWS - 1))
                    streams = []
                    for half in range(2):
                        rows = rows_of(2 * rep + half)
                        stream = noise_ref[wafer * wafer_dets + n, rows, :]
                        streams.append(stream - second_sums[wafer][0][group, rows, :])
                    target[0][at] = fold(*streams)
                    for c, ref in ((1, cos_ref), (2, sin_ref)):
                        target[c][at] = fold(*(ref[2 * at + h] * streams[h] for h in range(2)))
            return carry

        over_detectors(one_return, 0)
        merge_twins(target)

    merge_twins(image_map)
    for copy in tod_moves:
        copy.wait()
    sum_streams(lambda at, carry: ([tod_ref[2 * at + half] for half in range(2)], carry), 0)
    filter_streams()
    return_streams(r_map)

    factor = zero
    steps = []
    for iteration, d_map in enumerate(d_maps):
        last = iteration == ITERS - 1

        def seen_streams(at, carry):
            prior, energy = carry
            squares, products = zero, zero
            streams = [None, None]
            for c in range(3):
                residual = r_map[c][at]
                if iteration:
                    part = inverse_ref[c][at] * residual + factor * d_maps[iteration - 1][c][at]
                else:
                    inverse = 1.0 / (image_map[c][at] + prior_weight)
                    inverse_ref[c][at] = inverse
                    part = inverse * residual
                    products = products + residual * part
                d_map[c][at] = part
                squares = squares + part * part
                for half, seen in enumerate(unfold(part)):
                    if c == 0:
                        streams[half] = seen
                    else:
                        ref = cos_ref if c == 1 else sin_ref
                        streams[half] = streams[half] + ref[2 * at + half] * seen
            weight = weight_ref[at]
            if not iteration:
                energy = energy + weight * products
            return streams, (prior + weight * squares, energy)

        prior, first_energy = sum_streams(seen_streams, (zero, zero))
        if not iteration:
            energy = whole_sum(first_energy)
        product = filter_streams()
        return_streams(image_map)
        step = energy / whole_sum(product + prior_weight * prior)
        steps.append(step)

        def new_residual(at, c):
            return r_map[c][at] - step * (image_map[c][at] + prior_weight * d_map[c][at])

        if not last:

            def update(batch, carry):
                found = []
                for k in range(MAP_BATCH):
                    at = batch * MAP_BATCH + k
                    residual = [new_residual(at, c) for c in range(3)]
                    parts = zero
                    for c in range(3):
                        parts = parts + residual[c] * (inverse_ref[c][at] * residual[c])
                    carry = carry + weight_ref[at] * parts
                    found.append((at, residual))
                for at, residual in found:
                    for c in range(3):
                        r_map[c][at] = residual[c]
                return carry

            next_energy = whole_sum(loop(count // MAP_BATCH, update, zero, 2))
            factor = next_energy / energy
            energy = next_energy
        else:

            def place_pixels(at, carry):
                team = lax.rem(lax.div(at, reps * ROWS), dets)
                turn = (3 * (team * ROWS + (at & (ROWS - 1)))) & (PBLOCK - 1)
                inside = (lane & (PBLOCK - 1)) >= turn
                values = []
                for c in range(3):
                    value = steps[0] * d_maps[0][c][at]
                    for k in range(1, ITERS):
                        value = value + steps[k] * d_maps[k][c][at]
                    values.append(value)
                values += [new_residual(at, c) for c in range(3)]
                for c in range(3):
                    left, right = values[2 * c], values[2 * c + 1]
                    halves = (
                        jnp.where(low, left, turn_half(right)), jnp.where(low, turn_half(left), right)
                    )
                    for half, value in enumerate(halves):
                        value = jnp.where(
                            inside, pltpu.roll(value, turn, 1), pltpu.roll(value, turn + PBLOCK, 1)
                        )
                        rows = pl.ds(pl.multiple_of((2 * at + half) * ROWS, ROWS), ROWS)
                        rows_ref[rows, c * LANES : (c + 1) * LANES] = value
                return carry

            loop(count, place_pixels, 0, 8)

    def pick(device, carry):
        for c in range(capacity):
            move = move_ref[device, c]
            source, target = move & ((1 << 16) - 1), move >> 16
            sorted_ref[pl.ds(target, 1), :] = rows_ref[pl.ds(source, 1), :]
        return carry

    lax.fori_loop(0, devices, pick, 0)

    def turn_tile(tile, carry):
        columns = sorted_ref[pl.ds(pl.multiple_of(tile * LANES, LANES), LANES), :].T
        high = columns.astype(jnp.bfloat16)
        column_ref[tile, :, 0:LANES] = high
        column_ref[tile, :, LANES : 2 * LANES] = (columns - high.astype(jnp.float32)).astype(
            jnp.bfloat16
        )
        return carry

    lax.fori_loop(0, column_ref.shape[0], turn_tile, 0)


def write_kernel(start_ref, column_ref, place_ref, x_ref, r_ref, x_buffer, r_buffer, x_sem, r_sem):
    height = 3 * PBLOCK
    width = OUT_TILES * LANES
    steps = x_ref.shape[1] // width
    depth = lax.broadcasted_iota(jnp.int32, (LANES, LANES), 0)

    def copies(step, slot):
        to = pl.ds(pl.multiple_of(step * width, width), width)
        return (
            pltpu.make_async_copy(x_buffer.at[slot], x_ref.at[:, to], x_sem.at[slot]),
            pltpu.make_async_copy(r_buffer.at[slot], r_ref.at[:, to], r_sem.at[slot]),
        )

    def spread(group, tile):
        chosen = []
        for k in range(OUT_TILES):
            place = jnp.broadcast_to(place_ref[pl.ds(group + k, 1), :], (LANES, LANES))
            chosen.append(jnp.where(place == depth + tile * LANES, 1.0, 0.0).astype(jnp.bfloat16))
        chosen = jnp.concatenate(chosen, axis=1)
        chosen = jnp.concatenate([chosen, chosen], axis=0)
        return jnp.dot(column_ref[tile], chosen, preferred_element_type=jnp.float32)

    def one_step(step, carry):
        slot = lax.rem(step, WRITES)

        @pl.when(step >= WRITES)
        def _():
            for copy in copies(step - WRITES, slot):
                copy.wait()

        group = step * OUT_TILES
        start, end = start_ref[0, group], start_ref[0, group + OUT_TILES]
        first = lax.shift_right_logical(start, 7)
        last = lax.shift_right_logical(jnp.maximum(end - 1, start), 7)
        values = spread(group, first)
        x_buffer[slot] = values[:height]
        r_buffer[slot] = values[height:]

        def add_tile(tile, carry):
            values = spread(group, tile)
            x_buffer[slot] += values[:height]
            r_buffer[slot] += values[height:]
            return carry

        lax.fori_loop(first + 1, last + 1, add_tile, 0)
        for copy in copies(step, slot):
            copy.start()
        return carry

    lax.fori_loop(0, steps, one_step, 0)
    for step in range(steps - WRITES, steps):
        for copy in copies(step, step % WRITES):
            copy.wait()


def part_shape(sizes, tod, hit_list, band_lag):
    det_count, time_count = tod.shape[1:]
    owners, capacity = hit_list.shape[3:]
    return (
        sizes["wafer"], sizes["det"], sizes["rep"], time_count // SBLOCK,
        owners, capacity, BLOCKS // owners, band_lag.shape[2],
    ), det_count


def fits_one_device(shape, det_count):
    wafers, dets, reps, tiles, owners, capacity, owner_rows, lag_count = shape
    devices = wafers * dets * reps
    total = devices * tiles * det_count
    groups = owner_rows // LANES
    return (
        det_count == ROWS
        and owners == ROWS
        and tiles * ROWS == LANES
        and tiles == 2 * ROWS
        and (wafers, reps) == (2, 2)
        and (1 + lag_count) * ROWS <= LANES
        and capacity <= LANES
        and devices * capacity % LANES == 0
        and owner_rows % (LANES * OUT_TILES) == 0
        and owner_rows >= LANES * OUT_TILES * WRITES
        and groups + 1 <= 2 * LANES
        and devices % ROWS == 0
        and dets % (DET_BATCH // ROWS) == 0
        and total * total < BIG
    )


def whole_part(shape, tod, psi, point_row, hit_list, group_id, a_zero, band_coef, band_lag):
    wafers, dets, reps, tiles, owners, capacity, owner_rows, lag_count = shape
    devices = wafers * dets * reps
    octets = reps * tiles // ROWS
    detectors = wafers * dets * ROWS
    count = devices * tiles
    total = count * ROWS
    slots = devices * capacity
    height = 3 * PBLOCK
    f32, i32 = jnp.float32, jnp.int32
    vmem, smem = pl.BlockSpec(memory_space=pltpu.VMEM), pl.BlockSpec(memory_space=pltpu.SMEM)
    anywhere = pl.BlockSpec(memory_space=pl.ANY)

    def params(mebibytes):
        return pltpu.CompilerParams(vmem_limit_bytes=mebibytes << 20)

    swap = [(0, 1), (1, 0)]

    def along_det(block):
        moved = [
            lax.ppermute(block, "det", [(i, (i + shift) % dets) for i in range(dets)])
            for shift in range(1, dets)
        ]
        return [block] + moved

    def other_wafer(here):
        return lax.ppermute(here, "wafer", swap)

    def other_rep(here, across):
        return here, across, lax.ppermute(jnp.stack([here, across]), "rep", swap)

    angles, samples = pl.pallas_call(
        functools.partial(pack_kernel, shape),
        out_shape=[
            jax.ShapeDtypeStruct((ROWS + 1, tiles, LANES), f32),
            jax.ShapeDtypeStruct((ROWS, tiles, LANES), f32),
        ],
        in_specs=[vmem] * 8,
        out_specs=[vmem] * 2,
        compiler_params=params(60),
        name="pack",
    )(
        psi[0], tod[0], point_row[0], hit_list[0, 0, 0], group_id, a_zero, band_coef[0].T,
        band_lag[0].T,
    )
    riders = angles.reshape(tiles + 2, ROWS, LANES)
    samples = samples.reshape(tiles, ROWS, LANES)
    place_here = [
        lax.axis_index(axis).astype(i32).reshape(1) for axis in ("wafer", "det", "rep")
    ]
    samples = jnp.stack([samples, other_wafer(samples)])
    blocks = along_det(riders)
    tables = jnp.stack([block[tiles:] for block in blocks])
    angles = jnp.stack([block[:tiles] for block in blocks])
    tables = jnp.stack([tables, other_wafer(tables)])
    tables = lax.all_gather(tables, "rep", axis=0, tiled=False)
    samples, angles, tables = lax.optimization_barrier((samples, angles, tables))
    samples = along_det(samples)
    angles_across = other_wafer(angles)
    table_rows = jax.ShapeDtypeStruct((devices, LANES), i32)
    lists = pl.pallas_call(
        functools.partial(list_kernel, shape),
        out_shape=[
            jax.ShapeDtypeStruct((devices, LANES), f32),
            table_rows,
            jax.ShapeDtypeStruct((2 * LANES, LANES), i32),
            jax.ShapeDtypeStruct((ROWS, 2 * LANES), i32),
            table_rows,
            jax.ShapeDtypeStruct((2,), i32),
            jax.ShapeDtypeStruct((total,), i32),
            jax.ShapeDtypeStruct((total,), i32),
        ],
        in_specs=[smem, smem, anywhere],
        out_specs=[vmem] * 5 + [smem] * 3,
        scratch_shapes=[
            pltpu.VMEM((devices, 2, ROWS, LANES), f32),
            pltpu.VMEM((devices, LANES, LANES), f32),
            pltpu.VMEM((devices, LANES), f32),
            pltpu.VMEM((devices, LANES), f32),
            pltpu.VMEM((devices, LANES), i32),
            pltpu.VMEM((devices, LANES), i32),
            pltpu.VMEM((devices, LANES), i32),
            pltpu.SemaphoreType.DMA((devices,)),
        ],
        compiler_params=params(8),
        cost_estimate=pl.CostEstimate(flops=10**9, bytes_accessed=5 * 10**7, transcendentals=0),
        name="lists",
    )(*place_here[:2], tables)
    angles, angles_across, samples, lists = lax.optimization_barrier(
        (angles, angles_across, samples, lists)
    )
    floats, whole, place, start, moves, size, pair, group = lists
    angle_blocks = other_rep(angles, angles_across)
    samples = jnp.stack(samples)
    sample_blocks = samples, lax.ppermute(samples, "rep", swap)
    stream = pltpu.VMEM((count, ROWS, LANES), f32)
    sky = pltpu.VMEM((devices * ROWS + 1, ROWS, LANES), f32)
    group_sums = pltpu.VMEM((NSUB, octets * ROWS, LANES), f32)
    columns = pl.pallas_call(
        functools.partial(map_kernel, shape),
        out_shape=jax.ShapeDtypeStruct((slots // LANES + 1, 2 * height, 2 * LANES), jnp.bfloat16),
        in_specs=[smem] * 9 + [anywhere] * 5,
        out_specs=vmem,
        scratch_shapes=[
            stream, stream, stream, stream,
            pltpu.VMEM((detectors, octets * ROWS, LANES), f32),
            pltpu.VMEM((detectors, octets * ROWS, LANES), f32),
            sky,
            pltpu.VMEM((wafers * NSUB, ROWS, LANES), f32),
            pltpu.VMEM((total, 2 * height), f32),
            pltpu.VMEM((slots + LANES + ROWS, 2 * height), f32),
            pltpu.SemaphoreType.DMA((devices,)),
            pltpu.SemaphoreType.DMA((devices,)),
        ] + [sky] * (3 * (3 + ITERS)) + [group_sums] * (2 * wafers * SUM_SETS),
        compiler_params=params(30),
        name="map_maker",
    )(
        *place_here, size, pair, group, moves, floats, whole, *angle_blocks,
        *sample_blocks,
    )
    buffers = pltpu.VMEM((WRITES, height, OUT_TILES * LANES), f32)
    x_turned, r_turned = pl.pallas_call(
        write_kernel,
        out_shape=[jax.ShapeDtypeStruct((height, owner_rows), f32)] * 2,
        in_specs=[smem, vmem, vmem],
        out_specs=[anywhere] * 2,
        scratch_shapes=[buffers, buffers] + [pltpu.SemaphoreType.DMA((WRITES,))] * 2,
        compiler_params=params(16),
        name="write",
    )(start, columns, place)
    return x_turned.T, r_turned.T


def local(sizes, *arguments):
    tod, hit_list, band_lag = arguments[0], arguments[3], arguments[7]
    shape, det_count = part_shape(sizes, tod, hit_list, band_lag)
    if fits_one_device(shape, det_count):
        return whole_part(shape, *arguments)
    return distributed(*arguments)


def solution(mesh):
    placed = (
        P(("groups", "wafer"), "det", "rep"),
        P(("groups", "wafer"), "det", "rep"),
        P(("groups", "wafer"), "det", "rep"),
        P(("groups", "wafer"), "det", "rep", None, None),
        P(("groups", "wafer"), "det"),
        P(("groups", "wafer"), "det"),
        P(("groups", "wafer"), "det", None),
        P(("groups", "wafer"), "det", None),
    )
    return jax.shard_map(
        functools.partial(local, mesh.shape),
        mesh=mesh,
        in_specs=placed,
        out_specs=(P(("groups", "det", "wafer"), None), P(("groups", "det", "wafer"), None)),
        check_vma=False,
    )
```

```python
import functools

import jax
import jax.numpy as jnp
from jax import lax
from jax.experimental import pallas as pl
from jax.experimental.pallas import tpu as pltpu
from jax.sharding import PartitionSpec as P

BLOCKS = 196608
PBLOCK = 64
SBLOCK = 128
NSUB = 4
LAG = 16
ITERS = 3


prior_weight = 1.0


def with_halo(block, sides, width):
    for axis, dim in sides:
        count = lax.axis_size(axis)
        forward = [(i, i + 1) for i in range(count - 1)]
        backward = [(target, source) for source, target in forward]
        low = lax.ppermute(
            lax.slice_in_dim(block, block.shape[dim] - width, None, axis=dim), axis, forward
        )
        high = lax.ppermute(lax.slice_in_dim(block, 0, width, axis=dim), axis, backward)
        block = jnp.concatenate([low, block, high], axis=dim)
    return block


def distributed(tod, psi, point_row, hit_list, group_id, a_zero, band_coef, band_lag):
    highest = lax.Precision.HIGHEST
    samples = tod[0]
    angles = psi[0]
    det_count, time_count = samples.shape
    time_blocks = time_count // SBLOCK
    block_count = det_count * time_blocks
    send_table = hit_list[0, 0, 0]
    owner_count, capacity = send_table.shape
    owner_rows = BLOCKS // owner_count
    block_width = 3 * PBLOCK
    detector = lax.axis_index("det") * det_count + jnp.arange(det_count, dtype=jnp.int32)
    within = (jnp.arange(SBLOCK, dtype=jnp.int32)[None, :] + 3 * detector[:, None]) % PBLOCK
    pixel_table = (within[:, :, None] == jnp.arange(PBLOCK, dtype=jnp.int32)[None, None, :]).astype(
        jnp.float32
    )
    cosine_two = jnp.cos(2.0 * angles).reshape(det_count, time_blocks, SBLOCK)
    sine_two = jnp.sin(2.0 * angles).reshape(det_count, time_blocks, SBLOCK)
    slot_ids = send_table.reshape(-1)
    row_source = jnp.concatenate([point_row[0].reshape(-1), jnp.zeros((1,), jnp.int32)])
    slot_rows = row_source[slot_ids].astype(jnp.float32).reshape(owner_count, capacity)
    member = (group_id[0][:, None] == jnp.arange(NSUB, dtype=jnp.int32)[None, :]).astype(
        jnp.float32
    )
    member_count = jnp.sum(member, axis=0)
    lag_table = (
        band_lag[0][:, :, None] == jnp.arange(1, LAG + 1, dtype=jnp.int32)[None, None, :]
    ).astype(jnp.float32)
    lag_weight = jnp.einsum("dj,djl->dl", band_coef[0], lag_table, precision=highest)
    base_weight = a_zero[0]

    def slot_payload(by_block):
        width = by_block.shape[1]
        extended = jnp.concatenate([by_block, jnp.zeros((1, width), by_block.dtype)])
        return extended[slot_ids].reshape(owner_count, capacity, width)

    def deliver(payload):
        width = payload.shape[-1]
        got_values, got_rows = (
            lax.all_to_all(payload, ("det", "wafer"), split_axis=0, concat_axis=0, tiled=True),
            lax.all_to_all(slot_rows, ("det", "wafer"), split_axis=0, concat_axis=0, tiled=True),
        )
        return (got_values, got_rows)

    def back_project(stream, squared):
        shaped = stream.reshape(det_count, time_blocks, SBLOCK)
        first = cosine_two * cosine_two if squared else cosine_two
        second = sine_two * sine_two if squared else sine_two
        stacked = jnp.stack([shaped, first * shaped, second * shaped], axis=2)
        stokes = jnp.einsum("dkcs,dsp->dkcp", stacked, pixel_table, precision=highest)
        return stokes.reshape(block_count, block_width)

    def to_owners(stream, squared):
        got_values, got_rows = deliver(slot_payload(back_project(stream, squared)))
        pair_values, pair_rows = (
            lax.all_gather(got_values, "rep", axis=0, tiled=True),
            lax.all_gather(got_rows, "rep", axis=0, tiled=True),
        )
        target_rows = pair_rows.reshape(-1).astype(jnp.int32)
        summed = (
            jnp.zeros((owner_rows, block_width), jnp.float32)
            .at[target_rows]
            .add(pair_values.reshape(-1, block_width))
        )
        return (summed, got_rows.astype(jnp.int32))

    def remove_common(stream):
        local_sums = jnp.einsum("dg,dt->gt", member, stream, precision=highest)
        group_sums, group_counts = lax.psum((local_sums, member_count), "det")
        group_means = group_sums / jnp.maximum(group_counts, 1.0)[:, None]
        return stream - jnp.einsum("dg,gt->dt", member, group_means, precision=highest)

    def band_filter(stream):
        padded = with_halo(stream, (("rep", 1),), LAG)
        result = base_weight[:, None] * stream
        for offset in range(1, LAG + 1):
            later = padded[:, LAG + offset : LAG + offset + time_count]
            earlier = padded[:, LAG - offset : LAG - offset + time_count]
            result = result + lag_weight[:, offset - 1 : offset] * (later + earlier)
        return result

    def weigh_stream(stream):
        return remove_common(band_filter(remove_common(stream)))

    weight_stream = jnp.broadcast_to(base_weight[:, None], (det_count, time_count))
    diag_sum, serve_rows = to_owners(weight_stream, True)
    inverse_diag = 1.0 / (diag_sum + prior_weight)
    right_side = to_owners(weigh_stream(samples), False)[0]
    solution = jnp.zeros_like(right_side)
    residual = right_side

    def inner(left_map, right_map):
        return lax.psum(jnp.sum(left_map * right_map), ("det", "wafer"))

    precond = inverse_diag * residual
    direction = precond
    energy = inner(residual, precond)
    for iteration in range(ITERS):
        from_blocks = direction[serve_rows.reshape(-1)].reshape(owner_count, capacity, block_width)
        return_width = from_blocks.shape[-1]
        returned = lax.all_to_all(
            from_blocks, ("det", "wafer"), split_axis=0, concat_axis=0, tiled=True
        )
        return_placed = jnp.zeros((block_count + 1, return_width), jnp.float32)
        return_placed = return_placed.at[slot_ids].set(returned.reshape(-1, return_width))
        blocks = return_placed[:block_count].reshape(det_count, time_blocks, 3, PBLOCK)
        project_stokes = jnp.einsum("dkcp,dsp->dkcs", blocks, pixel_table, precision=highest)
        project_stream = (
            project_stokes[:, :, 0]
            + cosine_two * project_stokes[:, :, 1]
            + sine_two * project_stokes[:, :, 2]
        )
        seen_stream = project_stream.reshape(det_count, time_count)
        image_map = to_owners(weigh_stream(seen_stream), False)[0] + prior_weight * direction
        step_size = energy / inner(direction, image_map)
        solution = solution + step_size * direction
        residual = residual - step_size * image_map
        precond = inverse_diag * residual
        energy_next = inner(residual, precond)
        direction = precond + energy_next / energy * direction
        energy = energy_next
    return (solution, residual)


LANES = 128
ROWS = 8
OUT_TILES = 8
PAIR_BATCH = 8
WRITES = 6
DET_BATCH = 16
SUM_SETS = 2
MAP_BATCH = 8
BIG = float(1 << 24)


def wide(values):
    return jnp.broadcast_to(values, (ROWS, LANES))


def tile_iotas():
    lane = lax.broadcasted_iota(jnp.int32, (ROWS, LANES), 1)
    sub = lax.broadcasted_iota(jnp.int32, (ROWS, LANES), 0)
    return lane, sub


def cosine_sine_double(angle):
    turns = jnp.floor(angle * 0.3183098861837907 + 0.5)
    reduced = angle - turns * 3.140625
    reduced = reduced - turns * 9.67653589793e-4
    square = reduced * reduced
    sine = square * -2.5052108385e-8 + 2.7557319224e-6
    sine = sine * square - 1.9841269841e-4
    sine = sine * square + 8.3333333333e-3
    sine = sine * square - 1.6666666667e-1
    sine = sine * square * reduced + reduced
    cosine = square * 2.0876756988e-9 - 2.7557319224e-7
    cosine = cosine * square + 2.4801587302e-5
    cosine = cosine * square - 1.3888888889e-3
    cosine = cosine * square + 4.1666666667e-2
    cosine = cosine * square - 0.5
    cosine = cosine * square + 1.0
    twice = sine + sine
    return 1.0 - twice * sine, twice * cosine


def pack_kernel(
    shape, angle_ref, tod_ref, row_ref, hit_ref, group_ref, base_ref, coef_ref, lag_ref,
    table_ref, angle_rows_ref, tod_rows_ref,
):
    wafers, dets, reps, tiles, owners, capacity, owner_rows, lag_count = shape
    lane, sub = tile_iotas()
    lists = hit_ref[...]
    owner_hits = jnp.zeros((ROWS, LANES), jnp.float32)
    for c in range(capacity):
        owner_hits = owner_hits + jnp.where(wide(lists[:, c : c + 1]) == lane, 1.0, 0.0)
    owner_of = jnp.sum(owner_hits * sub.astype(jnp.float32), axis=0, keepdims=True)

    def spread(values, width):
        return jnp.concatenate(
            [values, jnp.zeros((values.shape[0], LANES - width), values.dtype)], axis=1
        )

    rows = spread(row_ref[...].astype(jnp.float32), tiles)
    ids = owner_of * float(owner_rows) + rows[0:1]
    for k in range(1, ROWS):
        ids = ids + pltpu.roll(rows[k : k + 1], k * tiles, 1)
    floats = spread(base_ref[...], ROWS)
    whole = spread(group_ref[...].astype(jnp.float32), ROWS)
    for j in range(lag_count):
        at = (j + 1) * ROWS
        floats = floats + pltpu.roll(spread(coef_ref[j : j + 1, :], ROWS), at, 1)
        lag = lag_ref[j : j + 1, :].astype(jnp.float32)
        whole = whole + pltpu.roll(spread(lag, ROWS), at, 1)
    table = jnp.where(sub == 0, wide(ids), jnp.where(sub == 1, wide(floats), wide(whole)))
    table_ref[0] = table
    table_ref[1] = spread(lists.astype(jnp.float32), capacity)
    for b in range(tiles):
        angle_rows_ref[:, b, :] = angle_ref[:, b * LANES : (b + 1) * LANES]
        tod_rows_ref[:, b, :] = tod_ref[:, b * LANES : (b + 1) * LANES]


def part_copies(shape, self_ref, source, target, sem):
    wafers, dets, reps = shape[:3]
    copies = []
    for swap_rep in range(reps):
        for swap_wafer in range(wafers):
            for shift in range(dets):
                det = self_ref[1] - shift
                det = jnp.where(det < 0, det + dets, det)
                device = ((self_ref[0] ^ swap_wafer) * dets + det) * reps
                device = device + (self_ref[2] ^ swap_rep)
                copies.append(
                    pltpu.make_async_copy(
                        source(swap_rep, swap_wafer, shift), target(device), sem.at[len(copies)]
                    )
                )
    return copies


def table_copies(shape, self_ref, source_ref, part_ref, sem):
    wafers, dets, reps = shape[:3]
    copies = []
    for swap_wafer in range(wafers):
        for shift in range(dets):
            det = self_ref[1] - shift
            det = jnp.where(det < 0, det + dets, det)
            device = ((self_ref[0] ^ swap_wafer) * dets + det) * reps
            copies.append(
                pltpu.make_async_copy(
                    source_ref.at[swap_wafer, shift], part_ref.at[pl.ds(device, reps)],
                    sem.at[len(copies)],
                )
            )
    for copy in copies:
        copy.start()
    for copy in copies:
        copy.wait()


def exact_dot(left, right, dims=((1,), (0,))):
    return lax.dot_general(
        left.astype(jnp.bfloat16), right.astype(jnp.bfloat16), (dims, ((), ())),
        preferred_element_type=jnp.float32,
    )


def list_kernel(
    shape, wafer_ref, det_ref, table_ref, float_ref, whole_ref, place_ref, start_ref, move_ref,
    size_ref, pair_ref, group_ref,
    part_ref, column_ref, code_ref, lead_ref, used_ref, rank_ref, hits_ref, part_sem,
):
    self_ref = wafer_ref[0], det_ref[0]
    table_copies(shape, self_ref, table_ref, part_ref, part_sem)
    list_twins(
        shape, float_ref, whole_ref, size_ref, pair_ref, group_ref, part_ref, column_ref, code_ref,
        lead_ref, used_ref,
    )
    list_places(shape, self_ref, place_ref, start_ref, move_ref, part_ref, rank_ref, hits_ref)


def list_twins(
    shape, float_ref, whole_ref, size_ref, pair_ref, group_ref, part_ref, column_ref, code_ref,
    lead_ref, used_ref,
):
    wafers, dets, reps, tiles, owners, capacity, owner_rows, lag_count = shape
    devices = wafers * dets * reps
    total = devices * LANES
    lane, sub = tile_iotas()
    sub_f = sub.astype(jnp.float32)
    none = jnp.full((ROWS, LANES), BIG, jnp.float32)
    along = lax.broadcasted_iota(jnp.int32, (1, LANES), 1).astype(jnp.float32)

    def turn(batch, carry):
        for k in range(4):
            device = 4 * batch + k
            float_ref[pl.ds(device, 1), :] = part_ref[device, 0, 1:2, :]
            whole_ref[pl.ds(device, 1), :] = part_ref[device, 0, 2:3, :].astype(jnp.int32)
            column_ref[device] = jnp.broadcast_to(part_ref[device, 0, 0:1, :], (LANES, LANES)).T
        return carry

    lax.fori_loop(0, devices // 4, turn, 0)

    def survey(device, carry):
        row = wide(part_ref[device, 0, 0:1, :])

        def compare(step, least):
            for k in range(2):
                other = 2 * step + k
                found = [none] * 4
                for j in range(tiles):
                    same = column_ref[other, j * ROWS : (j + 1) * ROWS, :] == row
                    at = jnp.where(same, sub_f + float(j * ROWS), BIG)
                    found[j % 4] = jnp.minimum(found[j % 4], at)
                here = jnp.minimum(jnp.minimum(found[0], found[1]), jnp.minimum(found[2], found[3]))
                least = jnp.minimum(least, here + (other * LANES).astype(jnp.float32))
            return least

        least = lax.fori_loop(0, lax.shift_right_logical(device, 1) + 1, compare, none)
        lead = jnp.min(least, axis=0, keepdims=True)
        mine = (device * LANES).astype(jnp.float32) + along
        later = lead < mine
        code_ref[pl.ds(device, 1), :] = jnp.where(later, mine * float(total) + lead, BIG)
        lead_ref[pl.ds(device, 1), :] = jnp.where(later, lead, BIG)
        return carry

    lax.fori_loop(0, devices, survey, 0)

    def next_code(last):
        found = none
        for tile in range(devices // ROWS):
            codes = code_ref[tile * ROWS : (tile + 1) * ROWS, :]
            found = jnp.minimum(found, jnp.where(codes > last, codes, BIG))
        return jnp.min(found)

    def detector(key):
        team = lax.rem(lax.div(key, reps * LANES), dets)
        return team * ROWS + lax.rem(lax.div(key, tiles), ROWS)

    number_of = [lane + (sub + tile * ROWS) * LANES for tile in range(devices // ROWS)]
    tile_rows = [slice(tile * ROWS, (tile + 1) * ROWS) for tile in range(devices // ROWS)]
    for rows in tile_rows:
        used_ref[rows, :] = jnp.zeros((ROWS, LANES), jnp.int32)

    def take(state):
        pairs, grouped, code = state
        number = code.astype(jnp.int32)
        key = lax.div(number, total)
        lead = lax.rem(number, total)
        shift = (3 * (detector(key) - detector(lead))) & (PBLOCK - 1)
        wanted = lead.astype(jnp.float32)
        same = jnp.zeros((ROWS, LANES), jnp.float32)
        for rows, numbers in zip(tile_rows, number_of):
            same = same + jnp.where(lead_ref[rows, :] == wanted, 1.0, 0.0)
            beside = numbers ^ ROWS
            beside = (beside == key) | (beside == lead)
            same = same + jnp.where(beside & (used_ref[rows, :] > 0), 2.0, 0.0)
        alone = jnp.sum(same) + jnp.where((key ^ lead) == ROWS, 2.0, 0.0) < 1.5
        mark = jnp.where(alone, 1, 0)
        for rows, numbers in zip(tile_rows, number_of):
            listed = (numbers == key) | (numbers == lead)
            used_ref[rows, :] = jnp.where(listed, mark, used_ref[rows, :])
        entry = twin_entry(key, lead, shift)
        pair_ref[pairs] = entry
        group_ref[grouped] = entry
        return (
            pairs + jnp.where(alone, 1, 0), grouped + jnp.where(alone, 0, 1), next_code(code)
        )

    pairs, grouped, _ = lax.while_loop(
        lambda state: state[2] < BIG, take,
        (jnp.int32(0), jnp.int32(0), next_code(jnp.float32(-1.0))),
    )
    batches = lax.div(pairs + PAIR_BATCH - 1, PAIR_BATCH)

    def fill(n, carry):
        pair_ref[n] = twin_entry(total, total + 1, 0)
        return carry

    lax.fori_loop(pairs, batches * PAIR_BATCH, fill, 0)
    size_ref[0] = batches
    size_ref[1] = grouped


def twin_entry(key, lead, shift):
    return key * (1 << 19) + lead * (1 << 6) + shift


def twin_of(entry):
    return entry >> 19, (entry >> 6) & ((1 << 13) - 1), entry & (PBLOCK - 1)


def list_places(shape, self_ref, place_ref, start_ref, move_ref, part_ref, rank_ref, hits_ref):
    wafers, dets, reps, tiles, owners, capacity, owner_rows, lag_count = shape
    devices = wafers * dets * reps
    slots = devices * capacity
    lane, sub = tile_iotas()
    own = self_ref[1] * wafers + self_ref[0]
    first_row = (own * owner_rows).astype(jnp.float32)
    depth = 2 * LANES
    tall = lax.broadcasted_iota(jnp.int32, (depth, LANES), 0).astype(jnp.float32)

    def one_hots(device):
        local_row = part_ref[device, 0, 0:1, :] - first_row
        high = jnp.floor(local_row * (1.0 / LANES))
        low = local_row - high * LANES
        high = (jnp.broadcast_to(high, (depth, LANES)) == tall).astype(jnp.float32)
        low = (jnp.broadcast_to(low, (LANES, LANES)) == tall[0:LANES]).astype(jnp.float32)
        return high, low

    def survey(batch, hits):
        for k in range(4):
            device = 4 * batch + k
            own_hits = jnp.where(sub == own, part_ref[device, 1], 0.0)
            own_hits = jnp.sum(own_hits, axis=0, keepdims=True)
            hits_ref[pl.ds(device, 1), :] = own_hits.astype(jnp.int32)
            high, low = one_hots(device)
            hits = hits + exact_dot(high, low, ((1,), (1,)))
        return hits

    hits = lax.fori_loop(0, devices // 4, survey, jnp.zeros((depth, LANES), jnp.float32))
    full = jnp.minimum(hits, 1.0)

    def ordered(size, axis):
        first = lax.broadcasted_iota(jnp.int32, (size, size), axis)
        second = lax.broadcasted_iota(jnp.int32, (size, size), 1 - axis)
        return (first < second).astype(jnp.float32)

    counts = exact_dot(jnp.ones((ROWS, LANES), jnp.float32), full, ((1,), (1,)))
    start_ref[...] = exact_dot(counts, ordered(depth, 0)).astype(jnp.int32)
    sums = exact_dot(full, jnp.ones((LANES, LANES), jnp.float32))
    place = exact_dot(full, ordered(LANES, 0)) + exact_dot(ordered(depth, 1), sums)
    place_ref[...] = jnp.where(full > 0.0, place, -1.0).astype(jnp.int32)
    place_high = jnp.floor(place * (1.0 / LANES))
    place_parts = jnp.concatenate([place_high, place - place_high * LANES], axis=0)

    def rank_of(batch, carry):
        for k in range(4):
            device = 4 * batch + k
            high, low = one_hots(device)
            parts = exact_dot(place_parts, low)
            rank = high * (parts[0:depth] * LANES + parts[depth : 2 * depth])
            rank = jnp.sum(rank, axis=0, keepdims=True)
            rank_ref[pl.ds(device, 1), :] = rank.astype(jnp.int32)
        return carry

    lax.fori_loop(0, devices // 4, rank_of, 0)
    for tile in range(devices // ROWS):
        rows = slice(tile * ROWS, (tile + 1) * ROWS)
        number = hits_ref[rows, :]
        valid = number < LANES
        number = number & (LANES - 1)
        rank = jnp.take_along_axis(rank_ref[rows, :], number, axis=1, mode="promise_in_bounds")
        target = jnp.where(valid, rank, slots + LANES)
        move_ref[rows, :] = target * (1 << 16) + (tile * ROWS + sub) * LANES + number


def map_kernel(
    shape, wafer_ref, det_ref, rep_ref, size_ref, pair_ref, group_ref, move_ref, float_smem, whole_smem,
    angle_here_ref, angle_across_ref, angle_other_ref, tod_here_ref, tod_other_ref, column_ref,
    angle_ref, tod_ref, cos_ref, sin_ref, clean_ref, noise_ref, weight_ref,
    share_ref, rows_ref, sorted_ref, angle_sem, tod_sem, *more_refs,
):
    wafers, dets, reps, tiles, owners, capacity, owner_rows, lag_count = shape
    devices = wafers * dets * reps
    octets = 2 * reps
    wafer_dets = dets * ROWS
    self_ref = wafer_ref[0], det_ref[0], rep_ref[0]
    count = devices * ROWS
    lane, sub = tile_iotas()
    zero = jnp.zeros((ROWS, LANES), jnp.float32)
    low = lane < PBLOCK
    skies = [more_refs[3 * k : 3 * k + 3] for k in range(3 + ITERS)]
    inverse_ref, r_map, image_map, *d_maps = skies
    sum_refs = more_refs[3 * len(skies) :]
    first_sums = [sum_refs[SUM_SETS * wafer : SUM_SETS * (wafer + 1)] for wafer in range(wafers)]
    sum_refs = sum_refs[SUM_SETS * wafers :]
    second_sums = [sum_refs[SUM_SETS * wafer : SUM_SETS * (wafer + 1)] for wafer in range(wafers)]

    def copies_of(source, to_ref, sem):
        return part_copies(
            shape, self_ref, source, lambda d: to_ref.at[pl.ds(d * tiles, tiles)], sem
        )

    def angle_source(swap_rep, swap_wafer, shift):
        if swap_rep:
            return angle_other_ref.at[swap_wafer, shift]
        return (angle_across_ref if swap_wafer else angle_here_ref).at[shift]

    def tod_source(swap_rep, swap_wafer, shift):
        return (tod_other_ref if swap_rep else tod_here_ref).at[shift, swap_wafer]

    angle_moves = copies_of(angle_source, angle_ref, angle_sem)
    tod_moves = copies_of(tod_source, tod_ref, tod_sem)
    for copy in angle_moves + tod_moves:
        copy.start()

    def turn_half(block):
        return pltpu.roll(block, PBLOCK, 1)

    def fold(first, second):
        return jnp.where(low, first, second) + turn_half(jnp.where(low, second, first))

    def unfold(block):
        turned = turn_half(block)
        return jnp.where(low, block, turned), jnp.where(low, turned, block)

    def whole_sum(values):
        values = jnp.sum(values, axis=0, keepdims=True)
        return wide(jnp.sum(values, axis=1, keepdims=True))

    def loop(times, body, carry, unroll):
        def several(n, carry):
            for k in range(unroll):
                carry = body(n * unroll + k, carry)
            return carry

        return lax.fori_loop(0, times // unroll, several, carry)

    def device_of(wafer, n):
        return (wafer * dets + lax.shift_right_logical(n, 3)) * reps

    def group_of(wafer, n):
        return whole_smem[device_of(wafer, n), n & (ROWS - 1)]

    def rows_of(octet):
        return pl.ds(octet * ROWS, ROWS)

    def count_members(n, counts):
        result = []
        for wafer in range(wafers):
            group = group_of(wafer, n)
            result += [
                counts[wafer * NSUB + g] + jnp.where(group == g, 1, 0) for g in range(NSUB)
            ]
        return tuple(result)

    members = lax.fori_loop(0, wafer_dets, count_members, (jnp.int32(0),) * (wafers * NSUB))
    for k, member in enumerate(members):
        share_ref[k] = 1.0 / jnp.maximum(zero + member.astype(jnp.float32), 1.0)
    for c in range(3):
        image_map[c][count] = zero
        r_map[c][count] = zero

    def clear_sorted(n, carry):
        at = pl.ds(pl.multiple_of(n * ROWS, ROWS), ROWS)
        sorted_ref[at, :] = jnp.zeros((ROWS, 6 * PBLOCK), jnp.float32)
        return carry

    lax.fori_loop(0, sorted_ref.shape[0] // ROWS, clear_sorted, 0)

    def spot_of(key):
        return lax.shift_right_logical(key, 4), (key >> 3) & 1, pl.ds(key & (ROWS - 1), 1)

    def in_half(half):
        return (lane[0:1] >> 6) == half

    def set_weight(at, carry):
        weight_ref[at] = zero + 1.0
        return carry

    loop(count, set_weight, 0, 16)

    def drop(list_ref):
        def one(n, carry):
            at, half, row = spot_of(twin_of(list_ref[n])[0])
            weight_ref[at, row, :] = jnp.where(in_half(half), 0.0, weight_ref[at, row, :])
            return carry

        return one

    lax.fori_loop(0, size_ref[0] * PAIR_BATCH, drop(pair_ref), 0)
    lax.fori_loop(0, size_ref[1], drop(group_ref), 0)

    def moved_from(target, spot, shift):
        at, half, row = spot
        result = []
        for ref in target:
            values = wide(ref[at, row, :])
            values = jnp.where((lane >> 6) == half, values, turn_half(values))
            result.append(pltpu.roll(values, shift, 1)[0:1])
        return result

    def merge_twins(target):
        def pair_batch(n, carry):
            found = []
            for k in range(PAIR_BATCH):
                key, lead, shift = twin_of(pair_ref[n * PAIR_BATCH + k])
                key, lead = spot_of(key), spot_of(lead)
                back = (PBLOCK - shift) & (PBLOCK - 1)
                for spot, values in (
                    (lead, moved_from(target, key, shift)), (key, moved_from(target, lead, back))
                ):
                    at, half, row = spot
                    for c in range(3):
                        values[c] = target[c][at, row, :] + jnp.where(in_half(half), values[c], 0.0)
                    found.append((at, row, values))
            for at, row, values in found:
                for c in range(3):
                    target[c][at, row, :] = values[c]
            return carry

        def gather_one(n, carry):
            key, lead, shift = twin_of(group_ref[n])
            values = moved_from(target, spot_of(key), shift)
            at, half, row = spot_of(lead)
            for c in range(3):
                target[c][at, row, :] += jnp.where(in_half(half), values[c], 0.0)
            return carry

        def spread_one(n, carry):
            key, lead, shift = twin_of(group_ref[n])
            values = moved_from(target, spot_of(lead), (PBLOCK - shift) & (PBLOCK - 1))
            at, half, row = spot_of(key)
            for c in range(3):
                target[c][at, row, :] = jnp.where(in_half(half), values[c], target[c][at, row, :])
            return carry

        lax.fori_loop(0, size_ref[0], pair_batch, 0)
        lax.fori_loop(0, size_ref[1], gather_one, 0)
        lax.fori_loop(0, size_ref[1], spread_one, 0)

    for copy in angle_moves:
        copy.wait()

    def survey(at, carry):
        base = float_smem[lax.shift_right_logical(at, 3), at & (ROWS - 1)]
        squares = []
        for half in range(2):
            first, second = cosine_sine_double(angle_ref[2 * at + half])
            cos_ref[2 * at + half] = first
            sin_ref[2 * at + half] = second
            squares.append((base * (first * first), base * (second * second)))
        image_map[0][at] = zero + (base + base)
        for c in range(2):
            image_map[c + 1][at] = fold(squares[0][c], squares[1][c])
        return carry

    loop(count, survey, 0, 8)

    def clear_sums(refs):
        for sets in refs:
            for ref in sets:
                for group in range(NSUB):
                    for octet in range(octets):
                        ref[group, rows_of(octet), :] = zero

    def average(refs):
        for wafer, sets in enumerate(refs):
            for group in range(NSUB):
                for octet in range(octets):
                    total = sets[0][group, rows_of(octet), :]
                    for ref in sets[1:]:
                        total = total + ref[group, rows_of(octet), :]
                    sets[0][group, rows_of(octet), :] = total * share_ref[wafer * NSUB + group]

    def over_detectors(body, carry):
        def several(step, carry):
            for k in range(DET_BATCH):
                carry = body(step * DET_BATCH + k, k % SUM_SETS, carry)
            return carry

        return lax.fori_loop(0, wafer_dets // DET_BATCH, several, carry)

    def sum_streams(streams_of, carry):
        clear_sums(first_sums)

        def one_detector(n, part, carry):
            for wafer in range(wafers):
                group = group_of(wafer, n)
                for rep in range(reps):
                    at = (device_of(wafer, n) + rep) * ROWS + (n & (ROWS - 1))
                    streams, carry = streams_of(at, carry)
                    for half, stream in enumerate(streams):
                        rows = rows_of(2 * rep + half)
                        clean_ref[wafer * wafer_dets + n, rows, :] = stream
                        first_sums[wafer][part][group, rows, :] += stream
            return carry

        carry = over_detectors(one_detector, carry)
        average(first_sums)
        return carry

    def filter_streams():
        clear_sums(second_sums)

        def one_filter(n, part, carry):
            for wafer in range(wafers):
                device, inside = device_of(wafer, n), n & (ROWS - 1)
                detector = wafer * wafer_dets + n
                group = group_of(wafer, n)
                base = float_smem[device, inside]
                coefs = [float_smem[device, (j + 1) * ROWS + inside] for j in range(lag_count)]
                lags = [whole_smem[device, (j + 1) * ROWS + inside] for j in range(lag_count)]
                clean = [
                    clean_ref[detector, rows_of(octet), :]
                    - first_sums[wafer][0][group, rows_of(octet), :]
                    for octet in range(octets)
                ]
                up = [pltpu.roll(here, ROWS - 1, 0) for here in clean] + [zero]
                down = [zero] + [pltpu.roll(here, 1, 0) for here in clean]
                for octet, here in enumerate(clean):
                    after = jnp.where(sub == ROWS - 1, up[octet + 1], up[octet])
                    ahead = jnp.where(sub == 0, down[octet], down[octet + 1])
                    result = base * here
                    for coef, lag in zip(coefs, lags):
                        later = pltpu.roll(jnp.where(lane < lag, after, here), LANES - lag, 1)
                        earlier = pltpu.roll(jnp.where(lane >= LANES - lag, ahead, here), lag, 1)
                        result = result + coef * (later + earlier)
                    noise_ref[detector, rows_of(octet), :] = result
                    second_sums[wafer][part][group, rows_of(octet), :] += result
                    carry = carry + here * result
            return carry

        product = over_detectors(one_filter, zero)
        average(second_sums)
        return product

    def return_streams(target):
        def one_return(n, part, carry):
            for wafer in range(wafers):
                group = group_of(wafer, n)
                for rep in range(reps):
                    at = (device_of(wafer, n) + rep) * ROWS + (n & (ROWS - 1))
                    streams = []
                    for half in range(2):
                        rows = rows_of(2 * rep + half)
                        stream = noise_ref[wafer * wafer_dets + n, rows, :]
                        streams.append(stream - second_sums[wafer][0][group, rows, :])
                    target[0][at] = fold(*streams)
                    for c, ref in ((1, cos_ref), (2, sin_ref)):
                        target[c][at] = fold(*(ref[2 * at + h] * streams[h] for h in range(2)))
            return carry

        over_detectors(one_return, 0)
        merge_twins(target)

    merge_twins(image_map)
    for copy in tod_moves:
        copy.wait()
    sum_streams(lambda at, carry: ([tod_ref[2 * at + half] for half in range(2)], carry), 0)
    filter_streams()
    return_streams(r_map)

    factor = zero
    steps = []
    for iteration, d_map in enumerate(d_maps):
        last = iteration == ITERS - 1

        def seen_streams(at, carry):
            prior, energy = carry
            squares, products = zero, zero
            streams = [None, None]
            for c in range(3):
                residual = r_map[c][at]
                if iteration:
                    part = inverse_ref[c][at] * residual + factor * d_maps[iteration - 1][c][at]
                else:
                    inverse = 1.0 / (image_map[c][at] + prior_weight)
                    inverse_ref[c][at] = inverse
                    part = inverse * residual
                    products = products + residual * part
                d_map[c][at] = part
                squares = squares + part * part
                for half, seen in enumerate(unfold(part)):
                    if c == 0:
                        streams[half] = seen
                    else:
                        ref = cos_ref if c == 1 else sin_ref
                        streams[half] = streams[half] + ref[2 * at + half] * seen
            weight = weight_ref[at]
            if not iteration:
                energy = energy + weight * products
            return streams, (prior + weight * squares, energy)

        prior, first_energy = sum_streams(seen_streams, (zero, zero))
        if not iteration:
            energy = whole_sum(first_energy)
        product = filter_streams()
        return_streams(image_map)
        step = energy / whole_sum(product + prior_weight * prior)
        steps.append(step)

        def new_residual(at, c):
            return r_map[c][at] - step * (image_map[c][at] + prior_weight * d_map[c][at])

        if not last:

            def update(batch, carry):
                found = []
                for k in range(MAP_BATCH):
                    at = batch * MAP_BATCH + k
                    residual = [new_residual(at, c) for c in range(3)]
                    parts = zero
                    for c in range(3):
                        parts = parts + residual[c] * (inverse_ref[c][at] * residual[c])
                    carry = carry + weight_ref[at] * parts
                    found.append((at, residual))
                for at, residual in found:
                    for c in range(3):
                        r_map[c][at] = residual[c]
                return carry

            next_energy = whole_sum(loop(count // MAP_BATCH, update, zero, 2))
            factor = next_energy / energy
            energy = next_energy
        else:

            def place_pixels(at, carry):
                team = lax.rem(lax.div(at, reps * ROWS), dets)
                turn = (3 * (team * ROWS + (at & (ROWS - 1)))) & (PBLOCK - 1)
                inside = (lane & (PBLOCK - 1)) >= turn
                values = []
                for c in range(3):
                    value = steps[0] * d_maps[0][c][at]
                    for k in range(1, ITERS):
                        value = value + steps[k] * d_maps[k][c][at]
                    values.append(value)
                values += [new_residual(at, c) for c in range(3)]
                for c in range(3):
                    left, right = values[2 * c], values[2 * c + 1]
                    halves = (
                        jnp.where(low, left, turn_half(right)), jnp.where(low, turn_half(left), right)
                    )
                    for half, value in enumerate(halves):
                        value = jnp.where(
                            inside, pltpu.roll(value, turn, 1), pltpu.roll(value, turn + PBLOCK, 1)
                        )
                        rows = pl.ds(pl.multiple_of((2 * at + half) * ROWS, ROWS), ROWS)
                        rows_ref[rows, c * LANES : (c + 1) * LANES] = value
                return carry

            loop(count, place_pixels, 0, 8)

    def pick(device, carry):
        for c in range(capacity):
            move = move_ref[device, c]
            source, target = move & ((1 << 16) - 1), move >> 16
            sorted_ref[pl.ds(target, 1), :] = rows_ref[pl.ds(source, 1), :]
        return carry

    lax.fori_loop(0, devices, pick, 0)

    def turn_tile(tile, carry):
        columns = sorted_ref[pl.ds(pl.multiple_of(tile * LANES, LANES), LANES), :].T
        high = columns.astype(jnp.bfloat16)
        column_ref[tile, :, 0:LANES] = high
        column_ref[tile, :, LANES : 2 * LANES] = (columns - high.astype(jnp.float32)).astype(
            jnp.bfloat16
        )
        return carry

    lax.fori_loop(0, column_ref.shape[0], turn_tile, 0)


def write_kernel(start_ref, column_ref, place_ref, x_ref, r_ref, x_buffer, r_buffer, x_sem, r_sem):
    height = 3 * PBLOCK
    width = OUT_TILES * LANES
    steps = x_ref.shape[1] // width
    depth = lax.broadcasted_iota(jnp.int32, (LANES, LANES), 0)

    def copies(step, slot):
        to = pl.ds(pl.multiple_of(step * width, width), width)
        return (
            pltpu.make_async_copy(x_buffer.at[slot], x_ref.at[:, to], x_sem.at[slot]),
            pltpu.make_async_copy(r_buffer.at[slot], r_ref.at[:, to], r_sem.at[slot]),
        )

    def spread(group, tile):
        chosen = []
        for k in range(OUT_TILES):
            place = jnp.broadcast_to(place_ref[pl.ds(group + k, 1), :], (LANES, LANES))
            chosen.append(jnp.where(place == depth + tile * LANES, 1.0, 0.0).astype(jnp.bfloat16))
        chosen = jnp.concatenate(chosen, axis=1)
        chosen = jnp.concatenate([chosen, chosen], axis=0)
        return jnp.dot(column_ref[tile], chosen, preferred_element_type=jnp.float32)

    def one_step(step, carry):
        slot = lax.rem(step, WRITES)

        @pl.when(step >= WRITES)
        def _():
            for copy in copies(step - WRITES, slot):
                copy.wait()

        group = step * OUT_TILES
        start, end = start_ref[0, group], start_ref[0, group + OUT_TILES]
        first = lax.shift_right_logical(start, 7)
        last = lax.shift_right_logical(jnp.maximum(end - 1, start), 7)
        values = spread(group, first)
        x_buffer[slot] = values[:height]
        r_buffer[slot] = values[height:]

        def add_tile(tile, carry):
            values = spread(group, tile)
            x_buffer[slot] += values[:height]
            r_buffer[slot] += values[height:]
            return carry

        lax.fori_loop(first + 1, last + 1, add_tile, 0)
        for copy in copies(step, slot):
            copy.start()
        return carry

    lax.fori_loop(0, steps, one_step, 0)
    for step in range(steps - WRITES, steps):
        for copy in copies(step, step % WRITES):
            copy.wait()


def part_shape(sizes, tod, hit_list, band_lag):
    det_count, time_count = tod.shape[1:]
    owners, capacity = hit_list.shape[3:]
    return (
        sizes["wafer"], sizes["det"], sizes["rep"], time_count // SBLOCK,
        owners, capacity, BLOCKS // owners, band_lag.shape[2],
    ), det_count


def fits_one_device(shape, det_count):
    wafers, dets, reps, tiles, owners, capacity, owner_rows, lag_count = shape
    devices = wafers * dets * reps
    total = devices * tiles * det_count
    groups = owner_rows // LANES
    return (
        det_count == ROWS
        and owners == ROWS
        and tiles * ROWS == LANES
        and tiles == 2 * ROWS
        and (wafers, reps) == (2, 2)
        and (1 + lag_count) * ROWS <= LANES
        and capacity <= LANES
        and devices * capacity % LANES == 0
        and owner_rows % (LANES * OUT_TILES) == 0
        and owner_rows >= LANES * OUT_TILES * WRITES
        and groups + 1 <= 2 * LANES
        and devices % ROWS == 0
        and dets % (DET_BATCH // ROWS) == 0
        and total * total < BIG
    )


def whole_part(shape, tod, psi, point_row, hit_list, group_id, a_zero, band_coef, band_lag):
    wafers, dets, reps, tiles, owners, capacity, owner_rows, lag_count = shape
    devices = wafers * dets * reps
    octets = reps * tiles // ROWS
    detectors = wafers * dets * ROWS
    count = devices * tiles
    total = count * ROWS
    slots = devices * capacity
    height = 3 * PBLOCK
    f32, i32 = jnp.float32, jnp.int32
    vmem, smem = pl.BlockSpec(memory_space=pltpu.VMEM), pl.BlockSpec(memory_space=pltpu.SMEM)
    anywhere = pl.BlockSpec(memory_space=pl.ANY)

    def params(mebibytes):
        return pltpu.CompilerParams(vmem_limit_bytes=mebibytes << 20)

    swap = [(0, 1), (1, 0)]

    def along_det(block):
        moved = [
            lax.ppermute(block, "det", [(i, (i + shift) % dets) for i in range(dets)])
            for shift in range(1, dets)
        ]
        return [block] + moved

    def other_wafer(here):
        return lax.ppermute(here, "wafer", swap)

    def other_rep(here, across):
        return here, across, lax.ppermute(jnp.stack([here, across]), "rep", swap)

    tables, angles, samples = pl.pallas_call(
        functools.partial(pack_kernel, shape),
        out_shape=[
            jax.ShapeDtypeStruct((2, ROWS, LANES), f32),
            jax.ShapeDtypeStruct((ROWS, tiles, LANES), f32),
            jax.ShapeDtypeStruct((ROWS, tiles, LANES), f32),
        ],
        in_specs=[vmem] * 8,
        out_specs=[vmem] * 3,
        compiler_params=params(60),
        name="pack",
    )(
        psi[0], tod[0], point_row[0], hit_list[0, 0, 0], group_id, a_zero, band_coef[0].T,
        band_lag[0].T,
    )
    angles, samples = (stream.reshape(tiles, ROWS, LANES) for stream in (angles, samples))
    place_here = [
        lax.axis_index(axis).astype(i32).reshape(1) for axis in ("wafer", "det", "rep")
    ]
    tables = lax.all_gather(tables, "rep", axis=0, tiled=False)
    riders = jnp.concatenate([angles, tables.reshape(2 * reps, ROWS, LANES)])
    samples, riders = lax.optimization_barrier((samples, riders))
    samples = jnp.stack([samples, other_wafer(samples)])
    samples, *blocks = lax.optimization_barrier((samples, *along_det(riders)))
    samples = along_det(samples)
    tables = jnp.stack([block[tiles:] for block in blocks])
    angles = jnp.stack([block[:tiles] for block in blocks])
    tables = jnp.stack([tables, other_wafer(tables)])
    tables = tables.reshape(wafers, dets, reps, 2, ROWS, LANES)
    angles, tables = lax.optimization_barrier((angles, tables))
    angles_across = other_wafer(angles)
    table_rows = jax.ShapeDtypeStruct((devices, LANES), i32)
    lists = pl.pallas_call(
        functools.partial(list_kernel, shape),
        out_shape=[
            jax.ShapeDtypeStruct((devices, LANES), f32),
            table_rows,
            jax.ShapeDtypeStruct((2 * LANES, LANES), i32),
            jax.ShapeDtypeStruct((ROWS, 2 * LANES), i32),
            table_rows,
            jax.ShapeDtypeStruct((2,), i32),
            jax.ShapeDtypeStruct((total,), i32),
            jax.ShapeDtypeStruct((total,), i32),
        ],
        in_specs=[smem, smem, anywhere],
        out_specs=[vmem] * 5 + [smem] * 3,
        scratch_shapes=[
            pltpu.VMEM((devices, 2, ROWS, LANES), f32),
            pltpu.VMEM((devices, LANES, LANES), f32),
            pltpu.VMEM((devices, LANES), f32),
            pltpu.VMEM((devices, LANES), f32),
            pltpu.VMEM((devices, LANES), i32),
            pltpu.VMEM((devices, LANES), i32),
            pltpu.VMEM((devices, LANES), i32),
            pltpu.SemaphoreType.DMA((devices,)),
        ],
        compiler_params=params(8),
        cost_estimate=pl.CostEstimate(flops=10**9, bytes_accessed=5 * 10**7, transcendentals=0),
        name="lists",
    )(*place_here[:2], tables)
    angles, angles_across, samples, lists = lax.optimization_barrier(
        (angles, angles_across, samples, lists)
    )
    floats, whole, place, start, moves, size, pair, group = lists
    angle_blocks = other_rep(angles, angles_across)
    samples = jnp.stack(samples)
    sample_blocks = samples, lax.ppermute(samples, "rep", swap)
    stream = pltpu.VMEM((count, ROWS, LANES), f32)
    sky = pltpu.VMEM((devices * ROWS + 1, ROWS, LANES), f32)
    group_sums = pltpu.VMEM((NSUB, octets * ROWS, LANES), f32)
    columns = pl.pallas_call(
        functools.partial(map_kernel, shape),
        out_shape=jax.ShapeDtypeStruct((slots // LANES + 1, 2 * height, 2 * LANES), jnp.bfloat16),
        in_specs=[smem] * 9 + [anywhere] * 5,
        out_specs=vmem,
        scratch_shapes=[
            stream, stream, stream, stream,
            pltpu.VMEM((detectors, octets * ROWS, LANES), f32),
            pltpu.VMEM((detectors, octets * ROWS, LANES), f32),
            sky,
            pltpu.VMEM((wafers * NSUB, ROWS, LANES), f32),
            pltpu.VMEM((total, 2 * height), f32),
            pltpu.VMEM((slots + LANES + ROWS, 2 * height), f32),
            pltpu.SemaphoreType.DMA((devices,)),
            pltpu.SemaphoreType.DMA((devices,)),
        ] + [sky] * (3 * (3 + ITERS)) + [group_sums] * (2 * wafers * SUM_SETS),
        compiler_params=params(30),
        name="map_maker",
    )(
        *place_here, size, pair, group, moves, floats, whole, *angle_blocks,
        *sample_blocks,
    )
    buffers = pltpu.VMEM((WRITES, height, OUT_TILES * LANES), f32)
    x_turned, r_turned = pl.pallas_call(
        write_kernel,
        out_shape=[jax.ShapeDtypeStruct((height, owner_rows), f32)] * 2,
        in_specs=[smem, vmem, vmem],
        out_specs=[anywhere] * 2,
        scratch_shapes=[buffers, buffers] + [pltpu.SemaphoreType.DMA((WRITES,))] * 2,
        compiler_params=params(16),
        name="write",
    )(start, columns, place)
    return x_turned.T, r_turned.T


def local(sizes, *arguments):
    tod, hit_list, band_lag = arguments[0], arguments[3], arguments[7]
    shape, det_count = part_shape(sizes, tod, hit_list, band_lag)
    if fits_one_device(shape, det_count):
        return whole_part(shape, *arguments)
    return distributed(*arguments)


def solution(mesh):
    placed = (
        P(("groups", "wafer"), "det", "rep"),
        P(("groups", "wafer"), "det", "rep"),
        P(("groups", "wafer"), "det", "rep"),
        P(("groups", "wafer"), "det", "rep", None, None),
        P(("groups", "wafer"), "det"),
        P(("groups", "wafer"), "det"),
        P(("groups", "wafer"), "det", None),
        P(("groups", "wafer"), "det", None),
    )
    return jax.shard_map(
        functools.partial(local, mesh.shape),
        mesh=mesh,
        in_specs=placed,
        out_specs=(P(("groups", "det", "wafer"), None), P(("groups", "det", "wafer"), None)),
        check_vma=False,
    )
```
